32 devices in a mesh: dp: 16 (over z, y, x), ctx: 2 (over core).
Axes of the slice: x: 2, y: 2, z: 4, core: 2. Of those that a mesh axis runs over, the one named last changes fastest.
Arguments:
- tokens: bfloat16 [16, 256, 1152], P('dp', 'ctx'), may hold values from -6 to 6
- cotangent: bfloat16 [16, 256, 1152], P('dp', 'ctx'), may hold values from -6 to 6
- segment: int32 [16, 256], P('dp'), may hold values from 0 to 3, as said below
- rows: int32 [16, 256], P('dp'), may hold values from 0 to 31, as said below
- columns: int32 [16, 256], P('dp'), may hold values from 0 to 7, as said below
- padding: int32 [16, 256], P('dp'), may hold values from 0 to 1, as said below
- timesteps: int32 [16, 4], P('dp'), may hold values from 0 to 999
- encoder_modulate: bfloat16 [1152, 6912], P('dp'), may hold values from -0.1875 to 0.1875
- encoder_offset: bfloat16 [6912], P('dp'), may hold values from -3 to 3
- encoder_triple: bfloat16 [1152, 3456], P('dp'), may hold values from -0.1875 to 0.1875
- encoder_gains: bfloat16 [2, 1152], P(None, 'dp'), may hold values from 0.25 to 1.75
- encoder_mixing: bfloat16 [1152, 1152], P('dp'), may hold values from -1.5 to 1.5
- encoder_expand: bfloat16 [1152, 6144], P('dp'), may hold values from -0.1875 to 0.1875
- encoder_reduce: bfloat16 [3072, 1152], P('dp'), may hold values from -0.109375 to 0.109375
- decoder_modulate: bfloat16 [1152, 6912], P('dp'), may hold values from -0.1875 to 0.1875
- decoder_offset: bfloat16 [6912], P('dp'), may hold values from -3 to 3
- decoder_triple: bfloat16 [1152, 3456], P('dp'), may hold values from -0.1875 to 0.1875
- decoder_gains: bfloat16 [2, 1152], P(None, 'dp'), may hold values from 0.25 to 1.75
- decoder_mixing: bfloat16 [1152, 1152], P('dp'), may hold values from -1.5 to 1.5
- decoder_expand: bfloat16 [1152, 6144], P('dp'), may hold values from -0.1875 to 0.1875
- decoder_reduce: bfloat16 [3072, 1152], P('dp'), may hold values from -0.109375 to 0.109375
Outputs:
- velocity: bfloat16 [16, 256, 1152], P('dp', 'ctx')
- latent: bfloat16 [16, 256, 1152], P('dp', 'ctx')
- token_grad: float32 [16, 256, 1152], P('dp', 'ctx')
- encoder_modulate_grad: float32 [1152, 6912], P('dp')
- encoder_offset_grad: float32 [6912], P('dp')
- encoder_triple_grad: float32 [1152, 3456], P('dp')
- encoder_gains_grad: float32 [2, 1152], P(None, 'dp')
- encoder_mixing_grad: float32 [1152, 1152], P('dp')
- encoder_expand_grad: float32 [1152, 6144], P('dp')
- encoder_reduce_grad: float32 [3072, 1152], P('dp')
- decoder_modulate_grad: float32 [1152, 6912], P('dp')
- decoder_offset_grad: float32 [6912], P('dp')
- decoder_triple_grad: float32 [1152, 3456], P('dp')
- decoder_gains_grad: float32 [2, 1152], P(None, 'dp')
- decoder_mixing_grad: float32 [1152, 1152], P('dp')
- decoder_expand_grad: float32 [1152, 6144], P('dp')
- decoder_reduce_grad: float32 [3072, 1152], P('dp')
The draws below stay inside these ranges and needn't reach their ends.
Inputs may be any that keep to these rules, and one draw needn't show every extreme that they name: `segment`: each sequence holds image 0 from slot 0, then image 1, then image 2 (which may be empty), each a full rectangle of patches in row-major order of width 2 to 8; all later slots are padding with number 3, at least one in each sequence. Image 1 covers slots 256/2 - 1 and 128. `rows`: row of the slot's patch in its image; 0 on padding. `columns`: column of the slot's patch in its image; 0 on padding. `padding`: 1 exactly where segment is 3.
All inputs are finite; a program needn't handle non-finite values.
Results may differ from the reference program's by a relative error of at most 0.04.
Values may be sent and summed in bfloat16 or wider, within the bound.
A program may use at most 576 MiB of HBM per device.

```python
import math
import jax
import jax.numpy as jnp
from jax import lax

D = 1152
HEADS = 16
HD = 72
FF = 3072
SLOTS = 256
SEGS = 4
SEQUENCES = 16


def packing(key):
    keys = jax.random.split(key, 6)
    quarter = SLOTS // 4
    first = jnp.arange(SEQUENCES, dtype=jnp.int32) == 0
    width_a = jnp.where(first, 2, jax.random.randint(keys[0], (SEQUENCES,), 2, 5, dtype=jnp.int32))
    height_drawn = jax.random.randint(keys[1], (SEQUENCES,), 1, quarter // width_a + 1, dtype=jnp.int32)
    height_a = jnp.where(first, quarter // 2, height_drawn)
    length_a = width_a * height_a
    width_b = jnp.where(first, 8, jax.random.randint(keys[2], (SEQUENCES,), 7, 9, dtype=jnp.int32))
    height_b = (SLOTS // 2 - length_a) // width_b + 1 + jax.random.randint(keys[3], (SEQUENCES,), 0, quarter // width_b, dtype=jnp.int32)
    end_b = length_a + width_b * height_b
    remain = SLOTS - end_b
    width_c = jax.random.randint(keys[4], (SEQUENCES,), 6, 9, dtype=jnp.int32)
    height_c = jax.random.randint(keys[5], (SEQUENCES,), 0, (remain - 1) // width_c + 1, dtype=jnp.int32)
    end_c = end_b + width_c * height_c
    place = jnp.arange(SLOTS, dtype=jnp.int32)[None, :]
    segment = (place >= length_a[:, None]).astype(jnp.int32) + (place >= end_b[:, None]).astype(jnp.int32) + (place >= end_c[:, None]).astype(jnp.int32)
    begin = jnp.where(segment == 0, 0, jnp.where(segment == 1, length_a[:, None], jnp.where(segment == 2, end_b[:, None], end_c[:, None])))
    widths = jnp.where(segment == 0, width_a[:, None], jnp.where(segment == 1, width_b[:, None], jnp.where(segment == 2, width_c[:, None], 1)))
    local = place - begin
    rows = jnp.where(segment < 3, local // widths, 0)
    columns = jnp.where(segment < 3, local % widths, 0)
    padding = (segment == 3).astype(jnp.int32)
    return (segment, rows, columns, padding)


def draw_segment(key, part):
    shared = packing(key)
    return shared[0]


def draw_rows(key, part):
    shared = packing(key)
    return shared[1]


def draw_columns(key, part):
    shared = packing(key)
    return shared[2]


def draw_padding(key, part):
    shared = packing(key)
    return shared[3]


def touch_ends(values, key, low, largest):
    extent = values.shape
    spot = [jax.random.randint(jax.random.fold_in(key, axis), (), 0, extent[axis]) for axis in range(len(extent))]
    values = values.at[tuple(spot)].set(low)
    longest = extent.index(max(extent))
    spot[longest] = (spot[longest] + 1) % extent[longest]
    return values.at[tuple(spot)].set(largest)


def levels(key, dims, shards, least, largest):
    level = 1.0
    for dim, parts in shards:
        draws = jax.random.uniform(jax.random.fold_in(jax.random.fold_in(key, 6), dim), (parts,), jnp.float32, least / len(shards), largest / len(shards))
        level = level * jnp.repeat(jnp.exp(draws), dims[dim] // parts).reshape((-1,) + (1,) * (len(dims) - 1 - dim))
    return level


def bell_draw(stream_key, extent, scale, bound, pieces=(), kind=jnp.bfloat16):
    values = jax.random.normal(stream_key, extent, jnp.float32) * scale
    if len(pieces) > 0:
        values = levels(stream_key, extent, pieces, -0.22, 0.18) * values
    return jnp.clip(values, min=-bound, max=bound).astype(kind)


def setup_inputs(seed: int = 0) -> dict:
    splits = jax.random.split(jax.random.key(seed), 22)
    tokens = bell_draw(splits[0], (SEQUENCES, SLOTS, D), 1.0, 6.0, ((0, 16), (1, 2)))
    cotangent = bell_draw(splits[1], (SEQUENCES, SLOTS, D), 1.0, 6.0, ((0, 16), (1, 2)))
    segment = draw_segment(jax.random.fold_in(splits[21], 71), 0)
    rows = draw_rows(jax.random.fold_in(splits[21], 71), 0)
    columns = draw_columns(jax.random.fold_in(splits[21], 71), 0)
    padding = draw_padding(jax.random.fold_in(splits[21], 71), 0)
    timesteps = touch_ends(jax.random.randint(splits[6], (SEQUENCES, SEGS), 0, 1000), jax.random.fold_in(splits[6], 1), 0, 999).astype(jnp.int32)
    encoder_modulate = bell_draw(splits[7], (D, 6 * D), D ** -0.5, 0.1875, ((0, 16),))
    encoder_offset = bell_draw(splits[8], (6 * D,), 0.5, 3.0, ((0, 16),))
    encoder_triple = bell_draw(splits[9], (D, 3 * D), D ** -0.5, 0.1875, ((0, 16),))
    encoder_gains = jnp.clip(1.0 + 0.15 * jax.random.normal(splits[10], (2, D), jnp.float32), 0.25, 1.75).astype(jnp.bfloat16)
    encoder_mixing = bell_draw(splits[11], (D, D), (D // 64) ** -0.5, 1.5, ((0, 16),))
    encoder_expand = bell_draw(splits[12], (D, 2 * FF), D ** -0.5, 0.1875, ((0, 16),))
    encoder_reduce = bell_draw(splits[13], (FF, D), FF ** -0.5, 0.109375, ((0, 16),))
    decoder_modulate = bell_draw(splits[14], (D, 6 * D), D ** -0.5, 0.1875, ((0, 16),))
    decoder_offset = bell_draw(splits[15], (6 * D,), 0.5, 3.0, ((0, 16),))
    decoder_triple = bell_draw(splits[16], (D, 3 * D), D ** -0.5, 0.1875, ((0, 16),))
    decoder_gains = jnp.clip(1.0 + 0.15 * jax.random.normal(splits[17], (2, D), jnp.float32), 0.25, 1.75).astype(jnp.bfloat16)
    decoder_mixing = bell_draw(splits[18], (D, D), (D // 64) ** -0.5, 1.5, ((0, 16),))
    decoder_expand = bell_draw(splits[19], (D, 2 * FF), D ** -0.5, 0.1875, ((0, 16),))
    decoder_reduce = bell_draw(splits[20], (FF, D), FF ** -0.5, 0.109375, ((0, 16),))
    return {"tokens": tokens, "cotangent": cotangent, "segment": segment, "rows": rows, "columns": columns, "padding": padding, "timesteps": timesteps, "encoder_modulate": encoder_modulate, "encoder_offset": encoder_offset, "encoder_triple": encoder_triple, "encoder_gains": encoder_gains, "encoder_mixing": encoder_mixing, "encoder_expand": encoder_expand, "encoder_reduce": encoder_reduce, "decoder_modulate": decoder_modulate, "decoder_offset": decoder_offset, "decoder_triple": decoder_triple, "decoder_gains": decoder_gains, "decoder_mixing": decoder_mixing, "decoder_expand": decoder_expand, "decoder_reduce": decoder_reduce}


@jax.custom_vjp
def low(v):
    return lax.optimization_barrier(v.astype(jnp.bfloat16)).astype(jnp.float32)

@jax.custom_vjp
def low_back(v):
    return v

def low_keep(v):
    return (low(v), None)

def low_pass(kept, grad):
    return (grad,)

def back_keep(v):
    return (v, None)

def back_low(kept, grad):
    return (low(grad),)
low.defvjp(low_keep, low_pass)
low_back.defvjp(back_keep, back_low)
exact = lax.Precision.HIGHEST

def product(left, right):
    return jnp.dot(left, right, precision=exact)

def layer_norm(values):
    center = values - lax.optimization_barrier(jnp.mean(values, axis=-1, keepdims=True))
    spread = lax.optimization_barrier(jnp.mean(center * center, axis=-1, keepdims=True))
    return center * lax.rsqrt(spread + 1e-06)

def head_norm(values, gain):
    shaped = values.reshape(values.shape[:-1] + (HEADS, HD))
    scaled = shaped * lax.rsqrt(lax.optimization_barrier(jnp.mean(shaped * shaped, axis=-1, keepdims=True)) + 1e-06)
    return scaled * gain.reshape(HEADS, HD)

def rope_tables(rows, columns):
    quarter = HD // 4
    freqs = jnp.exp(jnp.arange(quarter, dtype=jnp.float32) * (-math.log(10000.0) / quarter))
    places = jnp.stack([rows, columns], axis=-1).astype(jnp.float32)
    angles = places[..., None] * freqs
    return (jnp.cos(angles), jnp.sin(angles))

def rotate(values, cosine, sine):
    shaped = values.reshape(values.shape[:-1] + (2, 2, HD // 4))
    first = shaped[..., 0, :]
    second = shaped[..., 1, :]
    cosine = cosine[..., None, :, :]
    sine = sine[..., None, :, :]
    turned = jnp.stack([first * cosine - second * sine, first * sine + second * cosine], axis=-2)
    return turned.reshape(values.shape)

def time_embed(timesteps, segment, width):
    half_width = width // 2
    freqs = jnp.exp(jnp.arange(half_width, dtype=jnp.float32) * (-math.log(10000.0) / half_width))
    picks = (segment[..., None] == jnp.arange(timesteps.shape[-1], dtype=jnp.int32)).astype(jnp.float32)
    times = lax.optimization_barrier(jnp.sum(picks * timesteps[:, None, :].astype(jnp.float32), axis=-1))
    angles = times[..., None] * freqs
    return jnp.concatenate([jnp.cos(angles), jnp.sin(angles)], axis=-1)

def attend(queries, keys, values, segment, padding):
    raw = jnp.einsum('gqhd,gkhd->ghqk', queries, keys, precision=exact) * (1.0 / math.sqrt(HD))
    scores = low_back(raw)
    place = jnp.arange(segment.shape[1], dtype=jnp.int32)
    allowed = (segment[:, :, None] == segment[:, None, :]) & ((padding[:, None, :] == 0) | (place[:, None] == place[None, :]))
    scores = jnp.where(allowed[:, None], scores, -1e+30)
    top = lax.optimization_barrier(jnp.max(scores, axis=-1, keepdims=True))
    raised = jnp.exp(scores - top)
    weights = raised / lax.optimization_barrier(jnp.sum(raised, axis=-1, keepdims=True))
    return jnp.einsum('ghqk,gkhd->gqhd', low(weights), values, precision=exact)

def attend_group(group_in):
    return jax.checkpoint(attend)(*group_in)

def block(hidden_in, activation, weights, cosine, sine, segment, padding):
    modulate, offset, triple, gains, mixing, expand, reduce_w = weights
    batch, slots, width = hidden_in.shape
    modulation = low_back(product(low(activation), modulate) + offset)
    shift1, scale1, gate1, shift2, scale2, gate2 = jnp.split(modulation, 6, axis=-1)
    lifted1 = low(layer_norm(hidden_in) * (1.0 + scale1) + shift1)
    projected = low_back(product(lifted1, triple))
    query_raw, key_raw, value_raw = jnp.split(projected, 3, axis=-1)
    queries = low(rotate(head_norm(query_raw, gains[0]), cosine, sine))
    keys = low(rotate(head_norm(key_raw, gains[1]), cosine, sine))
    values = low(value_raw.reshape(batch, slots, HEADS, HD))
    group = math.gcd(batch, 16)

    def grouped(array):
        return array.reshape((batch // group, group) + array.shape[1:])
    mixed = lax.map(attend_group, (grouped(queries), grouped(keys), grouped(values), grouped(segment), grouped(padding)))
    mixed = low_back(low(mixed.reshape(batch, slots, width)))
    attended = low_back(product(mixed, mixing))
    resid = hidden_in + gate1 * attended
    lifted2 = low(layer_norm(resid) * (1.0 + scale2) + shift2)
    expanded = low_back(product(lifted2, expand))
    gate, up = jnp.split(expanded, 2, axis=-1)
    hidden = low(jax.nn.silu(gate) * up)
    feed = low_back(product(hidden, reduce_w))
    return resid + gate2 * feed

def reference(tokens, cotangent, segment, rows, columns, padding, timesteps, encoder_modulate, encoder_offset, encoder_triple, encoder_gains, encoder_mixing, encoder_expand, encoder_reduce, decoder_modulate, decoder_offset, decoder_triple, decoder_gains, decoder_mixing, decoder_expand, decoder_reduce):
    cond = time_embed(timesteps, segment, D)
    cosine, sine = rope_tables(rows, columns)
    valid = (1 - padding).astype(jnp.float32)[..., None]
    encoder = (encoder_modulate.astype(jnp.float32), encoder_offset.astype(jnp.float32), encoder_triple.astype(jnp.float32), encoder_gains.astype(jnp.float32), encoder_mixing.astype(jnp.float32), encoder_expand.astype(jnp.float32), encoder_reduce.astype(jnp.float32))
    decoder = (decoder_modulate.astype(jnp.float32), decoder_offset.astype(jnp.float32), decoder_triple.astype(jnp.float32), decoder_gains.astype(jnp.float32), decoder_mixing.astype(jnp.float32), decoder_expand.astype(jnp.float32), decoder_reduce.astype(jnp.float32))

    def forward(token_in, encoder_in, decoder_in):
        latent_full = valid * block(token_in, jax.nn.silu(cond), encoder_in, cosine, sine, segment, padding)
        velocity_full = valid * block(token_in, jax.nn.silu(latent_full + cond), decoder_in, cosine, sine, segment, padding)
        return (velocity_full, latent_full)
    (velocity_full, latent_full), pull = jax.vjp(forward, tokens.astype(jnp.float32), encoder, decoder)
    token_grad, encoder_grad, decoder_grad = pull((cotangent.astype(jnp.float32), jnp.zeros_like(latent_full)))
    return (velocity_full.astype(jnp.bfloat16), latent_full.astype(jnp.bfloat16), token_grad, encoder_grad[0], encoder_grad[1], encoder_grad[2], encoder_grad[3], encoder_grad[4], encoder_grad[5], encoder_grad[6], decoder_grad[0], decoder_grad[1], decoder_grad[2], decoder_grad[3], decoder_grad[4], decoder_grad[5], decoder_grad[6])
```

```python
import functools
import math

import jax
import jax.numpy as jnp
from jax import lax
from jax.experimental import pallas as pl
from jax.experimental.pallas import tpu as pltpu
from jax.sharding import PartitionSpec as P

HEADS = 16
HD = 72
MESH = pl.DeviceIdType.MESH
GRID = (4, 2, 2)
BF16 = jnp.bfloat16
F32 = jnp.float32


def coords():
    dp = lax.axis_index("dp")
    return (lax.div(dp, 4), lax.rem(lax.div(dp, 2), 2), lax.rem(dp, 2), lax.axis_index("ctx"))


def device(z, y, x, c):
    return (z * 4 + y * 2 + x, c)


def when(cond, body):
    if cond is True:
        body()
    else:
        pl.when(cond)(body)


def greet(z, y, x, c):
    barrier = pltpu.get_barrier_semaphore()

    def signal(target):
        pl.semaphore_signal(barrier, inc=1, device_id=target, device_id_type=MESH)

    signal(device(z, 1 - y, x, c))
    signal(device(z, y, 1 - x, c))
    signal(device(z, y, x, 1 - c))
    pl.when(z < 3)(lambda: signal(device(z + 1, y, x, c)))
    pl.when(z > 0)(lambda: signal(device(z - 1, y, x, c)))
    pl.semaphore_wait(barrier, 3 + lax.div(z + 3, 4) + lax.div(6 - z, 4))


def gather_kernel(units, count, stride, group, lag, *refs):
    w = refs[:count]
    o = refs[count : 2 * count]
    ssem, rsem, lsem, csem, crsem = refs[2 * count :]
    z, y, x, c = coords()
    greet(z, y, x, c)
    up = device(z + 1, y, x, c)
    down = device(z - 1, y, x, c)
    partner = {"y": device(z, 1 - y, x, c), "x": device(z, y, 1 - x, c)}
    every = slice(None)

    def run(mine, other):
        def view(u, index):
            m, first, cols, _ = mine[u]
            return o[m].at[index[0], index[1], index[2], :, pl.ds(first, cols)]

        def copy(u, index, k, target, own=False):
            m, first, cols, _ = mine[u]
            dst = view(u, index)
            src = w[m].at[:, pl.ds(first, cols)] if own else dst
            return pltpu.make_async_remote_copy(
                src, dst, ssem.at[u, k], rsem.at[u, k], device_id=target, device_id_type=MESH
            )

        def local_copy(u):
            m, first, cols, _ = mine[u]
            return pltpu.make_async_copy(
                w[m].at[:, pl.ds(first, cols)], view(u, (z, y, x)), lsem.at[u]
            )

        def plan(u):
            held = {"z": False, "y": False, "x": False}

            def index(zz=z, flip=None):
                return (
                    every if held["z"] else zz,
                    every if held["y"] else (1 - y if flip == "y" else y),
                    every if held["x"] else (1 - x if flip == "x" else x),
                )

            steps = []
            pending = []
            sends = []
            own = True
            pair = 0
            for axis in mine[u][3]:
                if axis != "z":
                    send = [(True, functools.partial(copy, u, index(), pair, partner[axis], own))]
                    steps.append((pending, send))
                    sends += send
                    pending = [
                        (True, functools.partial(copy, u, index(flip=axis), pair, partner[axis]))
                    ]
                    pair += 1
                else:

                    def chain(shift, k, target, first=False):
                        return functools.partial(copy, u, index(zz=z + shift), k, target, first)

                    one = [(z < 3, chain(0, 2, up, own)), (z > 0, chain(0, 5, down, own))]
                    steps.append((pending, one))
                    middle = (z > 0) & (z < 3)
                    two = [(middle, chain(-1, 3, up)), (middle, chain(1, 6, down))]
                    steps.append(([(z > 0, chain(-1, 2, down)), (z < 3, chain(1, 5, up))], two))
                    three = [(z == 2, chain(-2, 4, up)), (z == 1, chain(2, 7, down))]
                    steps.append(([(z > 1, chain(-2, 3, down)), (z < 2, chain(2, 6, up))], three))
                    pending = [(z == 3, chain(-3, 4, down)), (z == 0, chain(3, 7, up))]
                    sends += one + two + three
                held[axis] = True
                own = False
            return steps, pending, sends

        plans = [plan(u) for u in range(len(mine))]

        def to_core(u, which):
            m, first, cols, _ = which[u]
            block = o[m].at[:, :, :, :, pl.ds(first, cols)]
            return pltpu.make_async_remote_copy(
                block,
                block,
                csem.at[u],
                crsem.at[u],
                device_id=device(z, y, x, 1 - c),
                device_id_type=MESH,
            )

        for u in range(len(mine)):
            local_copy(u).start()
        starts = [(u // group) * stride for u in range(len(mine))]
        for turn in range(max(starts) + 6 + lag):
            for u in range(len(mine)):
                steps, pending, _ = plans[u]
                s = turn - starts[u]
                if 0 <= s < 5:
                    if s == 1:
                        local_copy(u).wait()
                    for cond, make in steps[s][0]:
                        when(cond, lambda make=make: make().wait_recv())
                    for cond, make in steps[s][1]:
                        when(cond, lambda make=make: make().start())
                elif s == 5 + lag:
                    for cond, make in pending:
                        when(cond, lambda make=make: make().wait_recv())
                    to_core(u, mine).start()
        for u in range(len(mine)):
            for cond, make in plans[u][2]:
                when(cond, lambda make=make: make().wait_send())
            to_core(u, mine).wait_send()
        for u in range(len(other)):
            to_core(u, other).wait_recv()

    pl.when(c == 0)(lambda: run(units[0], units[1]))
    pl.when(c == 1)(lambda: run(units[1], units[0]))


ANY = pl.BlockSpec(memory_space=pl.ANY)
DMA = pltpu.SemaphoreType.DMA


def gather(shards, units, collective_id, stride, group, lag, name):
    count = len(shards)
    most = max(len(units[0]), len(units[1]))
    return pl.pallas_call(
        functools.partial(gather_kernel, units, count, stride, group, lag),
        name=name,
        out_shape=[jax.ShapeDtypeStruct(GRID + s.shape, s.dtype) for s in shards],
        in_specs=[ANY] * count,
        out_specs=[ANY] * count,
        scratch_shapes=[DMA((most, 8)), DMA((most, 8)), DMA((most,)), DMA((most,)), DMA((most,))],
        compiler_params=pltpu.CompilerParams(collective_id=collective_id, has_side_effects=True),
    )(*shards)


def spans(matrix, tiles, shifts=0):
    orders = ("zyx", "zxy", "yzx", "xzy")
    out = []
    at = 0
    for k, t in enumerate(tiles):
        out.append((matrix, at * 128, t * 128, orders[(k + shifts) % 4]))
        at += t
    return out


def exchange_kernel(broadcast, in_ref, out_ref, ssem, rsem, lsem):
    me = lax.axis_index("dp")
    c = lax.axis_index("ctx")
    barrier = pltpu.get_barrier_semaphore()
    for k in range(1, 16):
        pl.semaphore_signal(
            barrier, inc=1, device_id=(lax.rem(me + k, 16), c), device_id_type=MESH
        )
    pl.semaphore_wait(barrier, 15)

    def source(target):
        return in_ref if broadcast else in_ref.at[target]

    def copy(k):
        target = lax.rem(me + k, 16)
        return pltpu.make_async_remote_copy(
            source(target),
            out_ref.at[me],
            ssem.at[k],
            rsem.at[k],
            device_id=(target, c),
            device_id_type=MESH,
        )

    def arrival(k):
        origin = lax.rem(me + 16 - k, 16)
        return pltpu.make_async_remote_copy(
            source(origin),
            out_ref.at[origin],
            ssem.at[k],
            rsem.at[k],
            device_id=(origin, c),
            device_id_type=MESH,
        )

    for k in range(1, 16):
        copy(k).start()
    own = pltpu.make_async_copy(source(me), out_ref.at[me], lsem.at[0])
    own.start()
    own.wait()
    for k in range(1, 16):
        copy(k).wait_send()
        arrival(k).wait_recv()


def exchange(values, broadcast, collective_id, name):
    shape = values.shape if broadcast else values.shape[1:]
    return pl.pallas_call(
        functools.partial(exchange_kernel, broadcast),
        name=name,
        out_shape=jax.ShapeDtypeStruct((16,) + shape, values.dtype),
        in_specs=[ANY],
        out_specs=ANY,
        scratch_shapes=[DMA((16,)), DMA((16,)), DMA((1,))],
        compiler_params=pltpu.CompilerParams(collective_id=collective_id, has_side_effects=True),
    )(values)


LAG = (0, 3, 5, 7, 9, 11)
RECV_SLOTS = 14
SEND_SLOTS = 13
FIRST_SLOTS = 6
UNIT = 384
ROWS = 72
PADDED = 80


def scatter_kernel(first, cols, source, dy_count, *refs):
    nv = len(first) - 1
    xt = refs[:nv]
    dy = refs[nv : nv + dy_count]
    out = refs[nv + dy_count]
    (
        xts, dys, a_s1, a_s2, a_t, a_su, a_sd, e_s1, e_t, e_su, e_sd, e_sq,
        a_b1, a_b2, a_bu, a_bd, e_b1, e_bu, e_bd, e_bq, outs,
        ssem, rsem, xl, xs, xr, yl, ys, yr, ol, os, orr,
    ) = refs[nv + dy_count + 1 :]
    z, y, x, c = coords()
    total = first[-1] // 2
    sibling = device(z, y, x, 1 - c)
    up = device(z + 1, y, x, c)
    down = device(z - 1, y, x, c)
    greet(z, y, x, c)
    lanes = pl.ds(pl.multiple_of(c * 128, 128), 128)
    offsets = []
    at = 0
    for k in range(dy_count):
        offsets.append(at)
        at += dy[k].shape[1]

    def remote(src, dst, send, recv, target):
        return pltpu.make_async_remote_copy(
            src, dst, send, recv, device_id=target, device_id_type=MESH
        )

    def x_views(v, k):
        o, b = k // 2, k % 2
        src = xt[v].at[:, :, b] if o == 0 else xt[v].at[:, b]
        return src, xts.at[v, o, b, :, :, :, lanes]

    def x_local(v, k):
        return pltpu.make_async_copy(*x_views(v, k), xl.at[v, k])

    def x_remote(v, k):
        return remote(*x_views(v, k), xs.at[v, k], xr.at[v, k], sibling)

    def y_views(k):
        return dy[k], dys.at[lanes, pl.ds(offsets[k], dy[k].shape[1])]

    def y_local(k):
        return pltpu.make_async_copy(*y_views(k), yl.at[k])

    def y_remote(k):
        return remote(*y_views(k), ys.at[k], yr.at[k], sibling)

    fresh = [source[v] not in source[:v] for v in range(nv)]
    for v in range(nv):
        for k in range(4):
            x_local(v, k).start()
            x_remote(v, k).start()
        if fresh[v]:
            y_local(source[v]).start()
            y_remote(source[v]).start()

    def arrive(tick):
        for v in range(nv):

            def wait(v=v):
                for k in range(4):
                    x_local(v, k).wait()
                    x_remote(v, k).wait_recv()
                if fresh[v]:
                    y_local(source[v]).wait()
                    y_remote(source[v]).wait_recv()

            pl.when(tick == (first[v] - c + 1) // 2)(wait)

    def unit(i):
        j = 2 * i + c
        v = jnp.int32(0)
        col = j * UNIT
        for k in range(1, nv):
            past = (j >= first[k]).astype(jnp.int32)
            v = v + past
            col = col + past * ((cols[k] - first[k] * UNIT) - (cols[k - 1] - first[k - 1] * UNIT))
        return v, pl.multiple_of(col, 128)

    def axes(i):
        o = lax.rem(i, 2)
        pb = x * (1 - o) + y * o
        qb = y * (1 - o) + x * o
        dp = z * 4 + y * 2 + x
        return o, pb, qb, (dp + (1 - 2 * pb) * (1 + o), c), (dp + (1 - 2 * qb) * (2 - o), c)

    def slots(i):
        return lax.rem(i, FIRST_SLOTS), lax.rem(i, SEND_SLOTS), lax.rem(i, RECV_SLOTS)

    def send(src, dst, i, k, target):
        return remote(
            src, dst, ssem.at[lax.rem(i, SEND_SLOTS), k], rsem.at[lax.rem(i, RECV_SLOTS), k], target
        )

    def first_copies(i):
        o, pb, qb, pn, qn = axes(i)
        f, s, w = slots(i)
        return [send(a_s1.at[f], a_b1.at[w], i, 0, pn), send(e_s1.at[f], e_b1.at[w], i, 8, pn)]

    def second_copy(i):
        o, pb, qb, pn, qn = axes(i)
        f, s, w = slots(i)
        return send(a_s2.at[s], a_b2.at[w], i, 1, qn)

    def last_copy(i):
        o, pb, qb, pn, qn = axes(i)
        f, s, w = slots(i)
        return send(e_sq.at[s], e_bq.at[w], i, 9, qn)

    def up_copy(i, k, e):
        f, s, w = slots(i)
        src, dst, n = (e_su, e_bu, 10) if e else (a_su, a_bu, 2)
        return send(src.at[s, k], dst.at[w, k], i, n + k, up)

    def down_copy(i, k, e):
        f, s, w = slots(i)
        src, dst, n = (e_sd, e_bd, 13) if e else (a_sd, a_bd, 5)
        return send(src.at[s, k], dst.at[w, k], i, n + k, down)

    def up_sends(k):
        return (z <= k) & (z < 3)

    def down_sends(k):
        return (3 - z <= k) & (z > 0)

    def up_comes(k):
        return (z >= 1) & (z <= k + 1)

    def down_comes(k):
        return (z <= 2) & (3 - z <= k + 1)

    def kept(i, e, d):
        f, s, w = slots(i)
        if e:
            return e_t.at[s, d]
        return a_t.at[s, d, axes(i)[2]]

    def z_send(i, k, e):
        f, s, w = slots(i)

        def pass_on(dest, stage, box, inner, copy):
            value = kept(i, e, dest)[...]
            if k == 0:
                stage[s, k] = value.astype(BF16)
            else:

                def add():
                    stage[s, k] = (value + box[w, k - 1].astype(F32)).astype(BF16)

                def begin():
                    stage[s, k] = value.astype(BF16)

                pl.when(inner)(add)
                pl.when(jnp.logical_not(inner))(begin)
            copy.start()

        pl.when(up_sends(k))(
            lambda: pass_on(
                z + 3 - k, e_su if e else a_su, e_bu if e else a_bu, z > 0, up_copy(i, k, e)
            )
        )
        pl.when(down_sends(k))(
            lambda: pass_on(
                z + k - 3, e_sd if e else a_sd, e_bd if e else a_bd, z < 3, down_copy(i, k, e)
            )
        )

    def z_wait(i, k, e):
        pl.when(up_comes(k))(lambda: up_copy(i, k, e).wait_recv())
        pl.when(down_comes(k))(lambda: down_copy(i, k, e).wait_recv())

    def z_close(i, e):
        f, s, w = slots(i)
        mine = kept(i, e, z)

        def below():
            mine[...] = mine[...] + (e_bu if e else a_bu)[w, 2].astype(F32)

        def above():
            mine[...] = mine[...] + (e_bd if e else a_bd)[w, 2].astype(F32)

        pl.when(z > 0)(below)
        pl.when(z < 3)(above)
        return mine

    def product(i, bit):
        v, col = unit(i)
        lhs = xts[v, axes(i)[0], bit].reshape(8 * PADDED, 256)
        whole = jnp.dot(lhs, dys[:, pl.ds(col, UNIT)], preferred_element_type=F32)
        return whole.reshape(8, PADDED, UNIT)[:, :ROWS]

    def stage0(i):
        f, s, w = slots(i)
        part = product(i, 1 - axes(i)[1])
        a_s1[f] = part[:, :, :128].astype(BF16).reshape(4, 2, ROWS, 128)
        e_s1[f] = part[:, :, 128:].astype(BF16).reshape(4, 2, ROWS, 256)
        for copy in first_copies(i):
            copy.start()

    def stage1(i):
        f, s, w = slots(i)
        o, pb, qb, pn, qn = axes(i)
        part = product(i, pb)
        for copy in first_copies(i):
            copy.wait_recv()
        a_t[s] = part[:, :, :128].reshape(4, 2, ROWS, 128) + a_b1[w].astype(F32)
        a_s2[s] = a_t[s, :, 1 - qb].astype(BF16)
        second_copy(i).start()
        e_t[s] = part[:, :, 128:].reshape(4, 2, ROWS, 256) + e_b1[w].astype(F32)
        z_send(i, 0, True)

    def stage2(i):
        f, s, w = slots(i)
        qb = axes(i)[2]
        second_copy(i).wait_recv()
        a_t[s, :, qb] = a_t[s, :, qb] + a_b2[w].astype(F32)
        z_send(i, 0, False)
        z_wait(i, 0, True)
        z_send(i, 1, True)

    def stage3(i):
        z_wait(i, 0, False)
        z_send(i, 1, False)
        z_wait(i, 1, True)
        z_send(i, 2, True)

    def stage4(i):
        f, s, w = slots(i)
        z_wait(i, 1, False)
        z_send(i, 2, False)
        z_wait(i, 2, True)
        z_close(i, True)
        e_sq[s] = e_t[s, z, 1 - axes(i)[2]].astype(BF16)
        last_copy(i).start()

    def out_view(i):
        return out.at[:, pl.ds(pl.multiple_of((2 * i + c) * UNIT, 128), UNIT)]

    def stage5(i):
        f, s, w = slots(i)
        z_wait(i, 2, False)
        outs[i, :, :128] = z_close(i, False)[...]
        last_copy(i).wait_recv()
        outs[i, :, 128:] = e_t[s, z, axes(i)[2]] + e_bq[w].astype(F32)
        pltpu.make_async_copy(outs.at[i], out_view(i), ol.at[0]).start()
        remote(outs.at[i], out_view(i), os.at[0], orr.at[0], sibling).start()

    def first_sent(i):
        for copy in first_copies(i):
            copy.wait_send()

    def sent(i):
        second_copy(i).wait_send()
        last_copy(i).wait_send()
        for e in (False, True):
            for k in range(3):
                pl.when(up_sends(k))(lambda k=k, e=e: up_copy(i, k, e).wait_send())
                pl.when(down_sends(k))(lambda k=k, e=e: down_copy(i, k, e).wait_send())

    stages = (stage0, stage1, stage2, stage3, stage4, stage5)

    def tick(t, carry):
        arrive(t)
        pl.when((t >= SEND_SLOTS) & (t - SEND_SLOTS < total))(lambda: sent(t - SEND_SLOTS))
        pl.when((t >= FIRST_SLOTS) & (t - FIRST_SLOTS < total))(lambda: first_sent(t - FIRST_SLOTS))
        for k in reversed(range(6)):
            i = t - LAG[k]
            pl.when((i >= 0) & (i < total))(functools.partial(stages[k], i))
        return carry

    lax.fori_loop(0, total + SEND_SLOTS, tick, 0)
    for v in range(nv):
        for k in range(4):
            x_remote(v, k).wait_send()
    for k in range(dy_count):
        y_remote(k).wait_send()
    half = out.at[:, pl.ds(0, total * UNIT)]
    pltpu.make_async_copy(half, half, ol.at[0]).wait()
    everything = remote(half, half, os.at[0], orr.at[0], sibling)
    everything.wait_send()
    everything.wait_recv()


def scatter(xts, dys, source, collective_id, name):
    nv = len(xts)
    starts = []
    width = 0
    for d in dys:
        starts.append(width)
        width += d.shape[1]
    first = [0]
    cols = []
    for v in range(nv):
        cols.append(starts[source[v]])
        first.append(first[-1] + dys[source[v]].shape[1] // UNIT)
    total = first[-1] // 2
    s, f, r = SEND_SLOTS, FIRST_SLOTS, RECV_SLOTS
    vmem = pltpu.VMEM
    return pl.pallas_call(
        functools.partial(scatter_kernel, tuple(first), tuple(cols), tuple(source), len(dys)),
        name=name,
        out_shape=jax.ShapeDtypeStruct((ROWS, first[-1] * UNIT), F32),
        in_specs=[ANY] * (nv + len(dys)),
        out_specs=ANY,
        scratch_shapes=[
            vmem((nv, 2, 2, 4, 2, PADDED, 256), BF16),
            vmem((256, width), BF16),
            vmem((f, 4, 2, ROWS, 128), BF16),
            vmem((s, 4, ROWS, 128), BF16),
            vmem((s, 4, 2, ROWS, 128), F32),
            vmem((s, 3, ROWS, 128), BF16),
            vmem((s, 3, ROWS, 128), BF16),
            vmem((f, 4, 2, ROWS, 256), BF16),
            vmem((s, 4, 2, ROWS, 256), F32),
            vmem((s, 3, 2, ROWS, 256), BF16),
            vmem((s, 3, 2, ROWS, 256), BF16),
            vmem((s, ROWS, 256), BF16),
            vmem((r, 4, 2, ROWS, 128), BF16),
            vmem((r, 4, ROWS, 128), BF16),
            vmem((r, 3, ROWS, 128), BF16),
            vmem((r, 3, ROWS, 128), BF16),
            vmem((r, 4, 2, ROWS, 256), BF16),
            vmem((r, 3, 2, ROWS, 256), BF16),
            vmem((r, 3, 2, ROWS, 256), BF16),
            vmem((r, ROWS, 256), BF16),
            vmem((total, ROWS, UNIT), F32),
            DMA((s, 16)),
            DMA((r, 16)),
            DMA((nv, 4)),
            DMA((nv, 4)),
            DMA((nv, 4)),
            DMA((len(dys),)),
            DMA((len(dys),)),
            DMA((len(dys),)),
            DMA((1,)),
            DMA((1,)),
            DMA((1,)),
        ],
        compiler_params=pltpu.CompilerParams(
            collective_id=collective_id, has_side_effects=True, vmem_limit_bytes=60 * 1024 * 1024
        ),
    )(*xts, *dys)


def layer_norm(values):
    center = values - jnp.mean(values, axis=-1, keepdims=True)
    spread = jnp.mean(center * center, axis=-1, keepdims=True)
    return center * lax.rsqrt(spread + 1e-06)


def head_norm(values, gain):
    shaped = values.reshape(values.shape[:-1] + (HEADS, HD))
    scaled = shaped * lax.rsqrt(jnp.mean(shaped * shaped, axis=-1, keepdims=True) + 1e-06)
    return scaled * gain.reshape(HEADS, HD)


def rope_tables(rows, columns):
    quarter = HD // 4
    freqs = jnp.exp(jnp.arange(quarter, dtype=F32) * (-math.log(10000.0) / quarter))
    places = jnp.stack([rows, columns], axis=-1).astype(F32)
    angles = places[..., None] * freqs
    return (jnp.cos(angles), jnp.sin(angles))


def rotate(values, cosine, sine):
    shaped = values.reshape(values.shape[:-1] + (2, 2, HD // 4))
    first = shaped[..., 0, :]
    second = shaped[..., 1, :]
    cosine = cosine[..., None, :, :]
    sine = sine[..., None, :, :]
    turned = jnp.stack([first * cosine - second * sine, first * sine + second * cosine], axis=-2)
    return turned.reshape(values.shape)


def embed_times(times, width):
    half_width = width // 2
    freqs = jnp.exp(jnp.arange(half_width, dtype=F32) * (-math.log(10000.0) / half_width))
    angles = times[..., None] * freqs
    return jnp.concatenate([jnp.cos(angles), jnp.sin(angles)], axis=-1)


def qk_prepare(query_raw, key_raw, gains, cosine, sine):
    return (
        rotate(head_norm(query_raw, gains[0]), cosine, sine),
        rotate(head_norm(key_raw, gains[1]), cosine, sine),
    )


def swish_product(gate, up):
    return jax.nn.silu(gate) * up


def attention_scores(queries, keys, allowed):
    scores = jnp.einsum("sqhd,skhd->shqk", queries, keys, preferred_element_type=F32) * (
        1.0 / math.sqrt(HD)
    )
    return jnp.where(allowed[:, None], scores, -1e30)


def dense(values, weight):
    return jnp.dot(values, weight, preferred_element_type=F32)


def dense_back(grads, weight):
    return lax.dot_general(grads, weight, (((1,), (1,)), ((), ())), preferred_element_type=F32)


def outer_sum(values, grads):
    return lax.dot_general(values, grads, (((0,), (0,)), ((), ())), preferred_element_type=F32)


def block_forward(flat, modulation, weights, context):
    batch, half, allowed, cosine, sine = context
    triple, mixing, expand, reduce_w, gains = weights
    width = flat.shape[1]
    shift1, scale1, gate1, shift2, scale2, gate2 = jnp.split(modulation, 6, axis=1)
    lifted1 = (layer_norm(flat) * (1.0 + scale1) + shift1).astype(BF16)
    projected = dense(lifted1, triple)
    query_raw, key_raw, value_raw = jnp.split(projected, 3, axis=1)
    queries, keys = qk_prepare(query_raw, key_raw, gains, cosine, sine)
    queries = queries.astype(BF16).reshape(batch, half, HEADS, HD)
    keys_local = keys.astype(BF16).reshape(batch, half, width)
    values_local = value_raw.astype(BF16).reshape(batch, half, width)
    key_heads = lax.all_gather(keys_local, "ctx", axis=1, tiled=True).reshape(batch, -1, HEADS, HD)
    value_heads = lax.all_gather(values_local, "ctx", axis=1, tiled=True)
    value_heads = value_heads.reshape(batch, -1, HEADS, HD)
    scores = attention_scores(queries, key_heads, allowed)
    top = jnp.max(scores, axis=-1, keepdims=True)
    raised = jnp.exp(scores - top)
    total = jnp.sum(raised, axis=-1, keepdims=True)
    softmax_low = (raised / total).astype(BF16)
    logsum = top + jnp.log(total)
    mixed = jnp.einsum("shqk,skhd->sqhd", softmax_low, value_heads, preferred_element_type=F32)
    mixed_low = mixed.reshape(-1, width).astype(BF16)
    attended = dense(mixed_low, mixing)
    resid = flat + gate1 * attended
    lifted2 = (layer_norm(resid) * (1.0 + scale2) + shift2).astype(BF16)
    expanded = dense(lifted2, expand)
    gate, up = jnp.split(expanded, 2, axis=1)
    hidden = swish_product(gate, up).astype(BF16)
    feed = dense(hidden, reduce_w)
    output = resid + gate2 * feed
    kept = (
        modulation,
        flat,
        lifted1,
        query_raw,
        key_raw,
        queries,
        key_heads,
        value_heads,
        logsum,
        mixed_low,
        attended,
        resid,
        lifted2,
        expanded,
        hidden,
        feed,
    )
    return (output, kept)


def block_backward(grad_out, kept, weights, context):
    batch, half, allowed, cosine, sine = context
    triple, mixing, expand, reduce_w, gains = weights
    (
        modulation,
        flat,
        lifted1,
        query_raw,
        key_raw,
        queries,
        key_heads,
        value_heads,
        logsum,
        mixed_low,
        attended,
        resid,
        lifted2,
        expanded,
        hidden,
        feed,
    ) = kept
    width = flat.shape[1]
    shift1, scale1, gate1, shift2, scale2, gate2 = jnp.split(modulation, 6, axis=1)
    grad_feed = (grad_out * gate2).astype(BF16)
    grad_hidden = dense_back(grad_feed, reduce_w)
    gate, up = jnp.split(expanded, 2, axis=1)
    unused_out, swish_pull = jax.vjp(swish_product, gate, up)
    grad_gate, grad_up = swish_pull(grad_hidden)
    grad_expanded = jnp.concatenate([grad_gate, grad_up], axis=1).astype(BF16)
    grad_lifted2 = dense_back(grad_expanded, expand)
    normed_second, second_pull = jax.vjp(layer_norm, resid)
    grad_resid = grad_out + second_pull(grad_lifted2 * (1.0 + scale2))[0]
    grad_attended = (grad_resid * gate1).astype(BF16)
    grad_mixed = dense_back(grad_attended, mixing).astype(BF16).reshape(batch, half, HEADS, HD)
    scores = attention_scores(queries, key_heads, allowed)
    chances = jnp.exp(scores - logsum)
    grad_chances = jnp.einsum(
        "sqhd,skhd->shqk", grad_mixed, value_heads, preferred_element_type=F32
    )
    grad_values = jnp.einsum(
        "shqk,sqhd->skhd", chances.astype(BF16), grad_mixed, preferred_element_type=F32
    )
    grad_scores = (
        chances * (grad_chances - jnp.sum(chances * grad_chances, axis=-1, keepdims=True))
    ).astype(BF16)
    scale = 1.0 / math.sqrt(HD)
    grad_queries = (
        jnp.einsum("shqk,skhd->sqhd", grad_scores, key_heads, preferred_element_type=F32) * scale
    )
    grad_keys = (
        jnp.einsum("shqk,sqhd->skhd", grad_scores, queries, preferred_element_type=F32) * scale
    )
    pair = jnp.stack(
        [grad_keys.reshape(batch, -1, width), grad_values.reshape(batch, -1, width)]
    ).astype(BF16)
    place = lax.axis_index("ctx")
    theirs = lax.dynamic_slice_in_dim(pair, (1 - place) * half, half, 2)
    theirs = lax.ppermute(theirs, "ctx", [(0, 1), (1, 0)])
    mine = lax.dynamic_slice_in_dim(pair, place * half, half, 2)
    pair = mine.astype(F32) + theirs.astype(F32)
    grad_keys, grad_values = pair[0], pair[1]

    def prepare(query_in, key_in, gain_in):
        return qk_prepare(query_in, key_in, gain_in, cosine, sine)

    unused_pair, prepare_pull = jax.vjp(prepare, query_raw, key_raw, gains)
    grad_query_raw, grad_key_raw, gains_grad = prepare_pull(
        (grad_queries.reshape(-1, HEADS, HD), grad_keys.reshape(-1, HEADS, HD))
    )
    grad_projected = jnp.concatenate(
        [grad_query_raw, grad_key_raw, grad_values.reshape(-1, width)], axis=1
    ).astype(BF16)
    grad_lifted1 = dense_back(grad_projected, triple)
    normed_first, first_pull = jax.vjp(layer_norm, flat)
    grad_flat = grad_resid + first_pull(grad_lifted1 * (1.0 + scale1))[0]
    grad_modulation = jnp.concatenate(
        [
            grad_lifted1,
            grad_lifted1 * normed_first,
            grad_resid * attended,
            grad_lifted2,
            grad_lifted2 * normed_second,
            grad_out * feed,
        ],
        axis=1,
    ).astype(BF16)
    factors = (
        (lifted1, grad_projected),
        (mixed_low, grad_attended),
        (lifted2, grad_expanded),
        (hidden, grad_feed),
    )
    return (grad_flat, grad_modulation, factors, gains_grad)


def shard_rows(values, groups):
    turned = values.T.reshape(16, groups, -1, values.shape[0])
    rows = turned.shape[2]
    turned = jnp.pad(turned, ((0, 0), (0, 0), (0, PADDED - rows), (0, 0)))
    return [turned[:, g].reshape(GRID + turned.shape[2:]) for g in range(groups)]


def fast_reduce(factors, extra, collective_id, name):
    tokens = factors[0][0].shape[0]
    xts = []
    dys = []
    source = []
    for k, (left, right) in enumerate(factors):
        groups = 3 if k == len(factors) - 1 else 1
        xts += shard_rows(left, groups)
        dys.append(right)
        source += [k] * groups
    count = extra.shape[1]
    lines = -(-count // tokens)
    packed = jnp.pad(extra, ((0, 0), (0, lines * tokens - count))).reshape(16, lines, tokens)
    packed = jnp.pad(packed, ((0, 0), (0, PADDED - lines), (0, 0))).astype(BF16)
    xts.append(packed.reshape(GRID + packed.shape[1:]))
    dys.append(jnp.eye(tokens, UNIT, dtype=BF16))
    source.append(len(factors))
    out = scatter(xts, dys, source, collective_id, name)
    grads = []
    at = 0
    for left, right in factors[:-1]:
        grads.append(out[:, at : at + right.shape[1]])
        at += right.shape[1]
    width = factors[-1][1].shape[1]
    rows = factors[-1][0].shape[1] // 48
    parts = [out[:rows, at + g * width : at + (g + 1) * width] for g in range(3)]
    grads.append(jnp.concatenate(parts, axis=0))
    at += 3 * width
    small = out[:lines, at : at + tokens].reshape(-1)[:count]
    return grads, small


def whole_rows(gathered):
    return gathered.reshape((-1,) + gathered.shape[4:])


def fast_step(flat, cotangent, context, segment_local, valid, timesteps, encoder, decoder):
    width = flat.shape[1]
    offset_size = encoder[1].shape[0]
    gain_size = 2 * encoder[3].shape[1]
    small = jnp.concatenate(
        [
            encoder[1].astype(F32),
            decoder[1].astype(F32),
            encoder[3].astype(F32).reshape(-1),
            decoder[3].astype(F32).reshape(-1),
            timesteps.astype(F32).reshape(-1),
        ]
    )
    size = small.shape[0]
    small = jnp.pad(small, (0, 2048 - size)).reshape(16, 128)
    small = exchange(small, True, 0, "small").reshape(16, -1)
    encoder_offset = small[:, :offset_size].reshape(-1)
    decoder_offset = small[:, offset_size : 2 * offset_size].reshape(-1)
    at = 2 * offset_size
    encoder_gains = small[:, at : at + gain_size].reshape(16, 2, -1).swapaxes(0, 1).reshape(2, -1)
    at += gain_size
    decoder_gains = small[:, at : at + gain_size].reshape(16, 2, -1).swapaxes(0, 1).reshape(2, -1)
    at += gain_size
    all_times = small[:, at : at + timesteps.size]
    segments = timesteps.shape[1]
    picks = (segment_local[..., None] == jnp.arange(segments, dtype=jnp.int32)).astype(F32)
    picks = picks.reshape(-1, segments)

    all_cond = embed_times(all_times, width).reshape(-1, width)
    act_rows = jax.nn.silu(all_cond).astype(BF16)
    me = lax.axis_index("dp")
    rows = encoder[0].shape[0]
    act_mine = lax.dynamic_slice_in_dim(act_rows, me * rows, rows, 1)
    partial = dense(act_mine, encoder[0]).reshape(16, -1, 1152)
    partial = exchange(partial, False, 1, "partial")
    modulation_rows = jnp.sum(partial, axis=0).reshape(segments, -1) + encoder_offset
    exact = lax.Precision.HIGHEST
    encoder_modulation = jnp.dot(picks, modulation_rows, precision=exact)
    cond_rows = lax.dynamic_slice_in_dim(all_cond, me * segments, segments, 0)
    cond = jnp.dot(picks, cond_rows, precision=exact)

    encoder_units = (
        tuple(spans(2, (6,) * 8) + spans(0, (6,))),
        tuple(
            [(0, 768 + at, n, o) for _, at, n, o in spans(0, (7, 7, 7))]
            + spans(1, (4, 5), 3)
            + spans(3, (2, 2, 2, 3), 1)
        ),
    )
    triple, mixing, expand, reduce_w = gather(
        [encoder[2], encoder[4], encoder[5], encoder[6]], encoder_units, 2, 1, 2, 1, "gather_encoder"
    )
    encoder_weights = (
        whole_rows(triple),
        whole_rows(mixing),
        whole_rows(expand),
        whole_rows(reduce_w),
        encoder_gains,
    )
    encoder_out, encoder_kept = block_forward(flat, encoder_modulation, encoder_weights, context)
    latent_full = valid * encoder_out
    decoder_pre = latent_full + cond
    decoder_act = jax.nn.silu(decoder_pre).astype(BF16)

    decoder_units = (
        tuple(spans(0, (7, 7, 7, 7, 7, 7, 6, 6)) + spans(1, (7, 7, 7, 6))),
        tuple(spans(3, (6,) * 8) + spans(4, (2, 2, 2, 3)) + spans(2, (2, 2, 2, 3))),
    )
    shards = (decoder[0], decoder[2], decoder[4], decoder[5], decoder[6])
    shards, decoder_act = lax.optimization_barrier((shards, decoder_act))
    modulate, triple, mixing, expand, reduce_w = gather(
        shards, decoder_units, 3, 1, 2, 1, "gather_decoder"
    )
    modulate = whole_rows(modulate)
    decoder_weights = (
        whole_rows(triple),
        whole_rows(mixing),
        whole_rows(expand),
        whole_rows(reduce_w),
        decoder_gains,
    )
    decoder_modulation = dense(decoder_act, modulate) + decoder_offset
    decoder_out, decoder_kept = block_forward(flat, decoder_modulation, decoder_weights, context)
    velocity = valid * decoder_out

    grad_out = valid * cotangent
    decoder_flat, grad_modulation, factors, gains_grad = block_backward(
        grad_out, decoder_kept, decoder_weights, context
    )
    grad_act = dense_back(grad_modulation, modulate)
    unused_silu, silu_pull = jax.vjp(jax.nn.silu, decoder_pre)
    grad_latent = valid * silu_pull(grad_act)[0]
    offset_grad = jnp.sum(grad_modulation, axis=0, dtype=F32)
    extra = jnp.concatenate(
        [
            offset_grad.reshape(16, -1),
            gains_grad.reshape(2, 16, -1).swapaxes(0, 1).reshape(16, -1),
        ],
        axis=1,
    )
    grads, small = fast_reduce(
        ((decoder_act, grad_modulation),) + factors, extra, 4, "scatter_decoder"
    )
    decoder_grads = (
        grads[0],
        small[:offset_size],
        grads[1],
        small[offset_size:].reshape(2, -1),
        grads[2],
        grads[3],
        grads[4],
    )

    encoder_flat, grad_modulation, factors, gains_grad = block_backward(
        grad_latent, encoder_kept, encoder_weights, context
    )
    grad_rows = lax.dot_general(
        picks.astype(BF16), grad_modulation, (((0,), (0,)), ((), ())), preferred_element_type=F32
    )
    grad_rows = grad_rows + lax.ppermute(grad_rows, "ctx", [(0, 1), (1, 0)])
    extra = gains_grad.reshape(2, 16, -1).swapaxes(0, 1).reshape(16, -1)
    grads, small = fast_reduce(factors, extra, 5, "scatter_encoder")
    grad_rows, grads = lax.optimization_barrier((grad_rows, grads))
    all_rows = exchange(grad_rows.reshape(-1, 1152), True, 6, "rows")
    all_rows = all_rows.reshape(16 * segments, -1)
    modulate_grad = lax.dot_general(
        act_mine.astype(F32), all_rows, (((0,), (0,)), ((), ())), precision=exact
    )
    offset_grad = lax.dynamic_slice_in_dim(
        jnp.sum(all_rows, axis=0), me * offset_size, offset_size, 0
    )
    encoder_grads = (
        modulate_grad,
        offset_grad,
        grads[0],
        small.reshape(2, -1),
        grads[1],
        grads[2],
        grads[3],
    )
    return velocity, latent_full, decoder_flat + encoder_flat, encoder_grads, decoder_grads


def plain_gather(block):
    parts = [lax.all_gather(block[k], "dp", axis=0, tiled=True) for k in (0, 1, 2, 4, 5, 6)]
    gains = lax.all_gather(block[3], "dp", axis=1, tiled=True).astype(F32)
    modulate, offset, triple, mixing, expand, reduce_w = parts
    return modulate, offset.astype(F32), (triple, mixing, expand, reduce_w, gains)


def plain_reduce(factors, grad_modulation, gains_grad):
    def rows(values, dim=0):
        part = lax.psum_scatter(values, "dp", scatter_dimension=dim, tiled=True)
        return lax.psum(part.astype(BF16), "ctx").astype(F32)

    offset = rows(jnp.sum(grad_modulation, axis=0, dtype=F32))
    modulate, triple, mixing, expand, reduce_w = [rows(outer_sum(a, b)) for a, b in factors]
    return modulate, offset, triple, rows(gains_grad, 1), mixing, expand, reduce_w


def plain_step(flat, cotangent, context, segment_local, valid, timesteps, encoder, decoder):
    picks = (
        segment_local[..., None] == jnp.arange(timesteps.shape[-1], dtype=jnp.int32)
    ).astype(F32)
    times = jnp.sum(picks * timesteps[:, None, :].astype(F32), axis=-1)
    cond = embed_times(times, flat.shape[1]).reshape(flat.shape)
    modulate, offset, encoder_weights = plain_gather(encoder)
    encoder_act = jax.nn.silu(cond).astype(BF16)
    encoder_out, encoder_kept = block_forward(
        flat, dense(encoder_act, modulate) + offset, encoder_weights, context
    )
    latent_full = valid * encoder_out
    decoder_pre = latent_full + cond
    decoder_act = jax.nn.silu(decoder_pre).astype(BF16)
    modulate, offset, decoder_weights = plain_gather(decoder)
    decoder_out, decoder_kept = block_forward(
        flat, dense(decoder_act, modulate) + offset, decoder_weights, context
    )
    decoder_flat, grad_modulation, factors, gains_grad = block_backward(
        valid * cotangent, decoder_kept, decoder_weights, context
    )
    grad_act = dense_back(grad_modulation, modulate)
    decoder_grads = plain_reduce(
        ((decoder_act, grad_modulation),) + factors, grad_modulation, gains_grad
    )
    unused_silu, silu_pull = jax.vjp(jax.nn.silu, decoder_pre)
    encoder_flat, grad_modulation, factors, gains_grad = block_backward(
        valid * silu_pull(grad_act)[0], encoder_kept, encoder_weights, context
    )
    encoder_grads = plain_reduce(
        ((encoder_act, grad_modulation),) + factors, grad_modulation, gains_grad
    )
    return valid * decoder_out, latent_full, decoder_flat + encoder_flat, encoder_grads, decoder_grads


def local(fast, tokens, cotangent, segment, rows, columns, padding, timesteps, *weights):
    batch, half, width = tokens.shape
    start = lax.axis_index("ctx") * half
    segment_local = lax.dynamic_slice_in_dim(segment, start, half, 1)
    rows_local = lax.dynamic_slice_in_dim(rows, start, half, 1)
    columns_local = lax.dynamic_slice_in_dim(columns, start, half, 1)
    padding_local = lax.dynamic_slice_in_dim(padding, start, half, 1)
    place_query = start + jnp.arange(half, dtype=jnp.int32)
    place_key = jnp.arange(segment.shape[1], dtype=jnp.int32)
    allowed = (segment_local[:, :, None] == segment[:, None, :]) & (
        (padding[:, None, :] == 0) | (place_query[None, :, None] == place_key[None, None, :])
    )
    cosine, sine = rope_tables(rows_local.reshape(-1), columns_local.reshape(-1))
    context = (batch, half, allowed, cosine, sine)
    valid = (1 - padding_local).astype(F32).reshape(-1, 1)
    flat = tokens.reshape(-1, width).astype(F32)
    step = fast_step if fast else plain_step
    velocity, latent, token_grad, encoder_grads, decoder_grads = step(
        flat,
        cotangent.reshape(-1, width).astype(F32),
        context,
        segment_local,
        valid,
        timesteps,
        weights[:7],
        weights[7:],
    )
    return (
        velocity.astype(BF16).reshape(batch, half, width),
        latent.astype(BF16).reshape(batch, half, width),
        token_grad.reshape(batch, half, width),
        *encoder_grads,
        *decoder_grads,
    )


def solution(mesh):
    fast = dict(mesh.shape) == {"dp": math.prod(GRID), "ctx": 2}
    block = (
        P("dp", None),
        P("dp"),
        P("dp", None),
        P(None, "dp"),
        P("dp", None),
        P("dp", None),
        P("dp", None),
    )
    slots = P("dp", "ctx", None)
    return jax.shard_map(
        functools.partial(local, fast),
        mesh=mesh,
        in_specs=(slots, slots) + (P("dp", None),) * 5 + block + block,
        out_specs=(slots, slots, slots) + block + block,
        check_vma=False,
    )
```

```python
import functools
import math

import jax
import jax.numpy as jnp
from jax import lax
from jax.experimental import pallas as pl
from jax.experimental.pallas import tpu as pltpu
from jax.sharding import PartitionSpec as P

HEADS = 16
HD = 72
MESH = pl.DeviceIdType.MESH
GRID = (4, 2, 2)
BF16 = jnp.bfloat16
F32 = jnp.float32


def coords():
    dp = lax.axis_index("dp")
    return (lax.div(dp, 4), lax.rem(lax.div(dp, 2), 2), lax.rem(dp, 2), lax.axis_index("ctx"))


def device(z, y, x, c):
    return (z * 4 + y * 2 + x, c)


def when(cond, body):
    if cond is True:
        body()
    else:
        pl.when(cond)(body)


def greet():
    barrier = pltpu.get_barrier_semaphore()
    me = lax.axis_index("dp")
    c = lax.axis_index("ctx")
    for k in range(1, 16):
        pl.semaphore_signal(
            barrier, inc=1, device_id=(lax.rem(me + k, 16), c), device_id_type=MESH
        )
    pl.semaphore_signal(barrier, inc=1, device_id=(me, 1 - c), device_id_type=MESH)
    pl.semaphore_wait(barrier, 16)


class Exchange:
    def __init__(self, broadcast, in_ref, out_ref, ssem, rsem, lsem):
        self.refs = (in_ref, out_ref, ssem, rsem, lsem)
        self.broadcast = broadcast
        self.me = lax.axis_index("dp")

    def source(self, target):
        return self.refs[0] if self.broadcast else self.refs[0].at[target]

    def copy(self, k, target, slot):
        return pltpu.make_async_remote_copy(
            self.source(target),
            self.refs[1].at[slot],
            self.refs[2].at[k],
            self.refs[3].at[k],
            device_id=(target, lax.axis_index("ctx")),
            device_id_type=MESH,
        )

    def own(self):
        return pltpu.make_async_copy(
            self.source(self.me), self.refs[1].at[self.me], self.refs[4].at[0]
        )

    def start(self):
        for k in range(1, 16):
            self.copy(k, lax.rem(self.me + k, 16), self.me).start()
        self.own().start()

    def wait(self):
        self.own().wait()
        for k in range(1, 16):
            self.copy(k, lax.rem(self.me + k, 16), self.me).wait_send()
            origin = lax.rem(self.me + 16 - k, 16)
            self.copy(k, origin, origin).wait_recv()


def gather_kernel(units, count, stride, group, lag, *refs):
    w = refs[:count]
    o = refs[count + 1 : 2 * count + 1]
    ssem, rsem, lsem, csem, crsem, es, er, el = refs[2 * count + 2 :]
    z, y, x, c = coords()
    greet()
    side = Exchange(False, refs[count], refs[2 * count + 1], es, er, el)
    side.start()
    up = device(z + 1, y, x, c)
    down = device(z - 1, y, x, c)
    partner = {"y": device(z, 1 - y, x, c), "x": device(z, y, 1 - x, c)}
    every = slice(None)

    def run(mine, other):
        def view(u, index):
            m, first, cols, _ = mine[u]
            return o[m].at[index[0], index[1], index[2], :, pl.ds(first, cols)]

        def copy(u, index, k, target, own=False):
            m, first, cols, _ = mine[u]
            dst = view(u, index)
            src = w[m].at[:, pl.ds(first, cols)] if own else dst
            return pltpu.make_async_remote_copy(
                src, dst, ssem.at[u, k], rsem.at[u, k], device_id=target, device_id_type=MESH
            )

        def local_copy(u):
            m, first, cols, _ = mine[u]
            return pltpu.make_async_copy(
                w[m].at[:, pl.ds(first, cols)], view(u, (z, y, x)), lsem.at[u]
            )

        def plan(u):
            held = {"z": False, "y": False, "x": False}

            def index(zz=z, flip=None):
                return (
                    every if held["z"] else zz,
                    every if held["y"] else (1 - y if flip == "y" else y),
                    every if held["x"] else (1 - x if flip == "x" else x),
                )

            steps = []
            pending = []
            sends = []
            own = True
            pair = 0
            for axis in mine[u][3]:
                if axis != "z":
                    send = [(True, functools.partial(copy, u, index(), pair, partner[axis], own))]
                    steps.append((pending, send))
                    sends += send
                    pending = [
                        (True, functools.partial(copy, u, index(flip=axis), pair, partner[axis]))
                    ]
                    pair += 1
                else:

                    def chain(shift, k, target, first=False):
                        return functools.partial(copy, u, index(zz=z + shift), k, target, first)

                    one = [(z < 3, chain(0, 2, up, own)), (z > 0, chain(0, 5, down, own))]
                    steps.append((pending, one))
                    middle = (z > 0) & (z < 3)
                    two = [(middle, chain(-1, 3, up)), (middle, chain(1, 6, down))]
                    steps.append(([(z > 0, chain(-1, 2, down)), (z < 3, chain(1, 5, up))], two))
                    three = [(z == 2, chain(-2, 4, up)), (z == 1, chain(2, 7, down))]
                    steps.append(([(z > 1, chain(-2, 3, down)), (z < 2, chain(2, 6, up))], three))
                    pending = [(z == 3, chain(-3, 4, down)), (z == 0, chain(3, 7, up))]
                    sends += one + two + three
                held[axis] = True
                own = False
            return steps, pending, sends

        plans = [plan(u) for u in range(len(mine))]

        def to_core(u, which):
            m, first, cols, _ = which[u]
            block = o[m].at[:, :, :, :, pl.ds(first, cols)]
            return pltpu.make_async_remote_copy(
                block,
                block,
                csem.at[u],
                crsem.at[u],
                device_id=device(z, y, x, 1 - c),
                device_id_type=MESH,
            )

        for u in range(len(mine)):
            local_copy(u).start()
        starts = [(u // group) * stride for u in range(len(mine))]
        for turn in range(max(starts) + 6 + lag):
            for u in range(len(mine)):
                steps, pending, _ = plans[u]
                s = turn - starts[u]
                if 0 <= s < 5:
                    if s == 1:
                        local_copy(u).wait()
                    for cond, make in steps[s][0]:
                        when(cond, lambda make=make: make().wait_recv())
                    for cond, make in steps[s][1]:
                        when(cond, lambda make=make: make().start())
                elif s == 5 + lag:
                    for cond, make in pending:
                        when(cond, lambda make=make: make().wait_recv())
                    to_core(u, mine).start()
        for u in range(len(mine)):
            for cond, make in plans[u][2]:
                when(cond, lambda make=make: make().wait_send())
            to_core(u, mine).wait_send()
        for u in range(len(other)):
            to_core(u, other).wait_recv()

    pl.when(c == 0)(lambda: run(units[0], units[1]))
    pl.when(c == 1)(lambda: run(units[1], units[0]))
    side.wait()


ANY = pl.BlockSpec(memory_space=pl.ANY)
DMA = pltpu.SemaphoreType.DMA


SIDE = [DMA((16,)), DMA((16,)), DMA((1,))]


def gather(shards, rows, units, collective_id, stride, group, lag, name):
    count = len(shards)
    most = max(len(units[0]), len(units[1]))
    shapes = [jax.ShapeDtypeStruct(GRID + s.shape, s.dtype) for s in shards]
    return pl.pallas_call(
        functools.partial(gather_kernel, units, count, stride, group, lag),
        name=name,
        out_shape=shapes + [jax.ShapeDtypeStruct(rows.shape, rows.dtype)],
        in_specs=[ANY] * (count + 1),
        out_specs=[ANY] * (count + 1),
        scratch_shapes=[DMA((most, 8)), DMA((most, 8)), DMA((most,)), DMA((most,)), DMA((most,))]
        + SIDE,
        compiler_params=pltpu.CompilerParams(collective_id=collective_id, has_side_effects=True),
    )(*shards, rows)


def gather_units(shards, size):
    orders = (
        ("xzy", "yzx", "zyx", "yzx", "xzy", "zxy"),
        ("yzx", "xzy", "zxy", "xzy", "yzx", "zyx"),
    )
    units = ([], [])
    load = [0, 0]
    for m, shard in enumerate(shards):
        rows, columns = shard.shape
        tiles = columns // 128
        cuts = max(1, round(tiles * rows / 72 / size))
        at = 0
        for k in range(cuts):
            n = tiles // cuts + (1 if k < tiles % cuts else 0)
            core = 0 if load[0] <= load[1] else 1
            order = orders[core][len(units[core]) % 6]
            units[core].append((m, at * 128, n * 128, order))
            load[core] += n * rows
            at += n
    return tuple(units[0]), tuple(units[1])


def exchange_kernel(in_ref, out_ref, *sems):
    greet()
    side = Exchange(True, in_ref, out_ref, *sems)
    side.start()
    side.wait()


def exchange(values, collective_id, name):
    return pl.pallas_call(
        exchange_kernel,
        name=name,
        out_shape=jax.ShapeDtypeStruct((16,) + values.shape, values.dtype),
        in_specs=[ANY],
        out_specs=ANY,
        scratch_shapes=SIDE,
        compiler_params=pltpu.CompilerParams(collective_id=collective_id, has_side_effects=True),
    )(values)


LAG = (0, 2, 3, 4, 5, 6)
RECV_SLOTS = 9
SEND_SLOTS = 8
FIRST_SLOTS = 4
UNIT = 384
ROWS = 72
PADDED = 80


def scatter_kernel(first, cols, source, dy_count, *refs):
    nv = len(first) - 1
    xt = refs[:nv]
    dy = refs[nv : nv + dy_count]
    out = refs[nv + dy_count + 1]
    (
        xts, dys, a_s1, a_s2, a_t, a_su, a_sd, e_s1, e_t, e_su, e_sd, e_sq,
        a_b1, a_b2, a_bu, a_bd, e_b1, e_bu, e_bd, e_bq, outs,
        ssem, rsem, xl, xs, xr, yl, ys, yr, ol, os, orr, es, er, el,
    ) = refs[nv + dy_count + 3 :]
    z, y, x, c = coords()
    total = first[-1] // 2
    sibling = device(z, y, x, 1 - c)
    up = device(z + 1, y, x, c)
    down = device(z - 1, y, x, c)
    greet()
    side = Exchange(True, refs[nv + dy_count], refs[nv + dy_count + 2], es, er, el)
    lanes = pl.ds(pl.multiple_of(c * 128, 128), 128)
    offsets = []
    at = 0
    for k in range(dy_count):
        offsets.append(at)
        at += dy[k].shape[1]

    def remote(src, dst, send, recv, target):
        return pltpu.make_async_remote_copy(
            src, dst, send, recv, device_id=target, device_id_type=MESH
        )

    def x_views(v):
        return xt[v], xts.at[v, :, :, lanes]

    def x_local(v):
        return pltpu.make_async_copy(*x_views(v), xl.at[v])

    def x_remote(v):
        return remote(*x_views(v), xs.at[v], xr.at[v], sibling)

    def y_views(k):
        return dy[k], dys.at[lanes, pl.ds(offsets[k], dy[k].shape[1])]

    def y_local(k):
        return pltpu.make_async_copy(*y_views(k), yl.at[k])

    def y_remote(k):
        return remote(*y_views(k), ys.at[k], yr.at[k], sibling)

    fresh = [source[v] not in source[:v] for v in range(nv)]
    for v in range(nv):
        x_local(v).start()
        x_remote(v).start()
        if fresh[v]:
            y_local(source[v]).start()
            y_remote(source[v]).start()
        if v == 0:
            side.start()

    def arrive(tick):
        for v in range(nv):

            def wait(v=v):
                x_local(v).wait()
                x_remote(v).wait_recv()
                if fresh[v]:
                    y_local(source[v]).wait()
                    y_remote(source[v]).wait_recv()

            pl.when(tick == (first[v] - c + 1) // 2)(wait)

    def unit(i):
        j = 2 * i + c
        v = jnp.int32(0)
        col = j * UNIT
        for k in range(1, nv):
            past = (j >= first[k]).astype(jnp.int32)
            v = v + past
            col = col + past * ((cols[k] - first[k] * UNIT) - (cols[k - 1] - first[k - 1] * UNIT))
        return v, pl.multiple_of(col, 128)

    def axes(i):
        o = lax.rem(i, 2)
        pb = x * (1 - o) + y * o
        qb = y * (1 - o) + x * o
        dp = z * 4 + y * 2 + x
        return o, pb, qb, (dp + (1 - 2 * pb) * (1 + o), c), (dp + (1 - 2 * qb) * (2 - o), c)

    def slots(i):
        return lax.rem(i, FIRST_SLOTS), lax.rem(i, SEND_SLOTS), lax.rem(i, RECV_SLOTS)

    def send(src, dst, i, k, target):
        return remote(
            src, dst, ssem.at[lax.rem(i, SEND_SLOTS), k], rsem.at[lax.rem(i, RECV_SLOTS), k], target
        )

    def first_copies(i):
        o, pb, qb, pn, qn = axes(i)
        f, s, w = slots(i)
        return [send(a_s1.at[f], a_b1.at[w], i, 0, pn), send(e_s1.at[f], e_b1.at[w], i, 8, pn)]

    def second_copy(i):
        o, pb, qb, pn, qn = axes(i)
        f, s, w = slots(i)
        return send(a_s2.at[s], a_b2.at[w], i, 1, qn)

    def last_copy(i):
        o, pb, qb, pn, qn = axes(i)
        f, s, w = slots(i)
        return send(e_sq.at[s], e_bq.at[w], i, 9, qn)

    def up_copy(i, k, e):
        f, s, w = slots(i)
        src, dst, n = (e_su, e_bu, 10) if e else (a_su, a_bu, 2)
        return send(src.at[s, k], dst.at[w, k], i, n + k, up)

    def down_copy(i, k, e):
        f, s, w = slots(i)
        src, dst, n = (e_sd, e_bd, 13) if e else (a_sd, a_bd, 5)
        return send(src.at[s, k], dst.at[w, k], i, n + k, down)

    def up_sends(k):
        return (z <= k) & (z < 3)

    def down_sends(k):
        return (3 - z <= k) & (z > 0)

    def up_comes(k):
        return (z >= 1) & (z <= k + 1)

    def down_comes(k):
        return (z <= 2) & (3 - z <= k + 1)

    def kept(i, e, d):
        f, s, w = slots(i)
        if e:
            return e_t.at[s, d]
        return a_t.at[s, d, axes(i)[2]]

    def z_send(i, k, e):
        f, s, w = slots(i)

        def pass_on(dest, stage, box, inner, copy):
            value = kept(i, e, dest)[...]
            if k == 0:
                stage[s, k] = value.astype(BF16)
            else:

                def add():
                    stage[s, k] = (value + box[w, k - 1].astype(F32)).astype(BF16)

                def begin():
                    stage[s, k] = value.astype(BF16)

                pl.when(inner)(add)
                pl.when(jnp.logical_not(inner))(begin)
            copy.start()

        pl.when(up_sends(k))(
            lambda: pass_on(
                z + 3 - k, e_su if e else a_su, e_bu if e else a_bu, z > 0, up_copy(i, k, e)
            )
        )
        pl.when(down_sends(k))(
            lambda: pass_on(
                z + k - 3, e_sd if e else a_sd, e_bd if e else a_bd, z < 3, down_copy(i, k, e)
            )
        )

    def z_wait(i, k, e):
        pl.when(up_comes(k))(lambda: up_copy(i, k, e).wait_recv())
        pl.when(down_comes(k))(lambda: down_copy(i, k, e).wait_recv())

    def z_close(i, e):
        f, s, w = slots(i)
        mine = kept(i, e, z)

        def below():
            mine[...] = mine[...] + (e_bu if e else a_bu)[w, 2].astype(F32)

        def above():
            mine[...] = mine[...] + (e_bd if e else a_bd)[w, 2].astype(F32)

        pl.when(z > 0)(below)
        pl.when(z < 3)(above)
        return mine

    def product(i, bit):
        v, col = unit(i)
        o = axes(i)[0]
        chips = [4 * k + bit * (1 + o) + q * (2 - o) for k in range(4) for q in range(2)]
        lhs = jnp.concatenate([xts[v, chip] for chip in chips], axis=0)
        whole = jnp.dot(lhs, dys[:, pl.ds(col, UNIT)], preferred_element_type=F32)
        return whole.reshape(8, PADDED, UNIT)[:, :ROWS]

    def stage0(i):
        f, s, w = slots(i)
        part = product(i, 1 - axes(i)[1])
        a_s1[f] = part[:, :, :128].astype(BF16).reshape(4, 2, ROWS, 128)
        e_s1[f] = part[:, :, 128:].astype(BF16).reshape(4, 2, ROWS, 256)
        for copy in first_copies(i):
            copy.start()

    def stage1(i):
        f, s, w = slots(i)
        o, pb, qb, pn, qn = axes(i)
        part = product(i, pb)
        for copy in first_copies(i):
            copy.wait_recv()
        a_t[s] = part[:, :, :128].reshape(4, 2, ROWS, 128) + a_b1[w].astype(F32)
        a_s2[s] = a_t[s, :, 1 - qb].astype(BF16)
        second_copy(i).start()
        e_t[s] = part[:, :, 128:].reshape(4, 2, ROWS, 256) + e_b1[w].astype(F32)
        z_send(i, 0, True)

    def stage2(i):
        f, s, w = slots(i)
        qb = axes(i)[2]
        second_copy(i).wait_recv()
        a_t[s, :, qb] = a_t[s, :, qb] + a_b2[w].astype(F32)
        z_send(i, 0, False)
        z_wait(i, 0, True)
        z_send(i, 1, True)

    def stage3(i):
        z_wait(i, 0, False)
        z_send(i, 1, False)
        z_wait(i, 1, True)
        z_send(i, 2, True)

    def stage4(i):
        f, s, w = slots(i)
        z_wait(i, 1, False)
        z_send(i, 2, False)
        z_wait(i, 2, True)
        z_close(i, True)
        e_sq[s] = e_t[s, z, 1 - axes(i)[2]].astype(BF16)
        last_copy(i).start()

    def out_view(i):
        return out.at[:, pl.ds(pl.multiple_of((2 * i + c) * UNIT, 128), UNIT)]

    def stage5(i):
        f, s, w = slots(i)
        z_wait(i, 2, False)
        outs[i, :, :128] = z_close(i, False)[...]
        last_copy(i).wait_recv()
        outs[i, :, 128:] = e_t[s, z, axes(i)[2]] + e_bq[w].astype(F32)
        pltpu.make_async_copy(outs.at[i], out_view(i), ol.at[0]).start()
        remote(outs.at[i], out_view(i), os.at[0], orr.at[0], sibling).start()

    def first_sent(i):
        for copy in first_copies(i):
            copy.wait_send()

    def sent(i):
        second_copy(i).wait_send()
        last_copy(i).wait_send()
        for e in (False, True):
            for k in range(3):
                pl.when(up_sends(k))(lambda k=k, e=e: up_copy(i, k, e).wait_send())
                pl.when(down_sends(k))(lambda k=k, e=e: down_copy(i, k, e).wait_send())

    stages = (stage0, stage1, stage2, stage3, stage4, stage5)

    def tick(t, carry):
        arrive(t)
        pl.when((t >= SEND_SLOTS) & (t - SEND_SLOTS < total))(lambda: sent(t - SEND_SLOTS))
        pl.when((t >= FIRST_SLOTS) & (t - FIRST_SLOTS < total))(lambda: first_sent(t - FIRST_SLOTS))
        for k in reversed(range(6)):
            i = t - LAG[k]
            pl.when((i >= 0) & (i < total))(functools.partial(stages[k], i))
        return carry

    lax.fori_loop(0, total + SEND_SLOTS, tick, 0)
    for v in range(nv):
        x_remote(v).wait_send()
    for k in range(dy_count):
        y_remote(k).wait_send()
    half = out.at[:, pl.ds(0, total * UNIT)]
    pltpu.make_async_copy(half, half, ol.at[0]).wait()
    everything = remote(half, half, os.at[0], orr.at[0], sibling)
    everything.wait_send()
    everything.wait_recv()
    side.wait()


def scatter(xts, dys, source, rows, collective_id, name):
    nv = len(xts)
    starts = []
    width = 0
    for d in dys:
        starts.append(width)
        width += d.shape[1]
    first = [0]
    cols = []
    for v in range(nv):
        cols.append(starts[source[v]])
        first.append(first[-1] + dys[source[v]].shape[1] // UNIT)
    total = first[-1] // 2
    s, f, r = SEND_SLOTS, FIRST_SLOTS, RECV_SLOTS
    vmem = pltpu.VMEM
    return pl.pallas_call(
        functools.partial(scatter_kernel, tuple(first), tuple(cols), tuple(source), len(dys)),
        name=name,
        out_shape=[
            jax.ShapeDtypeStruct((ROWS, first[-1] * UNIT), F32),
            jax.ShapeDtypeStruct((16,) + rows.shape, rows.dtype),
        ],
        in_specs=[ANY] * (nv + len(dys) + 1),
        out_specs=[ANY] * 2,
        scratch_shapes=[
            vmem((nv, 16, PADDED, 256), BF16),
            vmem((256, width), BF16),
            vmem((f, 4, 2, ROWS, 128), BF16),
            vmem((s, 4, ROWS, 128), BF16),
            vmem((s, 4, 2, ROWS, 128), F32),
            vmem((s, 3, ROWS, 128), BF16),
            vmem((s, 3, ROWS, 128), BF16),
            vmem((f, 4, 2, ROWS, 256), BF16),
            vmem((s, 4, 2, ROWS, 256), F32),
            vmem((s, 3, 2, ROWS, 256), BF16),
            vmem((s, 3, 2, ROWS, 256), BF16),
            vmem((s, ROWS, 256), BF16),
            vmem((r, 4, 2, ROWS, 128), BF16),
            vmem((r, 4, ROWS, 128), BF16),
            vmem((r, 3, ROWS, 128), BF16),
            vmem((r, 3, ROWS, 128), BF16),
            vmem((r, 4, 2, ROWS, 256), BF16),
            vmem((r, 3, 2, ROWS, 256), BF16),
            vmem((r, 3, 2, ROWS, 256), BF16),
            vmem((r, ROWS, 256), BF16),
            vmem((total, ROWS, UNIT), F32),
            DMA((s, 16)),
            DMA((r, 16)),
            DMA((nv,)),
            DMA((nv,)),
            DMA((nv,)),
            DMA((len(dys),)),
            DMA((len(dys),)),
            DMA((len(dys),)),
            DMA((1,)),
            DMA((1,)),
            DMA((1,)),
        ]
        + SIDE,
        compiler_params=pltpu.CompilerParams(
            collective_id=collective_id, has_side_effects=True, vmem_limit_bytes=62 * 1024 * 1024
        ),
    )(*xts, *dys, rows)


def layer_norm(values):
    center = values - jnp.mean(values, axis=-1, keepdims=True)
    spread = jnp.mean(center * center, axis=-1, keepdims=True)
    return center * lax.rsqrt(spread + 1e-06)


def head_norm(values, gain):
    shaped = values.reshape(values.shape[:-1] + (HEADS, HD))
    scaled = shaped * lax.rsqrt(jnp.mean(shaped * shaped, axis=-1, keepdims=True) + 1e-06)
    return scaled * gain.reshape(HEADS, HD)


def rope_tables(rows, columns):
    quarter = HD // 4
    freqs = jnp.exp(jnp.arange(quarter, dtype=F32) * (-math.log(10000.0) / quarter))
    places = jnp.stack([rows, columns], axis=-1).astype(F32)
    angles = places[..., None] * freqs
    return (jnp.cos(angles), jnp.sin(angles))


def rotate(values, cosine, sine):
    shaped = values.reshape(values.shape[:-1] + (2, 2, HD // 4))
    first = shaped[..., 0, :]
    second = shaped[..., 1, :]
    cosine = cosine[..., None, :, :]
    sine = sine[..., None, :, :]
    turned = jnp.stack([first * cosine - second * sine, first * sine + second * cosine], axis=-2)
    return turned.reshape(values.shape)


def embed_times(times, width):
    half_width = width // 2
    freqs = jnp.exp(jnp.arange(half_width, dtype=F32) * (-math.log(10000.0) / half_width))
    angles = times[..., None] * freqs
    return jnp.concatenate([jnp.cos(angles), jnp.sin(angles)], axis=-1)


def qk_prepare(query_raw, key_raw, gains, cosine, sine):
    return (
        rotate(head_norm(query_raw, gains[0]), cosine, sine),
        rotate(head_norm(key_raw, gains[1]), cosine, sine),
    )


def swish_product(gate, up):
    return jax.nn.silu(gate) * up


def attention_scores(queries, keys, allowed):
    scores = jnp.einsum("sqhd,skhd->shqk", queries, keys, preferred_element_type=F32) * (
        1.0 / math.sqrt(HD)
    )
    return jnp.where(allowed[:, None], scores, -1e30)


def dense(values, weight):
    return jnp.dot(values, weight, preferred_element_type=F32)


def dense_back(grads, weight):
    return lax.dot_general(grads, weight, (((1,), (1,)), ((), ())), preferred_element_type=F32)


def outer_sum(values, grads):
    return lax.dot_general(values, grads, (((0,), (0,)), ((), ())), preferred_element_type=F32)


def block_forward(flat, modulation, weights, context):
    batch, half, allowed, cosine, sine = context
    triple, mixing, expand, reduce_w, gains = weights
    width = flat.shape[1]
    shift1, scale1, gate1, shift2, scale2, gate2 = jnp.split(modulation, 6, axis=1)
    lifted1 = (layer_norm(flat) * (1.0 + scale1) + shift1).astype(BF16)
    projected = dense(lifted1, triple)
    query_raw, key_raw, value_raw = jnp.split(projected, 3, axis=1)
    queries, keys = qk_prepare(query_raw, key_raw, gains, cosine, sine)
    queries = queries.astype(BF16).reshape(batch, half, HEADS, HD)
    keys_local = keys.astype(BF16).reshape(batch, half, width)
    values_local = value_raw.astype(BF16).reshape(batch, half, width)
    key_heads = lax.all_gather(keys_local, "ctx", axis=1, tiled=True).reshape(batch, -1, HEADS, HD)
    value_heads = lax.all_gather(values_local, "ctx", axis=1, tiled=True)
    value_heads = value_heads.reshape(batch, -1, HEADS, HD)
    scores = attention_scores(queries, key_heads, allowed)
    top = jnp.max(scores, axis=-1, keepdims=True)
    raised = jnp.exp(scores - top)
    total = jnp.sum(raised, axis=-1, keepdims=True)
    softmax_low = (raised / total).astype(BF16)
    logsum = top + jnp.log(total)
    mixed = jnp.einsum("shqk,skhd->sqhd", softmax_low, value_heads, preferred_element_type=F32)
    mixed_low = mixed.reshape(-1, width).astype(BF16)
    attended = dense(mixed_low, mixing)
    resid = flat + gate1 * attended
    lifted2 = (layer_norm(resid) * (1.0 + scale2) + shift2).astype(BF16)
    expanded = dense(lifted2, expand)
    gate, up = jnp.split(expanded, 2, axis=1)
    hidden = swish_product(gate, up).astype(BF16)
    feed = dense(hidden, reduce_w)
    output = resid + gate2 * feed
    kept = (
        modulation,
        flat,
        lifted1,
        query_raw,
        key_raw,
        queries,
        key_heads,
        value_heads,
        logsum,
        mixed_low,
        attended,
        resid,
        lifted2,
        expanded,
        hidden,
        feed,
    )
    return (output, kept)


def block_backward(grad_out, kept, weights, context):
    batch, half, allowed, cosine, sine = context
    triple, mixing, expand, reduce_w, gains = weights
    (
        modulation,
        flat,
        lifted1,
        query_raw,
        key_raw,
        queries,
        key_heads,
        value_heads,
        logsum,
        mixed_low,
        attended,
        resid,
        lifted2,
        expanded,
        hidden,
        feed,
    ) = kept
    width = flat.shape[1]
    shift1, scale1, gate1, shift2, scale2, gate2 = jnp.split(modulation, 6, axis=1)
    grad_feed = (grad_out * gate2).astype(BF16)
    grad_hidden = dense_back(grad_feed, reduce_w)
    gate, up = jnp.split(expanded, 2, axis=1)
    unused_out, swish_pull = jax.vjp(swish_product, gate, up)
    grad_gate, grad_up = swish_pull(grad_hidden)
    grad_expanded = jnp.concatenate([grad_gate, grad_up], axis=1).astype(BF16)
    grad_lifted2 = dense_back(grad_expanded, expand)
    normed_second, second_pull = jax.vjp(layer_norm, resid)
    grad_resid = grad_out + second_pull(grad_lifted2 * (1.0 + scale2))[0]
    grad_attended = (grad_resid * gate1).astype(BF16)
    grad_mixed = dense_back(grad_attended, mixing).astype(BF16).reshape(batch, half, HEADS, HD)
    scores = attention_scores(queries, key_heads, allowed)
    chances = jnp.exp(scores - logsum)
    grad_chances = jnp.einsum(
        "sqhd,skhd->shqk", grad_mixed, value_heads, preferred_element_type=F32
    )
    grad_values = jnp.einsum(
        "shqk,sqhd->skhd", chances.astype(BF16), grad_mixed, preferred_element_type=F32
    )
    grad_scores = (
        chances * (grad_chances - jnp.sum(chances * grad_chances, axis=-1, keepdims=True))
    ).astype(BF16)
    scale = 1.0 / math.sqrt(HD)
    grad_queries = (
        jnp.einsum("shqk,skhd->sqhd", grad_scores, key_heads, preferred_element_type=F32) * scale
    )
    grad_keys = (
        jnp.einsum("shqk,sqhd->skhd", grad_scores, queries, preferred_element_type=F32) * scale
    )
    pair = jnp.stack(
        [grad_keys.reshape(batch, -1, width), grad_values.reshape(batch, -1, width)]
    ).astype(BF16)
    place = lax.axis_index("ctx")
    theirs = lax.dynamic_slice_in_dim(pair, (1 - place) * half, half, 2)
    theirs = lax.ppermute(theirs, "ctx", [(0, 1), (1, 0)])
    mine = lax.dynamic_slice_in_dim(pair, place * half, half, 2)
    pair = mine.astype(F32) + theirs.astype(F32)
    grad_keys, grad_values = pair[0], pair[1]

    def prepare(query_in, key_in, gain_in):
        return qk_prepare(query_in, key_in, gain_in, cosine, sine)

    unused_pair, prepare_pull = jax.vjp(prepare, query_raw, key_raw, gains)
    grad_query_raw, grad_key_raw, gains_grad = prepare_pull(
        (grad_queries.reshape(-1, HEADS, HD), grad_keys.reshape(-1, HEADS, HD))
    )
    grad_projected = jnp.concatenate(
        [grad_query_raw, grad_key_raw, grad_values.reshape(-1, width)], axis=1
    ).astype(BF16)
    grad_lifted1 = dense_back(grad_projected, triple)
    normed_first, first_pull = jax.vjp(layer_norm, flat)
    grad_flat = grad_resid + first_pull(grad_lifted1 * (1.0 + scale1))[0]
    grad_modulation = jnp.concatenate(
        [
            grad_lifted1,
            grad_lifted1 * normed_first,
            grad_resid * attended,
            grad_lifted2,
            grad_lifted2 * normed_second,
            grad_out * feed,
        ],
        axis=1,
    ).astype(BF16)
    factors = (
        (lifted1, grad_projected),
        (mixed_low, grad_attended),
        (lifted2, grad_expanded),
        (hidden, grad_feed),
    )
    return (grad_flat, grad_modulation, factors, gains_grad)


def shard_rows(values, groups):
    turned = values.T.reshape(16, groups, -1, values.shape[0])
    rows = turned.shape[2]
    turned = jnp.pad(turned, ((0, 0), (0, 0), (0, PADDED - rows), (0, 0)))
    return [turned[:, g] for g in range(groups)]


def fast_reduce(blocks, rows, collective_id, name):
    xts = []
    dys = []
    source = []
    for factors, extra in blocks:
        for k, (left, right) in enumerate(factors):
            groups = 3 if k == len(factors) - 1 else 1
            source += [len(dys)] * groups
            xts += shard_rows(left, groups)
            dys.append(right)
        tokens = left.shape[0]
        lines = -(-extra.shape[1] // tokens)
        packed = jnp.pad(extra, ((0, 0), (0, lines * tokens - extra.shape[1])))
        packed = packed.reshape(16, lines, tokens).astype(BF16)
        xts.append(jnp.pad(packed, ((0, 0), (0, PADDED - lines), (0, 0))))
        source.append(len(dys))
        dys.append(jnp.eye(tokens, UNIT, dtype=BF16))
    out, rows = scatter(xts, dys, source, rows, collective_id, name)
    results = []
    at = 0
    for factors, extra in blocks:
        grads = []
        for left, right in factors[:-1]:
            grads.append(out[:, at : at + right.shape[1]])
            at += right.shape[1]
        width = factors[-1][1].shape[1]
        count = factors[-1][0].shape[1] // 48
        parts = [out[:count, at + g * width : at + (g + 1) * width] for g in range(3)]
        grads.append(jnp.concatenate(parts, axis=0))
        at += 3 * width
        lines = -(-extra.shape[1] // tokens)
        small = out[:lines, at : at + tokens].reshape(-1)[: extra.shape[1]]
        at += UNIT
        results.append((grads, small))
    return results, rows


def whole_rows(gathered):
    return gathered.reshape((-1,) + gathered.shape[4:])


def fast_step(flat, cotangent, context, segment_local, valid, timesteps, encoder, decoder):
    width = flat.shape[1]
    offset_size = encoder[1].shape[0]
    gain_size = 2 * encoder[3].shape[1]
    small = jnp.concatenate(
        [
            encoder[1].astype(F32),
            decoder[1].astype(F32),
            encoder[3].astype(F32).reshape(-1),
            decoder[3].astype(F32).reshape(-1),
            timesteps.astype(F32).reshape(-1),
        ]
    )
    size = small.shape[0]
    small = jnp.pad(small, (0, 2048 - size)).reshape(16, 128)
    small = exchange(small, 0, "small").reshape(16, -1)
    encoder_offset = small[:, :offset_size].reshape(-1)
    decoder_offset = small[:, offset_size : 2 * offset_size].reshape(-1)
    at = 2 * offset_size
    encoder_gains = small[:, at : at + gain_size].reshape(16, 2, -1).swapaxes(0, 1).reshape(2, -1)
    at += gain_size
    decoder_gains = small[:, at : at + gain_size].reshape(16, 2, -1).swapaxes(0, 1).reshape(2, -1)
    at += gain_size
    all_times = small[:, at : at + timesteps.size]
    segments = timesteps.shape[1]
    picks = (segment_local[..., None] == jnp.arange(segments, dtype=jnp.int32)).astype(F32)
    picks = picks.reshape(-1, segments)

    all_cond = embed_times(all_times, width).reshape(-1, width)
    act_rows = jax.nn.silu(all_cond).astype(BF16)
    me = lax.axis_index("dp")
    rows = encoder[0].shape[0]
    act_mine = lax.dynamic_slice_in_dim(act_rows, me * rows, rows, 1)
    partial = dense(act_mine, encoder[0]).reshape(16, 8, -1)
    shards = (encoder[2], encoder[4], encoder[5], encoder[6])
    shards += (decoder[0], decoder[2], decoder[4], decoder[5], decoder[6])
    *wholes, partial = gather(shards, partial, gather_units(shards, 7), 1, 1, 3, 1, "gather")
    wholes = [whole_rows(w) for w in wholes]
    encoder_weights = (*wholes[:4], encoder_gains)
    modulate = wholes[4]
    decoder_weights = (*wholes[5:], decoder_gains)
    modulation_rows = jnp.sum(partial, axis=0).reshape(segments, -1) + encoder_offset
    exact = lax.Precision.HIGHEST
    encoder_modulation = jnp.dot(picks, modulation_rows, precision=exact)
    cond_rows = lax.dynamic_slice_in_dim(all_cond, me * segments, segments, 0)
    cond = jnp.dot(picks, cond_rows, precision=exact)

    encoder_out, encoder_kept = block_forward(flat, encoder_modulation, encoder_weights, context)
    latent_full = valid * encoder_out
    decoder_pre = latent_full + cond
    decoder_act = jax.nn.silu(decoder_pre).astype(BF16)

    decoder_modulation = dense(decoder_act, modulate) + decoder_offset
    decoder_out, decoder_kept = block_forward(flat, decoder_modulation, decoder_weights, context)
    velocity = valid * decoder_out

    grad_out = valid * cotangent
    decoder_flat, grad_modulation, factors, gains_grad = block_backward(
        grad_out, decoder_kept, decoder_weights, context
    )
    grad_act = dense_back(grad_modulation, modulate)
    unused_silu, silu_pull = jax.vjp(jax.nn.silu, decoder_pre)
    grad_latent = valid * silu_pull(grad_act)[0]
    offset_grad = jnp.sum(grad_modulation, axis=0, dtype=F32)
    extra = jnp.concatenate(
        [
            offset_grad.reshape(16, -1),
            gains_grad.reshape(2, 16, -1).swapaxes(0, 1).reshape(16, -1),
        ],
        axis=1,
    )
    decoder_block = (((decoder_act, grad_modulation),) + factors, extra)

    encoder_flat, grad_modulation, factors, gains_grad = block_backward(
        grad_latent, encoder_kept, encoder_weights, context
    )
    grad_rows = lax.dot_general(
        picks.astype(BF16), grad_modulation, (((0,), (0,)), ((), ())), preferred_element_type=F32
    )
    grad_rows = grad_rows + lax.ppermute(grad_rows, "ctx", [(0, 1), (1, 0)])
    extra = gains_grad.reshape(2, 16, -1).swapaxes(0, 1).reshape(16, -1)
    results, all_rows = fast_reduce(
        (decoder_block, (factors, extra)), grad_rows.astype(BF16).reshape(16, -1), 2, "scatter"
    )
    (grads, small), (encoder_parts, encoder_small) = results
    decoder_grads = (
        grads[0],
        small[:offset_size],
        grads[1],
        small[offset_size:].reshape(2, -1),
        grads[2],
        grads[3],
        grads[4],
    )
    all_rows = all_rows.reshape(16 * segments, -1)
    modulate_grad = outer_sum(act_mine, all_rows)
    offset_grad = lax.dynamic_slice_in_dim(
        jnp.sum(all_rows.astype(F32), axis=0), me * offset_size, offset_size, 0
    )
    encoder_grads = (
        modulate_grad,
        offset_grad,
        encoder_parts[0],
        encoder_small.reshape(2, -1),
        encoder_parts[1],
        encoder_parts[2],
        encoder_parts[3],
    )
    return velocity, latent_full, decoder_flat + encoder_flat, encoder_grads, decoder_grads


def plain_gather(block):
    parts = [lax.all_gather(block[k], "dp", axis=0, tiled=True) for k in (0, 1, 2, 4, 5, 6)]
    gains = lax.all_gather(block[3], "dp", axis=1, tiled=True).astype(F32)
    modulate, offset, triple, mixing, expand, reduce_w = parts
    return modulate, offset.astype(F32), (triple, mixing, expand, reduce_w, gains)


def plain_reduce(factors, grad_modulation, gains_grad):
    def rows(values, dim=0):
        part = lax.psum_scatter(values, "dp", scatter_dimension=dim, tiled=True)
        return lax.psum(part.astype(BF16), "ctx").astype(F32)

    offset = rows(jnp.sum(grad_modulation, axis=0, dtype=F32))
    modulate, triple, mixing, expand, reduce_w = [rows(outer_sum(a, b)) for a, b in factors]
    return modulate, offset, triple, rows(gains_grad, 1), mixing, expand, reduce_w


def plain_step(flat, cotangent, context, segment_local, valid, timesteps, encoder, decoder):
    picks = (
        segment_local[..., None] == jnp.arange(timesteps.shape[-1], dtype=jnp.int32)
    ).astype(F32)
    times = jnp.sum(picks * timesteps[:, None, :].astype(F32), axis=-1)
    cond = embed_times(times, flat.shape[1]).reshape(flat.shape)
    modulate, offset, encoder_weights = plain_gather(encoder)
    encoder_act = jax.nn.silu(cond).astype(BF16)
    encoder_out, encoder_kept = block_forward(
        flat, dense(encoder_act, modulate) + offset, encoder_weights, context
    )
    latent_full = valid * encoder_out
    decoder_pre = latent_full + cond
    decoder_act = jax.nn.silu(decoder_pre).astype(BF16)
    modulate, offset, decoder_weights = plain_gather(decoder)
    decoder_out, decoder_kept = block_forward(
        flat, dense(decoder_act, modulate) + offset, decoder_weights, context
    )
    decoder_flat, grad_modulation, factors, gains_grad = block_backward(
        valid * cotangent, decoder_kept, decoder_weights, context
    )
    grad_act = dense_back(grad_modulation, modulate)
    decoder_grads = plain_reduce(
        ((decoder_act, grad_modulation),) + factors, grad_modulation, gains_grad
    )
    unused_silu, silu_pull = jax.vjp(jax.nn.silu, decoder_pre)
    encoder_flat, grad_modulation, factors, gains_grad = block_backward(
        valid * silu_pull(grad_act)[0], encoder_kept, encoder_weights, context
    )
    encoder_grads = plain_reduce(
        ((encoder_act, grad_modulation),) + factors, grad_modulation, gains_grad
    )
    return valid * decoder_out, latent_full, decoder_flat + encoder_flat, encoder_grads, decoder_grads


def local(fast, tokens, cotangent, segment, rows, columns, padding, timesteps, *weights):
    batch, half, width = tokens.shape
    start = lax.axis_index("ctx") * half
    segment_local = lax.dynamic_slice_in_dim(segment, start, half, 1)
    rows_local = lax.dynamic_slice_in_dim(rows, start, half, 1)
    columns_local = lax.dynamic_slice_in_dim(columns, start, half, 1)
    padding_local = lax.dynamic_slice_in_dim(padding, start, half, 1)
    place_query = start + jnp.arange(half, dtype=jnp.int32)
    place_key = jnp.arange(segment.shape[1], dtype=jnp.int32)
    allowed = (segment_local[:, :, None] == segment[:, None, :]) & (
        (padding[:, None, :] == 0) | (place_query[None, :, None] == place_key[None, None, :])
    )
    cosine, sine = rope_tables(rows_local.reshape(-1), columns_local.reshape(-1))
    context = (batch, half, allowed, cosine, sine)
    valid = (1 - padding_local).astype(F32).reshape(-1, 1)
    flat = tokens.reshape(-1, width).astype(F32)
    step = fast_step if fast else plain_step
    velocity, latent, token_grad, encoder_grads, decoder_grads = step(
        flat,
        cotangent.reshape(-1, width).astype(F32),
        context,
        segment_local,
        valid,
        timesteps,
        weights[:7],
        weights[7:],
    )
    return (
        velocity.astype(BF16).reshape(batch, half, width),
        latent.astype(BF16).reshape(batch, half, width),
        token_grad.reshape(batch, half, width),
        *encoder_grads,
        *decoder_grads,
    )


def solution(mesh):
    fast = dict(mesh.shape) == {"dp": math.prod(GRID), "ctx": 2}
    block = (
        P("dp", None),
        P("dp"),
        P("dp", None),
        P(None, "dp"),
        P("dp", None),
        P("dp", None),
        P("dp", None),
    )
    slots = P("dp", "ctx", None)
    return jax.shard_map(
        functools.partial(local, fast),
        mesh=mesh,
        in_specs=(slots, slots) + (P("dp", None),) * 5 + block + block,
        out_specs=(slots, slots, slots) + block + block,
        check_vma=False,
    )
```

```python
import functools
import math

import jax
import jax.numpy as jnp
from jax import lax
from jax.experimental import pallas as pl
from jax.experimental.pallas import tpu as pltpu
from jax.sharding import PartitionSpec as P

HEADS = 16
HD = 72
MESH = pl.DeviceIdType.MESH
GRID = (4, 2, 2)
BF16 = jnp.bfloat16
F32 = jnp.float32


def coords():
    dp = lax.axis_index("dp")
    return (lax.div(dp, 4), lax.rem(lax.div(dp, 2), 2), lax.rem(dp, 2), lax.axis_index("ctx"))


def device(z, y, x, c):
    return (z * 4 + y * 2 + x, c)


def when(cond, body):
    if cond is True:
        body()
    else:
        pl.when(cond)(body)


def greet():
    barrier = pltpu.get_barrier_semaphore()
    me = lax.axis_index("dp")
    c = lax.axis_index("ctx")
    for k in range(1, 16):
        pl.semaphore_signal(
            barrier, inc=1, device_id=(lax.rem(me + k, 16), c), device_id_type=MESH
        )
    pl.semaphore_signal(barrier, inc=1, device_id=(me, 1 - c), device_id_type=MESH)
    pl.semaphore_wait(barrier, 16)


class Exchange:
    def __init__(self, broadcast, in_ref, out_ref, ssem, rsem, lsem):
        self.refs = (in_ref, out_ref, ssem, rsem, lsem)
        self.broadcast = broadcast
        self.me = lax.axis_index("dp")

    def source(self, target):
        return self.refs[0] if self.broadcast else self.refs[0].at[target]

    def copy(self, k, target, slot):
        return pltpu.make_async_remote_copy(
            self.source(target),
            self.refs[1].at[slot],
            self.refs[2].at[k],
            self.refs[3].at[k],
            device_id=(target, lax.axis_index("ctx")),
            device_id_type=MESH,
        )

    def own(self):
        return pltpu.make_async_copy(
            self.source(self.me), self.refs[1].at[self.me], self.refs[4].at[0]
        )

    def start(self):
        for k in range(1, 16):
            self.copy(k, lax.rem(self.me + k, 16), self.me).start()
        self.own().start()

    def wait(self):
        self.own().wait()
        for k in range(1, 16):
            self.copy(k, lax.rem(self.me + k, 16), self.me).wait_send()
            origin = lax.rem(self.me + 16 - k, 16)
            self.copy(k, origin, origin).wait_recv()


def gather_kernel(units, count, stride, group, lag, *refs):
    w = refs[:count]
    o = refs[count + 1 : 2 * count + 1]
    ssem, rsem, lsem, csem, crsem, es, er, el = refs[2 * count + 2 :]
    z, y, x, c = coords()
    greet()
    side = Exchange(False, refs[count], refs[2 * count + 1], es, er, el)
    side.start()
    up = device(z + 1, y, x, c)
    down = device(z - 1, y, x, c)
    partner = {"y": device(z, 1 - y, x, c), "x": device(z, y, 1 - x, c)}
    every = slice(None)

    def run(mine, other):
        def view(u, index):
            m, first, cols, _ = mine[u]
            return o[m].at[index[0], index[1], index[2], :, pl.ds(first, cols)]

        def copy(u, index, k, target, own=False):
            m, first, cols, _ = mine[u]
            dst = view(u, index)
            src = w[m].at[:, pl.ds(first, cols)] if own else dst
            return pltpu.make_async_remote_copy(
                src, dst, ssem.at[u, k], rsem.at[u, k], device_id=target, device_id_type=MESH
            )

        def local_copy(u):
            m, first, cols, _ = mine[u]
            return pltpu.make_async_copy(
                w[m].at[:, pl.ds(first, cols)], view(u, (z, y, x)), lsem.at[u]
            )

        def plan(u):
            held = {"z": False, "y": False, "x": False}

            def index(zz=z, flip=None):
                return (
                    every if held["z"] else zz,
                    every if held["y"] else (1 - y if flip == "y" else y),
                    every if held["x"] else (1 - x if flip == "x" else x),
                )

            steps = []
            pending = []
            sends = []
            own = True
            pair = 0
            for axis in mine[u][3]:
                if axis != "z":
                    send = [(True, functools.partial(copy, u, index(), pair, partner[axis], own))]
                    steps.append((pending, send))
                    sends += send
                    pending = [
                        (True, functools.partial(copy, u, index(flip=axis), pair, partner[axis]))
                    ]
                    pair += 1
                else:

                    def chain(shift, k, target, first=False):
                        return functools.partial(copy, u, index(zz=z + shift), k, target, first)

                    one = [(z < 3, chain(0, 2, up, own)), (z > 0, chain(0, 5, down, own))]
                    steps.append((pending, one))
                    middle = (z > 0) & (z < 3)
                    two = [(middle, chain(-1, 3, up)), (middle, chain(1, 6, down))]
                    steps.append(([(z > 0, chain(-1, 2, down)), (z < 3, chain(1, 5, up))], two))
                    three = [(z == 2, chain(-2, 4, up)), (z == 1, chain(2, 7, down))]
                    steps.append(([(z > 1, chain(-2, 3, down)), (z < 2, chain(2, 6, up))], three))
                    pending = [(z == 3, chain(-3, 4, down)), (z == 0, chain(3, 7, up))]
                    sends += one + two + three
                held[axis] = True
                own = False
            return steps, pending, sends

        plans = [plan(u) for u in range(len(mine))]

        def to_core(u, which):
            m, first, cols, _ = which[u]
            block = o[m].at[:, :, :, :, pl.ds(first, cols)]
            return pltpu.make_async_remote_copy(
                block,
                block,
                csem.at[u],
                crsem.at[u],
                device_id=device(z, y, x, 1 - c),
                device_id_type=MESH,
            )

        for u in range(len(mine)):
            local_copy(u).start()
        starts = [(u // group) * stride for u in range(len(mine))]
        for turn in range(max(starts) + 6 + lag):
            for u in range(len(mine)):
                steps, pending, _ = plans[u]
                s = turn - starts[u]
                if 0 <= s < 5:
                    if s == 1:
                        local_copy(u).wait()
                    for cond, make in steps[s][0]:
                        when(cond, lambda make=make: make().wait_recv())
                    for cond, make in steps[s][1]:
                        when(cond, lambda make=make: make().start())
                elif s == 5 + lag:
                    for cond, make in pending:
                        when(cond, lambda make=make: make().wait_recv())
                    to_core(u, mine).start()
        for u in range(len(mine)):
            for cond, make in plans[u][2]:
                when(cond, lambda make=make: make().wait_send())
            to_core(u, mine).wait_send()
        for u in range(len(other)):
            to_core(u, other).wait_recv()

    pl.when(c == 0)(lambda: run(units[0], units[1]))
    pl.when(c == 1)(lambda: run(units[1], units[0]))
    side.wait()


ANY = pl.BlockSpec(memory_space=pl.ANY)
DMA = pltpu.SemaphoreType.DMA


SIDE = [DMA((16,)), DMA((16,)), DMA((1,))]


def gather(shards, rows, units, collective_id, stride, group, lag, name):
    count = len(shards)
    most = max(len(units[0]), len(units[1]))
    shapes = [jax.ShapeDtypeStruct(GRID + s.shape, s.dtype) for s in shards]
    return pl.pallas_call(
        functools.partial(gather_kernel, units, count, stride, group, lag),
        name=name,
        out_shape=shapes + [jax.ShapeDtypeStruct(rows.shape, rows.dtype)],
        in_specs=[ANY] * (count + 1),
        out_specs=[ANY] * (count + 1),
        scratch_shapes=[DMA((most, 8)), DMA((most, 8)), DMA((most,)), DMA((most,)), DMA((most,))]
        + SIDE,
        compiler_params=pltpu.CompilerParams(collective_id=collective_id, has_side_effects=True),
    )(*shards, rows)


def gather_units(shards, size):
    orders = (
        ("xzy", "yzx", "zyx", "yzx", "xzy", "zxy"),
        ("yzx", "xzy", "zxy", "xzy", "yzx", "zyx"),
    )
    units = ([], [])
    load = [0, 0]
    for m, shard in enumerate(shards):
        rows, columns = shard.shape
        tiles = columns // 128
        cuts = max(1, round(tiles * rows / 72 / size))
        at = 0
        for k in range(cuts):
            n = tiles // cuts + (1 if k < tiles % cuts else 0)
            core = 0 if load[0] <= load[1] else 1
            order = orders[core][len(units[core]) % 6]
            units[core].append((m, at * 128, n * 128, order))
            load[core] += n * rows
            at += n
    return tuple(units[0]), tuple(units[1])


def exchange_kernel(in_ref, out_ref, *sems):
    greet()
    side = Exchange(True, in_ref, out_ref, *sems)
    side.start()
    side.wait()


def exchange(values, collective_id, name):
    return pl.pallas_call(
        exchange_kernel,
        name=name,
        out_shape=jax.ShapeDtypeStruct((16,) + values.shape, values.dtype),
        in_specs=[ANY],
        out_specs=ANY,
        scratch_shapes=SIDE,
        compiler_params=pltpu.CompilerParams(collective_id=collective_id, has_side_effects=True),
    )(values)


LAG = (0, 2, 3, 4, 5, 6)
RECV_SLOTS = 9
SEND_SLOTS = 8
FIRST_SLOTS = 4
UNIT = 384
ROWS = 72
PADDED = 80


def scatter_kernel(first, cols, source, dy_count, *refs):
    nv = len(first) - 1
    xt = refs[:nv]
    dy = refs[nv : nv + dy_count]
    out = refs[nv + dy_count + 1]
    (
        xts, dys, a_s1, a_s2, a_t, a_su, a_sd, e_s1, e_t, e_su, e_sd, e_sq,
        a_b1, a_b2, a_bu, a_bd, e_b1, e_bu, e_bd, e_bq, outs,
        ssem, rsem, xl, xs, xr, yl, ys, yr, ol, os, orr, es, er, el,
    ) = refs[nv + dy_count + 3 :]
    z, y, x, c = coords()
    total = first[-1] // 2
    sibling = device(z, y, x, 1 - c)
    up = device(z + 1, y, x, c)
    down = device(z - 1, y, x, c)
    greet()
    side = Exchange(True, refs[nv + dy_count], refs[nv + dy_count + 2], es, er, el)
    lanes = pl.ds(pl.multiple_of(c * 128, 128), 128)
    offsets = []
    at = 0
    for k in range(dy_count):
        offsets.append(at)
        at += dy[k].shape[1]

    def remote(src, dst, send, recv, target):
        return pltpu.make_async_remote_copy(
            src, dst, send, recv, device_id=target, device_id_type=MESH
        )

    def x_views(v):
        return xt[v], xts.at[v, :, :, lanes]

    def x_local(v):
        return pltpu.make_async_copy(*x_views(v), xl.at[v])

    def x_remote(v):
        return remote(*x_views(v), xs.at[v], xr.at[v], sibling)

    def y_views(k):
        return dy[k], dys.at[lanes, pl.ds(offsets[k], dy[k].shape[1])]

    def y_local(k):
        return pltpu.make_async_copy(*y_views(k), yl.at[k])

    def y_remote(k):
        return remote(*y_views(k), ys.at[k], yr.at[k], sibling)

    fresh = [source[v] not in source[:v] for v in range(nv)]
    for v in range(nv):
        x_local(v).start()
        x_remote(v).start()
        if fresh[v]:
            y_local(source[v]).start()
            y_remote(source[v]).start()
        if v == 0:
            side.start()

    def arrive(tick):
        for v in range(nv):

            def wait(v=v):
                x_local(v).wait()
                x_remote(v).wait_recv()
                if fresh[v]:
                    y_local(source[v]).wait()
                    y_remote(source[v]).wait_recv()

            pl.when(tick == (first[v] - c + 1) // 2)(wait)

    def unit(i):
        j = 2 * i + c
        v = jnp.int32(0)
        col = j * UNIT
        for k in range(1, nv):
            past = (j >= first[k]).astype(jnp.int32)
            v = v + past
            col = col + past * ((cols[k] - first[k] * UNIT) - (cols[k - 1] - first[k - 1] * UNIT))
        return v, pl.multiple_of(col, 128)

    def axes(i):
        o = lax.rem(i, 2)
        pb = x * (1 - o) + y * o
        qb = y * (1 - o) + x * o
        dp = z * 4 + y * 2 + x
        return o, pb, qb, (dp + (1 - 2 * pb) * (1 + o), c), (dp + (1 - 2 * qb) * (2 - o), c)

    def slots(i):
        return lax.rem(i, FIRST_SLOTS), lax.rem(i, SEND_SLOTS), lax.rem(i, RECV_SLOTS)

    def send(src, dst, i, k, target):
        return remote(
            src, dst, ssem.at[lax.rem(i, SEND_SLOTS), k], rsem.at[lax.rem(i, RECV_SLOTS), k], target
        )

    def first_copies(i):
        o, pb, qb, pn, qn = axes(i)
        f, s, w = slots(i)
        return [send(a_s1.at[f], a_b1.at[w], i, 0, pn), send(e_s1.at[f], e_b1.at[w], i, 8, pn)]

    def second_copy(i):
        o, pb, qb, pn, qn = axes(i)
        f, s, w = slots(i)
        return send(a_s2.at[s], a_b2.at[w], i, 1, qn)

    def last_copy(i):
        o, pb, qb, pn, qn = axes(i)
        f, s, w = slots(i)
        return send(e_sq.at[s], e_bq.at[w], i, 9, qn)

    def up_copy(i, k, e):
        f, s, w = slots(i)
        src, dst, n = (e_su, e_bu, 10) if e else (a_su, a_bu, 2)
        return send(src.at[s, k], dst.at[w, k], i, n + k, up)

    def down_copy(i, k, e):
        f, s, w = slots(i)
        src, dst, n = (e_sd, e_bd, 13) if e else (a_sd, a_bd, 5)
        return send(src.at[s, k], dst.at[w, k], i, n + k, down)

    def up_sends(k):
        return (z <= k) & (z < 3)

    def down_sends(k):
        return (3 - z <= k) & (z > 0)

    def up_comes(k):
        return (z >= 1) & (z <= k + 1)

    def down_comes(k):
        return (z <= 2) & (3 - z <= k + 1)

    def kept(i, e, d):
        f, s, w = slots(i)
        if e:
            return e_t.at[s, d]
        return a_t.at[s, d, axes(i)[2]]

    def z_send(i, k, e):
        f, s, w = slots(i)

        def pass_on(dest, stage, box, inner, copy):
            value = kept(i, e, dest)[...]
            if k == 0:
                stage[s, k] = value.astype(BF16)
            else:

                def add():
                    stage[s, k] = (value + box[w, k - 1].astype(F32)).astype(BF16)

                def begin():
                    stage[s, k] = value.astype(BF16)

                pl.when(inner)(add)
                pl.when(jnp.logical_not(inner))(begin)
            copy.start()

        pl.when(up_sends(k))(
            lambda: pass_on(
                z + 3 - k, e_su if e else a_su, e_bu if e else a_bu, z > 0, up_copy(i, k, e)
            )
        )
        pl.when(down_sends(k))(
            lambda: pass_on(
                z + k - 3, e_sd if e else a_sd, e_bd if e else a_bd, z < 3, down_copy(i, k, e)
            )
        )

    def z_wait(i, k, e):
        pl.when(up_comes(k))(lambda: up_copy(i, k, e).wait_recv())
        pl.when(down_comes(k))(lambda: down_copy(i, k, e).wait_recv())

    def z_close(i, e):
        f, s, w = slots(i)
        mine = kept(i, e, z)

        def below():
            mine[...] = mine[...] + (e_bu if e else a_bu)[w, 2].astype(F32)

        def above():
            mine[...] = mine[...] + (e_bd if e else a_bd)[w, 2].astype(F32)

        pl.when(z > 0)(below)
        pl.when(z < 3)(above)
        return mine

    def product(i, bit):
        v, col = unit(i)
        o = axes(i)[0]
        chips = [4 * k + bit * (1 + o) + q * (2 - o) for k in range(4) for q in range(2)]
        lhs = jnp.concatenate([xts[v, chip] for chip in chips], axis=0)
        whole = jnp.dot(lhs, dys[:, pl.ds(col, UNIT)], preferred_element_type=F32)
        return whole.reshape(8, PADDED, UNIT)[:, :ROWS]

    def stage0(i):
        f, s, w = slots(i)
        part = product(i, 1 - axes(i)[1])
        a_s1[f] = part[:, :, :128].astype(BF16).reshape(4, 2, ROWS, 128)
        e_s1[f] = part[:, :, 128:].astype(BF16).reshape(4, 2, ROWS, 256)
        for copy in first_copies(i):
            copy.start()

    def stage1(i):
        f, s, w = slots(i)
        o, pb, qb, pn, qn = axes(i)
        part = product(i, pb)
        for copy in first_copies(i):
            copy.wait_recv()
        a_t[s] = part[:, :, :128].reshape(4, 2, ROWS, 128) + a_b1[w].astype(F32)
        a_s2[s] = a_t[s, :, 1 - qb].astype(BF16)
        second_copy(i).start()
        e_t[s] = part[:, :, 128:].reshape(4, 2, ROWS, 256) + e_b1[w].astype(F32)
        z_send(i, 0, True)

    def stage2(i):
        f, s, w = slots(i)
        qb = axes(i)[2]
        second_copy(i).wait_recv()
        a_t[s, :, qb] = a_t[s, :, qb] + a_b2[w].astype(F32)
        z_send(i, 0, False)
        z_wait(i, 0, True)
        z_send(i, 1, True)

    def stage3(i):
        z_wait(i, 0, False)
        z_send(i, 1, False)
        z_wait(i, 1, True)
        z_send(i, 2, True)

    def stage4(i):
        f, s, w = slots(i)
        z_wait(i, 1, False)
        z_send(i, 2, False)
        z_wait(i, 2, True)
        z_close(i, True)
        e_sq[s] = e_t[s, z, 1 - axes(i)[2]].astype(BF16)
        last_copy(i).start()

    def out_view(i):
        return out.at[:, pl.ds(pl.multiple_of((2 * i + c) * UNIT, 128), UNIT)]

    def stage5(i):
        f, s, w = slots(i)
        z_wait(i, 2, False)
        outs[i, :, :128] = z_close(i, False)[...]
        last_copy(i).wait_recv()
        outs[i, :, 128:] = e_t[s, z, axes(i)[2]] + e_bq[w].astype(F32)
        pltpu.make_async_copy(outs.at[i], out_view(i), ol.at[0]).start()
        remote(outs.at[i], out_view(i), os.at[0], orr.at[0], sibling).start()

    def first_sent(i):
        for copy in first_copies(i):
            copy.wait_send()

    def sent(i):
        second_copy(i).wait_send()
        last_copy(i).wait_send()
        for e in (False, True):
            for k in range(3):
                pl.when(up_sends(k))(lambda k=k, e=e: up_copy(i, k, e).wait_send())
                pl.when(down_sends(k))(lambda k=k, e=e: down_copy(i, k, e).wait_send())

    stages = (stage0, stage1, stage2, stage3, stage4, stage5)

    def tick(t, carry):
        arrive(t)
        pl.when((t >= SEND_SLOTS) & (t - SEND_SLOTS < total))(lambda: sent(t - SEND_SLOTS))
        pl.when((t >= FIRST_SLOTS) & (t - FIRST_SLOTS < total))(lambda: first_sent(t - FIRST_SLOTS))
        for k in reversed(range(6)):
            i = t - LAG[k]
            pl.when((i >= 0) & (i < total))(functools.partial(stages[k], i))
        return carry

    lax.fori_loop(0, total + SEND_SLOTS, tick, 0)
    for v in range(nv):
        x_remote(v).wait_send()
    for k in range(dy_count):
        y_remote(k).wait_send()
    half = out.at[:, pl.ds(0, total * UNIT)]
    pltpu.make_async_copy(half, half, ol.at[0]).wait()
    everything = remote(half, half, os.at[0], orr.at[0], sibling)
    everything.wait_send()
    everything.wait_recv()
    side.wait()


def scatter(xts, dys, source, rows, collective_id, name):
    nv = len(xts)
    starts = []
    width = 0
    for d in dys:
        starts.append(width)
        width += d.shape[1]
    first = [0]
    cols = []
    for v in range(nv):
        cols.append(starts[source[v]])
        first.append(first[-1] + dys[source[v]].shape[1] // UNIT)
    total = first[-1] // 2
    s, f, r = SEND_SLOTS, FIRST_SLOTS, RECV_SLOTS
    vmem = pltpu.VMEM
    return pl.pallas_call(
        functools.partial(scatter_kernel, tuple(first), tuple(cols), tuple(source), len(dys)),
        name=name,
        out_shape=[
            jax.ShapeDtypeStruct((ROWS, first[-1] * UNIT), F32),
            jax.ShapeDtypeStruct((16,) + rows.shape, rows.dtype),
        ],
        in_specs=[ANY] * (nv + len(dys) + 1),
        out_specs=[ANY] * 2,
        scratch_shapes=[
            vmem((nv, 16, PADDED, 256), BF16),
            vmem((256, width), BF16),
            vmem((f, 4, 2, ROWS, 128), BF16),
            vmem((s, 4, ROWS, 128), BF16),
            vmem((s, 4, 2, ROWS, 128), F32),
            vmem((s, 3, ROWS, 128), BF16),
            vmem((s, 3, ROWS, 128), BF16),
            vmem((f, 4, 2, ROWS, 256), BF16),
            vmem((s, 4, 2, ROWS, 256), F32),
            vmem((s, 3, 2, ROWS, 256), BF16),
            vmem((s, 3, 2, ROWS, 256), BF16),
            vmem((s, ROWS, 256), BF16),
            vmem((r, 4, 2, ROWS, 128), BF16),
            vmem((r, 4, ROWS, 128), BF16),
            vmem((r, 3, ROWS, 128), BF16),
            vmem((r, 3, ROWS, 128), BF16),
            vmem((r, 4, 2, ROWS, 256), BF16),
            vmem((r, 3, 2, ROWS, 256), BF16),
            vmem((r, 3, 2, ROWS, 256), BF16),
            vmem((r, ROWS, 256), BF16),
            vmem((total, ROWS, UNIT), F32),
            DMA((s, 16)),
            DMA((r, 16)),
            DMA((nv,)),
            DMA((nv,)),
            DMA((nv,)),
            DMA((len(dys),)),
            DMA((len(dys),)),
            DMA((len(dys),)),
            DMA((1,)),
            DMA((1,)),
            DMA((1,)),
        ]
        + SIDE,
        compiler_params=pltpu.CompilerParams(
            collective_id=collective_id, has_side_effects=True, vmem_limit_bytes=62 * 1024 * 1024
        ),
    )(*xts, *dys, rows)


def layer_norm(values):
    center = values - jnp.mean(values, axis=-1, keepdims=True)
    spread = jnp.mean(center * center, axis=-1, keepdims=True)
    return center * lax.rsqrt(spread + 1e-06)


def head_norm(values, gain):
    shaped = values.reshape(values.shape[:-1] + (HEADS, HD))
    scaled = shaped * lax.rsqrt(jnp.mean(shaped * shaped, axis=-1, keepdims=True) + 1e-06)
    return scaled * gain.reshape(HEADS, HD)


def rope_tables(rows, columns):
    quarter = HD // 4
    freqs = jnp.exp(jnp.arange(quarter, dtype=F32) * (-math.log(10000.0) / quarter))
    places = jnp.stack([rows, columns], axis=-1).astype(F32)
    angles = places[..., None] * freqs
    return (jnp.cos(angles), jnp.sin(angles))


def rotate(values, cosine, sine):
    shaped = values.reshape(values.shape[:-1] + (2, 2, HD // 4))
    first = shaped[..., 0, :]
    second = shaped[..., 1, :]
    cosine = cosine[..., None, :, :]
    sine = sine[..., None, :, :]
    turned = jnp.stack([first * cosine - second * sine, first * sine + second * cosine], axis=-2)
    return turned.reshape(values.shape)


def embed_times(times, width):
    half_width = width // 2
    freqs = jnp.exp(jnp.arange(half_width, dtype=F32) * (-math.log(10000.0) / half_width))
    angles = times[..., None] * freqs
    return jnp.concatenate([jnp.cos(angles), jnp.sin(angles)], axis=-1)


def qk_prepare(query_raw, key_raw, gains, cosine, sine):
    return (
        rotate(head_norm(query_raw, gains[0]), cosine, sine),
        rotate(head_norm(key_raw, gains[1]), cosine, sine),
    )


def swish_product(gate, up):
    return jax.nn.silu(gate) * up


def attention_scores(queries, keys, allowed):
    scores = jnp.einsum("sqhd,skhd->shqk", queries, keys, preferred_element_type=F32) * (
        1.0 / math.sqrt(HD)
    )
    return jnp.where(allowed[:, None], scores, -1e30)


def dense(values, weight):
    return jnp.dot(values, weight, preferred_element_type=F32)


def dense_back(grads, weight):
    return lax.dot_general(grads, weight, (((1,), (1,)), ((), ())), preferred_element_type=F32)


def outer_sum(values, grads):
    return lax.dot_general(values, grads, (((0,), (0,)), ((), ())), preferred_element_type=F32)


def block_forward(flat, modulation, weights, context):
    batch, half, allowed, cosine, sine = context
    triple, mixing, expand, reduce_w, gains = weights
    width = flat.shape[1]
    shift1, scale1, gate1, shift2, scale2, gate2 = jnp.split(modulation, 6, axis=1)
    lifted1 = (layer_norm(flat) * (1.0 + scale1) + shift1).astype(BF16)
    projected = dense(lifted1, triple)
    query_raw, key_raw, value_raw = jnp.split(projected, 3, axis=1)
    queries, keys = qk_prepare(query_raw, key_raw, gains, cosine, sine)
    queries = queries.astype(BF16).reshape(batch, half, HEADS, HD)
    keys_local = keys.astype(BF16).reshape(batch, half, width)
    values_local = value_raw.astype(BF16).reshape(batch, half, width)
    key_heads = lax.all_gather(keys_local, "ctx", axis=1, tiled=True).reshape(batch, -1, HEADS, HD)
    value_heads = lax.all_gather(values_local, "ctx", axis=1, tiled=True)
    value_heads = value_heads.reshape(batch, -1, HEADS, HD)
    scores = attention_scores(queries, key_heads, allowed)
    top = jnp.max(scores, axis=-1, keepdims=True)
    raised = jnp.exp(scores - top)
    total = jnp.sum(raised, axis=-1, keepdims=True)
    softmax_low = (raised / total).astype(BF16)
    logsum = top + jnp.log(total)
    mixed = jnp.einsum("shqk,skhd->sqhd", softmax_low, value_heads, preferred_element_type=F32)
    mixed_low = mixed.reshape(-1, width).astype(BF16)
    attended = dense(mixed_low, mixing)
    resid = flat + gate1 * attended
    lifted2 = (layer_norm(resid) * (1.0 + scale2) + shift2).astype(BF16)
    expanded = dense(lifted2, expand)
    gate, up = jnp.split(expanded, 2, axis=1)
    hidden = swish_product(gate, up).astype(BF16)
    feed = dense(hidden, reduce_w)
    output = resid + gate2 * feed
    kept = (
        modulation,
        flat,
        lifted1,
        query_raw,
        key_raw,
        queries,
        key_heads,
        value_heads,
        logsum,
        mixed_low,
        attended,
        resid,
        lifted2,
        expanded,
        hidden,
        feed,
    )
    return (output, kept)


def block_backward(grad_out, kept, weights, context):
    batch, half, allowed, cosine, sine = context
    triple, mixing, expand, reduce_w, gains = weights
    (
        modulation,
        flat,
        lifted1,
        query_raw,
        key_raw,
        queries,
        key_heads,
        value_heads,
        logsum,
        mixed_low,
        attended,
        resid,
        lifted2,
        expanded,
        hidden,
        feed,
    ) = kept
    width = flat.shape[1]
    shift1, scale1, gate1, shift2, scale2, gate2 = jnp.split(modulation, 6, axis=1)
    grad_feed = (grad_out * gate2).astype(BF16)
    grad_hidden = dense_back(grad_feed, reduce_w)
    gate, up = jnp.split(expanded, 2, axis=1)
    unused_out, swish_pull = jax.vjp(swish_product, gate, up)
    grad_gate, grad_up = swish_pull(grad_hidden)
    grad_expanded = jnp.concatenate([grad_gate, grad_up], axis=1).astype(BF16)
    grad_lifted2 = dense_back(grad_expanded, expand)
    normed_second, second_pull = jax.vjp(layer_norm, resid)
    grad_resid = grad_out + second_pull(grad_lifted2 * (1.0 + scale2))[0]
    grad_attended = (grad_resid * gate1).astype(BF16)
    grad_mixed = dense_back(grad_attended, mixing).astype(BF16).reshape(batch, half, HEADS, HD)
    scores = attention_scores(queries, key_heads, allowed)
    chances = jnp.exp(scores - logsum)
    grad_chances = jnp.einsum(
        "sqhd,skhd->shqk", grad_mixed, value_heads, preferred_element_type=F32
    )
    grad_values = jnp.einsum(
        "shqk,sqhd->skhd", chances.astype(BF16), grad_mixed, preferred_element_type=F32
    )
    grad_scores = (
        chances * (grad_chances - jnp.sum(chances * grad_chances, axis=-1, keepdims=True))
    ).astype(BF16)
    scale = 1.0 / math.sqrt(HD)
    grad_queries = (
        jnp.einsum("shqk,skhd->sqhd", grad_scores, key_heads, preferred_element_type=F32) * scale
    )
    grad_keys = (
        jnp.einsum("shqk,sqhd->skhd", grad_scores, queries, preferred_element_type=F32) * scale
    )
    pair = jnp.stack(
        [grad_keys.reshape(batch, -1, width), grad_values.reshape(batch, -1, width)]
    ).astype(BF16)
    place = lax.axis_index("ctx")
    theirs = lax.dynamic_slice_in_dim(pair, (1 - place) * half, half, 2)
    theirs = lax.ppermute(theirs, "ctx", [(0, 1), (1, 0)])
    mine = lax.dynamic_slice_in_dim(pair, place * half, half, 2)
    pair = mine.astype(F32) + theirs.astype(F32)
    grad_keys, grad_values = pair[0], pair[1]

    def prepare(query_in, key_in, gain_in):
        return qk_prepare(query_in, key_in, gain_in, cosine, sine)

    unused_pair, prepare_pull = jax.vjp(prepare, query_raw, key_raw, gains)
    grad_query_raw, grad_key_raw, gains_grad = prepare_pull(
        (grad_queries.reshape(-1, HEADS, HD), grad_keys.reshape(-1, HEADS, HD))
    )
    grad_projected = jnp.concatenate(
        [grad_query_raw, grad_key_raw, grad_values.reshape(-1, width)], axis=1
    ).astype(BF16)
    grad_lifted1 = dense_back(grad_projected, triple)
    normed_first, first_pull = jax.vjp(layer_norm, flat)
    grad_flat = grad_resid + first_pull(grad_lifted1 * (1.0 + scale1))[0]
    grad_modulation = jnp.concatenate(
        [
            grad_lifted1,
            grad_lifted1 * normed_first,
            grad_resid * attended,
            grad_lifted2,
            grad_lifted2 * normed_second,
            grad_out * feed,
        ],
        axis=1,
    ).astype(BF16)
    factors = (
        (lifted1, grad_projected),
        (mixed_low, grad_attended),
        (lifted2, grad_expanded),
        (hidden, grad_feed),
    )
    return (grad_flat, grad_modulation, factors, gains_grad)


def meet_sibling():
    barrier = pltpu.get_barrier_semaphore()
    sibling = (lax.axis_index("dp"), 1 - lax.axis_index("ctx"))
    pl.semaphore_signal(barrier, inc=1, device_id=sibling, device_id_type=MESH)
    pl.semaphore_wait(barrier, 1)
    return sibling


def head_sum_matrix(width):
    channel = lax.broadcasted_iota(jnp.int32, (width, 128), 0)
    head = lax.broadcasted_iota(jnp.int32, (width, 128), 1)
    inside = (channel >= head * HD) & (channel < (head + 1) * HD)
    return jnp.where(inside, 1.0, 0.0).astype(F32)


def exact_dot(left, right):
    return jnp.dot(left, right, preferred_element_type=F32, precision=lax.Precision.HIGHEST)


def spread_heads(values, heads):
    return lax.dot_general(
        values,
        heads,
        (((1,), (1,)), ((), ())),
        preferred_element_type=F32,
        precision=lax.Precision.HIGHEST,
    )


def swap_pairs(values):
    width = values.shape[1]
    lane = lax.broadcasted_iota(jnp.int32, values.shape, 1)
    quarter = HD // 4
    early = lax.rem(lane, 2 * quarter) < quarter
    return jnp.where(
        early, pltpu.roll(values, width - quarter, 1), pltpu.roll(values, quarter, 1)
    )


def normalize(values):
    mean = jnp.mean(values, axis=1, keepdims=True)
    center = values - mean
    spread = jnp.mean(center * center, axis=1, keepdims=True)
    inverse = lax.rsqrt(spread + 1e-06)
    return center * inverse, inverse


def norm_back(normed, inverse, grad):
    mean = jnp.mean(grad, axis=1, keepdims=True)
    along = jnp.mean(grad * normed, axis=1, keepdims=True)
    return (grad - mean - normed * along) * inverse


def window(h, width):
    first = min((h * HD) // 128 * 128, width - 256)
    return first, h * HD - first


def head_mask(h, width, rows):
    first, at = window(h, width)
    lane = lax.broadcasted_iota(jnp.int32, (rows, 256), 1)
    return (lane >= at) & (lane < at + HD)


def turned(values):
    tokens, width = values.shape
    rows = values.T.reshape(-1, ROWS, tokens)
    return jnp.concatenate(
        [rows, jnp.zeros((width // ROWS, PADDED - ROWS, tokens), F32)], axis=1
    ).astype(BF16)


FF_TILE = 768
KV_TILE = 1152


def allowed_mask(seg_q, seg_k, pad_k, half):
    place_q = lax.axis_index("ctx") * half + lax.broadcasted_iota(jnp.int32, (half, 2 * half), 0)
    place_k = lax.broadcasted_iota(jnp.int32, (half, 2 * half), 1)
    return (seg_q[...] == seg_k[...]) & ((pad_k[...] == 0) | (place_q == place_k))


def forward_kernel(
    flat, mod, gains, cosine, sine, seg_q, seg_k, pad_k, triple_h, mixing_h, expand_h, reduce_h,
    output, raw, queries, kv, lse, attended, resid, expanded, feed, xt1, xtm, xt2, xth,
    triple, mixing, expand, reduce_w, mixed, wsem, ssem, rsem,
):
    half, width = flat.shape
    loads = [
        pltpu.make_async_copy(src, dst, wsem.at[k])
        for k, (src, dst) in enumerate(
            ((triple_h, triple), (mixing_h, mixing), (expand_h, expand), (reduce_h, reduce_w))
        )
    ]
    for load in loads:
        load.start()
    sibling = meet_sibling()
    c = lax.axis_index("ctx")
    mine = pl.ds(pl.multiple_of(c * half, 128), half)

    def part(k):
        return mod[:, k * width : (k + 1) * width]

    normed, unused = normalize(flat[...])
    lifted = normed * (1.0 + part(1)) + part(0)
    lifted_low = lifted.astype(BF16)
    xt1[...] = turned(lifted_low.astype(F32))
    heads = head_sum_matrix(width)
    loads[0].wait()

    def prepared(k):
        values = raw[:, k * width : (k + 1) * width]
        mean = exact_dot(values * values, heads) * (1.0 / HD)
        scaled = values * spread_heads(lax.rsqrt(mean + 1e-06), heads) * gains[k : k + 1, :]
        return scaled * cosine[...] + swap_pairs(scaled) * sine[...]

    def project(k):
        return jnp.dot(
            lifted_low, triple[:, k * width : (k + 1) * width], preferred_element_type=F32
        )

    raw[:, width:] = project(1)
    kv[0, mine] = prepared(1).astype(BF16)
    kv[1, mine] = project(2).astype(BF16)
    share = pltpu.make_async_remote_copy(
        kv.at[:, mine], kv.at[:, mine], ssem.at[0], rsem.at[0], device_id=sibling,
        device_id_type=MESH,
    )
    share.start()
    raw[:, :width] = project(0)
    queries[...] = prepared(0).astype(BF16)
    allowed = allowed_mask(seg_q, seg_k, pad_k, half)
    mixed[...] = jnp.zeros_like(mixed)
    lane = lax.broadcasted_iota(jnp.int32, (half, 128), 1)
    sums = jnp.zeros((half, 128), F32)
    theirs = pl.ds(pl.multiple_of((1 - c) * half, 128), half)
    pltpu.make_async_remote_copy(
        kv.at[:, theirs], kv.at[:, theirs], ssem.at[0], rsem.at[0], device_id=sibling,
        device_id_type=MESH,
    ).wait_recv()
    for h in range(width // HD):
        first, unused = window(h, width)
        span = slice(first, first + 256)
        mask = head_mask(h, width, half)
        query = jnp.where(mask, queries[:, span].astype(F32), 0.0).astype(BF16)
        scores = dense_back(query, kv[0, :, span]) * (1.0 / math.sqrt(HD))
        scores = jnp.where(allowed, scores, -1e30)
        top = jnp.max(scores, axis=1, keepdims=True)
        raised = jnp.exp(scores - top)
        total = jnp.sum(raised, axis=1, keepdims=True)
        low = (raised / total).astype(BF16)
        out = jnp.dot(low, kv[1, :, span], preferred_element_type=F32)
        mixed[:, span] = mixed[:, span] + jnp.where(mask, out, 0.0)
        sums = jnp.where(lane == h, top + jnp.log(total), sums)
    lse[...] = sums
    mixed_low = mixed[...].astype(BF16)
    xtm[...] = turned(mixed_low.astype(F32))
    loads[1].wait()
    attended[...] = jnp.dot(mixed_low, mixing[...], preferred_element_type=F32)
    resid[...] = flat[...] + part(2) * attended[...]
    normed, unused = normalize(resid[...])
    lifted_low = (normed * (1.0 + part(4)) + part(3)).astype(BF16)
    xt2[...] = turned(lifted_low.astype(F32))
    feed[...] = jnp.zeros_like(feed)
    loads[2].wait()
    loads[3].wait()
    hidden_size = reduce_w.shape[0]
    xth[...] = jnp.zeros_like(xth)
    for t in range(hidden_size // FF_TILE):
        gate = jnp.dot(
            lifted_low, expand[:, t * FF_TILE : (t + 1) * FF_TILE], preferred_element_type=F32
        )
        up = jnp.dot(
            lifted_low,
            expand[:, hidden_size + t * FF_TILE : hidden_size + (t + 1) * FF_TILE],
            preferred_element_type=F32,
        )
        expanded[:, t * FF_TILE : (t + 1) * FF_TILE] = gate
        expanded[:, hidden_size + t * FF_TILE : hidden_size + (t + 1) * FF_TILE] = up
        hidden = (gate * jax.nn.sigmoid(gate) * up).astype(BF16)
        pieces = hidden.astype(F32).T.astype(BF16).reshape(FF_TILE // 192, 3, 64, half)
        for g in range(3):
            xth[g, t * (FF_TILE // 192) : (t + 1) * (FF_TILE // 192), :64] = pieces[:, g]
        feed[...] = feed[...] + jnp.dot(
            hidden, reduce_w[t * FF_TILE : (t + 1) * FF_TILE], preferred_element_type=F32
        )
    output[...] = resid[...] + part(5) * feed[...]
    share.wait_send()


def backward_kernel(
    grad_out, flat, mod, gains, cosine, sine, seg_q, seg_k, pad_k,
    raw, queries, kv, lse, attended, resid, expanded, feed,
    triple_h, mixing_h, expand_h, reduce_h,
    grad_flat, grad_mod, grad_feed, grad_expanded, grad_attended, grad_projected, gains_grad,
    triple, mixing, expand, reduce_w, grad_q, grad_k, grad_v, lift, outgoing, incoming,
    wsem, ssem, rsem,
):
    half, width = flat.shape
    loads = [
        pltpu.make_async_copy(src, dst, wsem.at[k])
        for k, (src, dst) in enumerate(
            ((reduce_h, reduce_w), (expand_h, expand), (mixing_h, mixing), (triple_h, triple))
        )
    ]
    for load in loads:
        load.start()
    sibling = meet_sibling()
    c = lax.axis_index("ctx")
    mine = pl.ds(pl.multiple_of(c * half, 128), half)
    theirs = pl.ds(pl.multiple_of((1 - c) * half, 128), half)

    def part(k):
        return mod[:, k * width : (k + 1) * width]

    def keep(k, values):
        grad_mod[:, k * width : (k + 1) * width] = values.astype(BF16)

    keep(5, grad_out[...] * feed[...])
    feed_low = (grad_out[...] * part(5)).astype(BF16)
    grad_feed[...] = feed_low
    hidden_size = reduce_w.shape[0]
    lift[...] = jnp.zeros_like(lift)
    loads[0].wait()
    loads[1].wait()
    for t in range(hidden_size // FF_TILE):
        one = slice(t * FF_TILE, (t + 1) * FF_TILE)
        two = slice(hidden_size + t * FF_TILE, hidden_size + (t + 1) * FF_TILE)
        grad_hidden = dense_back(feed_low, reduce_w[one])
        gate = expanded[:, one]
        up = expanded[:, two]
        sig = jax.nn.sigmoid(gate)
        grad_gate = (grad_hidden * up * (sig * (1.0 + gate * (1.0 - sig)))).astype(BF16)
        grad_up = (grad_hidden * (gate * sig)).astype(BF16)
        grad_expanded[:, one] = grad_gate
        grad_expanded[:, two] = grad_up
        lift[...] = lift[...] + dense_back(grad_gate, expand[:, one])
        lift[...] = lift[...] + dense_back(grad_up, expand[:, two])
    normed, inverse = normalize(resid[...])
    keep(3, lift[...])
    keep(4, lift[...] * normed)
    grad_resid = grad_out[...] + norm_back(normed, inverse, lift[...] * (1.0 + part(4)))
    keep(2, grad_resid * attended[...])
    grad_flat[...] = grad_resid
    attended_low = (grad_resid * part(2)).astype(BF16)
    grad_attended[...] = attended_low
    loads[2].wait()
    lift[...] = dense_back(attended_low, mixing[...])
    allowed = allowed_mask(seg_q, seg_k, pad_k, half)
    grad_q[...] = jnp.zeros_like(grad_q)
    grad_k[...] = jnp.zeros_like(grad_k)
    grad_v[...] = jnp.zeros_like(grad_v)
    scale = 1.0 / math.sqrt(HD)
    lane = lax.broadcasted_iota(jnp.int32, (half, 128), 1)
    for h in range(width // HD):
        first, unused = window(h, width)
        span = slice(first, first + 256)
        mask = head_mask(h, width, half)
        query = jnp.where(mask, queries[:, span].astype(F32), 0.0).astype(BF16)
        grad_mixed = jnp.where(mask, lift[:, span], 0.0).astype(BF16)
        scores = dense_back(query, kv[0, :, span]) * scale
        logsum = jnp.sum(jnp.where(lane == h, lse[...], 0.0), axis=1, keepdims=True)
        chances = jnp.exp(jnp.where(allowed, scores, -1e30) - logsum)
        grad_chances = dense_back(grad_mixed, kv[1, :, span])
        along = jnp.sum(chances * grad_chances, axis=1, keepdims=True)
        grad_scores = chances * (grad_chances - along)
        scores_low = grad_scores.astype(BF16)
        out = jnp.dot(scores_low, kv[0, :, span], preferred_element_type=F32)
        grad_q[:, span] = grad_q[:, span] + jnp.where(mask, out, 0.0)
        grad_k[:, span] = grad_k[:, span] + outer_sum(scores_low, query)
        grad_v[:, span] = grad_v[:, span] + outer_sum(chances.astype(BF16), grad_mixed)
    outgoing[0] = (grad_k[theirs, :] * scale).astype(BF16)
    outgoing[1] = grad_v[theirs, :].astype(BF16)
    share = pltpu.make_async_remote_copy(
        outgoing, incoming, ssem.at[0], rsem.at[0], device_id=sibling, device_id_type=MESH
    )
    share.start()
    heads = head_sum_matrix(width)

    def prepare_back(k, grad):
        values = raw[:, k * width : (k + 1) * width]
        gain = gains[k : k + 1, :]
        mean = exact_dot(values * values, heads) * (1.0 / HD)
        inverse = spread_heads(lax.rsqrt(mean + 1e-06), heads)
        scaled = values * inverse
        turned_back = grad * cosine[...] + swap_pairs(grad * sine[...])
        gains_grad[k : k + 1, :] = jnp.sum(turned_back * scaled, axis=0, keepdims=True)
        turned_back = turned_back * gain
        along = spread_heads(exact_dot(turned_back * scaled, heads) * (1.0 / HD), heads)
        return (turned_back - scaled * along) * inverse

    grad_projected[:, :width] = prepare_back(0, grad_q[...] * scale).astype(BF16)
    share.wait()
    own_k = (grad_k[mine, :] * scale).astype(BF16).astype(F32) + incoming[0].astype(F32)
    own_v = grad_v[mine, :].astype(BF16).astype(F32) + incoming[1].astype(F32)
    grad_projected[:, width : 2 * width] = prepare_back(1, own_k).astype(BF16)
    grad_projected[:, 2 * width :] = own_v.astype(BF16)
    loads[3].wait()
    total = dense_back(grad_projected[:, :width], triple[:, :width])
    for k in (1, 2):
        span = slice(k * width, (k + 1) * width)
        total = total + dense_back(grad_projected[:, span], triple[:, span])
    normed, inverse = normalize(flat[...])
    keep(0, total)
    keep(1, total * normed)
    grad_flat[...] = grad_flat[...] + norm_back(normed, inverse, total * (1.0 + part(1)))


IN_VMEM = pl.BlockSpec(memory_space=pltpu.VMEM)


def weight_scratch(weights):
    return [pltpu.VMEM(w.shape, w.dtype) for w in weights]


def kernel_forward(flat, modulation, weights, context, name):
    cosine, sine, seg_q, seg_k, pad_k = context
    *weights, gains = weights
    half, width = flat.shape
    hidden_size = weights[3].shape[0]

    def struct(shape, dtype=F32):
        return jax.ShapeDtypeStruct(shape, dtype)

    rows = (16, PADDED, half)
    out_shape = [
        struct((half, width)),
        struct((half, 2 * width)),
        struct((half, width), BF16),
        struct((2, 2 * half, width), BF16),
        struct((half, 128)),
        struct((half, width)),
        struct((half, width)),
        struct((half, 2 * hidden_size)),
        struct((half, width)),
        struct(rows, BF16),
        struct(rows, BF16),
        struct(rows, BF16),
        struct((3,) + rows, BF16),
    ]
    output, *rest = pl.pallas_call(
        forward_kernel,
        name=name,
        out_shape=out_shape,
        in_specs=[IN_VMEM] * 8 + [ANY] * 4,
        out_specs=[IN_VMEM] * len(out_shape),
        scratch_shapes=weight_scratch(weights)
        + [pltpu.VMEM((half, width), F32), DMA((4,)), DMA((1,)), DMA((1,))],
        compiler_params=pltpu.CompilerParams(
            collective_id=5, has_side_effects=True, vmem_limit_bytes=60 * 1024 * 1024
        ),
    )(flat, modulation, gains, cosine, sine, seg_q, seg_k, pad_k, *weights)
    return output, (flat, modulation, rest[:8]), rest[8:]


def kernel_backward(grad_out, kept, weights, context, name):
    cosine, sine, seg_q, seg_k, pad_k = context
    flat, modulation, saved = kept
    *weights, gains = weights
    half, width = flat.shape
    hidden_size = weights[3].shape[0]

    def struct(columns, dtype=BF16):
        return jax.ShapeDtypeStruct((half, columns), dtype)

    out_shape = [
        struct(width, F32),
        struct(6 * width),
        struct(width),
        struct(2 * hidden_size),
        struct(width),
        struct(3 * width),
        jax.ShapeDtypeStruct((2, width), F32),
    ]
    vmem = pltpu.VMEM
    return pl.pallas_call(
        backward_kernel,
        name=name,
        out_shape=out_shape,
        in_specs=[IN_VMEM] * 17 + [ANY] * 4,
        out_specs=[IN_VMEM] * len(out_shape),
        scratch_shapes=weight_scratch(weights)
        + [
            vmem((half, width), F32),
            vmem((2 * half, width), F32),
            vmem((2 * half, width), F32),
            vmem((half, width), F32),
            vmem((2, half, width), BF16),
            vmem((2, half, width), BF16),
            DMA((4,)),
            DMA((1,)),
            DMA((1,)),
        ],
        compiler_params=pltpu.CompilerParams(
            collective_id=6, has_side_effects=True, vmem_limit_bytes=60 * 1024 * 1024
        ),
    )(
        grad_out, flat, modulation, gains, cosine, sine, seg_q, seg_k, pad_k, *saved, *weights
    )


def shard_rows(values):
    rows = values.T.reshape(16, -1, values.shape[0])
    return jnp.pad(rows, ((0, 0), (0, PADDED - rows.shape[1]), (0, 0)))


def rope_lanes(cosine, sine):
    tokens = cosine.shape[0]

    def lanes(table, signs):
        table = jnp.stack([signs[0] * table, signs[1] * table], axis=2).reshape(tokens, 1, HD)
        return jnp.broadcast_to(table, (tokens, HEADS, HD)).reshape(tokens, HEADS * HD)

    return lanes(cosine, (1.0, 1.0)), lanes(sine, (-1.0, 1.0))


def fast_reduce(blocks, rows, collective_id, name):
    xts = []
    dys = []
    source = []
    for factors, extra in blocks:
        for lefts, right in factors:
            source += [len(dys)] * len(lefts)
            xts += lefts
            dys.append(right)
        tokens = right.shape[0]
        lines = -(-extra.shape[1] // tokens)
        packed = jnp.pad(extra, ((0, 0), (0, lines * tokens - extra.shape[1])))
        packed = packed.reshape(16, lines, tokens).astype(BF16)
        xts.append(jnp.pad(packed, ((0, 0), (0, PADDED - lines), (0, 0))))
        source.append(len(dys))
        dys.append(jnp.eye(tokens, UNIT, dtype=BF16))
    out, rows = scatter(xts, dys, source, rows, collective_id, name)
    results = []
    at = 0
    for factors, extra in blocks:
        grads = []
        for lefts, right in factors[:-1]:
            grads.append(out[:, at : at + right.shape[1]])
            at += right.shape[1]
        width = factors[-1][1].shape[1]
        parts = [out[:64, at + g * width : at + (g + 1) * width] for g in range(3)]
        grads.append(jnp.concatenate(parts, axis=0))
        at += 3 * width
        lines = -(-extra.shape[1] // tokens)
        small = out[:lines, at : at + tokens].reshape(-1)[: extra.shape[1]]
        at += UNIT
        results.append((grads, small))
    return results, rows


def whole_rows(gathered):
    return gathered.reshape((-1,) + gathered.shape[4:])


def fast_step(flat, cotangent, context, segment_local, valid, timesteps, encoder, decoder):
    width = flat.shape[1]
    offset_size = encoder[1].shape[0]
    gain_size = 2 * encoder[3].shape[1]
    small = jnp.concatenate(
        [
            encoder[1].astype(F32),
            decoder[1].astype(F32),
            encoder[3].astype(F32).reshape(-1),
            decoder[3].astype(F32).reshape(-1),
            timesteps.astype(F32).reshape(-1),
        ]
    )
    size = small.shape[0]
    small = jnp.pad(small, (0, 2048 - size)).reshape(16, 128)
    small = exchange(small, 0, "small").reshape(16, -1)
    encoder_offset = small[:, :offset_size].reshape(-1)
    decoder_offset = small[:, offset_size : 2 * offset_size].reshape(-1)
    at = 2 * offset_size
    encoder_gains = small[:, at : at + gain_size].reshape(16, 2, -1).swapaxes(0, 1).reshape(2, -1)
    at += gain_size
    decoder_gains = small[:, at : at + gain_size].reshape(16, 2, -1).swapaxes(0, 1).reshape(2, -1)
    at += gain_size
    all_times = small[:, at : at + timesteps.size]
    segments = timesteps.shape[1]
    picks = (segment_local[..., None] == jnp.arange(segments, dtype=jnp.int32)).astype(F32)
    picks = picks.reshape(-1, segments)

    all_cond = embed_times(all_times, width).reshape(-1, width)
    act_rows = jax.nn.silu(all_cond).astype(BF16)
    me = lax.axis_index("dp")
    rows = encoder[0].shape[0]
    act_mine = lax.dynamic_slice_in_dim(act_rows, me * rows, rows, 1)
    partial = dense(act_mine, encoder[0]).reshape(16, 8, -1)
    shards = (encoder[2], encoder[4], encoder[5], encoder[6])
    shards += (decoder[0], decoder[2], decoder[4], decoder[5], decoder[6])
    *wholes, partial = gather(shards, partial, gather_units(shards, 7), 1, 1, 3, 1, "gather")
    wholes = [whole_rows(w) for w in wholes]
    encoder_weights = (*wholes[:4], encoder_gains)
    modulate = wholes[4]
    decoder_weights = (*wholes[5:], decoder_gains)
    modulation_rows = jnp.sum(partial, axis=0).reshape(segments, -1) + encoder_offset
    exact = lax.Precision.HIGHEST
    encoder_modulation = jnp.dot(picks, modulation_rows, precision=exact)
    cond_rows = lax.dynamic_slice_in_dim(all_cond, me * segments, segments, 0)
    cond = jnp.dot(picks, cond_rows, precision=exact)

    encoder_out, encoder_kept, encoder_left = kernel_forward(
        flat, encoder_modulation, encoder_weights, context, "encoder"
    )
    latent_full = valid * encoder_out
    decoder_pre = latent_full + cond
    decoder_act = jax.nn.silu(decoder_pre).astype(BF16)

    decoder_modulation = dense(decoder_act, modulate) + decoder_offset
    decoder_out, decoder_kept, decoder_left = kernel_forward(
        flat, decoder_modulation, decoder_weights, context, "decoder"
    )
    velocity = valid * decoder_out

    def pair_up(lefts, rights):
        feed, expanded, attended, projected = rights
        one, mixed, two, hidden = lefts
        return (
            ([one], projected),
            ([mixed], attended),
            ([two], expanded),
            ([hidden[g] for g in range(3)], feed),
        )

    grad_out = valid * cotangent
    decoder_flat, grad_modulation, *rights, gains_grad = kernel_backward(
        grad_out, decoder_kept, decoder_weights, context, "decoder_back"
    )
    factors = pair_up(decoder_left, rights)
    grad_act = dense_back(grad_modulation, modulate)
    unused_silu, silu_pull = jax.vjp(jax.nn.silu, decoder_pre)
    grad_latent = valid * silu_pull(grad_act)[0]
    offset_grad = jnp.sum(grad_modulation, axis=0, dtype=F32)
    extra = jnp.concatenate(
        [
            offset_grad.reshape(16, -1),
            gains_grad.reshape(2, 16, -1).swapaxes(0, 1).reshape(16, -1),
        ],
        axis=1,
    )
    first = ([shard_rows(decoder_act)], grad_modulation)
    decoder_block = ((first,) + factors, extra)

    encoder_flat, grad_modulation, *rights, gains_grad = kernel_backward(
        grad_latent, encoder_kept, encoder_weights, context, "encoder_back"
    )
    factors = pair_up(encoder_left, rights)
    grad_rows = lax.dot_general(
        picks.astype(BF16), grad_modulation, (((0,), (0,)), ((), ())), preferred_element_type=F32
    )
    grad_rows = grad_rows + lax.ppermute(grad_rows, "ctx", [(0, 1), (1, 0)])
    extra = gains_grad.reshape(2, 16, -1).swapaxes(0, 1).reshape(16, -1)
    results, all_rows = fast_reduce(
        (decoder_block, (factors, extra)), grad_rows.astype(BF16).reshape(16, -1), 2, "scatter"
    )
    (grads, small), (encoder_parts, encoder_small) = results
    decoder_grads = (
        grads[0],
        small[:offset_size],
        grads[1],
        small[offset_size:].reshape(2, -1),
        grads[2],
        grads[3],
        grads[4],
    )
    all_rows = all_rows.reshape(16 * segments, -1)
    modulate_grad = outer_sum(act_mine, all_rows)
    offset_grad = lax.dynamic_slice_in_dim(
        jnp.sum(all_rows.astype(F32), axis=0), me * offset_size, offset_size, 0
    )
    encoder_grads = (
        modulate_grad,
        offset_grad,
        encoder_parts[0],
        encoder_small.reshape(2, -1),
        encoder_parts[1],
        encoder_parts[2],
        encoder_parts[3],
    )
    return velocity, latent_full, decoder_flat + encoder_flat, encoder_grads, decoder_grads


def plain_gather(block):
    parts = [lax.all_gather(block[k], "dp", axis=0, tiled=True) for k in (0, 1, 2, 4, 5, 6)]
    gains = lax.all_gather(block[3], "dp", axis=1, tiled=True).astype(F32)
    modulate, offset, triple, mixing, expand, reduce_w = parts
    return modulate, offset.astype(F32), (triple, mixing, expand, reduce_w, gains)


def plain_reduce(factors, grad_modulation, gains_grad):
    def rows(values, dim=0):
        part = lax.psum_scatter(values, "dp", scatter_dimension=dim, tiled=True)
        return lax.psum(part.astype(BF16), "ctx").astype(F32)

    offset = rows(jnp.sum(grad_modulation, axis=0, dtype=F32))
    modulate, triple, mixing, expand, reduce_w = [rows(outer_sum(a, b)) for a, b in factors]
    return modulate, offset, triple, rows(gains_grad, 1), mixing, expand, reduce_w


def plain_step(flat, cotangent, context, segment_local, valid, timesteps, encoder, decoder):
    picks = (
        segment_local[..., None] == jnp.arange(timesteps.shape[-1], dtype=jnp.int32)
    ).astype(F32)
    times = jnp.sum(picks * timesteps[:, None, :].astype(F32), axis=-1)
    cond = embed_times(times, flat.shape[1]).reshape(flat.shape)
    modulate, offset, encoder_weights = plain_gather(encoder)
    encoder_act = jax.nn.silu(cond).astype(BF16)
    encoder_out, encoder_kept = block_forward(
        flat, dense(encoder_act, modulate) + offset, encoder_weights, context
    )
    latent_full = valid * encoder_out
    decoder_pre = latent_full + cond
    decoder_act = jax.nn.silu(decoder_pre).astype(BF16)
    modulate, offset, decoder_weights = plain_gather(decoder)
    decoder_out, decoder_kept = block_forward(
        flat, dense(decoder_act, modulate) + offset, decoder_weights, context
    )
    decoder_flat, grad_modulation, factors, gains_grad = block_backward(
        valid * cotangent, decoder_kept, decoder_weights, context
    )
    grad_act = dense_back(grad_modulation, modulate)
    decoder_grads = plain_reduce(
        ((decoder_act, grad_modulation),) + factors, grad_modulation, gains_grad
    )
    unused_silu, silu_pull = jax.vjp(jax.nn.silu, decoder_pre)
    encoder_flat, grad_modulation, factors, gains_grad = block_backward(
        valid * silu_pull(grad_act)[0], encoder_kept, encoder_weights, context
    )
    encoder_grads = plain_reduce(
        ((encoder_act, grad_modulation),) + factors, grad_modulation, gains_grad
    )
    return valid * decoder_out, latent_full, decoder_flat + encoder_flat, encoder_grads, decoder_grads


def local(fast, tokens, cotangent, segment, rows, columns, padding, timesteps, *weights):
    batch, half, width = tokens.shape
    start = lax.axis_index("ctx") * half
    segment_local = lax.dynamic_slice_in_dim(segment, start, half, 1)
    rows_local = lax.dynamic_slice_in_dim(rows, start, half, 1)
    columns_local = lax.dynamic_slice_in_dim(columns, start, half, 1)
    padding_local = lax.dynamic_slice_in_dim(padding, start, half, 1)
    place_query = start + jnp.arange(half, dtype=jnp.int32)
    place_key = jnp.arange(segment.shape[1], dtype=jnp.int32)
    allowed = (segment_local[:, :, None] == segment[:, None, :]) & (
        (padding[:, None, :] == 0) | (place_query[None, :, None] == place_key[None, None, :])
    )
    cosine, sine = rope_tables(rows_local.reshape(-1), columns_local.reshape(-1))
    context = (batch, half, allowed, cosine, sine)
    if fast:
        context = rope_lanes(cosine, sine)
        context += (segment_local.reshape(-1, 1), segment, padding)
    valid = (1 - padding_local).astype(F32).reshape(-1, 1)
    flat = tokens.reshape(-1, width).astype(F32)
    step = fast_step if fast else plain_step
    velocity, latent, token_grad, encoder_grads, decoder_grads = step(
        flat,
        cotangent.reshape(-1, width).astype(F32),
        context,
        segment_local,
        valid,
        timesteps,
        weights[:7],
        weights[7:],
    )
    return (
        velocity.astype(BF16).reshape(batch, half, width),
        latent.astype(BF16).reshape(batch, half, width),
        token_grad.reshape(batch, half, width),
        *encoder_grads,
        *decoder_grads,
    )


def solution(mesh):
    fast = dict(mesh.shape) == {"dp": math.prod(GRID), "ctx": 2}
    block = (
        P("dp", None),
        P("dp"),
        P("dp", None),
        P(None, "dp"),
        P("dp", None),
        P("dp", None),
        P("dp", None),
    )
    slots = P("dp", "ctx", None)
    return jax.shard_map(
        functools.partial(local, fast),
        mesh=mesh,
        in_specs=(slots, slots) + (P("dp", None),) * 5 + block + block,
        out_specs=(slots, slots, slots) + block + block,
        check_vma=False,
    )
```

```python
import functools
import math

import jax
import jax.numpy as jnp
from jax import lax
from jax.experimental import pallas as pl
from jax.experimental.pallas import tpu as pltpu
from jax.sharding import PartitionSpec as P

HEADS = 16
HD = 72
MESH = pl.DeviceIdType.MESH
GRID = (4, 2, 2)
BF16 = jnp.bfloat16
F32 = jnp.float32


def coords():
    dp = lax.axis_index("dp")
    return (lax.div(dp, 4), lax.rem(lax.div(dp, 2), 2), lax.rem(dp, 2), lax.axis_index("ctx"))


def device(z, y, x, c):
    return (z * 4 + y * 2 + x, c)


def when(cond, body):
    if cond is True:
        body()
    else:
        pl.when(cond)(body)


def greet():
    barrier = pltpu.get_barrier_semaphore()
    me = lax.axis_index("dp")
    c = lax.axis_index("ctx")
    for k in range(1, 16):
        pl.semaphore_signal(
            barrier, inc=1, device_id=(lax.rem(me + k, 16), c), device_id_type=MESH
        )
    pl.semaphore_signal(barrier, inc=1, device_id=(me, 1 - c), device_id_type=MESH)
    pl.semaphore_wait(barrier, 16)


class Exchange:
    def __init__(self, same, in_ref, out_ref, ssem, rsem, lsem):
        self.refs = (in_ref, out_ref, ssem, rsem, lsem)
        self.same = same
        self.me = lax.axis_index("dp")

    def source(self, target):
        return self.refs[0] if self.same else self.refs[0].at[target]

    def copy(self, k, target, slot):
        return pltpu.make_async_remote_copy(
            self.source(target),
            self.refs[1].at[slot],
            self.refs[2].at[k],
            self.refs[3].at[k],
            device_id=(target, lax.axis_index("ctx")),
            device_id_type=MESH,
        )

    def own(self):
        return pltpu.make_async_copy(
            self.source(self.me), self.refs[1].at[self.me], self.refs[4].at[0]
        )

    def start(self):
        for k in range(1, 16):
            self.copy(k, lax.rem(self.me + k, 16), self.me).start()
        self.own().start()

    def wait(self):
        self.own().wait()
        for k in range(1, 16):
            self.copy(k, lax.rem(self.me + k, 16), self.me).wait_send()
            origin = lax.rem(self.me + 16 - k, 16)
            self.copy(k, origin, origin).wait_recv()


class Broadcast:
    def __init__(self, in_ref, out_ref, ssem, rsem, lsem):
        self.refs = (in_ref, out_ref, ssem, rsem, lsem)
        self.z, self.y, self.x, self.c = coords()

    def own(self):
        return pltpu.make_async_copy(
            self.refs[0], self.refs[1].at[self.z, self.y, self.x], self.refs[4].at[0]
        )

    def along(self, k, arrival):
        there = lax.rem(self.z + (4 - k if arrival else k), 4)
        slot = there if arrival else self.z
        return pltpu.make_async_remote_copy(
            self.refs[0],
            self.refs[1].at[slot, self.y, self.x],
            self.refs[2].at[k],
            self.refs[3].at[k],
            device_id=device(there, self.y, self.x, self.c),
            device_id_type=MESH,
        )

    def across(self, k, arrival):
        y = lax.rem(self.y + k // 2, 2)
        x = lax.rem(self.x + k % 2, 2)
        block = self.refs[1].at[:, y, x] if arrival else self.refs[1].at[:, self.y, self.x]
        return pltpu.make_async_remote_copy(
            block,
            block,
            self.refs[2].at[3 + k],
            self.refs[3].at[3 + k],
            device_id=device(self.z, y, x, self.c),
            device_id_type=MESH,
        )

    def start(self):
        for k in range(1, 4):
            self.along(k, False).start()
        self.own().start()

    def forward(self):
        self.own().wait()
        for k in range(1, 4):
            self.along(k, True).wait_recv()
        for k in range(1, 4):
            self.across(k, False).start()

    def wait(self):
        for k in range(1, 4):
            self.along(k, False).wait_send()
            self.across(k, False).wait_send()
            self.across(k, True).wait_recv()


def gather_kernel(units, turns, count, *refs):
    w = refs[:count]
    o = refs[count + 1 : 2 * count + 1]
    ssem, rsem, lsem, csem, crsem, es, er, el = refs[2 * count + 2 :]
    z, y, x, c = coords()
    greet()
    side = Exchange(False, refs[count], refs[2 * count + 1], es, er, el)
    side.start()
    up = device(z + 1, y, x, c)
    down = device(z - 1, y, x, c)
    partner = {"y": device(z, 1 - y, x, c), "x": device(z, y, 1 - x, c)}
    every = slice(None)

    def run(mine, other, order):
        def view(u, index):
            m, first, cols, _ = mine[u]
            return o[m].at[index[0], index[1], index[2], :, pl.ds(first, cols)]

        def copy(u, index, k, target, own=False):
            m, first, cols, _ = mine[u]
            dst = view(u, index)
            src = w[m].at[:, pl.ds(first, cols)] if own else dst
            return pltpu.make_async_remote_copy(
                src, dst, ssem.at[u, k], rsem.at[u, k], device_id=target, device_id_type=MESH
            )

        def local_copy(u):
            m, first, cols, _ = mine[u]
            return pltpu.make_async_copy(
                w[m].at[:, pl.ds(first, cols)], view(u, (z, y, x)), lsem.at[u]
            )

        def plan(u):
            held = {"z": False, "y": False, "x": False}

            def index(zz=z, flip=None):
                return (
                    every if held["z"] else zz,
                    every if held["y"] else (1 - y if flip == "y" else y),
                    every if held["x"] else (1 - x if flip == "x" else x),
                )

            steps = []
            pending = []
            sends = []
            own = True
            pair = 0
            for axis in mine[u][3]:
                if axis != "z":
                    send = [(True, functools.partial(copy, u, index(), pair, partner[axis], own))]
                    steps.append((pending, send))
                    sends += send
                    pending = [
                        (True, functools.partial(copy, u, index(flip=axis), pair, partner[axis]))
                    ]
                    pair += 1
                else:

                    def chain(shift, k, target, first=False):
                        return functools.partial(copy, u, index(zz=z + shift), k, target, first)

                    one = [(z < 3, chain(0, 2, up, own)), (z > 0, chain(0, 5, down, own))]
                    steps.append((pending, one))
                    middle = (z > 0) & (z < 3)
                    two = [(middle, chain(-1, 3, up)), (middle, chain(1, 6, down))]
                    steps.append(([(z > 0, chain(-1, 2, down)), (z < 3, chain(1, 5, up))], two))
                    three = [(z == 2, chain(-2, 4, up)), (z == 1, chain(2, 7, down))]
                    steps.append(([(z > 1, chain(-2, 3, down)), (z < 2, chain(2, 6, up))], three))
                    pending = [(z == 3, chain(-3, 4, down)), (z == 0, chain(3, 7, up))]
                    sends += one + two + three
                held[axis] = True
                own = False
            return steps, pending, sends

        plans = [plan(u) for u in range(len(mine))]

        def to_core(u, which):
            m, first, cols, _ = which[u]
            block = o[m].at[:, :, :, :, pl.ds(first, cols)]
            return pltpu.make_async_remote_copy(
                block,
                block,
                csem.at[u],
                crsem.at[u],
                device_id=device(z, y, x, 1 - c),
                device_id_type=MESH,
            )

        for u in range(len(mine)):
            local_copy(u).start()
        for u, s in order:
            steps, pending, _ = plans[u]
            if s == 1:
                local_copy(u).wait()
            for cond, make in steps[s][0] if s < 5 else pending:
                when(cond, lambda make=make: make().wait_recv())
            for cond, make in steps[s][1] if s < 5 else ():
                when(cond, lambda make=make: make().start())
            if s == 5:
                to_core(u, mine).start()
        for u in range(len(mine)):
            for cond, make in plans[u][2]:
                when(cond, lambda make=make: make().wait_send())
            to_core(u, mine).wait_send()
        for u in range(len(other)):
            to_core(u, other).wait_recv()

    pl.when(c == 0)(lambda: run(units[0], units[1], turns[0]))
    pl.when(c == 1)(lambda: run(units[1], units[0], turns[1]))
    side.wait()


ANY = pl.BlockSpec(memory_space=pl.ANY)
DMA = pltpu.SemaphoreType.DMA


SIDE = [DMA((16,)), DMA((16,)), DMA((1,))]


def gather(shards, rows, units, turns, collective_id, name):
    count = len(shards)
    most = max(len(units[0]), len(units[1]))
    shapes = [jax.ShapeDtypeStruct(GRID + s.shape, s.dtype) for s in shards]
    return pl.pallas_call(
        functools.partial(gather_kernel, units, turns, count),
        name=name,
        out_shape=shapes + [jax.ShapeDtypeStruct(rows.shape, rows.dtype)],
        in_specs=[ANY] * (count + 1),
        out_specs=[ANY] * (count + 1),
        scratch_shapes=[DMA((most, 8)), DMA((most, 8)), DMA((most,)), DMA((most,)), DMA((most,))]
        + SIDE,
        compiler_params=pltpu.CompilerParams(collective_id=collective_id, has_side_effects=True),
    )(*shards, rows)


ORDERS = (
    ("zyx", "zxy", "xyz", "zxy", "zyx", "zxy", "zyx", "yxz", "zyx", "zxy"),
    ("zxy", "zyx", "yxz", "zyx", "zxy", "zyx", "zxy", "xyz", "zxy", "zyx"),
)
AFTER_Z = (0.6165, 0.4168, 0.3474, 1.6339, 4.4601)
AFTER_XY = (1.5672, 1.5028, 1.8589, 1.1737, 2.0677)
PER_TURN = 2.2835
SHIFT = 0.1931
SIZE = 4
TAIL = (0.1, 2)


def gather_units(shards):
    units = ([], [])
    load = [0, 0]
    whole = sum(s.size for s in shards) / (ROWS * 128)
    done = 0
    for m, shard in enumerate(shards):
        rows, columns = shard.shape
        tiles = columns // 128
        weight = rows / ROWS
        at = 0
        while at < tiles:
            size = SIZE if done < (1 - TAIL[0]) * whole else TAIL[1]
            step = max(1, round(size / weight))
            n = min(step, tiles - at)
            if 0 < tiles - at - n < max(1, round(size / weight / 2)):
                n = tiles - at
            core = 0 if load[0] <= load[1] else 1
            order = ORDERS[core][len(units[core]) % len(ORDERS[core])]
            units[core].append((m, at * 128, n * 128, order))
            load[core] += n * weight
            done += n * weight
            at += n
    turns = []
    for core in range(2):
        keys = []
        place = 0.0
        for u, (m, first, columns, order) in enumerate(units[core]):
            at = place / PER_TURN + core * SHIFT
            place += shards[m].shape[0] * columns / (ROWS * 128 * SIZE)
            keys.append((at, u, 0))
            for s, after in enumerate(AFTER_Z if order[0] == "z" else AFTER_XY):
                at += after
                keys.append((at, u, s + 1))
        turns.append(tuple((u, s) for _, u, s in sorted(keys)))
    return (tuple(units[0]), tuple(units[1])), tuple(turns)


def exchange_kernel(in_ref, out_ref, *sems):
    greet()
    side = Exchange(True, in_ref, out_ref, *sems)
    side.start()
    side.wait()


def exchange(values, collective_id, name):
    return pl.pallas_call(
        exchange_kernel,
        name=name,
        out_shape=jax.ShapeDtypeStruct((16,) + values.shape, values.dtype),
        in_specs=[ANY],
        out_specs=ANY,
        scratch_shapes=SIDE,
        compiler_params=pltpu.CompilerParams(collective_id=collective_id, has_side_effects=True),
    )(values)


LAG = (0, 2, 3, 4, 5, 6)
RECV_SLOTS = 9
SEND_SLOTS = 8
FIRST_SLOTS = 4
UNIT = 384
ROWS = 72
PADDED = 80


def scatter_kernel(first, cols, source, dy_count, *refs):
    nv = len(first) - 1
    xt = refs[:nv]
    dy = refs[nv : nv + dy_count]
    out = refs[nv + dy_count + 1]
    (
        xts, dys, a_s1, a_s2, a_t, a_su, a_sd, e_s1, e_t, e_su, e_sd, e_sq,
        a_b1, a_b2, a_bu, a_bd, e_b1, e_bu, e_bd, e_bq, outs,
        ssem, rsem, xl, xs, xr, yl, ys, yr, ol, os, orr, es, er, el,
    ) = refs[nv + dy_count + 3 :]
    z, y, x, c = coords()
    total = first[-1] // 2
    sibling = device(z, y, x, 1 - c)
    up = device(z + 1, y, x, c)
    down = device(z - 1, y, x, c)
    greet()
    side = Broadcast(refs[nv + dy_count], refs[nv + dy_count + 2], es, er, el)
    lanes = pl.ds(pl.multiple_of(c * 128, 128), 128)
    offsets = []
    at = 0
    for k in range(dy_count):
        offsets.append(at)
        at += dy[k].shape[1]

    def remote(src, dst, send, recv, target):
        return pltpu.make_async_remote_copy(
            src, dst, send, recv, device_id=target, device_id_type=MESH
        )

    def x_views(v):
        return xt[v], xts.at[v, :, :, lanes]

    def x_local(v):
        return pltpu.make_async_copy(*x_views(v), xl.at[v])

    def x_remote(v):
        return remote(*x_views(v), xs.at[v], xr.at[v], sibling)

    def y_views(k):
        return dy[k], dys.at[lanes, pl.ds(offsets[k], dy[k].shape[1])]

    def y_local(k):
        return pltpu.make_async_copy(*y_views(k), yl.at[k])

    def y_remote(k):
        return remote(*y_views(k), ys.at[k], yr.at[k], sibling)

    fresh = [source[v] not in source[:v] for v in range(nv)]
    for v in range(nv):
        x_local(v).start()
        x_remote(v).start()
        if fresh[v]:
            y_local(source[v]).start()
            y_remote(source[v]).start()
        if v == 0:
            side.start()

    def arrive(tick):
        for v in range(nv):

            def wait(v=v):
                x_local(v).wait()
                x_remote(v).wait_recv()
                if fresh[v]:
                    y_local(source[v]).wait()
                    y_remote(source[v]).wait_recv()

            pl.when(tick == (first[v] - c + 1) // 2)(wait)

    def unit(i):
        j = 2 * i + c
        v = jnp.int32(0)
        col = j * UNIT
        for k in range(1, nv):
            past = (j >= first[k]).astype(jnp.int32)
            v = v + past
            col = col + past * ((cols[k] - first[k] * UNIT) - (cols[k - 1] - first[k - 1] * UNIT))
        return v, pl.multiple_of(col, 128)

    def axes(i):
        o = lax.rem(i, 2)
        pb = x * (1 - o) + y * o
        qb = y * (1 - o) + x * o
        dp = z * 4 + y * 2 + x
        return o, pb, qb, (dp + (1 - 2 * pb) * (1 + o), c), (dp + (1 - 2 * qb) * (2 - o), c)

    def slots(i):
        return lax.rem(i, FIRST_SLOTS), lax.rem(i, SEND_SLOTS), lax.rem(i, RECV_SLOTS)

    def send(src, dst, i, k, target):
        return remote(
            src, dst, ssem.at[lax.rem(i, SEND_SLOTS), k], rsem.at[lax.rem(i, RECV_SLOTS), k], target
        )

    def first_copies(i):
        o, pb, qb, pn, qn = axes(i)
        f, s, w = slots(i)
        return [send(a_s1.at[f], a_b1.at[w], i, 0, pn), send(e_s1.at[f], e_b1.at[w], i, 8, pn)]

    def second_copy(i):
        o, pb, qb, pn, qn = axes(i)
        f, s, w = slots(i)
        return send(a_s2.at[s], a_b2.at[w], i, 1, qn)

    def last_copy(i):
        o, pb, qb, pn, qn = axes(i)
        f, s, w = slots(i)
        return send(e_sq.at[s], e_bq.at[w], i, 9, qn)

    def up_copy(i, k, e):
        f, s, w = slots(i)
        src, dst, n = (e_su, e_bu, 10) if e else (a_su, a_bu, 2)
        return send(src.at[s, k], dst.at[w, k], i, n + k, up)

    def down_copy(i, k, e):
        f, s, w = slots(i)
        src, dst, n = (e_sd, e_bd, 13) if e else (a_sd, a_bd, 5)
        return send(src.at[s, k], dst.at[w, k], i, n + k, down)

    def up_sends(k):
        return (z <= k) & (z < 3)

    def down_sends(k):
        return (3 - z <= k) & (z > 0)

    def up_comes(k):
        return (z >= 1) & (z <= k + 1)

    def down_comes(k):
        return (z <= 2) & (3 - z <= k + 1)

    def kept(i, e, d):
        f, s, w = slots(i)
        if e:
            return e_t.at[s, d]
        return a_t.at[s, d, axes(i)[2]]

    def z_send(i, k, e):
        f, s, w = slots(i)

        def pass_on(dest, stage, box, inner, copy):
            value = kept(i, e, dest)[...]
            if k == 0:
                stage[s, k] = value.astype(BF16)
            else:

                def add():
                    stage[s, k] = (value + box[w, k - 1].astype(F32)).astype(BF16)

                def begin():
                    stage[s, k] = value.astype(BF16)

                pl.when(inner)(add)
                pl.when(jnp.logical_not(inner))(begin)
            copy.start()

        pl.when(up_sends(k))(
            lambda: pass_on(
                z + 3 - k, e_su if e else a_su, e_bu if e else a_bu, z > 0, up_copy(i, k, e)
            )
        )
        pl.when(down_sends(k))(
            lambda: pass_on(
                z + k - 3, e_sd if e else a_sd, e_bd if e else a_bd, z < 3, down_copy(i, k, e)
            )
        )

    def z_wait(i, k, e):
        pl.when(up_comes(k))(lambda: up_copy(i, k, e).wait_recv())
        pl.when(down_comes(k))(lambda: down_copy(i, k, e).wait_recv())

    def z_close(i, e):
        f, s, w = slots(i)
        mine = kept(i, e, z)

        def below():
            mine[...] = mine[...] + (e_bu if e else a_bu)[w, 2].astype(F32)

        def above():
            mine[...] = mine[...] + (e_bd if e else a_bd)[w, 2].astype(F32)

        pl.when(z > 0)(below)
        pl.when(z < 3)(above)
        return mine

    def product(i, bit):
        v, col = unit(i)
        o = axes(i)[0]
        chips = [4 * k + bit * (1 + o) + q * (2 - o) for k in range(4) for q in range(2)]
        lhs = jnp.concatenate([xts[v, chip] for chip in chips], axis=0)
        whole = jnp.dot(lhs, dys[:, pl.ds(col, UNIT)], preferred_element_type=F32)
        return whole.reshape(8, PADDED, UNIT)[:, :ROWS]

    def stage0(i):
        f, s, w = slots(i)
        part = product(i, 1 - axes(i)[1])
        a_s1[f] = part[:, :, :128].astype(BF16).reshape(4, 2, ROWS, 128)
        e_s1[f] = part[:, :, 128:].astype(BF16).reshape(4, 2, ROWS, 256)
        for copy in first_copies(i):
            copy.start()

    def stage1(i):
        f, s, w = slots(i)
        o, pb, qb, pn, qn = axes(i)
        part = product(i, pb)
        for copy in first_copies(i):
            copy.wait_recv()
        a_t[s] = part[:, :, :128].reshape(4, 2, ROWS, 128) + a_b1[w].astype(F32)
        a_s2[s] = a_t[s, :, 1 - qb].astype(BF16)
        second_copy(i).start()
        e_t[s] = part[:, :, 128:].reshape(4, 2, ROWS, 256) + e_b1[w].astype(F32)
        z_send(i, 0, True)

    def a_second(i):
        f, s, w = slots(i)
        qb = axes(i)[2]
        second_copy(i).wait_recv()
        a_t[s, :, qb] = a_t[s, :, qb] + a_b2[w].astype(F32)
        z_send(i, 0, False)

    def z_step(i, k, e):
        z_wait(i, k - 1, e)
        z_send(i, k, e)

    def e_fourth(i):
        f, s, w = slots(i)
        z_wait(i, 2, True)
        z_close(i, True)
        e_sq[s] = e_t[s, z, 1 - axes(i)[2]].astype(BF16)
        last_copy(i).start()

    def out_view(i):
        return out.at[:, pl.ds(pl.multiple_of((2 * i + c) * UNIT, 128), UNIT)]

    def a_fifth(i):
        z_wait(i, 2, False)
        outs[i, :, :128] = z_close(i, False)[...]

    def e_fifth(i):
        f, s, w = slots(i)
        last_copy(i).wait_recv()
        outs[i, :, 128:] = e_t[s, z, axes(i)[2]] + e_bq[w].astype(F32)
        pltpu.make_async_copy(outs.at[i], out_view(i), ol.at[0]).start()
        remote(outs.at[i], out_view(i), os.at[0], orr.at[0], sibling).start()

    def first_sent(i):
        for copy in first_copies(i):
            copy.wait_send()

    def sent(i):
        second_copy(i).wait_send()
        last_copy(i).wait_send()
        for e in (False, True):
            for k in range(3):
                pl.when(up_sends(k))(lambda k=k, e=e: up_copy(i, k, e).wait_send())
                pl.when(down_sends(k))(lambda k=k, e=e: down_copy(i, k, e).wait_send())

    stages = (
        (a_fifth, LAG[5]),
        (functools.partial(z_step, k=1, e=False), LAG[3]),
        (functools.partial(z_step, k=2, e=True), LAG[3]),
        (e_fourth, LAG[4]),
        (stage0, LAG[0]),
        (functools.partial(z_step, k=1, e=True), LAG[2]),
        (a_second, LAG[2]),
        (functools.partial(z_step, k=2, e=False), LAG[4]),
        (e_fifth, LAG[5]),
        (stage1, LAG[1]),
    )

    def tick(t, carry):
        arrive(t)
        pl.when(t == 4)(side.forward)
        pl.when((t >= SEND_SLOTS) & (t - SEND_SLOTS < total))(lambda: sent(t - SEND_SLOTS))
        pl.when((t >= FIRST_SLOTS) & (t - FIRST_SLOTS < total))(lambda: first_sent(t - FIRST_SLOTS))
        for stage, lag in stages:
            i = t - lag
            pl.when((i >= 0) & (i < total))(functools.partial(stage, i))
        return carry

    lax.fori_loop(0, total + SEND_SLOTS, tick, 0)
    for v in range(nv):
        x_remote(v).wait_send()
    for k in range(dy_count):
        y_remote(k).wait_send()
    half = out.at[:, pl.ds(0, total * UNIT)]
    pltpu.make_async_copy(half, half, ol.at[0]).wait()
    everything = remote(half, half, os.at[0], orr.at[0], sibling)
    everything.wait_send()
    everything.wait_recv()
    side.wait()


def scatter(xts, dys, source, rows, collective_id, name):
    nv = len(xts)
    starts = []
    width = 0
    for d in dys:
        starts.append(width)
        width += d.shape[1]
    first = [0]
    cols = []
    for v in range(nv):
        cols.append(starts[source[v]])
        first.append(first[-1] + dys[source[v]].shape[1] // UNIT)
    total = first[-1] // 2
    s, f, r = SEND_SLOTS, FIRST_SLOTS, RECV_SLOTS
    vmem = pltpu.VMEM
    return pl.pallas_call(
        functools.partial(scatter_kernel, tuple(first), tuple(cols), tuple(source), len(dys)),
        name=name,
        out_shape=[
            jax.ShapeDtypeStruct((ROWS, first[-1] * UNIT), F32),
            jax.ShapeDtypeStruct(GRID + rows.shape, rows.dtype),
        ],
        in_specs=[ANY] * (nv + len(dys) + 1),
        out_specs=[ANY] * 2,
        scratch_shapes=[
            vmem((nv, 16, PADDED, 256), BF16),
            vmem((256, width), BF16),
            vmem((f, 4, 2, ROWS, 128), BF16),
            vmem((s, 4, ROWS, 128), BF16),
            vmem((s, 4, 2, ROWS, 128), F32),
            vmem((s, 3, ROWS, 128), BF16),
            vmem((s, 3, ROWS, 128), BF16),
            vmem((f, 4, 2, ROWS, 256), BF16),
            vmem((s, 4, 2, ROWS, 256), F32),
            vmem((s, 3, 2, ROWS, 256), BF16),
            vmem((s, 3, 2, ROWS, 256), BF16),
            vmem((s, ROWS, 256), BF16),
            vmem((r, 4, 2, ROWS, 128), BF16),
            vmem((r, 4, ROWS, 128), BF16),
            vmem((r, 3, ROWS, 128), BF16),
            vmem((r, 3, ROWS, 128), BF16),
            vmem((r, 4, 2, ROWS, 256), BF16),
            vmem((r, 3, 2, ROWS, 256), BF16),
            vmem((r, 3, 2, ROWS, 256), BF16),
            vmem((r, ROWS, 256), BF16),
            vmem((total, ROWS, UNIT), F32),
            DMA((s, 16)),
            DMA((r, 16)),
            DMA((nv,)),
            DMA((nv,)),
            DMA((nv,)),
            DMA((len(dys),)),
            DMA((len(dys),)),
            DMA((len(dys),)),
            DMA((1,)),
            DMA((1,)),
            DMA((1,)),
        ]
        + SIDE,
        compiler_params=pltpu.CompilerParams(
            collective_id=collective_id, has_side_effects=True, vmem_limit_bytes=62 * 1024 * 1024
        ),
    )(*xts, *dys, rows)


def layer_norm(values):
    center = values - jnp.mean(values, axis=-1, keepdims=True)
    spread = jnp.mean(center * center, axis=-1, keepdims=True)
    return center * lax.rsqrt(spread + 1e-06)


def head_norm(values, gain):
    shaped = values.reshape(values.shape[:-1] + (HEADS, HD))
    scaled = shaped * lax.rsqrt(jnp.mean(shaped * shaped, axis=-1, keepdims=True) + 1e-06)
    return scaled * gain.reshape(HEADS, HD)


def rope_tables(rows, columns):
    quarter = HD // 4
    freqs = jnp.exp(jnp.arange(quarter, dtype=F32) * (-math.log(10000.0) / quarter))
    places = jnp.stack([rows, columns], axis=-1).astype(F32)
    angles = places[..., None] * freqs
    return (jnp.cos(angles), jnp.sin(angles))


def rotate(values, cosine, sine):
    shaped = values.reshape(values.shape[:-1] + (2, 2, HD // 4))
    first = shaped[..., 0, :]
    second = shaped[..., 1, :]
    cosine = cosine[..., None, :, :]
    sine = sine[..., None, :, :]
    turned = jnp.stack([first * cosine - second * sine, first * sine + second * cosine], axis=-2)
    return turned.reshape(values.shape)


def embed_times(times, width):
    half_width = width // 2
    freqs = jnp.exp(jnp.arange(half_width, dtype=F32) * (-math.log(10000.0) / half_width))
    angles = times[..., None] * freqs
    return jnp.concatenate([jnp.cos(angles), jnp.sin(angles)], axis=-1)


def qk_prepare(query_raw, key_raw, gains, cosine, sine):
    return (
        rotate(head_norm(query_raw, gains[0]), cosine, sine),
        rotate(head_norm(key_raw, gains[1]), cosine, sine),
    )


def swish_product(gate, up):
    return jax.nn.silu(gate) * up


def attention_scores(queries, keys, allowed):
    scores = jnp.einsum("sqhd,skhd->shqk", queries, keys, preferred_element_type=F32) * (
        1.0 / math.sqrt(HD)
    )
    return jnp.where(allowed[:, None], scores, -1e30)


def dense(values, weight):
    return jnp.dot(values, weight, preferred_element_type=F32)


def dense_back(grads, weight):
    return lax.dot_general(grads, weight, (((1,), (1,)), ((), ())), preferred_element_type=F32)


def outer_sum(values, grads):
    return lax.dot_general(values, grads, (((0,), (0,)), ((), ())), preferred_element_type=F32)


def block_forward(flat, modulation, weights, context):
    batch, half, allowed, cosine, sine = context
    triple, mixing, expand, reduce_w, gains = weights
    width = flat.shape[1]
    shift1, scale1, gate1, shift2, scale2, gate2 = jnp.split(modulation, 6, axis=1)
    lifted1 = (layer_norm(flat) * (1.0 + scale1) + shift1).astype(BF16)
    projected = dense(lifted1, triple)
    query_raw, key_raw, value_raw = jnp.split(projected, 3, axis=1)
    queries, keys = qk_prepare(query_raw, key_raw, gains, cosine, sine)
    queries = queries.astype(BF16).reshape(batch, half, HEADS, HD)
    keys_local = keys.astype(BF16).reshape(batch, half, width)
    values_local = value_raw.astype(BF16).reshape(batch, half, width)
    key_heads = lax.all_gather(keys_local, "ctx", axis=1, tiled=True).reshape(batch, -1, HEADS, HD)
    value_heads = lax.all_gather(values_local, "ctx", axis=1, tiled=True)
    value_heads = value_heads.reshape(batch, -1, HEADS, HD)
    scores = attention_scores(queries, key_heads, allowed)
    top = jnp.max(scores, axis=-1, keepdims=True)
    raised = jnp.exp(scores - top)
    total = jnp.sum(raised, axis=-1, keepdims=True)
    softmax_low = (raised / total).astype(BF16)
    logsum = top + jnp.log(total)
    mixed = jnp.einsum("shqk,skhd->sqhd", softmax_low, value_heads, preferred_element_type=F32)
    mixed_low = mixed.reshape(-1, width).astype(BF16)
    attended = dense(mixed_low, mixing)
    resid = flat + gate1 * attended
    lifted2 = (layer_norm(resid) * (1.0 + scale2) + shift2).astype(BF16)
    expanded = dense(lifted2, expand)
    gate, up = jnp.split(expanded, 2, axis=1)
    hidden = swish_product(gate, up).astype(BF16)
    feed = dense(hidden, reduce_w)
    output = resid + gate2 * feed
    kept = (
        modulation,
        flat,
        lifted1,
        query_raw,
        key_raw,
        queries,
        key_heads,
        value_heads,
        logsum,
        mixed_low,
        attended,
        resid,
        lifted2,
        expanded,
        hidden,
        feed,
    )
    return (output, kept)


def block_backward(grad_out, kept, weights, context):
    batch, half, allowed, cosine, sine = context
    triple, mixing, expand, reduce_w, gains = weights
    (
        modulation,
        flat,
        lifted1,
        query_raw,
        key_raw,
        queries,
        key_heads,
        value_heads,
        logsum,
        mixed_low,
        attended,
        resid,
        lifted2,
        expanded,
        hidden,
        feed,
    ) = kept
    width = flat.shape[1]
    shift1, scale1, gate1, shift2, scale2, gate2 = jnp.split(modulation, 6, axis=1)
    grad_feed = (grad_out * gate2).astype(BF16)
    grad_hidden = dense_back(grad_feed, reduce_w)
    gate, up = jnp.split(expanded, 2, axis=1)
    unused_out, swish_pull = jax.vjp(swish_product, gate, up)
    grad_gate, grad_up = swish_pull(grad_hidden)
    grad_expanded = jnp.concatenate([grad_gate, grad_up], axis=1).astype(BF16)
    grad_lifted2 = dense_back(grad_expanded, expand)
    normed_second, second_pull = jax.vjp(layer_norm, resid)
    grad_resid = grad_out + second_pull(grad_lifted2 * (1.0 + scale2))[0]
    grad_attended = (grad_resid * gate1).astype(BF16)
    grad_mixed = dense_back(grad_attended, mixing).astype(BF16).reshape(batch, half, HEADS, HD)
    scores = attention_scores(queries, key_heads, allowed)
    chances = jnp.exp(scores - logsum)
    grad_chances = jnp.einsum(
        "sqhd,skhd->shqk", grad_mixed, value_heads, preferred_element_type=F32
    )
    grad_values = jnp.einsum(
        "shqk,sqhd->skhd", chances.astype(BF16), grad_mixed, preferred_element_type=F32
    )
    grad_scores = (
        chances * (grad_chances - jnp.sum(chances * grad_chances, axis=-1, keepdims=True))
    ).astype(BF16)
    scale = 1.0 / math.sqrt(HD)
    grad_queries = (
        jnp.einsum("shqk,skhd->sqhd", grad_scores, key_heads, preferred_element_type=F32) * scale
    )
    grad_keys = (
        jnp.einsum("shqk,sqhd->skhd", grad_scores, queries, preferred_element_type=F32) * scale
    )
    pair = jnp.stack(
        [grad_keys.reshape(batch, -1, width), grad_values.reshape(batch, -1, width)]
    ).astype(BF16)
    place = lax.axis_index("ctx")
    theirs = lax.dynamic_slice_in_dim(pair, (1 - place) * half, half, 2)
    theirs = lax.ppermute(theirs, "ctx", [(0, 1), (1, 0)])
    mine = lax.dynamic_slice_in_dim(pair, place * half, half, 2)
    pair = mine.astype(F32) + theirs.astype(F32)
    grad_keys, grad_values = pair[0], pair[1]

    def prepare(query_in, key_in, gain_in):
        return qk_prepare(query_in, key_in, gain_in, cosine, sine)

    unused_pair, prepare_pull = jax.vjp(prepare, query_raw, key_raw, gains)
    grad_query_raw, grad_key_raw, gains_grad = prepare_pull(
        (grad_queries.reshape(-1, HEADS, HD), grad_keys.reshape(-1, HEADS, HD))
    )
    grad_projected = jnp.concatenate(
        [grad_query_raw, grad_key_raw, grad_values.reshape(-1, width)], axis=1
    ).astype(BF16)
    grad_lifted1 = dense_back(grad_projected, triple)
    normed_first, first_pull = jax.vjp(layer_norm, flat)
    grad_flat = grad_resid + first_pull(grad_lifted1 * (1.0 + scale1))[0]
    grad_modulation = jnp.concatenate(
        [
            grad_lifted1,
            grad_lifted1 * normed_first,
            grad_resid * attended,
            grad_lifted2,
            grad_lifted2 * normed_second,
            grad_out * feed,
        ],
        axis=1,
    ).astype(BF16)
    factors = (
        (lifted1, grad_projected),
        (mixed_low, grad_attended),
        (lifted2, grad_expanded),
        (hidden, grad_feed),
    )
    return (grad_flat, grad_modulation, factors, gains_grad)


def meet_sibling():
    barrier = pltpu.get_barrier_semaphore()
    sibling = (lax.axis_index("dp"), 1 - lax.axis_index("ctx"))
    pl.semaphore_signal(barrier, inc=1, device_id=sibling, device_id_type=MESH)
    pl.semaphore_wait(barrier, 1)
    return sibling


def head_sum_matrix(width):
    channel = lax.broadcasted_iota(jnp.int32, (width, 128), 0)
    head = lax.broadcasted_iota(jnp.int32, (width, 128), 1)
    inside = (channel >= head * HD) & (channel < (head + 1) * HD)
    return jnp.where(inside, 1.0, 0.0).astype(F32)


def exact_dot(left, right):
    return jnp.dot(left, right, preferred_element_type=F32, precision=lax.Precision.HIGHEST)


def spread_heads(values, heads):
    return lax.dot_general(
        values,
        heads,
        (((1,), (1,)), ((), ())),
        preferred_element_type=F32,
        precision=lax.Precision.HIGHEST,
    )


def swap_pairs(values):
    width = values.shape[1]
    lane = lax.broadcasted_iota(jnp.int32, values.shape, 1)
    quarter = HD // 4
    early = lax.rem(lane, 2 * quarter) < quarter
    return jnp.where(
        early, pltpu.roll(values, width - quarter, 1), pltpu.roll(values, quarter, 1)
    )


def normalize(values):
    mean = jnp.mean(values, axis=1, keepdims=True)
    center = values - mean
    spread = jnp.mean(center * center, axis=1, keepdims=True)
    inverse = lax.rsqrt(spread + 1e-06)
    return center * inverse, inverse


def norm_back(normed, inverse, grad):
    mean = jnp.mean(grad, axis=1, keepdims=True)
    along = jnp.mean(grad * normed, axis=1, keepdims=True)
    return (grad - mean - normed * along) * inverse


def window(h, width):
    first = min((h * HD) // 128 * 128, width - 256)
    return first, h * HD - first


def head_mask(h, width, rows):
    first, at = window(h, width)
    lane = lax.broadcasted_iota(jnp.int32, (rows, 256), 1)
    return (lane >= at) & (lane < at + HD)


def turned(values):
    tokens, width = values.shape
    rows = values.T.reshape(-1, ROWS, tokens)
    return jnp.concatenate(
        [rows, jnp.zeros((width // ROWS, PADDED - ROWS, tokens), F32)], axis=1
    ).astype(BF16)


FF_TILE = 768
KV_TILE = 1152


def allowed_mask(seg_q, seg_k, pad_k, half):
    place_q = lax.axis_index("ctx") * half + lax.broadcasted_iota(jnp.int32, (half, 2 * half), 0)
    place_k = lax.broadcasted_iota(jnp.int32, (half, 2 * half), 1)
    return (seg_q[...] == seg_k[...]) & ((pad_k[...] == 0) | (place_q == place_k))


def forward_kernel(
    flat, mod, gains, cosine, sine, seg_q, seg_k, pad_k, triple_h, mixing_h, expand_h, reduce_h,
    output, raw, queries, kv, lse, attended, resid, expanded, feed, xt1, xtm, xt2, xth,
    triple, mixing, expand, reduce_w, mixed, wsem, ssem, rsem,
):
    half, width = flat.shape
    loads = [
        pltpu.make_async_copy(src, dst, wsem.at[k])
        for k, (src, dst) in enumerate(
            ((triple_h, triple), (mixing_h, mixing), (expand_h, expand), (reduce_h, reduce_w))
        )
    ]
    for load in loads:
        load.start()
    sibling = meet_sibling()
    c = lax.axis_index("ctx")
    mine = pl.ds(pl.multiple_of(c * half, 128), half)

    def part(k):
        return mod[:, k * width : (k + 1) * width]

    normed, unused = normalize(flat[...])
    lifted = normed * (1.0 + part(1)) + part(0)
    lifted_low = lifted.astype(BF16)
    xt1[...] = turned(lifted_low.astype(F32))
    heads = head_sum_matrix(width)
    loads[0].wait()

    def prepared(k):
        values = raw[:, k * width : (k + 1) * width]
        mean = exact_dot(values * values, heads) * (1.0 / HD)
        scaled = values * spread_heads(lax.rsqrt(mean + 1e-06), heads) * gains[k : k + 1, :]
        return scaled * cosine[...] + swap_pairs(scaled) * sine[...]

    def project(k):
        return jnp.dot(
            lifted_low, triple[:, k * width : (k + 1) * width], preferred_element_type=F32
        )

    raw[:, width:] = project(1)
    kv[0, mine] = prepared(1).astype(BF16)
    kv[1, mine] = project(2).astype(BF16)
    share = pltpu.make_async_remote_copy(
        kv.at[:, mine], kv.at[:, mine], ssem.at[0], rsem.at[0], device_id=sibling,
        device_id_type=MESH,
    )
    share.start()
    raw[:, :width] = project(0)
    queries[...] = prepared(0).astype(BF16)
    allowed = allowed_mask(seg_q, seg_k, pad_k, half)
    mixed[...] = jnp.zeros_like(mixed)
    lane = lax.broadcasted_iota(jnp.int32, (half, 128), 1)
    sums = jnp.zeros((half, 128), F32)
    theirs = pl.ds(pl.multiple_of((1 - c) * half, 128), half)
    pltpu.make_async_remote_copy(
        kv.at[:, theirs], kv.at[:, theirs], ssem.at[0], rsem.at[0], device_id=sibling,
        device_id_type=MESH,
    ).wait_recv()
    for h in range(width // HD):
        first, unused = window(h, width)
        span = slice(first, first + 256)
        mask = head_mask(h, width, half)
        query = jnp.where(mask, queries[:, span].astype(F32), 0.0).astype(BF16)
        scores = dense_back(query, kv[0, :, span]) * (1.0 / math.sqrt(HD))
        scores = jnp.where(allowed, scores, -1e30)
        top = jnp.max(scores, axis=1, keepdims=True)
        raised = jnp.exp(scores - top)
        total = jnp.sum(raised, axis=1, keepdims=True)
        low = (raised / total).astype(BF16)
        out = jnp.dot(low, kv[1, :, span], preferred_element_type=F32)
        mixed[:, span] = mixed[:, span] + jnp.where(mask, out, 0.0)
        sums = jnp.where(lane == h, top + jnp.log(total), sums)
    lse[...] = sums
    mixed_low = mixed[...].astype(BF16)
    xtm[...] = turned(mixed_low.astype(F32))
    loads[1].wait()
    attended[...] = jnp.dot(mixed_low, mixing[...], preferred_element_type=F32)
    resid[...] = flat[...] + part(2) * attended[...]
    normed, unused = normalize(resid[...])
    lifted_low = (normed * (1.0 + part(4)) + part(3)).astype(BF16)
    xt2[...] = turned(lifted_low.astype(F32))
    feed[...] = jnp.zeros_like(feed)
    loads[2].wait()
    loads[3].wait()
    hidden_size = reduce_w.shape[0]
    xth[...] = jnp.zeros_like(xth)
    for t in range(hidden_size // FF_TILE):
        gate = jnp.dot(
            lifted_low, expand[:, t * FF_TILE : (t + 1) * FF_TILE], preferred_element_type=F32
        )
        up = jnp.dot(
            lifted_low,
            expand[:, hidden_size + t * FF_TILE : hidden_size + (t + 1) * FF_TILE],
            preferred_element_type=F32,
        )
        expanded[:, t * FF_TILE : (t + 1) * FF_TILE] = gate
        expanded[:, hidden_size + t * FF_TILE : hidden_size + (t + 1) * FF_TILE] = up
        hidden = (gate * jax.nn.sigmoid(gate) * up).astype(BF16)
        pieces = hidden.astype(F32).T.astype(BF16).reshape(FF_TILE // 192, 3, 64, half)
        for g in range(3):
            xth[g, t * (FF_TILE // 192) : (t + 1) * (FF_TILE // 192), :64] = pieces[:, g]
        feed[...] = feed[...] + jnp.dot(
            hidden, reduce_w[t * FF_TILE : (t + 1) * FF_TILE], preferred_element_type=F32
        )
    output[...] = resid[...] + part(5) * feed[...]
    share.wait_send()


def backward_kernel(
    grad_out, flat, mod, gains, cosine, sine, seg_q, seg_k, pad_k,
    raw, queries, kv, lse, attended, resid, expanded, feed,
    triple_h, mixing_h, expand_h, reduce_h,
    grad_flat, grad_mod, grad_feed, grad_expanded, grad_attended, grad_projected, gains_grad,
    triple, mixing, expand, reduce_w, grad_q, grad_k, grad_v, lift, outgoing, incoming,
    wsem, ssem, rsem,
):
    half, width = flat.shape
    loads = [
        pltpu.make_async_copy(src, dst, wsem.at[k])
        for k, (src, dst) in enumerate(
            ((reduce_h, reduce_w), (expand_h, expand), (mixing_h, mixing), (triple_h, triple))
        )
    ]
    for load in loads:
        load.start()
    sibling = meet_sibling()
    c = lax.axis_index("ctx")
    mine = pl.ds(pl.multiple_of(c * half, 128), half)
    theirs = pl.ds(pl.multiple_of((1 - c) * half, 128), half)

    def part(k):
        return mod[:, k * width : (k + 1) * width]

    def keep(k, values):
        grad_mod[:, k * width : (k + 1) * width] = values.astype(BF16)

    keep(5, grad_out[...] * feed[...])
    feed_low = (grad_out[...] * part(5)).astype(BF16)
    grad_feed[...] = feed_low
    hidden_size = reduce_w.shape[0]
    lift[...] = jnp.zeros_like(lift)
    loads[0].wait()
    loads[1].wait()
    for t in range(hidden_size // FF_TILE):
        one = slice(t * FF_TILE, (t + 1) * FF_TILE)
        two = slice(hidden_size + t * FF_TILE, hidden_size + (t + 1) * FF_TILE)
        grad_hidden = dense_back(feed_low, reduce_w[one])
        gate = expanded[:, one]
        up = expanded[:, two]
        sig = jax.nn.sigmoid(gate)
        grad_gate = (grad_hidden * up * (sig * (1.0 + gate * (1.0 - sig)))).astype(BF16)
        grad_up = (grad_hidden * (gate * sig)).astype(BF16)
        grad_expanded[:, one] = grad_gate
        grad_expanded[:, two] = grad_up
        lift[...] = lift[...] + dense_back(grad_gate, expand[:, one])
        lift[...] = lift[...] + dense_back(grad_up, expand[:, two])
    normed, inverse = normalize(resid[...])
    keep(3, lift[...])
    keep(4, lift[...] * normed)
    grad_resid = grad_out[...] + norm_back(normed, inverse, lift[...] * (1.0 + part(4)))
    keep(2, grad_resid * attended[...])
    grad_flat[...] = grad_resid
    attended_low = (grad_resid * part(2)).astype(BF16)
    grad_attended[...] = attended_low
    loads[2].wait()
    lift[...] = dense_back(attended_low, mixing[...])
    allowed = allowed_mask(seg_q, seg_k, pad_k, half)
    grad_q[...] = jnp.zeros_like(grad_q)
    grad_k[...] = jnp.zeros_like(grad_k)
    grad_v[...] = jnp.zeros_like(grad_v)
    scale = 1.0 / math.sqrt(HD)
    lane = lax.broadcasted_iota(jnp.int32, (half, 128), 1)
    for h in range(width // HD):
        first, unused = window(h, width)
        span = slice(first, first + 256)
        mask = head_mask(h, width, half)
        query = jnp.where(mask, queries[:, span].astype(F32), 0.0).astype(BF16)
        grad_mixed = jnp.where(mask, lift[:, span], 0.0).astype(BF16)
        scores = dense_back(query, kv[0, :, span]) * scale
        logsum = jnp.sum(jnp.where(lane == h, lse[...], 0.0), axis=1, keepdims=True)
        chances = jnp.exp(jnp.where(allowed, scores, -1e30) - logsum)
        grad_chances = dense_back(grad_mixed, kv[1, :, span])
        along = jnp.sum(chances * grad_chances, axis=1, keepdims=True)
        grad_scores = chances * (grad_chances - along)
        scores_low = grad_scores.astype(BF16)
        out = jnp.dot(scores_low, kv[0, :, span], preferred_element_type=F32)
        grad_q[:, span] = grad_q[:, span] + jnp.where(mask, out, 0.0)
        grad_k[:, span] = grad_k[:, span] + outer_sum(scores_low, query)
        grad_v[:, span] = grad_v[:, span] + outer_sum(chances.astype(BF16), grad_mixed)
    outgoing[0] = (grad_k[theirs, :] * scale).astype(BF16)
    outgoing[1] = grad_v[theirs, :].astype(BF16)
    share = pltpu.make_async_remote_copy(
        outgoing, incoming, ssem.at[0], rsem.at[0], device_id=sibling, device_id_type=MESH
    )
    share.start()
    heads = head_sum_matrix(width)

    def prepare_back(k, grad):
        values = raw[:, k * width : (k + 1) * width]
        gain = gains[k : k + 1, :]
        mean = exact_dot(values * values, heads) * (1.0 / HD)
        inverse = spread_heads(lax.rsqrt(mean + 1e-06), heads)
        scaled = values * inverse
        turned_back = grad * cosine[...] + swap_pairs(grad * sine[...])
        gains_grad[k : k + 1, :] = jnp.sum(turned_back * scaled, axis=0, keepdims=True)
        turned_back = turned_back * gain
        along = spread_heads(exact_dot(turned_back * scaled, heads) * (1.0 / HD), heads)
        return (turned_back - scaled * along) * inverse

    grad_projected[:, :width] = prepare_back(0, grad_q[...] * scale).astype(BF16)
    share.wait()
    own_k = (grad_k[mine, :] * scale).astype(BF16).astype(F32) + incoming[0].astype(F32)
    own_v = grad_v[mine, :].astype(BF16).astype(F32) + incoming[1].astype(F32)
    grad_projected[:, width : 2 * width] = prepare_back(1, own_k).astype(BF16)
    grad_projected[:, 2 * width :] = own_v.astype(BF16)
    loads[3].wait()
    total = dense_back(grad_projected[:, :width], triple[:, :width])
    for k in (1, 2):
        span = slice(k * width, (k + 1) * width)
        total = total + dense_back(grad_projected[:, span], triple[:, span])
    normed, inverse = normalize(flat[...])
    keep(0, total)
    keep(1, total * normed)
    grad_flat[...] = grad_flat[...] + norm_back(normed, inverse, total * (1.0 + part(1)))


IN_VMEM = pl.BlockSpec(memory_space=pltpu.VMEM)


def weight_scratch(weights):
    return [pltpu.VMEM(w.shape, w.dtype) for w in weights]


def kernel_forward(flat, modulation, weights, context, name):
    cosine, sine, seg_q, seg_k, pad_k = context
    *weights, gains = weights
    half, width = flat.shape
    hidden_size = weights[3].shape[0]

    def struct(shape, dtype=F32):
        return jax.ShapeDtypeStruct(shape, dtype)

    rows = (16, PADDED, half)
    out_shape = [
        struct((half, width)),
        struct((half, 2 * width)),
        struct((half, width), BF16),
        struct((2, 2 * half, width), BF16),
        struct((half, 128)),
        struct((half, width)),
        struct((half, width)),
        struct((half, 2 * hidden_size)),
        struct((half, width)),
        struct(rows, BF16),
        struct(rows, BF16),
        struct(rows, BF16),
        struct((3,) + rows, BF16),
    ]
    output, *rest = pl.pallas_call(
        forward_kernel,
        name=name,
        out_shape=out_shape,
        in_specs=[IN_VMEM] * 8 + [ANY] * 4,
        out_specs=[IN_VMEM] * len(out_shape),
        scratch_shapes=weight_scratch(weights)
        + [pltpu.VMEM((half, width), F32), DMA((4,)), DMA((1,)), DMA((1,))],
        compiler_params=pltpu.CompilerParams(
            collective_id=5, has_side_effects=True, vmem_limit_bytes=60 * 1024 * 1024
        ),
    )(flat, modulation, gains, cosine, sine, seg_q, seg_k, pad_k, *weights)
    return output, (flat, modulation, rest[:8]), rest[8:]


def kernel_backward(grad_out, kept, weights, context, name):
    cosine, sine, seg_q, seg_k, pad_k = context
    flat, modulation, saved = kept
    *weights, gains = weights
    half, width = flat.shape
    hidden_size = weights[3].shape[0]

    def struct(columns, dtype=BF16):
        return jax.ShapeDtypeStruct((half, columns), dtype)

    out_shape = [
        struct(width, F32),
        struct(6 * width),
        struct(width),
        struct(2 * hidden_size),
        struct(width),
        struct(3 * width),
        jax.ShapeDtypeStruct((2, width), F32),
    ]
    vmem = pltpu.VMEM
    return pl.pallas_call(
        backward_kernel,
        name=name,
        out_shape=out_shape,
        in_specs=[IN_VMEM] * 17 + [ANY] * 4,
        out_specs=[IN_VMEM] * len(out_shape),
        scratch_shapes=weight_scratch(weights)
        + [
            vmem((half, width), F32),
            vmem((2 * half, width), F32),
            vmem((2 * half, width), F32),
            vmem((half, width), F32),
            vmem((2, half, width), BF16),
            vmem((2, half, width), BF16),
            DMA((4,)),
            DMA((1,)),
            DMA((1,)),
        ],
        compiler_params=pltpu.CompilerParams(
            collective_id=6, has_side_effects=True, vmem_limit_bytes=60 * 1024 * 1024
        ),
    )(
        grad_out, flat, modulation, gains, cosine, sine, seg_q, seg_k, pad_k, *saved, *weights
    )


def shard_rows(values):
    rows = values.T.reshape(16, -1, values.shape[0])
    return jnp.pad(rows, ((0, 0), (0, PADDED - rows.shape[1]), (0, 0)))


def split_kernel(pieces, in_ref, *refs):
    *outs, held, arrived, left = refs
    for k, (n, row, rows, columns, at) in enumerate(pieces):
        span = (pl.ds(0, rows), pl.ds(at, columns))
        pltpu.make_async_copy(in_ref.at[span], held.at[span], arrived.at[k]).start()

    def leave(k):
        n, row, rows, columns, at = pieces[k]
        span = (pl.ds(0, rows), pl.ds(at, columns))
        return pltpu.make_async_copy(held.at[span], outs[n].at[pl.ds(row, rows), :], left.at[k])

    for k, (n, row, rows, columns, at) in enumerate(pieces):
        span = (pl.ds(0, rows), pl.ds(at, columns))
        pltpu.make_async_copy(in_ref.at[span], held.at[span], arrived.at[k]).wait()
        leave(k).start()
    for k in range(len(pieces)):
        leave(k).wait()


def split(values, shapes, pieces):
    return pl.pallas_call(
        functools.partial(split_kernel, tuple(pieces)),
        name="split",
        out_shape=[jax.ShapeDtypeStruct(shape, values.dtype) for shape in shapes],
        in_specs=[ANY],
        out_specs=[ANY] * len(shapes),
        scratch_shapes=[
            pltpu.VMEM(values.shape, values.dtype),
            DMA((len(pieces),)),
            DMA((len(pieces),)),
        ],
        compiler_params=pltpu.CompilerParams(vmem_limit_bytes=32 * 1024 * 1024),
    )(values)


def rope_lanes(cosine, sine):
    tokens = cosine.shape[0]

    def lanes(table, signs):
        table = jnp.stack([signs[0] * table, signs[1] * table], axis=2).reshape(tokens, 1, HD)
        return jnp.broadcast_to(table, (tokens, HEADS, HD)).reshape(tokens, HEADS * HD)

    return lanes(cosine, (1.0, 1.0)), lanes(sine, (-1.0, 1.0))


def fast_reduce(blocks, rows, collective_id, name):
    xts = []
    dys = []
    source = []
    for factors, extra in blocks:
        for lefts, right in factors:
            source += [len(dys)] * len(lefts)
            xts += lefts
            dys.append(right)
        tokens = right.shape[0]
        lines = -(-extra.shape[1] // tokens)
        packed = jnp.pad(extra, ((0, 0), (0, lines * tokens - extra.shape[1])))
        packed = packed.reshape(16, lines, tokens).astype(BF16)
        xts.append(jnp.pad(packed, ((0, 0), (0, PADDED - lines), (0, 0))))
        source.append(len(dys))
        dys.append(jnp.eye(tokens, UNIT, dtype=BF16))
    out, rows = scatter(xts, dys, source, rows, collective_id, name)
    shapes = []
    pieces = []
    smalls = []
    at = 0
    for factors, extra in blocks:
        for lefts, right in factors[:-1]:
            pieces.append((len(shapes), 0, ROWS, right.shape[1], at))
            shapes.append((ROWS, right.shape[1]))
            at += right.shape[1]
        width = factors[-1][1].shape[1]
        for g in range(3):
            pieces.append((len(shapes), 64 * g, 64, width, at))
            at += width
        shapes.append((192, width))
        lines = -(-extra.shape[1] // tokens)
        smalls.append(out[:lines, at : at + tokens].reshape(-1)[: extra.shape[1]])
        at += UNIT
    grads = split(out, shapes, pieces)
    results = []
    for (factors, extra), small in zip(blocks, smalls):
        results.append((grads[: len(factors)], small))
        grads = grads[len(factors) :]
    return results, rows


def whole_rows(gathered):
    return gathered.reshape((-1,) + gathered.shape[4:])


def fast_step(flat, cotangent, context, segment_local, valid, timesteps, encoder, decoder):
    width = flat.shape[1]
    offset_size = encoder[1].shape[0]
    gain_size = 2 * encoder[3].shape[1]
    small = jnp.concatenate(
        [
            encoder[1].astype(F32),
            decoder[1].astype(F32),
            encoder[3].astype(F32).reshape(-1),
            decoder[3].astype(F32).reshape(-1),
            timesteps.astype(F32).reshape(-1),
        ]
    )
    size = small.shape[0]
    small = jnp.pad(small, (0, 2048 - size)).reshape(16, 128)
    small = exchange(small, 0, "small").reshape(16, -1)
    encoder_offset = small[:, :offset_size].reshape(-1)
    decoder_offset = small[:, offset_size : 2 * offset_size].reshape(-1)
    at = 2 * offset_size
    encoder_gains = small[:, at : at + gain_size].reshape(16, 2, -1).swapaxes(0, 1).reshape(2, -1)
    at += gain_size
    decoder_gains = small[:, at : at + gain_size].reshape(16, 2, -1).swapaxes(0, 1).reshape(2, -1)
    at += gain_size
    all_times = small[:, at : at + timesteps.size]
    segments = timesteps.shape[1]
    picks = (segment_local[..., None] == jnp.arange(segments, dtype=jnp.int32)).astype(F32)
    picks = picks.reshape(-1, segments)

    all_cond = embed_times(all_times, width).reshape(-1, width)
    act_rows = jax.nn.silu(all_cond).astype(BF16)
    me = lax.axis_index("dp")
    rows = encoder[0].shape[0]
    act_mine = lax.dynamic_slice_in_dim(act_rows, me * rows, rows, 1)
    core = lax.axis_index("ctx")
    share = encoder[0].shape[1] // 2
    partial = dense(act_mine, lax.dynamic_slice_in_dim(encoder[0], core * share, share, 1))
    partial = partial.reshape(16, 8, -1)
    shards = (encoder[2], encoder[4], encoder[5], encoder[6])
    shards += (decoder[0], decoder[2], decoder[4], decoder[5], decoder[6])
    *wholes, partial = gather(shards, partial, *gather_units(shards), 1, "gather")
    wholes = [whole_rows(w) for w in wholes]
    encoder_weights = (*wholes[:4], encoder_gains)
    modulate = wholes[4]
    decoder_weights = (*wholes[5:], decoder_gains)
    partial = jnp.sum(partial, axis=0).reshape(segments, -1)
    others = lax.ppermute(partial, "ctx", [(0, 1), (1, 0)])
    modulation_rows = jnp.where(
        core == 0,
        jnp.concatenate([partial, others], axis=1),
        jnp.concatenate([others, partial], axis=1),
    )
    modulation_rows = modulation_rows + encoder_offset
    exact = lax.Precision.HIGHEST
    encoder_modulation = jnp.dot(picks, modulation_rows, precision=exact)
    cond_rows = lax.dynamic_slice_in_dim(all_cond, me * segments, segments, 0)
    cond = jnp.dot(picks, cond_rows, precision=exact)

    encoder_out, encoder_kept, encoder_left = kernel_forward(
        flat, encoder_modulation, encoder_weights, context, "encoder"
    )
    latent_full = valid * encoder_out
    decoder_pre = latent_full + cond
    decoder_act = jax.nn.silu(decoder_pre).astype(BF16)

    decoder_modulation = dense(decoder_act, modulate) + decoder_offset
    decoder_out, decoder_kept, decoder_left = kernel_forward(
        flat, decoder_modulation, decoder_weights, context, "decoder"
    )
    velocity = valid * decoder_out

    def pair_up(lefts, rights):
        feed, expanded, attended, projected = rights
        one, mixed, two, hidden = lefts
        return (
            ([one], projected),
            ([mixed], attended),
            ([two], expanded),
            ([hidden[g] for g in range(3)], feed),
        )

    grad_out = valid * cotangent
    decoder_flat, grad_modulation, *rights, gains_grad = kernel_backward(
        grad_out, decoder_kept, decoder_weights, context, "decoder_back"
    )
    factors = pair_up(decoder_left, rights)
    grad_act = dense_back(grad_modulation, modulate)
    unused_silu, silu_pull = jax.vjp(jax.nn.silu, decoder_pre)
    grad_latent = valid * silu_pull(grad_act)[0]
    offset_grad = jnp.sum(grad_modulation, axis=0, dtype=F32)
    extra = jnp.concatenate(
        [
            offset_grad.reshape(16, -1),
            gains_grad.reshape(2, 16, -1).swapaxes(0, 1).reshape(16, -1),
        ],
        axis=1,
    )
    first = ([shard_rows(decoder_act)], grad_modulation)
    decoder_block = ((first,) + factors, extra)

    encoder_flat, grad_modulation, *rights, gains_grad = kernel_backward(
        grad_latent, encoder_kept, encoder_weights, context, "encoder_back"
    )
    factors = pair_up(encoder_left, rights)
    grad_rows = lax.dot_general(
        picks.astype(BF16), grad_modulation, (((0,), (0,)), ((), ())), preferred_element_type=F32
    )
    grad_rows = grad_rows + lax.ppermute(grad_rows, "ctx", [(0, 1), (1, 0)])
    extra = gains_grad.reshape(2, 16, -1).swapaxes(0, 1).reshape(16, -1)
    results, all_rows = fast_reduce(
        (decoder_block, (factors, extra)), grad_rows.astype(BF16).reshape(16, -1), 2, "scatter"
    )
    (grads, small), (encoder_parts, encoder_small) = results
    decoder_grads = (
        grads[0],
        small[:offset_size],
        grads[1],
        small[offset_size:].reshape(2, -1),
        grads[2],
        grads[3],
        grads[4],
    )
    all_rows = all_rows.reshape(16 * segments, -1)
    modulate_grad = outer_sum(act_mine, all_rows)
    offset_grad = lax.dynamic_slice_in_dim(
        jnp.sum(all_rows.astype(F32), axis=0), me * offset_size, offset_size, 0
    )
    encoder_grads = (
        modulate_grad,
        offset_grad,
        encoder_parts[0],
        encoder_small.reshape(2, -1),
        encoder_parts[1],
        encoder_parts[2],
        encoder_parts[3],
    )
    return velocity, latent_full, decoder_flat + encoder_flat, encoder_grads, decoder_grads


def plain_gather(block):
    parts = [lax.all_gather(block[k], "dp", axis=0, tiled=True) for k in (0, 1, 2, 4, 5, 6)]
    gains = lax.all_gather(block[3], "dp", axis=1, tiled=True).astype(F32)
    modulate, offset, triple, mixing, expand, reduce_w = parts
    return modulate, offset.astype(F32), (triple, mixing, expand, reduce_w, gains)


def plain_reduce(factors, grad_modulation, gains_grad):
    def rows(values, dim=0):
        part = lax.psum_scatter(values, "dp", scatter_dimension=dim, tiled=True)
        return lax.psum(part.astype(BF16), "ctx").astype(F32)

    offset = rows(jnp.sum(grad_modulation, axis=0, dtype=F32))
    modulate, triple, mixing, expand, reduce_w = [rows(outer_sum(a, b)) for a, b in factors]
    return modulate, offset, triple, rows(gains_grad, 1), mixing, expand, reduce_w


def plain_step(flat, cotangent, context, segment_local, valid, timesteps, encoder, decoder):
    picks = (
        segment_local[..., None] == jnp.arange(timesteps.shape[-1], dtype=jnp.int32)
    ).astype(F32)
    times = jnp.sum(picks * timesteps[:, None, :].astype(F32), axis=-1)
    cond = embed_times(times, flat.shape[1]).reshape(flat.shape)
    modulate, offset, encoder_weights = plain_gather(encoder)
    encoder_act = jax.nn.silu(cond).astype(BF16)
    encoder_out, encoder_kept = block_forward(
        flat, dense(encoder_act, modulate) + offset, encoder_weights, context
    )
    latent_full = valid * encoder_out
    decoder_pre = latent_full + cond
    decoder_act = jax.nn.silu(decoder_pre).astype(BF16)
    modulate, offset, decoder_weights = plain_gather(decoder)
    decoder_out, decoder_kept = block_forward(
        flat, dense(decoder_act, modulate) + offset, decoder_weights, context
    )
    decoder_flat, grad_modulation, factors, gains_grad = block_backward(
        valid * cotangent, decoder_kept, decoder_weights, context
    )
    grad_act = dense_back(grad_modulation, modulate)
    decoder_grads = plain_reduce(
        ((decoder_act, grad_modulation),) + factors, grad_modulation, gains_grad
    )
    unused_silu, silu_pull = jax.vjp(jax.nn.silu, decoder_pre)
    encoder_flat, grad_modulation, factors, gains_grad = block_backward(
        valid * silu_pull(grad_act)[0], encoder_kept, encoder_weights, context
    )
    encoder_grads = plain_reduce(
        ((encoder_act, grad_modulation),) + factors, grad_modulation, gains_grad
    )
    return valid * decoder_out, latent_full, decoder_flat + encoder_flat, encoder_grads, decoder_grads


def local(fast, tokens, cotangent, segment, rows, columns, padding, timesteps, *weights):
    batch, half, width = tokens.shape
    start = lax.axis_index("ctx") * half
    segment_local = lax.dynamic_slice_in_dim(segment, start, half, 1)
    rows_local = lax.dynamic_slice_in_dim(rows, start, half, 1)
    columns_local = lax.dynamic_slice_in_dim(columns, start, half, 1)
    padding_local = lax.dynamic_slice_in_dim(padding, start, half, 1)
    place_query = start + jnp.arange(half, dtype=jnp.int32)
    place_key = jnp.arange(segment.shape[1], dtype=jnp.int32)
    allowed = (segment_local[:, :, None] == segment[:, None, :]) & (
        (padding[:, None, :] == 0) | (place_query[None, :, None] == place_key[None, None, :])
    )
    cosine, sine = rope_tables(rows_local.reshape(-1), columns_local.reshape(-1))
    context = (batch, half, allowed, cosine, sine)
    if fast:
        context = rope_lanes(cosine, sine)
        context += (segment_local.reshape(-1, 1), segment, padding)
    valid = (1 - padding_local).astype(F32).reshape(-1, 1)
    flat = tokens.reshape(-1, width).astype(F32)
    step = fast_step if fast else plain_step
    velocity, latent, token_grad, encoder_grads, decoder_grads = step(
        flat,
        cotangent.reshape(-1, width).astype(F32),
        context,
        segment_local,
        valid,
        timesteps,
        weights[:7],
        weights[7:],
    )
    return (
        velocity.astype(BF16).reshape(batch, half, width),
        latent.astype(BF16).reshape(batch, half, width),
        token_grad.reshape(batch, half, width),
        *encoder_grads,
        *decoder_grads,
    )


def solution(mesh):
    fast = dict(mesh.shape) == {"dp": math.prod(GRID), "ctx": 2}
    block = (
        P("dp", None),
        P("dp"),
        P("dp", None),
        P(None, "dp"),
        P("dp", None),
        P("dp", None),
        P("dp", None),
    )
    slots = P("dp", "ctx", None)
    return jax.shard_map(
        functools.partial(local, fast),
        mesh=mesh,
        in_specs=(slots, slots) + (P("dp", None),) * 5 + block + block,
        out_specs=(slots, slots, slots) + block + block,
        check_vma=False,
    )
```

```python
import functools
import math

import jax
import jax.numpy as jnp
from jax import lax
from jax.experimental import pallas as pl
from jax.experimental.pallas import tpu as pltpu
from jax.sharding import PartitionSpec as P

HEADS = 16
HD = 72
MESH = pl.DeviceIdType.MESH
GRID = (4, 2, 2)
BF16 = jnp.bfloat16
F32 = jnp.float32


def coords():
    dp = lax.axis_index("dp")
    return (lax.div(dp, 4), lax.rem(lax.div(dp, 2), 2), lax.rem(dp, 2), lax.axis_index("ctx"))


def device(z, y, x, c):
    return (z * 4 + y * 2 + x, c)


def when(cond, body):
    if cond is True:
        body()
    else:
        pl.when(cond)(body)


def greet():
    barrier = pltpu.get_barrier_semaphore()
    me = lax.axis_index("dp")
    c = lax.axis_index("ctx")
    for k in range(1, 16):
        pl.semaphore_signal(
            barrier, inc=1, device_id=(lax.rem(me + k, 16), c), device_id_type=MESH
        )
    pl.semaphore_signal(barrier, inc=1, device_id=(me, 1 - c), device_id_type=MESH)
    pl.semaphore_wait(barrier, 16)


class Exchange:
    def __init__(self, same, in_ref, out_ref, ssem, rsem, lsem):
        self.refs = (in_ref, out_ref, ssem, rsem, lsem)
        self.same = same
        self.me = lax.axis_index("dp")

    def source(self, target):
        return self.refs[0] if self.same else self.refs[0].at[target]

    def copy(self, k, target, slot):
        return pltpu.make_async_remote_copy(
            self.source(target),
            self.refs[1].at[slot],
            self.refs[2].at[k],
            self.refs[3].at[k],
            device_id=(target, lax.axis_index("ctx")),
            device_id_type=MESH,
        )

    def own(self):
        return pltpu.make_async_copy(
            self.source(self.me), self.refs[1].at[self.me], self.refs[4].at[0]
        )

    def start(self):
        for k in range(1, 16):
            self.copy(k, lax.rem(self.me + k, 16), self.me).start()
        self.own().start()

    def wait(self):
        self.own().wait()
        for k in range(1, 16):
            self.copy(k, lax.rem(self.me + k, 16), self.me).wait_send()
            origin = lax.rem(self.me + 16 - k, 16)
            self.copy(k, origin, origin).wait_recv()


class Sums:
    def __init__(self, in_ref, out_ref, box, total, ssem, rsem, lsem):
        self.refs = (in_ref, out_ref, box, total)
        self.sems = (ssem, rsem, lsem)
        self.z, self.y, self.x, self.c = coords()

    def remote(self, src, dst, k, target):
        return pltpu.make_async_remote_copy(
            src,
            dst,
            self.sems[0].at[k],
            self.sems[1].at[k],
            device_id=target,
            device_id_type=MESH,
        )

    def across(self, k):
        y = lax.rem(self.y + k // 2, 2)
        x = lax.rem(self.x + k % 2, 2)
        target = device(self.z, y, x, self.c)
        return self.remote(self.refs[0].at[:, y, x], self.refs[2].at[k], k, target)

    def own(self):
        return pltpu.make_async_copy(
            self.refs[0].at[:, self.y, self.x], self.refs[2].at[0], self.sems[2].at[0]
        )

    def along(self, k, arrival):
        there = lax.rem(self.z + (4 - k if arrival else k), 4)
        slot = there if arrival else self.z
        target = device(there, self.y, self.x, self.c)
        return self.remote(self.refs[3].at[there], self.refs[1].at[slot], 3 + k, target)

    def kept(self):
        return pltpu.make_async_copy(
            self.refs[3].at[self.z], self.refs[1].at[self.z], self.sems[2].at[1]
        )

    def start(self):
        for k in range(1, 4):
            self.across(k).start()
        self.own().start()

    def forward(self):
        self.own().wait()
        for k in range(1, 4):
            self.across(k).wait_recv()
        box = self.refs[2]
        self.refs[3][...] = (box[0] + box[1]) + (box[2] + box[3])
        for k in range(1, 4):
            self.along(k, False).start()
        self.kept().start()

    def wait(self):
        self.kept().wait()
        for k in range(1, 4):
            self.across(k).wait_send()
            self.along(k, False).wait_send()
            self.along(k, True).wait_recv()


class Broadcast:
    def __init__(self, in_ref, out_ref, ssem, rsem, lsem):
        self.refs = (in_ref, out_ref, ssem, rsem, lsem)
        self.z, self.y, self.x, self.c = coords()

    def own(self):
        return pltpu.make_async_copy(
            self.refs[0], self.refs[1].at[self.z, self.y, self.x], self.refs[4].at[0]
        )

    def along(self, k, arrival):
        there = lax.rem(self.z + (4 - k if arrival else k), 4)
        slot = there if arrival else self.z
        return pltpu.make_async_remote_copy(
            self.refs[0],
            self.refs[1].at[slot, self.y, self.x],
            self.refs[2].at[k],
            self.refs[3].at[k],
            device_id=device(there, self.y, self.x, self.c),
            device_id_type=MESH,
        )

    def across(self, k, arrival):
        y = lax.rem(self.y + k // 2, 2)
        x = lax.rem(self.x + k % 2, 2)
        block = self.refs[1].at[:, y, x] if arrival else self.refs[1].at[:, self.y, self.x]
        return pltpu.make_async_remote_copy(
            block,
            block,
            self.refs[2].at[3 + k],
            self.refs[3].at[3 + k],
            device_id=device(self.z, y, x, self.c),
            device_id_type=MESH,
        )

    def start(self):
        for k in range(1, 4):
            self.along(k, False).start()
        self.own().start()

    def forward(self):
        self.own().wait()
        for k in range(1, 4):
            self.along(k, True).wait_recv()
        for k in range(1, 4):
            self.across(k, False).start()

    def wait(self):
        for k in range(1, 4):
            self.along(k, False).wait_send()
            self.across(k, False).wait_send()
            self.across(k, True).wait_recv()


def gather_kernel(units, turns, count, *refs):
    w = refs[:count]
    o = refs[count + 1 : 2 * count + 1]
    ssem, rsem, lsem, csem, crsem, box, sums, es, er, el = refs[2 * count + 2 :]
    z, y, x, c = coords()
    greet()
    side = Sums(refs[count], refs[2 * count + 1], box, sums, es, er, el)
    side.start()
    up = device(z + 1, y, x, c)
    down = device(z - 1, y, x, c)
    partner = {"y": device(z, 1 - y, x, c), "x": device(z, y, 1 - x, c)}
    every = slice(None)

    def run(mine, other, order):
        def view(u, index):
            m, first, cols, _ = mine[u]
            return o[m].at[index[0], index[1], index[2], :, pl.ds(first, cols)]

        def copy(u, index, k, target, own=False):
            m, first, cols, _ = mine[u]
            dst = view(u, index)
            src = w[m].at[:, pl.ds(first, cols)] if own else dst
            return pltpu.make_async_remote_copy(
                src, dst, ssem.at[u, k], rsem.at[u, k], device_id=target, device_id_type=MESH
            )

        def local_copy(u):
            m, first, cols, _ = mine[u]
            return pltpu.make_async_copy(
                w[m].at[:, pl.ds(first, cols)], view(u, (z, y, x)), lsem.at[u]
            )

        def plan(u):
            held = {"z": False, "y": False, "x": False}

            def index(zz=z, flip=None):
                return (
                    every if held["z"] else zz,
                    every if held["y"] else (1 - y if flip == "y" else y),
                    every if held["x"] else (1 - x if flip == "x" else x),
                )

            steps = []
            pending = []
            sends = []
            own = True
            pair = 0
            for axis in mine[u][3]:
                if axis != "z":
                    send = [(True, functools.partial(copy, u, index(), pair, partner[axis], own))]
                    steps.append((pending, send))
                    sends += send
                    pending = [
                        (True, functools.partial(copy, u, index(flip=axis), pair, partner[axis]))
                    ]
                    pair += 1
                else:

                    def chain(shift, k, target, first=False):
                        return functools.partial(copy, u, index(zz=z + shift), k, target, first)

                    one = [(z < 3, chain(0, 2, up, own)), (z > 0, chain(0, 5, down, own))]
                    steps.append((pending, one))
                    middle = (z > 0) & (z < 3)
                    two = [(middle, chain(-1, 3, up)), (middle, chain(1, 6, down))]
                    steps.append(([(z > 0, chain(-1, 2, down)), (z < 3, chain(1, 5, up))], two))
                    three = [(z == 2, chain(-2, 4, up)), (z == 1, chain(2, 7, down))]
                    steps.append(([(z > 1, chain(-2, 3, down)), (z < 2, chain(2, 6, up))], three))
                    pending = [(z == 3, chain(-3, 4, down)), (z == 0, chain(3, 7, up))]
                    sends += one + two + three
                held[axis] = True
                own = False
            return steps, pending, sends

        plans = [plan(u) for u in range(len(mine))]

        def to_core(u, which):
            m, first, cols, _ = which[u]
            block = o[m].at[:, :, :, :, pl.ds(first, cols)]
            return pltpu.make_async_remote_copy(
                block,
                block,
                csem.at[u],
                crsem.at[u],
                device_id=device(z, y, x, 1 - c),
                device_id_type=MESH,
            )

        for u in range(len(mine)):
            local_copy(u).start()
        for at, (u, s) in enumerate(order):
            if at == FORWARD_AT:
                side.forward()
            steps, pending, _ = plans[u]
            if s == 1:
                local_copy(u).wait()
            for cond, make in steps[s][0] if s < 5 else pending:
                when(cond, lambda make=make: make().wait_recv())
            for cond, make in steps[s][1] if s < 5 else ():
                when(cond, lambda make=make: make().start())
            if s == 5:
                to_core(u, mine).start()
        for u in range(len(mine)):
            for cond, make in plans[u][2]:
                when(cond, lambda make=make: make().wait_send())
            to_core(u, mine).wait_send()
        for u in range(len(other)):
            to_core(u, other).wait_recv()

    pl.when(c == 0)(lambda: run(units[0], units[1], turns[0]))
    pl.when(c == 1)(lambda: run(units[1], units[0], turns[1]))
    side.wait()


ANY = pl.BlockSpec(memory_space=pl.ANY)
DMA = pltpu.SemaphoreType.DMA


SIDE = [DMA((16,)), DMA((16,)), DMA((1,))]


def gather(shards, rows, units, turns, collective_id, name):
    count = len(shards)
    most = max(len(units[0]), len(units[1]))
    shapes = [jax.ShapeDtypeStruct(GRID + s.shape, s.dtype) for s in shards]
    return pl.pallas_call(
        functools.partial(gather_kernel, units, turns, count),
        name=name,
        out_shape=shapes + [jax.ShapeDtypeStruct(GRID[:1] + rows.shape[3:], rows.dtype)],
        in_specs=[ANY] * (count + 1),
        out_specs=[ANY] * (count + 1),
        scratch_shapes=[
            DMA((most, 8)),
            DMA((most, 8)),
            DMA((most,)),
            DMA((most,)),
            DMA((most,)),
            pltpu.VMEM((4,) + GRID[:1] + rows.shape[3:], rows.dtype),
            pltpu.VMEM(GRID[:1] + rows.shape[3:], rows.dtype),
            DMA((7,)),
            DMA((7,)),
            DMA((2,)),
        ],
        compiler_params=pltpu.CompilerParams(collective_id=collective_id, has_side_effects=True),
    )(*shards, rows)


ORDERS = (
    ("zyx", "zxy", "xyz", "zxy", "zyx", "zxy", "zyx", "yxz", "zyx", "zxy"),
    ("zxy", "zyx", "yxz", "zyx", "zxy", "zyx", "zxy", "xyz", "zxy", "zyx"),
)
AFTER_Z = (0.6165, 0.4168, 0.3474, 1.6339, 4.4601)
AFTER_XY = (1.5672, 1.5028, 1.8589, 1.1737, 2.0677)
PER_TURN = 2.2835
FORWARD_AT = 40
SHIFT = 0.1931
SIZE = 4
TAIL = (0.1, 2)


def gather_units(shards):
    units = ([], [])
    load = [0, 0]
    whole = sum(s.size for s in shards) / (ROWS * 128)
    done = 0
    for m, shard in enumerate(shards):
        rows, columns = shard.shape
        tiles = columns // 128
        weight = rows / ROWS
        at = 0
        while at < tiles:
            size = SIZE if done < (1 - TAIL[0]) * whole else TAIL[1]
            step = max(1, round(size / weight))
            n = min(step, tiles - at)
            if 0 < tiles - at - n < max(1, round(size / weight / 2)):
                n = tiles - at
            core = 0 if load[0] <= load[1] else 1
            order = ORDERS[core][len(units[core]) % len(ORDERS[core])]
            units[core].append((m, at * 128, n * 128, order))
            load[core] += n * weight
            done += n * weight
            at += n
    turns = []
    for core in range(2):
        keys = []
        place = 0.0
        for u, (m, first, columns, order) in enumerate(units[core]):
            at = place / PER_TURN + core * SHIFT
            place += shards[m].shape[0] * columns / (ROWS * 128 * SIZE)
            keys.append((at, u, 0))
            for s, after in enumerate(AFTER_Z if order[0] == "z" else AFTER_XY):
                at += after
                keys.append((at, u, s + 1))
        turns.append(tuple((u, s) for _, u, s in sorted(keys)))
    return (tuple(units[0]), tuple(units[1])), tuple(turns)


def exchange_kernel(in_ref, out_ref, *sems):
    greet()
    side = Exchange(True, in_ref, out_ref, *sems)
    side.start()
    side.wait()


def exchange(values, collective_id, name):
    return pl.pallas_call(
        exchange_kernel,
        name=name,
        out_shape=jax.ShapeDtypeStruct((16,) + values.shape, values.dtype),
        in_specs=[ANY],
        out_specs=ANY,
        scratch_shapes=SIDE,
        compiler_params=pltpu.CompilerParams(collective_id=collective_id, has_side_effects=True),
    )(values)


LAG = (0, 2, 3, 4, 5, 6)
RECV_SLOTS = 9
SEND_SLOTS = 8
FIRST_SLOTS = 4
UNIT = 384
ROWS = 72
PADDED = 80


def scatter_kernel(first, cols, source, dy_count, *refs):
    nv = len(first) - 1
    xt = refs[:nv]
    dy = refs[nv : nv + dy_count]
    out = refs[nv + dy_count + 1]
    (
        xts, dys, a_s1, a_s2, a_t, a_su, a_sd, e_s1, e_t, e_su, e_sd, e_sq,
        a_b1, a_b2, a_bu, a_bd, e_b1, e_bu, e_bd, e_bq, outs,
        ssem, rsem, xl, xs, xr, yl, ys, yr, ol, os, orr, es, er, el,
    ) = refs[nv + dy_count + 3 :]
    z, y, x, c = coords()
    total = first[-1] // 2
    sibling = device(z, y, x, 1 - c)
    up = device(z + 1, y, x, c)
    down = device(z - 1, y, x, c)
    greet()
    side = Broadcast(refs[nv + dy_count], refs[nv + dy_count + 2], es, er, el)
    lanes = pl.ds(pl.multiple_of(c * 128, 128), 128)
    offsets = []
    at = 0
    for k in range(dy_count):
        offsets.append(at)
        at += dy[k].shape[1]

    def remote(src, dst, send, recv, target):
        return pltpu.make_async_remote_copy(
            src, dst, send, recv, device_id=target, device_id_type=MESH
        )

    def x_views(v):
        return xt[v], xts.at[v, :, :, lanes]

    def x_local(v):
        return pltpu.make_async_copy(*x_views(v), xl.at[v])

    def x_remote(v):
        return remote(*x_views(v), xs.at[v], xr.at[v], sibling)

    def y_views(k):
        return dy[k], dys.at[lanes, pl.ds(offsets[k], dy[k].shape[1])]

    def y_local(k):
        return pltpu.make_async_copy(*y_views(k), yl.at[k])

    def y_remote(k):
        return remote(*y_views(k), ys.at[k], yr.at[k], sibling)

    fresh = [source[v] not in source[:v] for v in range(nv)]

    def bring(v):
        x_local(v).start()
        x_remote(v).start()
        if fresh[v]:
            y_local(source[v]).start()
            y_remote(source[v]).start()

    bring(0)
    bring(1)
    side.start()

    def arrive(tick):
        for v in range(nv):

            def wait(v=v):
                x_local(v).wait()
                x_remote(v).wait_recv()
                if fresh[v]:
                    y_local(source[v]).wait()
                    y_remote(source[v]).wait_recv()
                if v + 2 < nv:
                    bring(v + 2)

            pl.when(tick == (first[v] - c + 1) // 2)(wait)

    def unit(i):
        j = 2 * i + c
        v = jnp.int32(0)
        col = j * UNIT
        for k in range(1, nv):
            past = (j >= first[k]).astype(jnp.int32)
            v = v + past
            col = col + past * ((cols[k] - first[k] * UNIT) - (cols[k - 1] - first[k - 1] * UNIT))
        return v, pl.multiple_of(col, 128)

    def axes(i):
        o = lax.rem(i, 2)
        pb = x * (1 - o) + y * o
        qb = y * (1 - o) + x * o
        dp = z * 4 + y * 2 + x
        return o, pb, qb, (dp + (1 - 2 * pb) * (1 + o), c), (dp + (1 - 2 * qb) * (2 - o), c)

    def slots(i):
        return lax.rem(i, FIRST_SLOTS), lax.rem(i, SEND_SLOTS), lax.rem(i, RECV_SLOTS)

    def send(src, dst, i, k, target):
        return remote(
            src, dst, ssem.at[lax.rem(i, SEND_SLOTS), k], rsem.at[lax.rem(i, RECV_SLOTS), k], target
        )

    def first_copies(i):
        o, pb, qb, pn, qn = axes(i)
        f, s, w = slots(i)
        return [send(a_s1.at[f], a_b1.at[w], i, 0, pn), send(e_s1.at[f], e_b1.at[w], i, 8, pn)]

    def second_copy(i):
        o, pb, qb, pn, qn = axes(i)
        f, s, w = slots(i)
        return send(a_s2.at[s], a_b2.at[w], i, 1, qn)

    def last_copy(i):
        o, pb, qb, pn, qn = axes(i)
        f, s, w = slots(i)
        return send(e_sq.at[s], e_bq.at[w], i, 9, qn)

    def up_copy(i, k, e):
        f, s, w = slots(i)
        src, dst, n = (e_su, e_bu, 10) if e else (a_su, a_bu, 2)
        return send(src.at[s, k], dst.at[w, k], i, n + k, up)

    def down_copy(i, k, e):
        f, s, w = slots(i)
        src, dst, n = (e_sd, e_bd, 13) if e else (a_sd, a_bd, 5)
        return send(src.at[s, k], dst.at[w, k], i, n + k, down)

    def up_sends(k):
        return (z <= k) & (z < 3)

    def down_sends(k):
        return (3 - z <= k) & (z > 0)

    def up_comes(k):
        return (z >= 1) & (z <= k + 1)

    def down_comes(k):
        return (z <= 2) & (3 - z <= k + 1)

    def kept(i, e, d):
        f, s, w = slots(i)
        if e:
            return e_t.at[s, d]
        return a_t.at[s, d, axes(i)[2]]

    def z_send(i, k, e):
        f, s, w = slots(i)

        def pass_on(dest, stage, box, inner, copy):
            value = kept(i, e, dest)[...]
            if k == 0:
                stage[s, k] = value.astype(BF16)
            else:

                def add():
                    stage[s, k] = (value + box[w, k - 1].astype(F32)).astype(BF16)

                def begin():
                    stage[s, k] = value.astype(BF16)

                pl.when(inner)(add)
                pl.when(jnp.logical_not(inner))(begin)
            copy.start()

        pl.when(up_sends(k))(
            lambda: pass_on(
                z + 3 - k, e_su if e else a_su, e_bu if e else a_bu, z > 0, up_copy(i, k, e)
            )
        )
        pl.when(down_sends(k))(
            lambda: pass_on(
                z + k - 3, e_sd if e else a_sd, e_bd if e else a_bd, z < 3, down_copy(i, k, e)
            )
        )

    def z_wait(i, k, e):
        pl.when(up_comes(k))(lambda: up_copy(i, k, e).wait_recv())
        pl.when(down_comes(k))(lambda: down_copy(i, k, e).wait_recv())

    def z_close(i, e):
        f, s, w = slots(i)
        mine = kept(i, e, z)

        def below():
            mine[...] = mine[...] + (e_bu if e else a_bu)[w, 2].astype(F32)

        def above():
            mine[...] = mine[...] + (e_bd if e else a_bd)[w, 2].astype(F32)

        pl.when(z > 0)(below)
        pl.when(z < 3)(above)
        return mine

    def product(i, bit):
        v, col = unit(i)
        o = axes(i)[0]
        chips = [4 * k + bit * (1 + o) + q * (2 - o) for k in range(4) for q in range(2)]
        lhs = jnp.concatenate([xts[v, chip] for chip in chips], axis=0)
        whole = jnp.dot(lhs, dys[:, pl.ds(col, UNIT)], preferred_element_type=F32)
        return whole.reshape(8, PADDED, UNIT)[:, :ROWS]

    def stage0(i):
        f, s, w = slots(i)
        part = product(i, 1 - axes(i)[1])
        a_s1[f] = part[:, :, :128].astype(BF16).reshape(4, 2, ROWS, 128)
        e_s1[f] = part[:, :, 128:].astype(BF16).reshape(4, 2, ROWS, 256)
        for copy in first_copies(i):
            copy.start()

    def stage1(i):
        f, s, w = slots(i)
        o, pb, qb, pn, qn = axes(i)
        part = product(i, pb)
        for copy in first_copies(i):
            copy.wait_recv()
        a_t[s] = part[:, :, :128].reshape(4, 2, ROWS, 128) + a_b1[w].astype(F32)
        a_s2[s] = a_t[s, :, 1 - qb].astype(BF16)
        second_copy(i).start()
        e_t[s] = part[:, :, 128:].reshape(4, 2, ROWS, 256) + e_b1[w].astype(F32)
        z_send(i, 0, True)

    def a_second(i):
        f, s, w = slots(i)
        qb = axes(i)[2]
        second_copy(i).wait_recv()
        a_t[s, :, qb] = a_t[s, :, qb] + a_b2[w].astype(F32)
        z_send(i, 0, False)

    def z_step(i, k, e):
        z_wait(i, k - 1, e)
        z_send(i, k, e)

    def e_fourth(i):
        f, s, w = slots(i)
        z_wait(i, 2, True)
        z_close(i, True)
        e_sq[s] = e_t[s, z, 1 - axes(i)[2]].astype(BF16)
        last_copy(i).start()

    def out_view(i):
        return out.at[:, pl.ds(pl.multiple_of((2 * i + c) * UNIT, 128), UNIT)]

    def a_fifth(i):
        z_wait(i, 2, False)
        outs[i, :, :128] = z_close(i, False)[...]

    def e_fifth(i):
        f, s, w = slots(i)
        last_copy(i).wait_recv()
        outs[i, :, 128:] = e_t[s, z, axes(i)[2]] + e_bq[w].astype(F32)
        pltpu.make_async_copy(outs.at[i], out_view(i), ol.at[0]).start()
        remote(outs.at[i], out_view(i), os.at[0], orr.at[0], sibling).start()

    def first_sent(i):
        for copy in first_copies(i):
            copy.wait_send()

    def sent(i):
        second_copy(i).wait_send()
        last_copy(i).wait_send()
        for e in (False, True):
            for k in range(3):
                pl.when(up_sends(k))(lambda k=k, e=e: up_copy(i, k, e).wait_send())
                pl.when(down_sends(k))(lambda k=k, e=e: down_copy(i, k, e).wait_send())

    stages = (
        (a_fifth, LAG[5]),
        (functools.partial(z_step, k=1, e=False), LAG[3]),
        (functools.partial(z_step, k=2, e=True), LAG[3]),
        (e_fourth, LAG[4]),
        (stage0, LAG[0]),
        (functools.partial(z_step, k=1, e=True), LAG[2]),
        (a_second, LAG[2]),
        (functools.partial(z_step, k=2, e=False), LAG[4]),
        (e_fifth, LAG[5]),
        (stage1, LAG[1]),
    )

    def tick(t, carry):
        arrive(t)
        pl.when(t == 4)(side.forward)
        pl.when((t >= SEND_SLOTS) & (t - SEND_SLOTS < total))(lambda: sent(t - SEND_SLOTS))
        pl.when((t >= FIRST_SLOTS) & (t - FIRST_SLOTS < total))(lambda: first_sent(t - FIRST_SLOTS))
        for stage, lag in stages:
            i = t - lag
            pl.when((i >= 0) & (i < total))(functools.partial(stage, i))
        return carry

    lax.fori_loop(0, total + SEND_SLOTS, tick, 0)
    for v in range(nv):
        x_remote(v).wait_send()
    for k in range(dy_count):
        y_remote(k).wait_send()
    half = out.at[:, pl.ds(0, total * UNIT)]
    pltpu.make_async_copy(half, half, ol.at[0]).wait()
    everything = remote(half, half, os.at[0], orr.at[0], sibling)
    everything.wait_send()
    everything.wait_recv()
    side.wait()


def scatter(xts, dys, source, rows, collective_id, name):
    nv = len(xts)
    starts = []
    width = 0
    for d in dys:
        starts.append(width)
        width += d.shape[1]
    first = [0]
    cols = []
    for v in range(nv):
        cols.append(starts[source[v]])
        first.append(first[-1] + dys[source[v]].shape[1] // UNIT)
    total = first[-1] // 2
    s, f, r = SEND_SLOTS, FIRST_SLOTS, RECV_SLOTS
    vmem = pltpu.VMEM
    return pl.pallas_call(
        functools.partial(scatter_kernel, tuple(first), tuple(cols), tuple(source), len(dys)),
        name=name,
        out_shape=[
            jax.ShapeDtypeStruct((ROWS, first[-1] * UNIT), F32),
            jax.ShapeDtypeStruct(GRID + rows.shape, rows.dtype),
        ],
        in_specs=[ANY] * (nv + len(dys) + 1),
        out_specs=[ANY] * 2,
        scratch_shapes=[
            vmem((nv, 16, PADDED, 256), BF16),
            vmem((256, width), BF16),
            vmem((f, 4, 2, ROWS, 128), BF16),
            vmem((s, 4, ROWS, 128), BF16),
            vmem((s, 4, 2, ROWS, 128), F32),
            vmem((s, 3, ROWS, 128), BF16),
            vmem((s, 3, ROWS, 128), BF16),
            vmem((f, 4, 2, ROWS, 256), BF16),
            vmem((s, 4, 2, ROWS, 256), F32),
            vmem((s, 3, 2, ROWS, 256), BF16),
            vmem((s, 3, 2, ROWS, 256), BF16),
            vmem((s, ROWS, 256), BF16),
            vmem((r, 4, 2, ROWS, 128), BF16),
            vmem((r, 4, ROWS, 128), BF16),
            vmem((r, 3, ROWS, 128), BF16),
            vmem((r, 3, ROWS, 128), BF16),
            vmem((r, 4, 2, ROWS, 256), BF16),
            vmem((r, 3, 2, ROWS, 256), BF16),
            vmem((r, 3, 2, ROWS, 256), BF16),
            vmem((r, ROWS, 256), BF16),
            vmem((total, ROWS, UNIT), F32),
            DMA((s, 16)),
            DMA((r, 16)),
            DMA((nv,)),
            DMA((nv,)),
            DMA((nv,)),
            DMA((len(dys),)),
            DMA((len(dys),)),
            DMA((len(dys),)),
            DMA((1,)),
            DMA((1,)),
            DMA((1,)),
        ]
        + SIDE,
        compiler_params=pltpu.CompilerParams(
            collective_id=collective_id, has_side_effects=True, vmem_limit_bytes=62 * 1024 * 1024
        ),
    )(*xts, *dys, rows)


def layer_norm(values):
    center = values - jnp.mean(values, axis=-1, keepdims=True)
    spread = jnp.mean(center * center, axis=-1, keepdims=True)
    return center * lax.rsqrt(spread + 1e-06)


def head_norm(values, gain):
    shaped = values.reshape(values.shape[:-1] + (HEADS, HD))
    scaled = shaped * lax.rsqrt(jnp.mean(shaped * shaped, axis=-1, keepdims=True) + 1e-06)
    return scaled * gain.reshape(HEADS, HD)


def rope_tables(rows, columns):
    quarter = HD // 4
    freqs = jnp.exp(jnp.arange(quarter, dtype=F32) * (-math.log(10000.0) / quarter))
    places = jnp.stack([rows, columns], axis=-1).astype(F32)
    angles = places[..., None] * freqs
    return (jnp.cos(angles), jnp.sin(angles))


def rotate(values, cosine, sine):
    shaped = values.reshape(values.shape[:-1] + (2, 2, HD // 4))
    first = shaped[..., 0, :]
    second = shaped[..., 1, :]
    cosine = cosine[..., None, :, :]
    sine = sine[..., None, :, :]
    turned = jnp.stack([first * cosine - second * sine, first * sine + second * cosine], axis=-2)
    return turned.reshape(values.shape)


def embed_times(times, width):
    half_width = width // 2
    freqs = jnp.exp(jnp.arange(half_width, dtype=F32) * (-math.log(10000.0) / half_width))
    angles = times[..., None] * freqs
    return jnp.concatenate([jnp.cos(angles), jnp.sin(angles)], axis=-1)


def qk_prepare(query_raw, key_raw, gains, cosine, sine):
    return (
        rotate(head_norm(query_raw, gains[0]), cosine, sine),
        rotate(head_norm(key_raw, gains[1]), cosine, sine),
    )


def swish_product(gate, up):
    return jax.nn.silu(gate) * up


def attention_scores(queries, keys, allowed):
    scores = jnp.einsum("sqhd,skhd->shqk", queries, keys, preferred_element_type=F32) * (
        1.0 / math.sqrt(HD)
    )
    return jnp.where(allowed[:, None], scores, -1e30)


def dense(values, weight):
    return jnp.dot(values, weight, preferred_element_type=F32)


def dense_back(grads, weight):
    return lax.dot_general(grads, weight, (((1,), (1,)), ((), ())), preferred_element_type=F32)


def outer_sum(values, grads):
    return lax.dot_general(values, grads, (((0,), (0,)), ((), ())), preferred_element_type=F32)


def block_forward(flat, modulation, weights, context):
    batch, half, allowed, cosine, sine = context
    triple, mixing, expand, reduce_w, gains = weights
    width = flat.shape[1]
    shift1, scale1, gate1, shift2, scale2, gate2 = jnp.split(modulation, 6, axis=1)
    lifted1 = (layer_norm(flat) * (1.0 + scale1) + shift1).astype(BF16)
    projected = dense(lifted1, triple)
    query_raw, key_raw, value_raw = jnp.split(projected, 3, axis=1)
    queries, keys = qk_prepare(query_raw, key_raw, gains, cosine, sine)
    queries = queries.astype(BF16).reshape(batch, half, HEADS, HD)
    keys_local = keys.astype(BF16).reshape(batch, half, width)
    values_local = value_raw.astype(BF16).reshape(batch, half, width)
    key_heads = lax.all_gather(keys_local, "ctx", axis=1, tiled=True).reshape(batch, -1, HEADS, HD)
    value_heads = lax.all_gather(values_local, "ctx", axis=1, tiled=True)
    value_heads = value_heads.reshape(batch, -1, HEADS, HD)
    scores = attention_scores(queries, key_heads, allowed)
    top = jnp.max(scores, axis=-1, keepdims=True)
    raised = jnp.exp(scores - top)
    total = jnp.sum(raised, axis=-1, keepdims=True)
    softmax_low = (raised / total).astype(BF16)
    logsum = top + jnp.log(total)
    mixed = jnp.einsum("shqk,skhd->sqhd", softmax_low, value_heads, preferred_element_type=F32)
    mixed_low = mixed.reshape(-1, width).astype(BF16)
    attended = dense(mixed_low, mixing)
    resid = flat + gate1 * attended
    lifted2 = (layer_norm(resid) * (1.0 + scale2) + shift2).astype(BF16)
    expanded = dense(lifted2, expand)
    gate, up = jnp.split(expanded, 2, axis=1)
    hidden = swish_product(gate, up).astype(BF16)
    feed = dense(hidden, reduce_w)
    output = resid + gate2 * feed
    kept = (
        modulation,
        flat,
        lifted1,
        query_raw,
        key_raw,
        queries,
        key_heads,
        value_heads,
        logsum,
        mixed_low,
        attended,
        resid,
        lifted2,
        expanded,
        hidden,
        feed,
    )
    return (output, kept)


def block_backward(grad_out, kept, weights, context):
    batch, half, allowed, cosine, sine = context
    triple, mixing, expand, reduce_w, gains = weights
    (
        modulation,
        flat,
        lifted1,
        query_raw,
        key_raw,
        queries,
        key_heads,
        value_heads,
        logsum,
        mixed_low,
        attended,
        resid,
        lifted2,
        expanded,
        hidden,
        feed,
    ) = kept
    width = flat.shape[1]
    shift1, scale1, gate1, shift2, scale2, gate2 = jnp.split(modulation, 6, axis=1)
    grad_feed = (grad_out * gate2).astype(BF16)
    grad_hidden = dense_back(grad_feed, reduce_w)
    gate, up = jnp.split(expanded, 2, axis=1)
    unused_out, swish_pull = jax.vjp(swish_product, gate, up)
    grad_gate, grad_up = swish_pull(grad_hidden)
    grad_expanded = jnp.concatenate([grad_gate, grad_up], axis=1).astype(BF16)
    grad_lifted2 = dense_back(grad_expanded, expand)
    normed_second, second_pull = jax.vjp(layer_norm, resid)
    grad_resid = grad_out + second_pull(grad_lifted2 * (1.0 + scale2))[0]
    grad_attended = (grad_resid * gate1).astype(BF16)
    grad_mixed = dense_back(grad_attended, mixing).astype(BF16).reshape(batch, half, HEADS, HD)
    scores = attention_scores(queries, key_heads, allowed)
    chances = jnp.exp(scores - logsum)
    grad_chances = jnp.einsum(
        "sqhd,skhd->shqk", grad_mixed, value_heads, preferred_element_type=F32
    )
    grad_values = jnp.einsum(
        "shqk,sqhd->skhd", chances.astype(BF16), grad_mixed, preferred_element_type=F32
    )
    grad_scores = (
        chances * (grad_chances - jnp.sum(chances * grad_chances, axis=-1, keepdims=True))
    ).astype(BF16)
    scale = 1.0 / math.sqrt(HD)
    grad_queries = (
        jnp.einsum("shqk,skhd->sqhd", grad_scores, key_heads, preferred_element_type=F32) * scale
    )
    grad_keys = (
        jnp.einsum("shqk,sqhd->skhd", grad_scores, queries, preferred_element_type=F32) * scale
    )
    pair = jnp.stack(
        [grad_keys.reshape(batch, -1, width), grad_values.reshape(batch, -1, width)]
    ).astype(BF16)
    place = lax.axis_index("ctx")
    theirs = lax.dynamic_slice_in_dim(pair, (1 - place) * half, half, 2)
    theirs = lax.ppermute(theirs, "ctx", [(0, 1), (1, 0)])
    mine = lax.dynamic_slice_in_dim(pair, place * half, half, 2)
    pair = mine.astype(F32) + theirs.astype(F32)
    grad_keys, grad_values = pair[0], pair[1]

    def prepare(query_in, key_in, gain_in):
        return qk_prepare(query_in, key_in, gain_in, cosine, sine)

    unused_pair, prepare_pull = jax.vjp(prepare, query_raw, key_raw, gains)
    grad_query_raw, grad_key_raw, gains_grad = prepare_pull(
        (grad_queries.reshape(-1, HEADS, HD), grad_keys.reshape(-1, HEADS, HD))
    )
    grad_projected = jnp.concatenate(
        [grad_query_raw, grad_key_raw, grad_values.reshape(-1, width)], axis=1
    ).astype(BF16)
    grad_lifted1 = dense_back(grad_projected, triple)
    normed_first, first_pull = jax.vjp(layer_norm, flat)
    grad_flat = grad_resid + first_pull(grad_lifted1 * (1.0 + scale1))[0]
    grad_modulation = jnp.concatenate(
        [
            grad_lifted1,
            grad_lifted1 * normed_first,
            grad_resid * attended,
            grad_lifted2,
            grad_lifted2 * normed_second,
            grad_out * feed,
        ],
        axis=1,
    ).astype(BF16)
    factors = (
        (lifted1, grad_projected),
        (mixed_low, grad_attended),
        (lifted2, grad_expanded),
        (hidden, grad_feed),
    )
    return (grad_flat, grad_modulation, factors, gains_grad)


def meet_sibling():
    barrier = pltpu.get_barrier_semaphore()
    sibling = (lax.axis_index("dp"), 1 - lax.axis_index("ctx"))
    pl.semaphore_signal(barrier, inc=1, device_id=sibling, device_id_type=MESH)
    pl.semaphore_wait(barrier, 1)
    return sibling


def head_sum_matrix(width):
    channel = lax.broadcasted_iota(jnp.int32, (width, 128), 0)
    head = lax.broadcasted_iota(jnp.int32, (width, 128), 1)
    inside = (channel >= head * HD) & (channel < (head + 1) * HD)
    return jnp.where(inside, 1.0, 0.0).astype(F32)


def exact_dot(left, right):
    return jnp.dot(left, right, preferred_element_type=F32, precision=lax.Precision.HIGHEST)


def spread_heads(values, heads):
    return lax.dot_general(
        values,
        heads,
        (((1,), (1,)), ((), ())),
        preferred_element_type=F32,
        precision=lax.Precision.HIGHEST,
    )


def swap_pairs(values):
    width = values.shape[1]
    lane = lax.broadcasted_iota(jnp.int32, values.shape, 1)
    quarter = HD // 4
    early = lax.rem(lane, 2 * quarter) < quarter
    return jnp.where(
        early, pltpu.roll(values, width - quarter, 1), pltpu.roll(values, quarter, 1)
    )


def normalize(values):
    mean = jnp.mean(values, axis=1, keepdims=True)
    center = values - mean
    spread = jnp.mean(center * center, axis=1, keepdims=True)
    inverse = lax.rsqrt(spread + 1e-06)
    return center * inverse, inverse


def norm_back(normed, inverse, grad):
    mean = jnp.mean(grad, axis=1, keepdims=True)
    along = jnp.mean(grad * normed, axis=1, keepdims=True)
    return (grad - mean - normed * along) * inverse


def window(h, width):
    first = min((h * HD) // 128 * 128, width - 256)
    return first, h * HD - first


def head_mask(h, width, rows):
    first, at = window(h, width)
    lane = lax.broadcasted_iota(jnp.int32, (rows, 256), 1)
    return (lane >= at) & (lane < at + HD)


def turned(values):
    tokens, width = values.shape
    rows = values.T.reshape(-1, ROWS, tokens)
    return jnp.concatenate(
        [rows, jnp.zeros((width // ROWS, PADDED - ROWS, tokens), F32)], axis=1
    ).astype(BF16)


FF_TILE = 768
KV_TILE = 1152


def allowed_mask(seg_q, seg_k, pad_k, half):
    place_q = lax.axis_index("ctx") * half + lax.broadcasted_iota(jnp.int32, (half, 2 * half), 0)
    place_k = lax.broadcasted_iota(jnp.int32, (half, 2 * half), 1)
    return (seg_q[...] == seg_k[...]) & ((pad_k[...] == 0) | (place_q == place_k))


class Traffic:
    def __init__(self, held, sources, targets, lsem, ssem):
        self.held = held
        names = [n for n in sources]
        self.loads = {
            n: pltpu.make_async_copy(sources[n], held[n], lsem.at[k]) for k, n in enumerate(names)
        }
        self.sources = sources
        self.tiles = {}
        self.stores = {
            n: pltpu.make_async_copy(held[n], targets[n], ssem.at[k])
            for k, n in enumerate(targets)
        }
        self.waiting = set(names)

    def __getattr__(self, name):
        return self.held[name]

    def fetch(self, *names):
        for n in names:
            if n in self.loads:
                self.loads[n].start()

    def fetch_tile(self, t, size, rows, columns, sem):
        spans = [(n, (pl.ds(t * size, size), slice(None))) for n in rows]
        for n in columns:
            for first in (0, self.held[n].shape[1] // 2):
                spans.append((n, (slice(None), pl.ds(first + t * size, size))))
        self.tiles[t] = [
            pltpu.make_async_copy(self.sources[n].at[at], self.held[n].at[at], sem.at[t, k])
            for k, (n, at) in enumerate(spans)
        ]
        for copy in self.tiles[t]:
            copy.start()
        self.waiting.difference_update(rows + columns)

    def need_tile(self, t):
        for copy in self.tiles.pop(t, ()):
            copy.wait()

    def need(self, *names):
        for n in names:
            if n in self.waiting:
                self.loads[n].wait()
                self.waiting.discard(n)

    def emit(self, *names):
        for n in names:
            if n in self.stores:
                self.stores[n].start()

    def close(self):
        for store in self.stores.values():
            store.wait()


def forward_body(r, sibling, ssem, rsem):
    half, width = r.flat.shape
    c = lax.axis_index("ctx")
    mine = pl.ds(pl.multiple_of(c * half, 128), half)
    theirs = pl.ds(pl.multiple_of((1 - c) * half, 128), half)
    hidden_size = r.reduce.shape[0]

    def part(k):
        return r.mod[:, k * width : (k + 1) * width]

    r.need("flat", "mod")
    normed, unused = normalize(r.flat[...])
    lifted_low = (normed * (1.0 + part(1)) + part(0)).astype(BF16)
    r.need("triple")
    r.fetch("mixing", "expand", "reduce")
    heads = head_sum_matrix(width)

    def prepared(k):
        values = r.raw[:, k * width : (k + 1) * width]
        mean = exact_dot(values * values, heads) * (1.0 / HD)
        scaled = values * spread_heads(lax.rsqrt(mean + 1e-06), heads) * r.gains[k : k + 1, :]
        return scaled * r.cosine[...] + swap_pairs(scaled) * r.sine[...]

    def project(k):
        return jnp.dot(
            lifted_low, r.triple[:, k * width : (k + 1) * width], preferred_element_type=F32
        )

    r.raw[:, width:] = project(1)
    r.need("gains", "cosine", "sine")
    r.kv[0, mine] = prepared(1).astype(BF16)
    r.kv[1, mine] = project(2).astype(BF16)
    share = pltpu.make_async_remote_copy(
        r.kv.at[:, mine], r.kv.at[:, mine], ssem.at[0], rsem.at[0], device_id=sibling,
        device_id_type=MESH,
    )
    share.start()
    r.raw[:, :width] = project(0)
    r.emit("raw")
    r.queries[...] = prepared(0).astype(BF16)
    r.emit("queries")
    r.xt1[...] = turned(lifted_low.astype(F32))
    r.emit("xt1")
    r.need("seg_q", "seg_k", "pad_k")
    allowed = allowed_mask(r.seg_q, r.seg_k, r.pad_k, half)
    r.lift[...] = jnp.zeros_like(r.lift)
    lane = lax.broadcasted_iota(jnp.int32, (half, 128), 1)
    sums = jnp.zeros((half, 128), F32)
    pltpu.make_async_remote_copy(
        r.kv.at[:, theirs], r.kv.at[:, theirs], ssem.at[0], rsem.at[0], device_id=sibling,
        device_id_type=MESH,
    ).wait_recv()
    r.emit("kv")
    for h in range(width // HD):
        first, unused = window(h, width)
        span = slice(first, first + 256)
        mask = head_mask(h, width, half)
        query = jnp.where(mask, r.queries[:, span].astype(F32), 0.0).astype(BF16)
        scores = dense_back(query, r.kv[0, :, span]) * (1.0 / math.sqrt(HD))
        scores = jnp.where(allowed, scores, -1e30)
        top = jnp.max(scores, axis=1, keepdims=True)
        raised = jnp.exp(scores - top)
        total = jnp.sum(raised, axis=1, keepdims=True)
        low = (raised / total).astype(BF16)
        out = jnp.dot(low, r.kv[1, :, span], preferred_element_type=F32)
        r.lift[:, span] = r.lift[:, span] + jnp.where(mask, out, 0.0)
        sums = jnp.where(lane == h, top + jnp.log(total), sums)
    r.lse[...] = sums
    r.emit("lse")
    mixed_low = r.lift[...].astype(BF16)
    r.xtm[...] = turned(mixed_low.astype(F32))
    r.emit("xtm")
    r.need("mixing")
    r.attended[...] = jnp.dot(mixed_low, r.mixing[...], preferred_element_type=F32)
    r.emit("attended")
    r.resid[...] = r.flat[...] + part(2) * r.attended[...]
    r.emit("resid")
    normed, unused = normalize(r.resid[...])
    lifted_low = (normed * (1.0 + part(4)) + part(3)).astype(BF16)
    r.xt2[...] = turned(lifted_low.astype(F32))
    r.emit("xt2")
    r.feed[...] = jnp.zeros_like(r.feed)
    r.need("expand", "reduce")
    xth = (r.xth0, r.xth1, r.xth2)
    for g in range(3):
        xth[g][...] = jnp.zeros_like(xth[g])
    for t in range(hidden_size // FF_TILE):
        one = slice(t * FF_TILE, (t + 1) * FF_TILE)
        two = slice(hidden_size + t * FF_TILE, hidden_size + (t + 1) * FF_TILE)
        gate = jnp.dot(lifted_low, r.expand[:, one], preferred_element_type=F32)
        up = jnp.dot(lifted_low, r.expand[:, two], preferred_element_type=F32)
        r.expanded[:, one] = gate
        r.expanded[:, two] = up
        hidden = (gate * jax.nn.sigmoid(gate) * up).astype(BF16)
        pieces = hidden.astype(F32).T.astype(BF16).reshape(FF_TILE // 192, 3, 64, half)
        for g in range(3):
            xth[g][t * (FF_TILE // 192) : (t + 1) * (FF_TILE // 192), :64] = pieces[:, g]
        r.feed[...] = r.feed[...] + jnp.dot(hidden, r.reduce[one], preferred_element_type=F32)
    r.emit("expanded", "feed", "xth0", "xth1", "xth2")
    r.output[...] = r.resid[...] + part(5) * r.feed[...]
    r.emit("output")
    share.wait_send()


def backward_body(r, sibling, ssem, rsem):
    half, width = r.flat.shape
    c = lax.axis_index("ctx")
    mine = pl.ds(pl.multiple_of(c * half, 128), half)
    theirs = pl.ds(pl.multiple_of((1 - c) * half, 128), half)
    hidden_size = r.reduce.shape[0]

    def part(k):
        return r.mod[:, k * width : (k + 1) * width]

    def keep(k, values):
        r.grad_mod[:, k * width : (k + 1) * width] = values.astype(BF16)

    r.need("grad_out", "feed", "mod")
    keep(5, r.grad_out[...] * r.feed[...])
    feed_low = (r.grad_out[...] * part(5)).astype(BF16)
    r.grad_feed[...] = feed_low
    r.emit("grad_feed")
    r.lift[...] = jnp.zeros_like(r.lift)
    for t in range(hidden_size // FF_TILE):
        r.need_tile(t)
        if t == 1:
            r.fetch("attended", "resid", "mixing", "queries", "kv", "lse", "raw", "flat", "triple")
        one = slice(t * FF_TILE, (t + 1) * FF_TILE)
        two = slice(hidden_size + t * FF_TILE, hidden_size + (t + 1) * FF_TILE)
        grad_hidden = dense_back(feed_low, r.reduce[one])
        gate = r.expanded[:, one]
        up = r.expanded[:, two]
        sig = jax.nn.sigmoid(gate)
        grad_gate = (grad_hidden * up * (sig * (1.0 + gate * (1.0 - sig)))).astype(BF16)
        grad_up = (grad_hidden * (gate * sig)).astype(BF16)
        r.grad_expanded[:, one] = grad_gate
        r.grad_expanded[:, two] = grad_up
        r.lift[...] = r.lift[...] + dense_back(grad_gate, r.expand[:, one])
        r.lift[...] = r.lift[...] + dense_back(grad_up, r.expand[:, two])
    r.emit("grad_expanded")
    r.need("resid", "attended")
    normed, inverse = normalize(r.resid[...])
    keep(3, r.lift[...])
    keep(4, r.lift[...] * normed)
    grad_resid = r.grad_out[...] + norm_back(normed, inverse, r.lift[...] * (1.0 + part(4)))
    keep(2, grad_resid * r.attended[...])
    if "output" in r.stores:
        r.stores.pop("output").wait()
    r.grad_flat[...] = grad_resid
    attended_low = (grad_resid * part(2)).astype(BF16)
    r.grad_attended[...] = attended_low
    r.emit("grad_attended")
    r.need("mixing")
    r.lift[...] = dense_back(attended_low, r.mixing[...])
    r.need("seg_q", "seg_k", "pad_k", "queries", "kv", "lse")
    allowed = allowed_mask(r.seg_q, r.seg_k, r.pad_k, half)
    r.feed[...] = jnp.zeros_like(r.feed)
    r.grad_k[...] = jnp.zeros_like(r.grad_k)
    r.grad_v[...] = jnp.zeros_like(r.grad_v)
    scale = 1.0 / math.sqrt(HD)
    lane = lax.broadcasted_iota(jnp.int32, (half, 128), 1)
    for h in range(width // HD):
        first, unused = window(h, width)
        span = slice(first, first + 256)
        mask = head_mask(h, width, half)
        query = jnp.where(mask, r.queries[:, span].astype(F32), 0.0).astype(BF16)
        grad_mixed = jnp.where(mask, r.lift[:, span], 0.0).astype(BF16)
        scores = dense_back(query, r.kv[0, :, span]) * scale
        logsum = jnp.sum(jnp.where(lane == h, r.lse[...], 0.0), axis=1, keepdims=True)
        chances = jnp.exp(jnp.where(allowed, scores, -1e30) - logsum)
        grad_chances = dense_back(grad_mixed, r.kv[1, :, span])
        along = jnp.sum(chances * grad_chances, axis=1, keepdims=True)
        scores_low = (chances * (grad_chances - along)).astype(BF16)
        out = jnp.dot(scores_low, r.kv[0, :, span], preferred_element_type=F32)
        r.feed[:, span] = r.feed[:, span] + jnp.where(mask, out, 0.0)
        r.grad_k[:, span] = r.grad_k[:, span] + outer_sum(scores_low, query)
        r.grad_v[:, span] = r.grad_v[:, span] + outer_sum(chances.astype(BF16), grad_mixed)
    r.outgoing[0] = (r.grad_k[theirs, :] * scale).astype(BF16)
    r.outgoing[1] = r.grad_v[theirs, :].astype(BF16)
    share = pltpu.make_async_remote_copy(
        r.outgoing, r.incoming, ssem.at[1], rsem.at[1], device_id=sibling, device_id_type=MESH
    )
    share.start()
    heads = head_sum_matrix(width)
    r.need("raw", "gains", "cosine", "sine")

    def prepare_back(k, grad):
        values = r.raw[:, k * width : (k + 1) * width]
        gain = r.gains[k : k + 1, :]
        mean = exact_dot(values * values, heads) * (1.0 / HD)
        inverse = spread_heads(lax.rsqrt(mean + 1e-06), heads)
        scaled = values * inverse
        turned_back = grad * r.cosine[...] + swap_pairs(grad * r.sine[...])
        r.gains_grad[k : k + 1, :] = jnp.sum(turned_back * scaled, axis=0, keepdims=True)
        turned_back = turned_back * gain
        along = spread_heads(exact_dot(turned_back * scaled, heads) * (1.0 / HD), heads)
        return (turned_back - scaled * along) * inverse

    r.grad_projected[:, :width] = prepare_back(0, r.feed[...] * scale).astype(BF16)
    r.need("triple")
    total = dense_back(r.grad_projected[:, :width], r.triple[:, :width])
    share.wait()
    own_k = (r.grad_k[mine, :] * scale).astype(BF16).astype(F32) + r.incoming[0].astype(F32)
    own_v = r.grad_v[mine, :].astype(BF16).astype(F32) + r.incoming[1].astype(F32)
    r.grad_projected[:, width : 2 * width] = prepare_back(1, own_k).astype(BF16)
    r.grad_projected[:, 2 * width :] = own_v.astype(BF16)
    r.emit("grad_projected", "gains_grad")
    for k in (1, 2):
        span = slice(k * width, (k + 1) * width)
        total = total + dense_back(r.grad_projected[:, span], r.triple[:, span])
    r.need("flat")
    normed, inverse = normalize(r.flat[...])
    keep(0, total)
    keep(1, total * normed)
    r.emit("grad_mod")
    r.grad_flat[...] = r.grad_flat[...] + norm_back(normed, inverse, total * (1.0 + part(1)))
    r.emit("grad_flat")


def block_shapes(half, width, hidden_size):
    rows = ((16, PADDED, half), BF16)
    token = ((half, width), F32)
    low = ((half, width), BF16)
    return {
        "flat": token,
        "mod": ((half, 6 * width), F32),
        "gains": ((2, width), F32),
        "cosine": token,
        "sine": token,
        "seg_q": ((half, 1), jnp.int32),
        "seg_k": ((1, 2 * half), jnp.int32),
        "pad_k": ((1, 2 * half), jnp.int32),
        "triple": ((width, 3 * width), BF16),
        "mixing": ((width, width), BF16),
        "expand": ((width, 2 * hidden_size), BF16),
        "reduce": ((hidden_size, width), BF16),
        "output": token,
        "raw": ((half, 2 * width), F32),
        "queries": low,
        "kv": ((2, 2 * half, width), BF16),
        "lse": ((half, 128), F32),
        "attended": token,
        "resid": token,
        "expanded": ((half, 2 * hidden_size), F32),
        "feed": token,
        "xt1": rows,
        "xtm": rows,
        "xt2": rows,
        "xth0": rows,
        "xth1": rows,
        "xth2": rows,
        "lift": token,
        "grad_out": token,
        "grad_flat": token,
        "grad_mod": ((half, 6 * width), BF16),
        "grad_feed": low,
        "grad_expanded": ((half, 2 * hidden_size), BF16),
        "grad_attended": low,
        "grad_projected": ((half, 3 * width), BF16),
        "gains_grad": ((2, width), F32),
        "grad_k": ((2 * half, width), F32),
        "grad_v": ((2 * half, width), F32),
        "outgoing": ((2, half, width), BF16),
        "incoming": ((2, half, width), BF16),
    }


WEIGHTS = ("triple", "mixing", "expand", "reduce")
GIVEN = ("gains", "cosine", "sine", "seg_q", "seg_k", "pad_k") + WEIGHTS
SAVED = ("raw", "queries", "kv", "lse", "attended", "resid", "expanded", "feed")
LEFTS = ("xt1", "xtm", "xt2", "xth0", "xth1", "xth2")
GRADS = (
    "grad_flat", "grad_mod", "grad_feed", "grad_expanded", "grad_attended", "grad_projected",
    "gains_grad",
)
WORK = ("grad_k", "grad_v", "outgoing", "incoming")
EARLY = ("gains", "cosine", "sine", "seg_q", "seg_k", "pad_k")
PLANS = {
    "forward": (("flat", "mod") + GIVEN, ("output",) + SAVED + LEFTS, ("lift",)),
    "backward": (("grad_out", "flat", "mod") + GIVEN + SAVED, GRADS, ("lift",) + WORK),
    "both": (("grad_out", "flat", "mod") + GIVEN, ("output",) + LEFTS + GRADS, SAVED + ("lift",) + WORK),
}


def held_names(kind):
    inputs, outputs, others = PLANS[kind]
    names = inputs + outputs + others
    return tuple(n for n in names if kind != "both" or n != "output")


def block_kernel(kind, *refs):
    inputs, outputs, others = PLANS[kind]
    sources = dict(zip(inputs, refs))
    targets = dict(zip(outputs, refs[len(inputs) :]))
    names = held_names(kind)
    held = dict(zip(names, refs[len(inputs) + len(outputs) :]))
    if kind == "both":
        held["output"] = held["grad_flat"]
    lsem, wsem, tsem, ssem, rsem = refs[len(inputs) + len(outputs) + len(names) :]
    r = Traffic(held, sources, targets, lsem, wsem)
    if kind == "backward":
        r.fetch("grad_out", "feed", "mod", *EARLY)
        for t in range(r.reduce.shape[0] // FF_TILE):
            r.fetch_tile(t, FF_TILE, ("reduce",), ("expanded", "expand"), tsem)
    else:
        r.fetch("flat", "mod", "triple", *EARLY)
    sibling = meet_sibling()
    if kind != "backward":
        forward_body(r, sibling, ssem, rsem)
    if kind == "both":
        r.fetch("grad_out")
        r.loads = {"grad_out": r.loads["grad_out"]}
    if kind != "forward":
        backward_body(r, sibling, ssem, rsem)
    r.close()


def run_block(kind, values, name):
    inputs, outputs, others = PLANS[kind]
    half, width = values["flat"].shape
    table = block_shapes(half, width, values["reduce"].shape[0])
    names = held_names(kind)
    results = pl.pallas_call(
        functools.partial(block_kernel, kind),
        name=name,
        out_shape=[jax.ShapeDtypeStruct(*table[n]) for n in outputs],
        in_specs=[ANY] * len(inputs),
        out_specs=[ANY] * len(outputs),
        scratch_shapes=[pltpu.VMEM(*table[n]) for n in names]
        + [DMA((len(inputs),)), DMA((len(outputs),)), DMA((4, 5)), DMA((2,)), DMA((2,))],
        compiler_params=pltpu.CompilerParams(
            collective_id={"forward": 5, "backward": 6, "both": 7}[kind],
            has_side_effects=True,
            vmem_limit_bytes=63 * 1024 * 1024,
        ),
    )(*[values[n] for n in inputs])
    return dict(zip(outputs, results))


def shard_rows(values):
    rows = values.T.reshape(16, -1, values.shape[0])
    return jnp.pad(rows, ((0, 0), (0, PADDED - rows.shape[1]), (0, 0)))


def split_kernel(pieces, in_ref, *refs):
    *outs, held, arrived, left = refs
    for k, (n, row, rows, columns, at) in enumerate(pieces):
        span = (pl.ds(0, rows), pl.ds(at, columns))
        pltpu.make_async_copy(in_ref.at[span], held.at[span], arrived.at[k]).start()

    def leave(k):
        n, row, rows, columns, at = pieces[k]
        span = (pl.ds(0, rows), pl.ds(at, columns))
        return pltpu.make_async_copy(held.at[span], outs[n].at[pl.ds(row, rows), :], left.at[k])

    for k, (n, row, rows, columns, at) in enumerate(pieces):
        span = (pl.ds(0, rows), pl.ds(at, columns))
        pltpu.make_async_copy(in_ref.at[span], held.at[span], arrived.at[k]).wait()
        leave(k).start()
    for k in range(len(pieces)):
        leave(k).wait()


def split(values, shapes, pieces):
    return pl.pallas_call(
        functools.partial(split_kernel, tuple(pieces)),
        name="split",
        out_shape=[jax.ShapeDtypeStruct(shape, values.dtype) for shape in shapes],
        in_specs=[ANY],
        out_specs=[ANY] * len(shapes),
        scratch_shapes=[
            pltpu.VMEM(values.shape, values.dtype),
            DMA((len(pieces),)),
            DMA((len(pieces),)),
        ],
        compiler_params=pltpu.CompilerParams(vmem_limit_bytes=32 * 1024 * 1024),
    )(values)


def rope_lanes(cosine, sine):
    tokens = cosine.shape[0]

    def lanes(table, signs):
        table = jnp.stack([signs[0] * table, signs[1] * table], axis=2).reshape(tokens, 1, HD)
        return jnp.broadcast_to(table, (tokens, HEADS, HD)).reshape(tokens, HEADS * HD)

    return lanes(cosine, (1.0, 1.0)), lanes(sine, (-1.0, 1.0))


def fast_reduce(blocks, rows, collective_id, name):
    xts = []
    dys = []
    source = []
    for factors, extra in blocks:
        for lefts, right in factors:
            source += [len(dys)] * len(lefts)
            xts += lefts
            dys.append(right)
        tokens = right.shape[0]
        lines = -(-extra.shape[1] // tokens)
        packed = jnp.pad(extra, ((0, 0), (0, lines * tokens - extra.shape[1])))
        packed = packed.reshape(16, lines, tokens).astype(BF16)
        xts.append(jnp.pad(packed, ((0, 0), (0, PADDED - lines), (0, 0))))
        source.append(len(dys))
        dys.append(jnp.eye(tokens, UNIT, dtype=BF16))
    out, rows = scatter(xts, dys, source, rows, collective_id, name)
    shapes = []
    pieces = []
    smalls = []
    at = 0
    for factors, extra in blocks:
        for lefts, right in factors[:-1]:
            pieces.append((len(shapes), 0, ROWS, right.shape[1], at))
            shapes.append((ROWS, right.shape[1]))
            at += right.shape[1]
        width = factors[-1][1].shape[1]
        for g in range(3):
            pieces.append((len(shapes), 64 * g, 64, width, at))
            at += width
        shapes.append((192, width))
        lines = -(-extra.shape[1] // tokens)
        smalls.append(out[:lines, at : at + tokens].reshape(-1)[: extra.shape[1]])
        at += UNIT
    grads = split(out, shapes, pieces)
    results = []
    for (factors, extra), small in zip(blocks, smalls):
        results.append((grads[: len(factors)], small))
        grads = grads[len(factors) :]
    return results, rows


def whole_rows(gathered):
    return gathered.reshape((-1,) + gathered.shape[4:])


def fast_step(flat, cotangent, context, segment_local, valid, timesteps, encoder, decoder):
    width = flat.shape[1]
    offset_size = encoder[1].shape[0]
    gain_size = 2 * encoder[3].shape[1]
    small = jnp.concatenate(
        [
            encoder[1].astype(F32),
            decoder[1].astype(F32),
            encoder[3].astype(F32).reshape(-1),
            decoder[3].astype(F32).reshape(-1),
            timesteps.astype(F32).reshape(-1),
        ]
    )
    size = small.shape[0]
    small = jnp.pad(small, (0, 2048 - size)).reshape(16, 128)
    small = exchange(small, 0, "small").reshape(16, -1)
    encoder_offset = small[:, :offset_size].reshape(-1)
    decoder_offset = small[:, offset_size : 2 * offset_size].reshape(-1)
    at = 2 * offset_size
    encoder_gains = small[:, at : at + gain_size].reshape(16, 2, -1).swapaxes(0, 1).reshape(2, -1)
    at += gain_size
    decoder_gains = small[:, at : at + gain_size].reshape(16, 2, -1).swapaxes(0, 1).reshape(2, -1)
    at += gain_size
    all_times = small[:, at : at + timesteps.size]
    segments = timesteps.shape[1]
    picks = (segment_local[..., None] == jnp.arange(segments, dtype=jnp.int32)).astype(F32)
    picks = picks.reshape(-1, segments)

    all_cond = embed_times(all_times, width).reshape(-1, width)
    act_rows = jax.nn.silu(all_cond).astype(BF16)
    me = lax.axis_index("dp")
    rows = encoder[0].shape[0]
    act_mine = lax.dynamic_slice_in_dim(act_rows, me * rows, rows, 1)
    core = lax.axis_index("ctx")
    share = encoder[0].shape[1] // 2
    partial = dense(act_mine, lax.dynamic_slice_in_dim(encoder[0], core * share, share, 1))
    partial = partial.reshape(GRID + (8, -1))
    shards = (encoder[2], encoder[4], encoder[5], encoder[6])
    shards += (decoder[0], decoder[2], decoder[4], decoder[5], decoder[6])
    *wholes, partial = gather(shards, partial, *gather_units(shards), 1, "gather")
    wholes = [whole_rows(w) for w in wholes]
    encoder_weights = (*wholes[:4], encoder_gains)
    modulate = wholes[4]
    decoder_weights = (*wholes[5:], decoder_gains)
    partial = jnp.sum(partial, axis=0).reshape(segments, -1)
    others = lax.ppermute(partial, "ctx", [(0, 1), (1, 0)])
    modulation_rows = jnp.where(
        core == 0,
        jnp.concatenate([partial, others], axis=1),
        jnp.concatenate([others, partial], axis=1),
    )
    modulation_rows = modulation_rows + encoder_offset

    def pick(rows):
        return sum(jnp.where(picks[:, j : j + 1] > 0, rows[j], 0.0) for j in range(segments))

    encoder_modulation = pick(modulation_rows)
    cond_rows = lax.dynamic_slice_in_dim(all_cond, me * segments, segments, 0)
    cond = pick(cond_rows)

    shared = dict(zip(("cosine", "sine", "seg_q", "seg_k", "pad_k"), context), flat=flat)
    encoder_in = dict(zip(WEIGHTS + ("gains",), encoder_weights), mod=encoder_modulation, **shared)
    forward = run_block("forward", encoder_in, "encoder")
    latent_full = valid * forward["output"]
    decoder_pre = latent_full + cond
    decoder_act = jax.nn.silu(decoder_pre).astype(BF16)

    decoder_modulation = dense(decoder_act, modulate) + decoder_offset
    decoder_in = dict(
        zip(WEIGHTS + ("gains",), decoder_weights),
        mod=decoder_modulation,
        grad_out=valid * cotangent,
        **shared,
    )
    both = run_block("both", decoder_in, "decoder")
    velocity = valid * both["output"]

    def pair_up(lefts, grads):
        return (
            ([lefts["xt1"]], grads["grad_projected"]),
            ([lefts["xtm"]], grads["grad_attended"]),
            ([lefts["xt2"]], grads["grad_expanded"]),
            ([lefts["xth0"], lefts["xth1"], lefts["xth2"]], grads["grad_feed"]),
        )

    factors = pair_up(both, both)
    grad_modulation = both["grad_mod"]
    gains_grad = both["gains_grad"]
    grad_act = dense_back(grad_modulation, modulate)
    unused_silu, silu_pull = jax.vjp(jax.nn.silu, decoder_pre)
    grad_latent = valid * silu_pull(grad_act)[0]
    offset_grad = jnp.sum(grad_modulation, axis=0, dtype=F32)
    extra = jnp.concatenate(
        [
            offset_grad.reshape(16, -1),
            gains_grad.reshape(2, 16, -1).swapaxes(0, 1).reshape(16, -1),
        ],
        axis=1,
    )
    first = ([shard_rows(decoder_act)], grad_modulation)
    decoder_block = ((factors[1], factors[0], factors[2], first, factors[3]), extra)

    encoder_in["grad_out"] = grad_latent
    backward = run_block("backward", {**encoder_in, **forward}, "encoder_back")
    factors = pair_up(forward, backward)
    grad_modulation = backward["grad_mod"]
    gains_grad = backward["gains_grad"]
    grad_rows = lax.dot_general(
        picks.astype(BF16), grad_modulation, (((0,), (0,)), ((), ())), preferred_element_type=F32
    )
    grad_rows = grad_rows + lax.ppermute(grad_rows, "ctx", [(0, 1), (1, 0)])
    extra = gains_grad.reshape(2, 16, -1).swapaxes(0, 1).reshape(16, -1)
    results, all_rows = fast_reduce(
        (decoder_block, (factors, extra)), grad_rows.astype(BF16).reshape(16, -1), 2, "scatter"
    )
    (grads, small), (encoder_parts, encoder_small) = results
    decoder_grads = (
        grads[3],
        small[:offset_size],
        grads[1],
        small[offset_size:].reshape(2, -1),
        grads[0],
        grads[2],
        grads[4],
    )
    all_rows = all_rows.reshape(16 * segments, -1)
    modulate_grad = outer_sum(act_mine, all_rows)
    offset_grad = lax.dynamic_slice_in_dim(
        jnp.sum(all_rows.astype(F32), axis=0), me * offset_size, offset_size, 0
    )
    encoder_grads = (
        modulate_grad,
        offset_grad,
        encoder_parts[0],
        encoder_small.reshape(2, -1),
        encoder_parts[1],
        encoder_parts[2],
        encoder_parts[3],
    )
    token_grad = both["grad_flat"] + backward["grad_flat"]
    return velocity, latent_full, token_grad, encoder_grads, decoder_grads


def plain_gather(block):
    parts = [lax.all_gather(block[k], "dp", axis=0, tiled=True) for k in (0, 1, 2, 4, 5, 6)]
    gains = lax.all_gather(block[3], "dp", axis=1, tiled=True).astype(F32)
    modulate, offset, triple, mixing, expand, reduce_w = parts
    return modulate, offset.astype(F32), (triple, mixing, expand, reduce_w, gains)


def plain_reduce(factors, grad_modulation, gains_grad):
    def rows(values, dim=0):
        part = lax.psum_scatter(values, "dp", scatter_dimension=dim, tiled=True)
        return lax.psum(part.astype(BF16), "ctx").astype(F32)

    offset = rows(jnp.sum(grad_modulation, axis=0, dtype=F32))
    modulate, triple, mixing, expand, reduce_w = [rows(outer_sum(a, b)) for a, b in factors]
    return modulate, offset, triple, rows(gains_grad, 1), mixing, expand, reduce_w


def plain_step(flat, cotangent, context, segment_local, valid, timesteps, encoder, decoder):
    picks = (
        segment_local[..., None] == jnp.arange(timesteps.shape[-1], dtype=jnp.int32)
    ).astype(F32)
    times = jnp.sum(picks * timesteps[:, None, :].astype(F32), axis=-1)
    cond = embed_times(times, flat.shape[1]).reshape(flat.shape)
    modulate, offset, encoder_weights = plain_gather(encoder)
    encoder_act = jax.nn.silu(cond).astype(BF16)
    encoder_out, encoder_kept = block_forward(
        flat, dense(encoder_act, modulate) + offset, encoder_weights, context
    )
    latent_full = valid * encoder_out
    decoder_pre = latent_full + cond
    decoder_act = jax.nn.silu(decoder_pre).astype(BF16)
    modulate, offset, decoder_weights = plain_gather(decoder)
    decoder_out, decoder_kept = block_forward(
        flat, dense(decoder_act, modulate) + offset, decoder_weights, context
    )
    decoder_flat, grad_modulation, factors, gains_grad = block_backward(
        valid * cotangent, decoder_kept, decoder_weights, context
    )
    grad_act = dense_back(grad_modulation, modulate)
    decoder_grads = plain_reduce(
        ((decoder_act, grad_modulation),) + factors, grad_modulation, gains_grad
    )
    unused_silu, silu_pull = jax.vjp(jax.nn.silu, decoder_pre)
    encoder_flat, grad_modulation, factors, gains_grad = block_backward(
        valid * silu_pull(grad_act)[0], encoder_kept, encoder_weights, context
    )
    encoder_grads = plain_reduce(
        ((encoder_act, grad_modulation),) + factors, grad_modulation, gains_grad
    )
    return valid * decoder_out, latent_full, decoder_flat + encoder_flat, encoder_grads, decoder_grads


def local(fast, tokens, cotangent, segment, rows, columns, padding, timesteps, *weights):
    batch, half, width = tokens.shape
    start = lax.axis_index("ctx") * half
    segment_local = lax.dynamic_slice_in_dim(segment, start, half, 1)
    rows_local = lax.dynamic_slice_in_dim(rows, start, half, 1)
    columns_local = lax.dynamic_slice_in_dim(columns, start, half, 1)
    padding_local = lax.dynamic_slice_in_dim(padding, start, half, 1)
    place_query = start + jnp.arange(half, dtype=jnp.int32)
    place_key = jnp.arange(segment.shape[1], dtype=jnp.int32)
    allowed = (segment_local[:, :, None] == segment[:, None, :]) & (
        (padding[:, None, :] == 0) | (place_query[None, :, None] == place_key[None, None, :])
    )
    cosine, sine = rope_tables(rows_local.reshape(-1), columns_local.reshape(-1))
    context = (batch, half, allowed, cosine, sine)
    if fast:
        context = rope_lanes(cosine, sine)
        context += (segment_local.reshape(-1, 1), segment, padding)
    valid = (1 - padding_local).astype(F32).reshape(-1, 1)
    flat = tokens.reshape(-1, width).astype(F32)
    step = fast_step if fast else plain_step
    velocity, latent, token_grad, encoder_grads, decoder_grads = step(
        flat,
        cotangent.reshape(-1, width).astype(F32),
        context,
        segment_local,
        valid,
        timesteps,
        weights[:7],
        weights[7:],
    )
    return (
        velocity.astype(BF16).reshape(batch, half, width),
        latent.astype(BF16).reshape(batch, half, width),
        token_grad.reshape(batch, half, width),
        *encoder_grads,
        *decoder_grads,
    )


def solution(mesh):
    fast = dict(mesh.shape) == {"dp": math.prod(GRID), "ctx": 2}
    block = (
        P("dp", None),
        P("dp"),
        P("dp", None),
        P(None, "dp"),
        P("dp", None),
        P("dp", None),
        P("dp", None),
    )
    slots = P("dp", "ctx", None)
    return jax.shard_map(
        functools.partial(local, fast),
        mesh=mesh,
        in_specs=(slots, slots) + (P("dp", None),) * 5 + block + block,
        out_specs=(slots, slots, slots) + block + block,
        check_vma=False,
    )
```

```python
import enum
import functools
import math

import jax
import jax.numpy as jnp
from jax import lax
from jax.experimental import pallas as pl
from jax.experimental.pallas import tpu as pltpu
from jax.sharding import PartitionSpec as P

HEADS = 16
HD = 72
MESH = pl.DeviceIdType.MESH
GRID = (4, 2, 2)
BF16 = jnp.bfloat16
F32 = jnp.float32


def coords():
    dp = lax.axis_index("dp")
    return (lax.div(dp, 4), lax.rem(lax.div(dp, 2), 2), lax.rem(dp, 2), lax.axis_index("ctx"))


def device(z, y, x, c):
    return (z * 4 + y * 2 + x, c)


def when(cond, body):
    if cond is True:
        body()
    else:
        pl.when(cond)(body)


def greet():
    barrier = pltpu.get_barrier_semaphore()
    me = lax.axis_index("dp")
    c = lax.axis_index("ctx")
    for k in range(1, 16):
        pl.semaphore_signal(
            barrier, inc=1, device_id=(lax.rem(me + k, 16), c), device_id_type=MESH
        )
    pl.semaphore_signal(barrier, inc=1, device_id=(me, 1 - c), device_id_type=MESH)
    pl.semaphore_wait(barrier, 16)


class Exchange:
    def __init__(self, same, in_ref, out_ref, ssem, rsem, lsem):
        self.refs = (in_ref, out_ref, ssem, rsem, lsem)
        self.same = same
        self.me = lax.axis_index("dp")

    def source(self, target):
        return self.refs[0] if self.same else self.refs[0].at[target]

    def copy(self, k, target, slot):
        return pltpu.make_async_remote_copy(
            self.source(target),
            self.refs[1].at[slot],
            self.refs[2].at[k],
            self.refs[3].at[k],
            device_id=(target, lax.axis_index("ctx")),
            device_id_type=MESH,
        )

    def own(self):
        return pltpu.make_async_copy(
            self.source(self.me), self.refs[1].at[self.me], self.refs[4].at[0]
        )

    def start(self):
        for k in range(1, 16):
            self.copy(k, lax.rem(self.me + k, 16), self.me).start()
        self.own().start()

    def wait(self):
        self.own().wait()
        for k in range(1, 16):
            self.copy(k, lax.rem(self.me + k, 16), self.me).wait_send()
            origin = lax.rem(self.me + 16 - k, 16)
            self.copy(k, origin, origin).wait_recv()


class Sums:
    def __init__(self, in_ref, out_ref, box, total, ssem, rsem, lsem):
        self.refs = (in_ref, out_ref, box, total)
        self.sems = (ssem, rsem, lsem)
        self.z, self.y, self.x, self.c = coords()

    def remote(self, src, dst, k, target):
        return pltpu.make_async_remote_copy(
            src,
            dst,
            self.sems[0].at[k],
            self.sems[1].at[k],
            device_id=target,
            device_id_type=MESH,
        )

    def across(self, k):
        y = lax.rem(self.y + k // 2, 2)
        x = lax.rem(self.x + k % 2, 2)
        target = device(self.z, y, x, self.c)
        return self.remote(self.refs[0].at[:, y, x], self.refs[2].at[k], k, target)

    def own(self):
        return pltpu.make_async_copy(
            self.refs[0].at[:, self.y, self.x], self.refs[2].at[0], self.sems[2].at[0]
        )

    def along(self, k, arrival):
        there = lax.rem(self.z + (4 - k if arrival else k), 4)
        slot = there if arrival else self.z
        target = device(there, self.y, self.x, self.c)
        return self.remote(self.refs[3].at[there], self.refs[1].at[slot], 3 + k, target)

    def kept(self):
        return pltpu.make_async_copy(
            self.refs[3].at[self.z], self.refs[1].at[self.z], self.sems[2].at[1]
        )

    def start(self):
        for k in range(1, 4):
            self.across(k).start()
        self.own().start()

    def forward(self):
        self.own().wait()
        for k in range(1, 4):
            self.across(k).wait_recv()
        box = self.refs[2]
        self.refs[3][...] = (box[0] + box[1]) + (box[2] + box[3])
        for k in range(1, 4):
            self.along(k, False).start()
        self.kept().start()

    def wait(self):
        self.kept().wait()
        for k in range(1, 4):
            self.across(k).wait_send()
            self.along(k, False).wait_send()
            self.along(k, True).wait_recv()


class Broadcast:
    def __init__(self, in_ref, out_ref, ssem, rsem, lsem):
        self.refs = (in_ref, out_ref, ssem, rsem, lsem)
        self.z, self.y, self.x, self.c = coords()

    def own(self):
        return pltpu.make_async_copy(
            self.refs[0], self.refs[1].at[self.z, self.y, self.x], self.refs[4].at[0]
        )

    def along(self, k, arrival):
        there = lax.rem(self.z + (4 - k if arrival else k), 4)
        slot = there if arrival else self.z
        return pltpu.make_async_remote_copy(
            self.refs[0],
            self.refs[1].at[slot, self.y, self.x],
            self.refs[2].at[k],
            self.refs[3].at[k],
            device_id=device(there, self.y, self.x, self.c),
            device_id_type=MESH,
        )

    def across(self, k, arrival):
        y = lax.rem(self.y + k // 2, 2)
        x = lax.rem(self.x + k % 2, 2)
        block = self.refs[1].at[:, y, x] if arrival else self.refs[1].at[:, self.y, self.x]
        return pltpu.make_async_remote_copy(
            block,
            block,
            self.refs[2].at[3 + k],
            self.refs[3].at[3 + k],
            device_id=device(self.z, y, x, self.c),
            device_id_type=MESH,
        )

    def start(self):
        for k in range(1, 4):
            self.along(k, False).start()
        self.own().start()

    def forward(self):
        self.own().wait()
        for k in range(1, 4):
            self.along(k, True).wait_recv()
        for k in range(1, 4):
            self.across(k, False).start()

    def wait(self):
        for k in range(1, 4):
            self.along(k, False).wait_send()
            self.across(k, False).wait_send()
            self.across(k, True).wait_recv()


def gather_kernel(units, turns, count, *refs):
    w = refs[:count]
    o = refs[count + 1 : 2 * count + 1]
    ssem, rsem, lsem, csem, crsem, box, sums, es, er, el = refs[2 * count + 2 :]
    z, y, x, c = coords()
    greet()
    side = Sums(refs[count], refs[2 * count + 1], box, sums, es, er, el)
    side.start()
    up = device(z + 1, y, x, c)
    down = device(z - 1, y, x, c)
    partner = {"y": device(z, 1 - y, x, c), "x": device(z, y, 1 - x, c)}
    every = slice(None)

    def run(mine, other, order):
        def view(u, index):
            m, first, cols, _ = mine[u]
            return o[m].at[index[0], index[1], index[2], :, pl.ds(first, cols)]

        def copy(u, index, k, target, own=False):
            m, first, cols, _ = mine[u]
            dst = view(u, index)
            src = w[m].at[:, pl.ds(first, cols)] if own else dst
            return pltpu.make_async_remote_copy(
                src, dst, ssem.at[u, k], rsem.at[u, k], device_id=target, device_id_type=MESH
            )

        def local_copy(u):
            m, first, cols, _ = mine[u]
            return pltpu.make_async_copy(
                w[m].at[:, pl.ds(first, cols)], view(u, (z, y, x)), lsem.at[u]
            )

        def plan(u):
            held = {"z": False, "y": False, "x": False}

            def index(zz=z, flip=None):
                return (
                    every if held["z"] else zz,
                    every if held["y"] else (1 - y if flip == "y" else y),
                    every if held["x"] else (1 - x if flip == "x" else x),
                )

            steps = []
            pending = []
            sends = []
            own = True
            pair = 0
            for axis in mine[u][3]:
                if axis != "z":
                    send = [(True, functools.partial(copy, u, index(), pair, partner[axis], own))]
                    steps.append((pending, send))
                    sends += send
                    pending = [
                        (True, functools.partial(copy, u, index(flip=axis), pair, partner[axis]))
                    ]
                    pair += 1
                else:

                    def chain(shift, k, target, first=False):
                        return functools.partial(copy, u, index(zz=z + shift), k, target, first)

                    one = [(z < 3, chain(0, 2, up, own)), (z > 0, chain(0, 5, down, own))]
                    steps.append((pending, one))
                    middle = (z > 0) & (z < 3)
                    two = [(middle, chain(-1, 3, up)), (middle, chain(1, 6, down))]
                    steps.append(([(z > 0, chain(-1, 2, down)), (z < 3, chain(1, 5, up))], two))
                    three = [(z == 2, chain(-2, 4, up)), (z == 1, chain(2, 7, down))]
                    steps.append(([(z > 1, chain(-2, 3, down)), (z < 2, chain(2, 6, up))], three))
                    pending = [(z == 3, chain(-3, 4, down)), (z == 0, chain(3, 7, up))]
                    sends += one + two + three
                held[axis] = True
                own = False
            return steps, pending, sends

        plans = [plan(u) for u in range(len(mine))]

        def to_core(u, which):
            m, first, cols, _ = which[u]
            block = o[m].at[:, :, :, :, pl.ds(first, cols)]
            return pltpu.make_async_remote_copy(
                block,
                block,
                csem.at[u],
                crsem.at[u],
                device_id=device(z, y, x, 1 - c),
                device_id_type=MESH,
            )

        for u in range(len(mine)):
            local_copy(u).start()
        for at, (u, s) in enumerate(order):
            if at == FORWARD_AT:
                side.forward()
            steps, pending, _ = plans[u]
            if s == 1:
                local_copy(u).wait()
            for cond, make in steps[s][0] if s < 5 else pending:
                when(cond, lambda make=make: make().wait_recv())
            for cond, make in steps[s][1] if s < 5 else ():
                when(cond, lambda make=make: make().start())
            if s == 5:
                to_core(u, mine).start()
        for u in range(len(mine)):
            for cond, make in plans[u][2]:
                when(cond, lambda make=make: make().wait_send())
            to_core(u, mine).wait_send()
        for u in range(len(other)):
            to_core(u, other).wait_recv()

    pl.when(c == 0)(lambda: run(units[0], units[1], turns[0]))
    pl.when(c == 1)(lambda: run(units[1], units[0], turns[1]))
    side.wait()


ANY = pl.BlockSpec(memory_space=pl.ANY)
DMA = pltpu.SemaphoreType.DMA


SIDE = [DMA((16,)), DMA((16,)), DMA((1,))]


def gather(shards, rows, units, turns, collective_id, name):
    count = len(shards)
    most = max(len(units[0]), len(units[1]))
    shapes = [jax.ShapeDtypeStruct(GRID + s.shape, s.dtype) for s in shards]
    return pl.pallas_call(
        functools.partial(gather_kernel, units, turns, count),
        name=name,
        out_shape=shapes + [jax.ShapeDtypeStruct(GRID[:1] + rows.shape[3:], rows.dtype)],
        in_specs=[ANY] * (count + 1),
        out_specs=[ANY] * (count + 1),
        scratch_shapes=[
            DMA((most, 8)),
            DMA((most, 8)),
            DMA((most,)),
            DMA((most,)),
            DMA((most,)),
            pltpu.VMEM((4,) + GRID[:1] + rows.shape[3:], rows.dtype),
            pltpu.VMEM(GRID[:1] + rows.shape[3:], rows.dtype),
            DMA((7,)),
            DMA((7,)),
            DMA((2,)),
        ],
        compiler_params=pltpu.CompilerParams(collective_id=collective_id, has_side_effects=True),
    )(*shards, rows)


ORDERS = (
    ("zyx", "zxy", "xyz", "zxy", "zyx", "zxy", "zyx", "yxz", "zyx", "zxy"),
    ("zxy", "zyx", "yxz", "zyx", "zxy", "zyx", "zxy", "xyz", "zxy", "zyx"),
)
AFTER_Z = (0.6165, 0.4168, 0.3474, 1.6339, 4.4601)
AFTER_XY = (1.5672, 1.5028, 1.8589, 1.1737, 2.0677)
PER_TURN = 2.2835
FORWARD_AT = 40
SHIFT = 0.1931
SIZE = 4
TAIL = (0.1, 2)


def gather_units(shards):
    units = ([], [])
    load = [0, 0]
    whole = sum(s.size for s in shards) / (ROWS * 128)
    done = 0
    for m, shard in enumerate(shards):
        rows, columns = shard.shape
        tiles = columns // 128
        weight = rows / ROWS
        at = 0
        while at < tiles:
            size = SIZE if done < (1 - TAIL[0]) * whole else TAIL[1]
            step = max(1, round(size / weight))
            n = min(step, tiles - at)
            if 0 < tiles - at - n < max(1, round(size / weight / 2)):
                n = tiles - at
            core = 0 if load[0] <= load[1] else 1
            order = ORDERS[core][len(units[core]) % len(ORDERS[core])]
            units[core].append((m, at * 128, n * 128, order))
            load[core] += n * weight
            done += n * weight
            at += n
    turns = []
    for core in range(2):
        keys = []
        place = 0.0
        for u, (m, first, columns, order) in enumerate(units[core]):
            at = place / PER_TURN + core * SHIFT
            place += shards[m].shape[0] * columns / (ROWS * 128 * SIZE)
            keys.append((at, u, 0))
            for s, after in enumerate(AFTER_Z if order[0] == "z" else AFTER_XY):
                at += after
                keys.append((at, u, s + 1))
        turns.append(tuple((u, s) for _, u, s in sorted(keys)))
    return (tuple(units[0]), tuple(units[1])), tuple(turns)


def exchange_kernel(in_ref, out_ref, *sems):
    greet()
    side = Exchange(True, in_ref, out_ref, *sems)
    side.start()
    side.wait()


def exchange(values, collective_id, name):
    return pl.pallas_call(
        exchange_kernel,
        name=name,
        out_shape=jax.ShapeDtypeStruct((16,) + values.shape, values.dtype),
        in_specs=[ANY],
        out_specs=ANY,
        scratch_shapes=SIDE,
        compiler_params=pltpu.CompilerParams(collective_id=collective_id, has_side_effects=True),
    )(values)


LAG = (0, 2, 3, 4, 5, 6)
RECV_SLOTS = 9
SEND_SLOTS = 8
FIRST_SLOTS = 4
UNIT = 384
ROWS = 72
PADDED = 80


def scatter_kernel(first, cols, source, dy_count, *refs):
    nv = len(first) - 1
    xt = refs[:nv]
    dy = refs[nv : nv + dy_count]
    out = refs[nv + dy_count + 1]
    (
        xts, dys, a_s1, a_s2, a_t, a_su, a_sd, e_s1, e_t, e_su, e_sd, e_sq,
        a_b1, a_b2, a_bu, a_bd, e_b1, e_bu, e_bd, e_bq, outs,
        ssem, rsem, xl, xs, xr, yl, ys, yr, ol, os, orr, es, er, el,
    ) = refs[nv + dy_count + 3 :]
    z, y, x, c = coords()
    total = first[-1] // 2
    sibling = device(z, y, x, 1 - c)
    up = device(z + 1, y, x, c)
    down = device(z - 1, y, x, c)
    greet()
    side = Broadcast(refs[nv + dy_count], refs[nv + dy_count + 2], es, er, el)
    lanes = pl.ds(pl.multiple_of(c * 128, 128), 128)
    offsets = []
    at = 0
    for k in range(dy_count):
        offsets.append(at)
        at += dy[k].shape[1]

    def remote(src, dst, send, recv, target):
        return pltpu.make_async_remote_copy(
            src, dst, send, recv, device_id=target, device_id_type=MESH
        )

    def x_views(v):
        return xt[v], xts.at[v, :, :, lanes]

    def x_local(v):
        return pltpu.make_async_copy(*x_views(v), xl.at[v])

    def x_remote(v):
        return remote(*x_views(v), xs.at[v], xr.at[v], sibling)

    def y_views(k):
        return dy[k], dys.at[lanes, pl.ds(offsets[k], dy[k].shape[1])]

    def y_local(k):
        return pltpu.make_async_copy(*y_views(k), yl.at[k])

    def y_remote(k):
        return remote(*y_views(k), ys.at[k], yr.at[k], sibling)

    fresh = [source[v] not in source[:v] for v in range(nv)]

    def bring(v):
        x_local(v).start()
        x_remote(v).start()
        if fresh[v]:
            y_local(source[v]).start()
            y_remote(source[v]).start()

    bring(0)
    bring(1)
    side.start()

    def arrive(tick):
        for v in range(nv):

            def wait(v=v):
                x_local(v).wait()
                x_remote(v).wait_recv()
                if fresh[v]:
                    y_local(source[v]).wait()
                    y_remote(source[v]).wait_recv()
                if v + 2 < nv:
                    bring(v + 2)

            pl.when(tick == (first[v] - c + 1) // 2)(wait)

    def unit(i):
        j = 2 * i + c
        v = jnp.int32(0)
        col = j * UNIT
        for k in range(1, nv):
            past = (j >= first[k]).astype(jnp.int32)
            v = v + past
            col = col + past * ((cols[k] - first[k] * UNIT) - (cols[k - 1] - first[k - 1] * UNIT))
        return v, pl.multiple_of(col, 128)

    def axes(i):
        o = lax.rem(i, 2)
        pb = x * (1 - o) + y * o
        qb = y * (1 - o) + x * o
        dp = z * 4 + y * 2 + x
        return o, pb, qb, (dp + (1 - 2 * pb) * (1 + o), c), (dp + (1 - 2 * qb) * (2 - o), c)

    def slots(i):
        return lax.rem(i, FIRST_SLOTS), lax.rem(i, SEND_SLOTS), lax.rem(i, RECV_SLOTS)

    def send(src, dst, i, k, target):
        return remote(
            src, dst, ssem.at[lax.rem(i, SEND_SLOTS), k], rsem.at[lax.rem(i, RECV_SLOTS), k], target
        )

    def first_copies(i):
        o, pb, qb, pn, qn = axes(i)
        f, s, w = slots(i)
        return [send(a_s1.at[f], a_b1.at[w], i, 0, pn), send(e_s1.at[f], e_b1.at[w], i, 8, pn)]

    def second_copy(i):
        o, pb, qb, pn, qn = axes(i)
        f, s, w = slots(i)
        return send(a_s2.at[s], a_b2.at[w], i, 1, qn)

    def last_copy(i):
        o, pb, qb, pn, qn = axes(i)
        f, s, w = slots(i)
        return send(e_sq.at[s], e_bq.at[w], i, 9, qn)

    def up_copy(i, k, e):
        f, s, w = slots(i)
        src, dst, n = (e_su, e_bu, 10) if e else (a_su, a_bu, 2)
        return send(src.at[s, k], dst.at[w, k], i, n + k, up)

    def down_copy(i, k, e):
        f, s, w = slots(i)
        src, dst, n = (e_sd, e_bd, 13) if e else (a_sd, a_bd, 5)
        return send(src.at[s, k], dst.at[w, k], i, n + k, down)

    def up_sends(k):
        return (z <= k) & (z < 3)

    def down_sends(k):
        return (3 - z <= k) & (z > 0)

    def up_comes(k):
        return (z >= 1) & (z <= k + 1)

    def down_comes(k):
        return (z <= 2) & (3 - z <= k + 1)

    def kept(i, e, d):
        f, s, w = slots(i)
        if e:
            return e_t.at[s, d]
        return a_t.at[s, d, axes(i)[2]]

    def z_send(i, k, e):
        f, s, w = slots(i)

        def pass_on(dest, stage, box, inner, copy):
            value = kept(i, e, dest)[...]
            if k == 0:
                stage[s, k] = value.astype(BF16)
            else:

                def add():
                    stage[s, k] = (value + box[w, k - 1].astype(F32)).astype(BF16)

                def begin():
                    stage[s, k] = value.astype(BF16)

                pl.when(inner)(add)
                pl.when(jnp.logical_not(inner))(begin)
            copy.start()

        pl.when(up_sends(k))(
            lambda: pass_on(
                z + 3 - k, e_su if e else a_su, e_bu if e else a_bu, z > 0, up_copy(i, k, e)
            )
        )
        pl.when(down_sends(k))(
            lambda: pass_on(
                z + k - 3, e_sd if e else a_sd, e_bd if e else a_bd, z < 3, down_copy(i, k, e)
            )
        )

    def z_wait(i, k, e):
        pl.when(up_comes(k))(lambda: up_copy(i, k, e).wait_recv())
        pl.when(down_comes(k))(lambda: down_copy(i, k, e).wait_recv())

    def z_close(i, e):
        f, s, w = slots(i)
        mine = kept(i, e, z)

        def below():
            mine[...] = mine[...] + (e_bu if e else a_bu)[w, 2].astype(F32)

        def above():
            mine[...] = mine[...] + (e_bd if e else a_bd)[w, 2].astype(F32)

        pl.when(z > 0)(below)
        pl.when(z < 3)(above)
        return mine

    def product(i, bit):
        v, col = unit(i)
        o = axes(i)[0]
        chips = [4 * k + bit * (1 + o) + q * (2 - o) for k in range(4) for q in range(2)]
        lhs = jnp.concatenate([xts[v, chip] for chip in chips], axis=0)
        whole = jnp.dot(lhs, dys[:, pl.ds(col, UNIT)], preferred_element_type=F32)
        return whole.reshape(8, PADDED, UNIT)[:, :ROWS]

    def stage0(i):
        f, s, w = slots(i)
        part = product(i, 1 - axes(i)[1])
        a_s1[f] = part[:, :, :128].astype(BF16).reshape(4, 2, ROWS, 128)
        e_s1[f] = part[:, :, 128:].astype(BF16).reshape(4, 2, ROWS, 256)
        for copy in first_copies(i):
            copy.start()

    def stage1(i):
        f, s, w = slots(i)
        o, pb, qb, pn, qn = axes(i)
        part = product(i, pb)
        for copy in first_copies(i):
            copy.wait_recv()
        a_t[s] = part[:, :, :128].reshape(4, 2, ROWS, 128) + a_b1[w].astype(F32)
        a_s2[s] = a_t[s, :, 1 - qb].astype(BF16)
        second_copy(i).start()
        e_t[s] = part[:, :, 128:].reshape(4, 2, ROWS, 256) + e_b1[w].astype(F32)
        z_send(i, 0, True)

    def a_second(i):
        f, s, w = slots(i)
        qb = axes(i)[2]
        second_copy(i).wait_recv()
        a_t[s, :, qb] = a_t[s, :, qb] + a_b2[w].astype(F32)
        z_send(i, 0, False)

    def z_step(i, k, e):
        z_wait(i, k - 1, e)
        z_send(i, k, e)

    def e_fourth(i):
        f, s, w = slots(i)
        z_wait(i, 2, True)
        z_close(i, True)
        e_sq[s] = e_t[s, z, 1 - axes(i)[2]].astype(BF16)
        last_copy(i).start()

    def out_view(i):
        return out.at[:, pl.ds(pl.multiple_of((2 * i + c) * UNIT, 128), UNIT)]

    def a_fifth(i):
        z_wait(i, 2, False)
        outs[i, :, :128] = z_close(i, False)[...]

    def e_fifth(i):
        f, s, w = slots(i)
        last_copy(i).wait_recv()
        outs[i, :, 128:] = e_t[s, z, axes(i)[2]] + e_bq[w].astype(F32)
        pltpu.make_async_copy(outs.at[i], out_view(i), ol.at[0]).start()
        remote(outs.at[i], out_view(i), os.at[0], orr.at[0], sibling).start()

    def first_sent(i):
        for copy in first_copies(i):
            copy.wait_send()

    def sent(i):
        second_copy(i).wait_send()
        last_copy(i).wait_send()
        for e in (False, True):
            for k in range(3):
                pl.when(up_sends(k))(lambda k=k, e=e: up_copy(i, k, e).wait_send())
                pl.when(down_sends(k))(lambda k=k, e=e: down_copy(i, k, e).wait_send())

    stages = (
        (a_fifth, LAG[5]),
        (functools.partial(z_step, k=1, e=False), LAG[3]),
        (functools.partial(z_step, k=2, e=True), LAG[3]),
        (e_fourth, LAG[4]),
        (stage0, LAG[0]),
        (functools.partial(z_step, k=1, e=True), LAG[2]),
        (a_second, LAG[2]),
        (functools.partial(z_step, k=2, e=False), LAG[4]),
        (e_fifth, LAG[5]),
        (stage1, LAG[1]),
    )

    def tick(t, carry):
        arrive(t)
        pl.when(t == 4)(side.forward)
        pl.when((t >= SEND_SLOTS) & (t - SEND_SLOTS < total))(lambda: sent(t - SEND_SLOTS))
        pl.when((t >= FIRST_SLOTS) & (t - FIRST_SLOTS < total))(lambda: first_sent(t - FIRST_SLOTS))
        for stage, lag in stages:
            i = t - lag
            pl.when((i >= 0) & (i < total))(functools.partial(stage, i))
        return carry

    lax.fori_loop(0, total + SEND_SLOTS, tick, 0)
    for v in range(nv):
        x_remote(v).wait_send()
    for k in range(dy_count):
        y_remote(k).wait_send()
    half = out.at[:, pl.ds(0, total * UNIT)]
    pltpu.make_async_copy(half, half, ol.at[0]).wait()
    everything = remote(half, half, os.at[0], orr.at[0], sibling)
    everything.wait_send()
    everything.wait_recv()
    side.wait()


def scatter(xts, dys, source, rows, collective_id, name):
    nv = len(xts)
    starts = []
    width = 0
    for d in dys:
        starts.append(width)
        width += d.shape[1]
    first = [0]
    cols = []
    for v in range(nv):
        cols.append(starts[source[v]])
        first.append(first[-1] + dys[source[v]].shape[1] // UNIT)
    total = first[-1] // 2
    s, f, r = SEND_SLOTS, FIRST_SLOTS, RECV_SLOTS
    vmem = pltpu.VMEM
    return pl.pallas_call(
        functools.partial(scatter_kernel, tuple(first), tuple(cols), tuple(source), len(dys)),
        name=name,
        out_shape=[
            jax.ShapeDtypeStruct((ROWS, first[-1] * UNIT), F32),
            jax.ShapeDtypeStruct(GRID + rows.shape, rows.dtype),
        ],
        in_specs=[ANY] * (nv + len(dys) + 1),
        out_specs=[ANY] * 2,
        scratch_shapes=[
            vmem((nv, 16, PADDED, 256), BF16),
            vmem((256, width), BF16),
            vmem((f, 4, 2, ROWS, 128), BF16),
            vmem((s, 4, ROWS, 128), BF16),
            vmem((s, 4, 2, ROWS, 128), F32),
            vmem((s, 3, ROWS, 128), BF16),
            vmem((s, 3, ROWS, 128), BF16),
            vmem((f, 4, 2, ROWS, 256), BF16),
            vmem((s, 4, 2, ROWS, 256), F32),
            vmem((s, 3, 2, ROWS, 256), BF16),
            vmem((s, 3, 2, ROWS, 256), BF16),
            vmem((s, ROWS, 256), BF16),
            vmem((r, 4, 2, ROWS, 128), BF16),
            vmem((r, 4, ROWS, 128), BF16),
            vmem((r, 3, ROWS, 128), BF16),
            vmem((r, 3, ROWS, 128), BF16),
            vmem((r, 4, 2, ROWS, 256), BF16),
            vmem((r, 3, 2, ROWS, 256), BF16),
            vmem((r, 3, 2, ROWS, 256), BF16),
            vmem((r, ROWS, 256), BF16),
            vmem((total, ROWS, UNIT), F32),
            DMA((s, 16)),
            DMA((r, 16)),
            DMA((nv,)),
            DMA((nv,)),
            DMA((nv,)),
            DMA((len(dys),)),
            DMA((len(dys),)),
            DMA((len(dys),)),
            DMA((1,)),
            DMA((1,)),
            DMA((1,)),
        ]
        + SIDE,
        compiler_params=pltpu.CompilerParams(
            collective_id=collective_id, has_side_effects=True, vmem_limit_bytes=62 * 1024 * 1024
        ),
    )(*xts, *dys, rows)


def layer_norm(values):
    center = values - jnp.mean(values, axis=-1, keepdims=True)
    spread = jnp.mean(center * center, axis=-1, keepdims=True)
    return center * lax.rsqrt(spread + 1e-06)


def head_norm(values, gain):
    shaped = values.reshape(values.shape[:-1] + (HEADS, HD))
    scaled = shaped * lax.rsqrt(jnp.mean(shaped * shaped, axis=-1, keepdims=True) + 1e-06)
    return scaled * gain.reshape(HEADS, HD)


def rope_tables(rows, columns):
    quarter = HD // 4
    freqs = jnp.exp(jnp.arange(quarter, dtype=F32) * (-math.log(10000.0) / quarter))
    places = jnp.stack([rows, columns], axis=-1).astype(F32)
    angles = places[..., None] * freqs
    return (jnp.cos(angles), jnp.sin(angles))


def rotate(values, cosine, sine):
    shaped = values.reshape(values.shape[:-1] + (2, 2, HD // 4))
    first = shaped[..., 0, :]
    second = shaped[..., 1, :]
    cosine = cosine[..., None, :, :]
    sine = sine[..., None, :, :]
    turned = jnp.stack([first * cosine - second * sine, first * sine + second * cosine], axis=-2)
    return turned.reshape(values.shape)


def embed_times(times, width):
    half_width = width // 2
    freqs = jnp.exp(jnp.arange(half_width, dtype=F32) * (-math.log(10000.0) / half_width))
    angles = times[..., None] * freqs
    return jnp.concatenate([jnp.cos(angles), jnp.sin(angles)], axis=-1)


def qk_prepare(query_raw, key_raw, gains, cosine, sine):
    return (
        rotate(head_norm(query_raw, gains[0]), cosine, sine),
        rotate(head_norm(key_raw, gains[1]), cosine, sine),
    )


def swish_product(gate, up):
    return jax.nn.silu(gate) * up


def attention_scores(queries, keys, allowed):
    scores = jnp.einsum("sqhd,skhd->shqk", queries, keys, preferred_element_type=F32) * (
        1.0 / math.sqrt(HD)
    )
    return jnp.where(allowed[:, None], scores, -1e30)


def dense(values, weight):
    return jnp.dot(values, weight, preferred_element_type=F32)


def dense_back(grads, weight):
    return lax.dot_general(grads, weight, (((1,), (1,)), ((), ())), preferred_element_type=F32)


def outer_sum(values, grads):
    return lax.dot_general(values, grads, (((0,), (0,)), ((), ())), preferred_element_type=F32)


def block_forward(flat, modulation, weights, context):
    batch, half, allowed, cosine, sine = context
    triple, mixing, expand, reduce_w, gains = weights
    width = flat.shape[1]
    shift1, scale1, gate1, shift2, scale2, gate2 = jnp.split(modulation, 6, axis=1)
    lifted1 = (layer_norm(flat) * (1.0 + scale1) + shift1).astype(BF16)
    projected = dense(lifted1, triple)
    query_raw, key_raw, value_raw = jnp.split(projected, 3, axis=1)
    queries, keys = qk_prepare(query_raw, key_raw, gains, cosine, sine)
    queries = queries.astype(BF16).reshape(batch, half, HEADS, HD)
    keys_local = keys.astype(BF16).reshape(batch, half, width)
    values_local = value_raw.astype(BF16).reshape(batch, half, width)
    key_heads = lax.all_gather(keys_local, "ctx", axis=1, tiled=True).reshape(batch, -1, HEADS, HD)
    value_heads = lax.all_gather(values_local, "ctx", axis=1, tiled=True)
    value_heads = value_heads.reshape(batch, -1, HEADS, HD)
    scores = attention_scores(queries, key_heads, allowed)
    top = jnp.max(scores, axis=-1, keepdims=True)
    raised = jnp.exp(scores - top)
    total = jnp.sum(raised, axis=-1, keepdims=True)
    softmax_low = (raised / total).astype(BF16)
    logsum = top + jnp.log(total)
    mixed = jnp.einsum("shqk,skhd->sqhd", softmax_low, value_heads, preferred_element_type=F32)
    mixed_low = mixed.reshape(-1, width).astype(BF16)
    attended = dense(mixed_low, mixing)
    resid = flat + gate1 * attended
    lifted2 = (layer_norm(resid) * (1.0 + scale2) + shift2).astype(BF16)
    expanded = dense(lifted2, expand)
    gate, up = jnp.split(expanded, 2, axis=1)
    hidden = swish_product(gate, up).astype(BF16)
    feed = dense(hidden, reduce_w)
    output = resid + gate2 * feed
    kept = (
        modulation,
        flat,
        lifted1,
        query_raw,
        key_raw,
        queries,
        key_heads,
        value_heads,
        logsum,
        mixed_low,
        attended,
        resid,
        lifted2,
        expanded,
        hidden,
        feed,
    )
    return (output, kept)


def block_backward(grad_out, kept, weights, context):
    batch, half, allowed, cosine, sine = context
    triple, mixing, expand, reduce_w, gains = weights
    (
        modulation,
        flat,
        lifted1,
        query_raw,
        key_raw,
        queries,
        key_heads,
        value_heads,
        logsum,
        mixed_low,
        attended,
        resid,
        lifted2,
        expanded,
        hidden,
        feed,
    ) = kept
    width = flat.shape[1]
    shift1, scale1, gate1, shift2, scale2, gate2 = jnp.split(modulation, 6, axis=1)
    grad_feed = (grad_out * gate2).astype(BF16)
    grad_hidden = dense_back(grad_feed, reduce_w)
    gate, up = jnp.split(expanded, 2, axis=1)
    unused_out, swish_pull = jax.vjp(swish_product, gate, up)
    grad_gate, grad_up = swish_pull(grad_hidden)
    grad_expanded = jnp.concatenate([grad_gate, grad_up], axis=1).astype(BF16)
    grad_lifted2 = dense_back(grad_expanded, expand)
    normed_second, second_pull = jax.vjp(layer_norm, resid)
    grad_resid = grad_out + second_pull(grad_lifted2 * (1.0 + scale2))[0]
    grad_attended = (grad_resid * gate1).astype(BF16)
    grad_mixed = dense_back(grad_attended, mixing).astype(BF16).reshape(batch, half, HEADS, HD)
    scores = attention_scores(queries, key_heads, allowed)
    chances = jnp.exp(scores - logsum)
    grad_chances = jnp.einsum(
        "sqhd,skhd->shqk", grad_mixed, value_heads, preferred_element_type=F32
    )
    grad_values = jnp.einsum(
        "shqk,sqhd->skhd", chances.astype(BF16), grad_mixed, preferred_element_type=F32
    )
    grad_scores = (
        chances * (grad_chances - jnp.sum(chances * grad_chances, axis=-1, keepdims=True))
    ).astype(BF16)
    scale = 1.0 / math.sqrt(HD)
    grad_queries = (
        jnp.einsum("shqk,skhd->sqhd", grad_scores, key_heads, preferred_element_type=F32) * scale
    )
    grad_keys = (
        jnp.einsum("shqk,sqhd->skhd", grad_scores, queries, preferred_element_type=F32) * scale
    )
    pair = jnp.stack(
        [grad_keys.reshape(batch, -1, width), grad_values.reshape(batch, -1, width)]
    ).astype(BF16)
    place = lax.axis_index("ctx")
    theirs = lax.dynamic_slice_in_dim(pair, (1 - place) * half, half, 2)
    theirs = lax.ppermute(theirs, "ctx", [(0, 1), (1, 0)])
    mine = lax.dynamic_slice_in_dim(pair, place * half, half, 2)
    pair = mine.astype(F32) + theirs.astype(F32)
    grad_keys, grad_values = pair[0], pair[1]

    def prepare(query_in, key_in, gain_in):
        return qk_prepare(query_in, key_in, gain_in, cosine, sine)

    unused_pair, prepare_pull = jax.vjp(prepare, query_raw, key_raw, gains)
    grad_query_raw, grad_key_raw, gains_grad = prepare_pull(
        (grad_queries.reshape(-1, HEADS, HD), grad_keys.reshape(-1, HEADS, HD))
    )
    grad_projected = jnp.concatenate(
        [grad_query_raw, grad_key_raw, grad_values.reshape(-1, width)], axis=1
    ).astype(BF16)
    grad_lifted1 = dense_back(grad_projected, triple)
    normed_first, first_pull = jax.vjp(layer_norm, flat)
    grad_flat = grad_resid + first_pull(grad_lifted1 * (1.0 + scale1))[0]
    grad_modulation = jnp.concatenate(
        [
            grad_lifted1,
            grad_lifted1 * normed_first,
            grad_resid * attended,
            grad_lifted2,
            grad_lifted2 * normed_second,
            grad_out * feed,
        ],
        axis=1,
    ).astype(BF16)
    factors = (
        (lifted1, grad_projected),
        (mixed_low, grad_attended),
        (lifted2, grad_expanded),
        (hidden, grad_feed),
    )
    return (grad_flat, grad_modulation, factors, gains_grad)


def meet_sibling():
    barrier = pltpu.get_barrier_semaphore()
    sibling = (lax.axis_index("dp"), 1 - lax.axis_index("ctx"))
    pl.semaphore_signal(barrier, inc=1, device_id=sibling, device_id_type=MESH)
    pl.semaphore_wait(barrier, 1)
    return sibling


def head_sum_matrix(width):
    channel = lax.broadcasted_iota(jnp.int32, (width, 128), 0)
    head = lax.broadcasted_iota(jnp.int32, (width, 128), 1)
    inside = (channel >= head * HD) & (channel < (head + 1) * HD)
    return jnp.where(inside, 1.0, 0.0).astype(F32)


def exact_dot(left, right):
    return jnp.dot(left, right, preferred_element_type=F32, precision=lax.Precision.HIGHEST)


def spread_heads(values, heads):
    return lax.dot_general(
        values,
        heads,
        (((1,), (1,)), ((), ())),
        preferred_element_type=F32,
        precision=lax.Precision.HIGHEST,
    )


def swap_pairs(values):
    width = values.shape[1]
    lane = lax.broadcasted_iota(jnp.int32, values.shape, 1)
    quarter = HD // 4
    early = lax.rem(lane, 2 * quarter) < quarter
    return jnp.where(
        early, pltpu.roll(values, width - quarter, 1), pltpu.roll(values, quarter, 1)
    )


def normalize(values):
    mean = jnp.mean(values, axis=1, keepdims=True)
    center = values - mean
    spread = jnp.mean(center * center, axis=1, keepdims=True)
    inverse = lax.rsqrt(spread + 1e-06)
    return center * inverse, inverse


def norm_back(normed, inverse, grad):
    mean = jnp.mean(grad, axis=1, keepdims=True)
    along = jnp.mean(grad * normed, axis=1, keepdims=True)
    return (grad - mean - normed * along) * inverse


def window(h, width):
    first = min((h * HD) // 128 * 128, width - 256)
    return first, h * HD - first


def head_mask(h, width, rows):
    first, at = window(h, width)
    lane = lax.broadcasted_iota(jnp.int32, (rows, 256), 1)
    return (lane >= at) & (lane < at + HD)


def turned(values):
    tokens, width = values.shape
    rows = values.T.reshape(-1, ROWS, tokens)
    return jnp.concatenate(
        [rows, jnp.zeros((width // ROWS, PADDED - ROWS, tokens), F32)], axis=1
    ).astype(BF16)


FF_TILE = 768
KV_TILE = 1152


def allowed_mask(seg_q, seg_k, pad_k, half):
    place_q = lax.axis_index("ctx") * half + lax.broadcasted_iota(jnp.int32, (half, 2 * half), 0)
    place_k = lax.broadcasted_iota(jnp.int32, (half, 2 * half), 1)
    return (seg_q[...] == seg_k[...]) & ((pad_k[...] == 0) | (place_q == place_k))


MOD_TILE = 768


def weight_tiles(weight, held, sem):
    tiles = []
    for t in range(weight.shape[1] // MOD_TILE):
        span = slice(t * MOD_TILE, (t + 1) * MOD_TILE)
        copy = pltpu.make_async_copy(
            weight.at[:, pl.ds(t * MOD_TILE, MOD_TILE)],
            held.at[:, pl.ds(t * MOD_TILE, MOD_TILE)],
            sem.at[t],
        )
        copy.start()
        tiles.append((span, copy))
    return tiles


def modulation_kernel(block, valid, cond, offset, weight, mod, before, latent, xt, held, sem):
    tiles = weight_tiles(weight, held, sem)
    kept = block[...] * valid[...]
    latent[...] = kept.astype(BF16)
    total = kept + cond[...]
    before[...] = total
    act = (total * jax.nn.sigmoid(total)).astype(BF16)
    xt[...] = turned(act.astype(F32))
    for span, copy in tiles:
        copy.wait()
        part = jnp.dot(act, held[:, span], preferred_element_type=F32)
        mod[:, span] = part + offset[:, span]


def modulation_back_kernel(grad, valid, before, weight, out, held, sem):
    tiles = weight_tiles(weight, held, sem)
    out[...] = jnp.zeros_like(out)
    for span, copy in tiles:
        copy.wait()
        out[...] = out[...] + dense_back(grad[:, span], held[:, span])
    sig = jax.nn.sigmoid(before[...])
    out[...] = valid[...] * (out[...] * (sig * (1.0 + before[...] * (1.0 - sig))))


def modulation_call(kernel, name, inputs, weight, outs):
    in_vmem = pl.BlockSpec(memory_space=pltpu.VMEM)
    return pl.pallas_call(
        kernel,
        name=name,
        out_shape=outs,
        in_specs=[in_vmem] * len(inputs) + [ANY],
        out_specs=[in_vmem] * len(outs),
        scratch_shapes=[pltpu.VMEM(weight.shape, BF16), DMA((weight.shape[1] // MOD_TILE,))],
        compiler_params=pltpu.CompilerParams(vmem_limit_bytes=62 * 1024 * 1024),
    )(*inputs, weight)


def decoder_modulation_of(block, valid, cond, offset, weight):
    rows, width = block.shape
    outs = [
        jax.ShapeDtypeStruct((rows, weight.shape[1]), F32),
        jax.ShapeDtypeStruct((rows, width), F32),
        jax.ShapeDtypeStruct((rows, width), BF16),
        jax.ShapeDtypeStruct((16, PADDED, rows), BF16),
    ]
    inputs = (block, valid, cond, offset.reshape(1, -1))
    return modulation_call(modulation_kernel, "modulation", inputs, weight, outs)


def modulation_back(grad, valid, before, weight):
    outs = [jax.ShapeDtypeStruct(before.shape, F32)]
    return modulation_call(
        modulation_back_kernel, "modulation_back", (grad, valid, before), weight, outs
    )[0]


class A(enum.IntEnum):
    flat = 1
    mod = 2
    gains = 3
    cosine = 4
    sine = 5
    seg_q = 6
    seg_k = 7
    pad_k = 8
    triple = 9
    mixing = 10
    expand = 11
    reduce = 12
    output = 13
    raw = 14
    queries = 15
    kv = 16
    lse = 17
    attended = 18
    resid = 19
    expanded = 20
    feed = 21
    xt1 = 22
    xtm = 23
    xt2 = 24
    xth0 = 25
    xth1 = 26
    xth2 = 27
    lift = 28
    grad_out = 29
    grad_flat = 30
    grad_mod = 31
    grad_feed = 32
    grad_expanded = 33
    grad_attended = 34
    grad_projected = 35
    gains_grad = 36
    grad_v = 38
    outgoing = 39
    incoming = 40
    marks = 41
    mark_sums = 42


class Traffic:
    def __init__(self, held, sources, targets, lsem, ssem):
        self.held = held
        names = [n for n in sources]
        self.loads = {
            n: pltpu.make_async_copy(sources[n], held[n], lsem.at[k]) for k, n in enumerate(names)
        }
        self.sources = sources
        self.tiles = {}
        self.more = None
        self.stores = {
            n: pltpu.make_async_copy(held[n], targets[n], ssem.at[k])
            for k, n in enumerate(targets)
        }
        self.waiting = set(names)

    def __getattr__(self, name):
        return self.held[A[name]]

    def fetch(self, *names):
        for n in names:
            if n in self.loads:
                self.loads[n].start()

    def fetch_tile(self, size, rows, columns, sem, t):
        spans = [(n, (pl.ds(t * size, size), slice(None))) for n in rows]
        for n in columns:
            for first in (0, self.held[n].shape[1] // 2):
                spans.append((n, (slice(None), pl.ds(first + t * size, size))))
        self.tiles[t] = [
            pltpu.make_async_copy(self.sources[n].at[at], self.held[n].at[at], sem.at[t, k])
            for k, (n, at) in enumerate(spans)
        ]
        for copy in self.tiles[t]:
            copy.start()
        self.waiting.difference_update(rows + columns)

    def need_tile(self, t):
        for copy in self.tiles.pop(t, ()):
            copy.wait()

    def need(self, *names):
        for n in names:
            if n in self.waiting:
                self.loads[n].wait()
                self.waiting.discard(n)

    def emit(self, *names):
        for n in names:
            if n in self.stores:
                self.stores[n].start()

    def close(self):
        for store in self.stores.values():
            store.wait()


def forward_body(r, sibling, ssem, rsem):
    half, width = r.flat.shape
    c = lax.axis_index("ctx")
    mine = pl.ds(pl.multiple_of(c * half, 128), half)
    theirs = pl.ds(pl.multiple_of((1 - c) * half, 128), half)
    hidden_size = r.reduce.shape[0]

    def part(k):
        return r.mod[:, k * width : (k + 1) * width]

    r.need(A.flat, A.mod)
    normed, unused = normalize(r.flat[...])
    lifted_low = (normed * (1.0 + part(1)) + part(0)).astype(BF16)
    r.need(A.triple)
    r.fetch(A.mixing, A.expand, A.reduce)
    heads = head_sum_matrix(width)

    def prepared(k):
        values = r.raw[:, k * width : (k + 1) * width]
        mean = exact_dot(values * values, heads) * (1.0 / HD)
        scaled = values * spread_heads(lax.rsqrt(mean + 1e-06), heads) * r.gains[k : k + 1, :]
        return scaled * r.cosine[...] + swap_pairs(scaled) * r.sine[...]

    def project(k):
        return jnp.dot(
            lifted_low, r.triple[:, k * width : (k + 1) * width], preferred_element_type=F32
        )

    r.raw[:, width:] = project(1)
    r.need(A.gains, A.cosine, A.sine)
    r.kv[0, mine] = prepared(1).astype(BF16)
    r.kv[1, mine] = project(2).astype(BF16)
    share = pltpu.make_async_remote_copy(
        r.kv.at[:, mine], r.kv.at[:, mine], ssem.at[0], rsem.at[0], device_id=sibling,
        device_id_type=MESH,
    )
    share.start()
    r.raw[:, :width] = project(0)
    r.emit(A.raw)
    r.queries[...] = prepared(0).astype(BF16)
    r.emit(A.queries)
    r.xt1[...] = turned(lifted_low.astype(F32))
    r.emit(A.xt1)
    r.need(A.seg_q, A.seg_k, A.pad_k)
    allowed = allowed_mask(r.seg_q, r.seg_k, r.pad_k, half)
    r.lift[...] = jnp.zeros_like(r.lift)
    lane = lax.broadcasted_iota(jnp.int32, (half, 128), 1)
    sums = jnp.zeros((half, 128), F32)
    pltpu.make_async_remote_copy(
        r.kv.at[:, theirs], r.kv.at[:, theirs], ssem.at[0], rsem.at[0], device_id=sibling,
        device_id_type=MESH,
    ).wait_recv()
    r.emit(A.kv)
    for h in range(width // HD):
        first, unused = window(h, width)
        span = slice(first, first + 256)
        mask = head_mask(h, width, half)
        query = jnp.where(mask, r.queries[:, span].astype(F32), 0.0).astype(BF16)
        scores = dense_back(query, r.kv[0, :, span]) * (1.0 / math.sqrt(HD))
        scores = jnp.where(allowed, scores, -1e30)
        top = jnp.max(scores, axis=1, keepdims=True)
        raised = jnp.exp(scores - top)
        total = jnp.sum(raised, axis=1, keepdims=True)
        low = (raised / total).astype(BF16)
        out = jnp.dot(low, r.kv[1, :, span], preferred_element_type=F32)
        r.lift[:, span] = r.lift[:, span] + jnp.where(mask, out, 0.0)
        sums = jnp.where(lane == h, top + jnp.log(total), sums)
    r.lse[...] = sums
    r.emit(A.lse)
    mixed_low = r.lift[...].astype(BF16)
    r.xtm[...] = turned(mixed_low.astype(F32))
    r.emit(A.xtm)
    r.need(A.mixing)
    r.attended[...] = jnp.dot(mixed_low, r.mixing[...], preferred_element_type=F32)
    r.emit(A.attended)
    r.resid[...] = r.flat[...] + part(2) * r.attended[...]
    r.emit(A.resid)
    normed, unused = normalize(r.resid[...])
    lifted_low = (normed * (1.0 + part(4)) + part(3)).astype(BF16)
    r.xt2[...] = turned(lifted_low.astype(F32))
    r.emit(A.xt2)
    r.feed[...] = jnp.zeros_like(r.feed)
    r.need(A.expand, A.reduce)
    xth = (r.xth0, r.xth1, r.xth2)
    for g in range(3):
        xth[g][...] = jnp.zeros_like(xth[g])
    for t in range(hidden_size // FF_TILE):
        one = slice(t * FF_TILE, (t + 1) * FF_TILE)
        two = slice(hidden_size + t * FF_TILE, hidden_size + (t + 1) * FF_TILE)
        gate = jnp.dot(lifted_low, r.expand[:, one], preferred_element_type=F32)
        up = jnp.dot(lifted_low, r.expand[:, two], preferred_element_type=F32)
        r.expanded[:, one] = gate
        r.expanded[:, two] = up
        hidden = (gate * jax.nn.sigmoid(gate) * up).astype(BF16)
        pieces = hidden.astype(F32).T.astype(BF16).reshape(FF_TILE // 192, 3, 64, half)
        for g in range(3):
            xth[g][t * (FF_TILE // 192) : (t + 1) * (FF_TILE // 192), :64] = pieces[:, g]
        r.feed[...] = r.feed[...] + jnp.dot(hidden, r.reduce[one], preferred_element_type=F32)
    r.emit(A.expanded, A.feed, A.xth0, A.xth1, A.xth2)
    r.output[...] = r.resid[...] + part(5) * r.feed[...]
    r.emit(A.output)
    share.wait_send()


def backward_body(r, sibling, ssem, rsem):
    half, width = r.flat.shape
    c = lax.axis_index("ctx")
    mine = pl.ds(pl.multiple_of(c * half, 128), half)
    theirs = pl.ds(pl.multiple_of((1 - c) * half, 128), half)
    hidden_size = r.reduce.shape[0]

    def part(k):
        return r.mod[:, k * width : (k + 1) * width]

    def keep(k, values):
        r.grad_mod[:, k * width : (k + 1) * width] = values.astype(BF16)

    r.need(A.grad_out, A.feed, A.mod)
    keep(5, r.grad_out[...] * r.feed[...])
    feed_low = (r.grad_out[...] * part(5)).astype(BF16)
    r.grad_feed[...] = feed_low
    r.emit(A.grad_feed)
    r.lift[...] = jnp.zeros_like(r.lift)
    for t in range(hidden_size // FF_TILE):
        r.need_tile(t)
        if r.more and t + 2 < hidden_size // FF_TILE:
            r.more(t + 2)
        if t == 2:
            r.fetch(A.attended, A.resid, A.mixing, A.queries, A.kv, A.lse, A.raw, A.flat, A.triple)
        one = slice(t * FF_TILE, (t + 1) * FF_TILE)
        two = slice(hidden_size + t * FF_TILE, hidden_size + (t + 1) * FF_TILE)
        grad_hidden = dense_back(feed_low, r.reduce[one])
        gate = r.expanded[:, one]
        up = r.expanded[:, two]
        sig = jax.nn.sigmoid(gate)
        grad_gate = (grad_hidden * up * (sig * (1.0 + gate * (1.0 - sig)))).astype(BF16)
        grad_up = (grad_hidden * (gate * sig)).astype(BF16)
        r.grad_expanded[:, one] = grad_gate
        r.grad_expanded[:, two] = grad_up
        r.lift[...] = r.lift[...] + dense_back(grad_gate, r.expand[:, one])
        r.lift[...] = r.lift[...] + dense_back(grad_up, r.expand[:, two])
    r.emit(A.grad_expanded)
    r.need(A.resid, A.attended)
    normed, inverse = normalize(r.resid[...])
    keep(3, r.lift[...])
    keep(4, r.lift[...] * normed)
    grad_resid = r.grad_out[...] + norm_back(normed, inverse, r.lift[...] * (1.0 + part(4)))
    keep(2, grad_resid * r.attended[...])
    if A.output in r.stores:
        r.stores.pop(A.output).wait()
    r.grad_flat[...] = grad_resid
    attended_low = (grad_resid * part(2)).astype(BF16)
    r.grad_attended[...] = attended_low
    r.emit(A.grad_attended)
    r.need(A.mixing)
    r.lift[...] = dense_back(attended_low, r.mixing[...])
    r.need(A.seg_q, A.seg_k, A.pad_k, A.queries, A.kv, A.lse)
    allowed = allowed_mask(r.seg_q, r.seg_k, r.pad_k, half)
    r.feed[...] = jnp.zeros_like(r.feed)
    r.resid[...] = jnp.zeros_like(r.resid)
    r.attended[...] = jnp.zeros_like(r.attended)
    r.grad_v[...] = jnp.zeros_like(r.grad_v)
    scale = 1.0 / math.sqrt(HD)
    lane = lax.broadcasted_iota(jnp.int32, (half, 128), 1)
    for h in range(width // HD):
        first, unused = window(h, width)
        span = slice(first, first + 256)
        mask = head_mask(h, width, half)
        query = jnp.where(mask, r.queries[:, span].astype(F32), 0.0).astype(BF16)
        grad_mixed = jnp.where(mask, r.lift[:, span], 0.0).astype(BF16)
        scores = dense_back(query, r.kv[0, :, span]) * scale
        logsum = jnp.sum(jnp.where(lane == h, r.lse[...], 0.0), axis=1, keepdims=True)
        chances = jnp.exp(jnp.where(allowed, scores, -1e30) - logsum)
        grad_chances = dense_back(grad_mixed, r.kv[1, :, span])
        along = jnp.sum(chances * grad_chances, axis=1, keepdims=True)
        scores_low = (chances * (grad_chances - along)).astype(BF16)
        out = jnp.dot(scores_low, r.kv[0, :, span], preferred_element_type=F32)
        r.feed[:, span] = r.feed[:, span] + jnp.where(mask, out, 0.0)
        part_k = outer_sum(scores_low, query)
        r.resid[:, span] = r.resid[:, span] + part_k[:half]
        r.attended[:, span] = r.attended[:, span] + part_k[half:]
        r.grad_v[:, span] = r.grad_v[:, span] + outer_sum(chances.astype(BF16), grad_mixed)
    their_k = jnp.where(c == 0, r.attended[...], r.resid[...])
    r.outgoing[0] = (their_k * scale).astype(BF16)
    r.outgoing[1] = r.grad_v[theirs, :].astype(BF16)
    share = pltpu.make_async_remote_copy(
        r.outgoing, r.incoming, ssem.at[1], rsem.at[1], device_id=sibling, device_id_type=MESH
    )
    share.start()
    heads = head_sum_matrix(width)
    r.need(A.raw, A.gains, A.cosine, A.sine)

    def prepare_back(k, grad):
        values = r.raw[:, k * width : (k + 1) * width]
        gain = r.gains[k : k + 1, :]
        mean = exact_dot(values * values, heads) * (1.0 / HD)
        inverse = spread_heads(lax.rsqrt(mean + 1e-06), heads)
        scaled = values * inverse
        turned_back = grad * r.cosine[...] + swap_pairs(grad * r.sine[...])
        r.gains_grad[k : k + 1, :] = jnp.sum(turned_back * scaled, axis=0, keepdims=True)
        turned_back = turned_back * gain
        along = spread_heads(exact_dot(turned_back * scaled, heads) * (1.0 / HD), heads)
        return (turned_back - scaled * along) * inverse

    r.grad_projected[:, :width] = prepare_back(0, r.feed[...] * scale).astype(BF16)
    r.need(A.triple)
    total = dense_back(r.grad_projected[:, :width], r.triple[:, :width])
    share.wait()
    own_k = jnp.where(c == 0, r.resid[...], r.attended[...]) * scale
    own_k = own_k.astype(BF16).astype(F32) + r.incoming[0].astype(F32)
    own_v = r.grad_v[mine, :].astype(BF16).astype(F32) + r.incoming[1].astype(F32)
    r.grad_projected[:, width : 2 * width] = prepare_back(1, own_k).astype(BF16)
    r.grad_projected[:, 2 * width :] = own_v.astype(BF16)
    r.emit(A.grad_projected, A.gains_grad)
    for k in (1, 2):
        span = slice(k * width, (k + 1) * width)
        total = total + dense_back(r.grad_projected[:, span], r.triple[:, span])
    r.need(A.flat)
    normed, inverse = normalize(r.flat[...])
    keep(0, total)
    keep(1, total * normed)
    r.emit(A.grad_mod)
    r.need(A.marks)
    for k in range(6):
        span = slice(k * width, (k + 1) * width)
        r.mark_sums[:, span] = jnp.dot(
            r.marks[...], r.grad_mod[:, span], preferred_element_type=F32
        )
    r.emit(A.mark_sums)
    r.grad_flat[...] = r.grad_flat[...] + norm_back(normed, inverse, total * (1.0 + part(1)))
    r.emit(A.grad_flat)


def block_shapes(half, width, hidden_size):
    rows = ((16, PADDED, half), BF16)
    token = ((half, width), F32)
    low = ((half, width), BF16)
    return {
        A.flat: token,
        A.mod: ((half, 6 * width), F32),
        A.gains: ((2, width), F32),
        A.cosine: token,
        A.sine: token,
        A.seg_q: ((half, 1), jnp.int32),
        A.seg_k: ((1, 2 * half), jnp.int32),
        A.pad_k: ((1, 2 * half), jnp.int32),
        A.triple: ((width, 3 * width), BF16),
        A.mixing: ((width, width), BF16),
        A.expand: ((width, 2 * hidden_size), BF16),
        A.reduce: ((hidden_size, width), BF16),
        A.output: token,
        A.raw: ((half, 2 * width), F32),
        A.queries: low,
        A.kv: ((2, 2 * half, width), BF16),
        A.lse: ((half, 128), F32),
        A.attended: token,
        A.resid: token,
        A.expanded: ((half, 2 * hidden_size), F32),
        A.feed: token,
        A.xt1: rows,
        A.xtm: rows,
        A.xt2: rows,
        A.xth0: rows,
        A.xth1: rows,
        A.xth2: rows,
        A.lift: token,
        A.grad_out: token,
        A.grad_flat: token,
        A.grad_mod: ((half, 6 * width), BF16),
        A.grad_feed: low,
        A.grad_expanded: ((half, 2 * hidden_size), BF16),
        A.grad_attended: low,
        A.grad_projected: ((half, 3 * width), BF16),
        A.gains_grad: ((2, width), F32),
        A.grad_v: ((2 * half, width), F32),
        A.outgoing: ((2, half, width), BF16),
        A.incoming: ((2, half, width), BF16),
        A.marks: ((8, half), BF16),
        A.mark_sums: ((8, 6 * width), F32),
    }


WEIGHTS = (A.triple, A.mixing, A.expand, A.reduce)
GIVEN = (A.gains, A.cosine, A.sine, A.seg_q, A.seg_k, A.pad_k) + WEIGHTS
SAVED = (A.raw, A.queries, A.kv, A.lse, A.attended, A.resid, A.expanded, A.feed)
LEFTS = (A.xt1, A.xtm, A.xt2, A.xth0, A.xth1, A.xth2)
GRADS = (
    A.grad_flat, A.grad_mod, A.grad_feed, A.grad_expanded, A.grad_attended, A.grad_projected,
    A.gains_grad, A.mark_sums,
)
WORK = (A.grad_v, A.outgoing, A.incoming)
EARLY = (A.gains, A.cosine, A.sine, A.seg_q, A.seg_k, A.pad_k)
PLANS = {
    "forward": ((A.flat, A.mod) + GIVEN, (A.output,) + SAVED + LEFTS, (A.lift,)),
    "backward": ((A.grad_out, A.marks, A.flat, A.mod) + GIVEN + SAVED, GRADS, (A.lift,) + WORK),
    "both": ((A.grad_out, A.marks, A.flat, A.mod) + GIVEN, (A.output,) + LEFTS + GRADS, SAVED + (A.lift,) + WORK),
}


def held_names(kind):
    inputs, outputs, others = PLANS[kind]
    names = inputs + outputs + others
    return tuple(n for n in names if kind != "both" or n != A.output)


def block_kernel(kind, *refs):
    inputs, outputs, others = PLANS[kind]
    sources = dict(zip(inputs, refs))
    targets = dict(zip(outputs, refs[len(inputs) :]))
    names = held_names(kind)
    held = dict(zip(names, refs[len(inputs) + len(outputs) :]))
    if kind == "both":
        held[A.output] = held[A.grad_flat]
    lsem, wsem, tsem, ssem, rsem = refs[len(inputs) + len(outputs) + len(names) :]
    r = Traffic(held, sources, targets, lsem, wsem)
    if kind == "backward":
        r.fetch(A.grad_out, A.feed, A.mod, A.marks, *EARLY)
        r.more = functools.partial(r.fetch_tile, FF_TILE, (A.reduce,), (A.expanded, A.expand), tsem)
        r.more(0)
        r.more(1)
    else:
        r.fetch(A.flat, A.mod, A.triple, *EARLY)
    sibling = meet_sibling()
    if kind != "backward":
        forward_body(r, sibling, ssem, rsem)
    if kind == "both":
        r.fetch(A.grad_out, A.marks)
        r.loads = {n: r.loads[n] for n in (A.grad_out, A.marks)}
    if kind != "forward":
        backward_body(r, sibling, ssem, rsem)
    r.close()


def run_block(kind, values, name):
    inputs, outputs, others = PLANS[kind]
    half, width = values[A.flat].shape
    table = block_shapes(half, width, values[A.reduce].shape[0])
    names = held_names(kind)
    results = pl.pallas_call(
        functools.partial(block_kernel, kind),
        name=name,
        out_shape=[jax.ShapeDtypeStruct(*table[n]) for n in outputs],
        in_specs=[ANY] * len(inputs),
        out_specs=[ANY] * len(outputs),
        scratch_shapes=[pltpu.VMEM(*table[n]) for n in names]
        + [DMA((len(inputs),)), DMA((len(outputs),)), DMA((4, 5)), DMA((2,)), DMA((2,))],
        compiler_params=pltpu.CompilerParams(
            collective_id={"forward": 5, "backward": 6, "both": 7}[kind],
            has_side_effects=True,
            vmem_limit_bytes=63 * 1024 * 1024,
        ),
    )(*[values[n] for n in inputs])
    return dict(zip(outputs, results))


def split_kernel(pieces, in_ref, *refs):
    *outs, held, arrived, left = refs
    for k, (n, row, rows, columns, at) in enumerate(pieces):
        span = (pl.ds(0, rows), pl.ds(at, columns))
        pltpu.make_async_copy(in_ref.at[span], held.at[span], arrived.at[k]).start()

    def leave(k):
        n, row, rows, columns, at = pieces[k]
        span = (pl.ds(0, rows), pl.ds(at, columns))
        return pltpu.make_async_copy(held.at[span], outs[n].at[pl.ds(row, rows), :], left.at[k])

    for k, (n, row, rows, columns, at) in enumerate(pieces):
        span = (pl.ds(0, rows), pl.ds(at, columns))
        pltpu.make_async_copy(in_ref.at[span], held.at[span], arrived.at[k]).wait()
        leave(k).start()
    for k in range(len(pieces)):
        leave(k).wait()


def split(values, shapes, pieces):
    return pl.pallas_call(
        functools.partial(split_kernel, tuple(pieces)),
        name="split",
        out_shape=[jax.ShapeDtypeStruct(shape, values.dtype) for shape in shapes],
        in_specs=[ANY],
        out_specs=[ANY] * len(shapes),
        scratch_shapes=[
            pltpu.VMEM(values.shape, values.dtype),
            DMA((len(pieces),)),
            DMA((len(pieces),)),
        ],
        compiler_params=pltpu.CompilerParams(vmem_limit_bytes=62 * 1024 * 1024),
    )(values)


def rope_lanes(cosine, sine):
    tokens = cosine.shape[0]

    def lanes(table, signs):
        table = jnp.stack([signs[0] * table, signs[1] * table], axis=2).reshape(tokens, 1, HD)
        return jnp.broadcast_to(table, (tokens, HEADS, HD)).reshape(tokens, HEADS * HD)

    return lanes(cosine, (1.0, 1.0)), lanes(sine, (-1.0, 1.0))


def fast_reduce(blocks, rows, collective_id, name):
    xts = []
    dys = []
    source = []
    for factors, extra in blocks:
        for lefts, right in factors:
            source += [len(dys)] * len(lefts)
            xts += lefts
            dys.append(right)
        tokens = right.shape[0]
        lines = -(-extra.shape[1] // tokens)
        packed = jnp.pad(extra, ((0, 0), (0, lines * tokens - extra.shape[1])))
        packed = packed.reshape(16, lines, tokens).astype(BF16)
        xts.append(jnp.pad(packed, ((0, 0), (0, PADDED - lines), (0, 0))))
        source.append(len(dys))
        dys.append(jnp.eye(tokens, UNIT, dtype=BF16))
    out, rows = scatter(xts, dys, source, rows, collective_id, name)
    shapes = []
    pieces = []
    smalls = []
    at = 0
    for factors, extra in blocks:
        for lefts, right in factors[:-1]:
            pieces.append((len(shapes), 0, ROWS, right.shape[1], at))
            shapes.append((ROWS, right.shape[1]))
            at += right.shape[1]
        width = factors[-1][1].shape[1]
        for g in range(3):
            pieces.append((len(shapes), 64 * g, 64, width, at))
            at += width
        shapes.append((192, width))
        lines = -(-extra.shape[1] // tokens)
        smalls.append(out[:lines, at : at + tokens].reshape(-1)[: extra.shape[1]])
        at += UNIT
    grads = split(out, shapes, pieces)
    results = []
    for (factors, extra), small in zip(blocks, smalls):
        results.append((grads[: len(factors)], small))
        grads = grads[len(factors) :]
    return results, rows


def whole_rows(gathered):
    return gathered.reshape((-1,) + gathered.shape[4:])


def fast_step(flat, cotangent, context, segment_local, valid, timesteps, encoder, decoder):
    width = flat.shape[1]
    offset_size = encoder[1].shape[0]
    gain_size = 2 * encoder[3].shape[1]
    small = jnp.concatenate(
        [
            encoder[1].astype(F32),
            decoder[1].astype(F32),
            encoder[3].astype(F32).reshape(-1),
            decoder[3].astype(F32).reshape(-1),
            timesteps.astype(F32).reshape(-1),
        ]
    )
    size = small.shape[0]
    small = jnp.pad(small, (0, 2048 - size)).reshape(16, 128)
    small = exchange(small, 0, "small").reshape(16, -1)
    encoder_offset = small[:, :offset_size].reshape(-1)
    decoder_offset = small[:, offset_size : 2 * offset_size].reshape(-1)
    at = 2 * offset_size
    encoder_gains = small[:, at : at + gain_size].reshape(16, 2, -1).swapaxes(0, 1).reshape(2, -1)
    at += gain_size
    decoder_gains = small[:, at : at + gain_size].reshape(16, 2, -1).swapaxes(0, 1).reshape(2, -1)
    at += gain_size
    all_times = small[:, at : at + timesteps.size]
    segments = timesteps.shape[1]
    picks = (segment_local[..., None] == jnp.arange(segments, dtype=jnp.int32)).astype(F32)
    picks = picks.reshape(-1, segments)

    all_cond = embed_times(all_times, width).reshape(-1, width)
    act_rows = jax.nn.silu(all_cond).astype(BF16)
    me = lax.axis_index("dp")
    rows = encoder[0].shape[0]
    act_mine = lax.dynamic_slice_in_dim(act_rows, me * rows, rows, 1)
    core = lax.axis_index("ctx")
    share = encoder[0].shape[1] // 2
    partial = dense(act_mine, lax.dynamic_slice_in_dim(encoder[0], core * share, share, 1))
    partial = partial.reshape(GRID + (8, -1))
    shards = (encoder[2], encoder[4], encoder[5], encoder[6])
    shards += (decoder[0], decoder[2], decoder[4], decoder[5], decoder[6])
    *wholes, partial = gather(shards, partial, *gather_units(shards), 1, "gather")
    wholes = [whole_rows(w) for w in wholes]
    encoder_weights = (*wholes[:4], encoder_gains)
    modulate = wholes[4]
    decoder_weights = (*wholes[5:], decoder_gains)
    partial = jnp.sum(partial, axis=0).reshape(segments, -1)
    others = lax.ppermute(partial, "ctx", [(0, 1), (1, 0)])
    modulation_rows = jnp.where(
        core == 0,
        jnp.concatenate([partial, others], axis=1),
        jnp.concatenate([others, partial], axis=1),
    )
    modulation_rows = modulation_rows + encoder_offset

    def pick(rows):
        return sum(jnp.where(picks[:, j : j + 1] > 0, rows[j], 0.0) for j in range(segments))

    encoder_modulation = pick(modulation_rows)
    cond_rows = lax.dynamic_slice_in_dim(all_cond, me * segments, segments, 0)
    cond = pick(cond_rows)

    shared = {**dict(zip(EARLY[1:], context)), A.flat: flat}
    encoder_in = {**dict(zip(WEIGHTS + EARLY[:1], encoder_weights)), **shared}
    encoder_in[A.mod] = encoder_modulation
    forward = run_block("forward", encoder_in, "encoder")
    decoder_modulation, decoder_pre, latent, act_xt = decoder_modulation_of(
        forward[A.output], valid, cond, decoder_offset, modulate
    )
    decoder_in = {**dict(zip(WEIGHTS + EARLY[:1], decoder_weights)), **shared}
    decoder_in[A.mod] = decoder_modulation
    decoder_in[A.grad_out] = valid * cotangent
    decoder_in[A.marks] = jnp.ones((8, flat.shape[0]), BF16)
    both = run_block("both", decoder_in, "decoder")
    velocity = valid * both[A.output]

    def pair_up(lefts, grads):
        return (
            ([lefts[A.xt1]], grads[A.grad_projected]),
            ([lefts[A.xtm]], grads[A.grad_attended]),
            ([lefts[A.xt2]], grads[A.grad_expanded]),
            ([lefts[A.xth0], lefts[A.xth1], lefts[A.xth2]], grads[A.grad_feed]),
        )

    factors = pair_up(both, both)
    grad_modulation = both[A.grad_mod]
    gains_grad = both[A.gains_grad]
    grad_latent = modulation_back(grad_modulation, valid, decoder_pre, modulate)
    offset_grad = both[A.mark_sums][0]
    extra = jnp.concatenate(
        [
            offset_grad.reshape(16, -1),
            gains_grad.reshape(2, 16, -1).swapaxes(0, 1).reshape(16, -1),
        ],
        axis=1,
    )
    first = ([act_xt], grad_modulation)
    decoder_block = ((factors[1], factors[0], factors[2], first, factors[3]), extra)

    encoder_in[A.grad_out] = grad_latent
    encoder_in[A.marks] = jnp.pad(picks.T, ((0, 8 - segments), (0, 0))).astype(BF16)
    backward = run_block("backward", {**encoder_in, **forward}, "encoder_back")
    factors = pair_up(forward, backward)
    grad_modulation = backward[A.grad_mod]
    gains_grad = backward[A.gains_grad]
    grad_rows = backward[A.mark_sums][:segments]
    grad_rows = grad_rows + lax.ppermute(grad_rows, "ctx", [(0, 1), (1, 0)])
    extra = gains_grad.reshape(2, 16, -1).swapaxes(0, 1).reshape(16, -1)
    results, all_rows = fast_reduce(
        (decoder_block, (factors, extra)), grad_rows.astype(BF16).reshape(16, -1), 2, "scatter"
    )
    (grads, small), (encoder_parts, encoder_small) = results
    decoder_grads = (
        grads[3],
        small[:offset_size],
        grads[1],
        small[offset_size:].reshape(2, -1),
        grads[0],
        grads[2],
        grads[4],
    )
    all_rows = all_rows.reshape(16 * segments, -1)
    modulate_grad = outer_sum(act_mine, all_rows)
    offset_grad = lax.dynamic_slice_in_dim(
        jnp.sum(all_rows.astype(F32), axis=0), me * offset_size, offset_size, 0
    )
    encoder_grads = (
        modulate_grad,
        offset_grad,
        encoder_parts[0],
        encoder_small.reshape(2, -1),
        encoder_parts[1],
        encoder_parts[2],
        encoder_parts[3],
    )
    token_grad = both[A.grad_flat] + backward[A.grad_flat]
    return velocity, latent, token_grad, encoder_grads, decoder_grads


def plain_gather(block):
    parts = [lax.all_gather(block[k], "dp", axis=0, tiled=True) for k in (0, 1, 2, 4, 5, 6)]
    gains = lax.all_gather(block[3], "dp", axis=1, tiled=True).astype(F32)
    modulate, offset, triple, mixing, expand, reduce_w = parts
    return modulate, offset.astype(F32), (triple, mixing, expand, reduce_w, gains)


def plain_reduce(factors, grad_modulation, gains_grad):
    def rows(values, dim=0):
        part = lax.psum_scatter(values, "dp", scatter_dimension=dim, tiled=True)
        return lax.psum(part.astype(BF16), "ctx").astype(F32)

    offset = rows(jnp.sum(grad_modulation, axis=0, dtype=F32))
    modulate, triple, mixing, expand, reduce_w = [rows(outer_sum(a, b)) for a, b in factors]
    return modulate, offset, triple, rows(gains_grad, 1), mixing, expand, reduce_w


def plain_step(flat, cotangent, context, segment_local, valid, timesteps, encoder, decoder):
    picks = (
        segment_local[..., None] == jnp.arange(timesteps.shape[-1], dtype=jnp.int32)
    ).astype(F32)
    times = jnp.sum(picks * timesteps[:, None, :].astype(F32), axis=-1)
    cond = embed_times(times, flat.shape[1]).reshape(flat.shape)
    modulate, offset, encoder_weights = plain_gather(encoder)
    encoder_act = jax.nn.silu(cond).astype(BF16)
    encoder_out, encoder_kept = block_forward(
        flat, dense(encoder_act, modulate) + offset, encoder_weights, context
    )
    latent_full = valid * encoder_out
    decoder_pre = latent_full + cond
    decoder_act = jax.nn.silu(decoder_pre).astype(BF16)
    modulate, offset, decoder_weights = plain_gather(decoder)
    decoder_out, decoder_kept = block_forward(
        flat, dense(decoder_act, modulate) + offset, decoder_weights, context
    )
    decoder_flat, grad_modulation, factors, gains_grad = block_backward(
        valid * cotangent, decoder_kept, decoder_weights, context
    )
    grad_act = dense_back(grad_modulation, modulate)
    decoder_grads = plain_reduce(
        ((decoder_act, grad_modulation),) + factors, grad_modulation, gains_grad
    )
    unused_silu, silu_pull = jax.vjp(jax.nn.silu, decoder_pre)
    encoder_flat, grad_modulation, factors, gains_grad = block_backward(
        valid * silu_pull(grad_act)[0], encoder_kept, encoder_weights, context
    )
    encoder_grads = plain_reduce(
        ((encoder_act, grad_modulation),) + factors, grad_modulation, gains_grad
    )
    return valid * decoder_out, latent_full, decoder_flat + encoder_flat, encoder_grads, decoder_grads


def local(fast, tokens, cotangent, segment, rows, columns, padding, timesteps, *weights):
    batch, half, width = tokens.shape
    start = lax.axis_index("ctx") * half
    segment_local = lax.dynamic_slice_in_dim(segment, start, half, 1)
    rows_local = lax.dynamic_slice_in_dim(rows, start, half, 1)
    columns_local = lax.dynamic_slice_in_dim(columns, start, half, 1)
    padding_local = lax.dynamic_slice_in_dim(padding, start, half, 1)
    place_query = start + jnp.arange(half, dtype=jnp.int32)
    place_key = jnp.arange(segment.shape[1], dtype=jnp.int32)
    allowed = (segment_local[:, :, None] == segment[:, None, :]) & (
        (padding[:, None, :] == 0) | (place_query[None, :, None] == place_key[None, None, :])
    )
    cosine, sine = rope_tables(rows_local.reshape(-1), columns_local.reshape(-1))
    context = (batch, half, allowed, cosine, sine)
    if fast:
        context = rope_lanes(cosine, sine)
        context += (segment_local.reshape(-1, 1), segment, padding)
    valid = (1 - padding_local).astype(F32).reshape(-1, 1)
    flat = tokens.reshape(-1, width).astype(F32)
    step = fast_step if fast else plain_step
    velocity, latent, token_grad, encoder_grads, decoder_grads = step(
        flat,
        cotangent.reshape(-1, width).astype(F32),
        context,
        segment_local,
        valid,
        timesteps,
        weights[:7],
        weights[7:],
    )
    return (
        velocity.astype(BF16).reshape(batch, half, width),
        latent.astype(BF16).reshape(batch, half, width),
        token_grad.reshape(batch, half, width),
        *encoder_grads,
        *decoder_grads,
    )


def solution(mesh):
    fast = dict(mesh.shape) == {"dp": math.prod(GRID), "ctx": 2}
    block = (
        P("dp", None),
        P("dp"),
        P("dp", None),
        P(None, "dp"),
        P("dp", None),
        P("dp", None),
        P("dp", None),
    )
    slots = P("dp", "ctx", None)
    return jax.shard_map(
        functools.partial(local, fast),
        mesh=mesh,
        in_specs=(slots, slots) + (P("dp", None),) * 5 + block + block,
        out_specs=(slots, slots, slots) + block + block,
        check_vma=False,
    )
```

```python
import enum
import functools
import math

import jax
import jax.numpy as jnp
from jax import lax
from jax.experimental import pallas as pl
from jax.experimental.pallas import tpu as pltpu
from jax.sharding import PartitionSpec as P

HEADS = 16
HD = 72
MESH = pl.DeviceIdType.MESH
GRID = (4, 2, 2)
BF16 = jnp.bfloat16
F32 = jnp.float32


def coords():
    dp = lax.axis_index("dp")
    return (lax.div(dp, 4), lax.rem(lax.div(dp, 2), 2), lax.rem(dp, 2), lax.axis_index("ctx"))


def device(z, y, x, c):
    return (z * 4 + y * 2 + x, c)


def when(cond, body):
    if cond is True:
        body()
    else:
        pl.when(cond)(body)


def greet():
    barrier = pltpu.get_barrier_semaphore()
    me = lax.axis_index("dp")
    c = lax.axis_index("ctx")
    for k in range(1, 16):
        pl.semaphore_signal(
            barrier, inc=1, device_id=(lax.rem(me + k, 16), c), device_id_type=MESH
        )
    pl.semaphore_signal(barrier, inc=1, device_id=(me, 1 - c), device_id_type=MESH)
    pl.semaphore_wait(barrier, 16)


class Exchange:
    def __init__(self, same, in_ref, out_ref, ssem, rsem, lsem):
        self.refs = (in_ref, out_ref, ssem, rsem, lsem)
        self.same = same
        self.me = lax.axis_index("dp")

    def source(self, target):
        return self.refs[0] if self.same else self.refs[0].at[target]

    def copy(self, k, target, slot):
        return pltpu.make_async_remote_copy(
            self.source(target),
            self.refs[1].at[slot],
            self.refs[2].at[k],
            self.refs[3].at[k],
            device_id=(target, lax.axis_index("ctx")),
            device_id_type=MESH,
        )

    def own(self):
        return pltpu.make_async_copy(
            self.source(self.me), self.refs[1].at[self.me], self.refs[4].at[0]
        )

    def start(self):
        for k in range(1, 16):
            self.copy(k, lax.rem(self.me + k, 16), self.me).start()
        self.own().start()

    def wait(self):
        self.own().wait()
        for k in range(1, 16):
            self.copy(k, lax.rem(self.me + k, 16), self.me).wait_send()
            origin = lax.rem(self.me + 16 - k, 16)
            self.copy(k, origin, origin).wait_recv()


class Sums:
    def __init__(self, in_ref, out_ref, box, total, ssem, rsem, lsem):
        self.refs = (in_ref, out_ref, box, total)
        self.sems = (ssem, rsem, lsem)
        self.z, self.y, self.x, self.c = coords()

    def remote(self, src, dst, k, target):
        return pltpu.make_async_remote_copy(
            src,
            dst,
            self.sems[0].at[k],
            self.sems[1].at[k],
            device_id=target,
            device_id_type=MESH,
        )

    def across(self, k):
        y = lax.rem(self.y + k // 2, 2)
        x = lax.rem(self.x + k % 2, 2)
        target = device(self.z, y, x, self.c)
        return self.remote(self.refs[0].at[:, y, x], self.refs[2].at[k], k, target)

    def own(self):
        return pltpu.make_async_copy(
            self.refs[0].at[:, self.y, self.x], self.refs[2].at[0], self.sems[2].at[0]
        )

    def along(self, k, arrival):
        there = lax.rem(self.z + (4 - k if arrival else k), 4)
        slot = there if arrival else self.z
        target = device(there, self.y, self.x, self.c)
        return self.remote(self.refs[3].at[there], self.refs[1].at[slot], 3 + k, target)

    def kept(self):
        return pltpu.make_async_copy(
            self.refs[3].at[self.z], self.refs[1].at[self.z], self.sems[2].at[1]
        )

    def start(self):
        for k in range(1, 4):
            self.across(k).start()
        self.own().start()

    def forward(self):
        self.own().wait()
        for k in range(1, 4):
            self.across(k).wait_recv()
        box = self.refs[2]
        self.refs[3][...] = (box[0] + box[1]) + (box[2] + box[3])
        for k in range(1, 4):
            self.along(k, False).start()
        self.kept().start()

    def wait(self):
        self.kept().wait()
        for k in range(1, 4):
            self.across(k).wait_send()
            self.along(k, False).wait_send()
            self.along(k, True).wait_recv()


class Broadcast:
    def __init__(self, in_ref, out_ref, ssem, rsem, lsem):
        self.refs = (in_ref, out_ref, ssem, rsem, lsem)
        self.z, self.y, self.x, self.c = coords()

    def own(self):
        return pltpu.make_async_copy(
            self.refs[0], self.refs[1].at[self.z, self.y, self.x], self.refs[4].at[0]
        )

    def along(self, k, arrival):
        there = lax.rem(self.z + (4 - k if arrival else k), 4)
        slot = there if arrival else self.z
        return pltpu.make_async_remote_copy(
            self.refs[0],
            self.refs[1].at[slot, self.y, self.x],
            self.refs[2].at[k],
            self.refs[3].at[k],
            device_id=device(there, self.y, self.x, self.c),
            device_id_type=MESH,
        )

    def across(self, k, arrival):
        y = lax.rem(self.y + k // 2, 2)
        x = lax.rem(self.x + k % 2, 2)
        block = self.refs[1].at[:, y, x] if arrival else self.refs[1].at[:, self.y, self.x]
        return pltpu.make_async_remote_copy(
            block,
            block,
            self.refs[2].at[3 + k],
            self.refs[3].at[3 + k],
            device_id=device(self.z, y, x, self.c),
            device_id_type=MESH,
        )

    def start(self):
        for k in range(1, 4):
            self.along(k, False).start()
        self.own().start()

    def forward(self):
        self.own().wait()
        for k in range(1, 4):
            self.along(k, True).wait_recv()
        for k in range(1, 4):
            self.across(k, False).start()

    def wait(self):
        for k in range(1, 4):
            self.along(k, False).wait_send()
            self.across(k, False).wait_send()
            self.across(k, True).wait_recv()


def gather_kernel(units, turns, count, *refs):
    w = refs[:count]
    o = refs[count + 1 : 2 * count + 1]
    ssem, rsem, lsem, csem, crsem, box, sums, es, er, el = refs[2 * count + 2 :]
    z, y, x, c = coords()
    greet()
    side = Sums(refs[count], refs[2 * count + 1], box, sums, es, er, el)
    side.start()
    up = device(z + 1, y, x, c)
    down = device(z - 1, y, x, c)
    partner = {"y": device(z, 1 - y, x, c), "x": device(z, y, 1 - x, c)}
    every = slice(None)

    def run(mine, other, order):
        def view(u, index):
            m, first, cols, _ = mine[u]
            return o[m].at[index[0], index[1], index[2], :, pl.ds(first, cols)]

        def copy(u, index, k, target, own=False):
            m, first, cols, _ = mine[u]
            dst = view(u, index)
            src = w[m].at[:, pl.ds(first, cols)] if own else dst
            return pltpu.make_async_remote_copy(
                src, dst, ssem.at[u, k], rsem.at[u, k], device_id=target, device_id_type=MESH
            )

        def local_copy(u):
            m, first, cols, _ = mine[u]
            return pltpu.make_async_copy(
                w[m].at[:, pl.ds(first, cols)], view(u, (z, y, x)), lsem.at[u]
            )

        def plan(u):
            held = {"z": False, "y": False, "x": False}

            def index(zz=z, flip=None):
                return (
                    every if held["z"] else zz,
                    every if held["y"] else (1 - y if flip == "y" else y),
                    every if held["x"] else (1 - x if flip == "x" else x),
                )

            steps = []
            pending = []
            sends = []
            own = True
            pair = 0
            for axis in mine[u][3]:
                if axis != "z":
                    send = [(True, functools.partial(copy, u, index(), pair, partner[axis], own))]
                    steps.append((pending, send))
                    sends += send
                    pending = [
                        (True, functools.partial(copy, u, index(flip=axis), pair, partner[axis]))
                    ]
                    pair += 1
                else:

                    def chain(shift, k, target, first=False):
                        return functools.partial(copy, u, index(zz=z + shift), k, target, first)

                    one = [(z < 3, chain(0, 2, up, own)), (z > 0, chain(0, 5, down, own))]
                    steps.append((pending, one))
                    middle = (z > 0) & (z < 3)
                    two = [(middle, chain(-1, 3, up)), (middle, chain(1, 6, down))]
                    steps.append(([(z > 0, chain(-1, 2, down)), (z < 3, chain(1, 5, up))], two))
                    three = [(z == 2, chain(-2, 4, up)), (z == 1, chain(2, 7, down))]
                    steps.append(([(z > 1, chain(-2, 3, down)), (z < 2, chain(2, 6, up))], three))
                    pending = [(z == 3, chain(-3, 4, down)), (z == 0, chain(3, 7, up))]
                    sends += one + two + three
                held[axis] = True
                own = False
            return steps, pending, sends

        plans = [plan(u) for u in range(len(mine))]

        def to_core(u, which):
            m, first, cols, _ = which[u]
            block = o[m].at[:, :, :, :, pl.ds(first, cols)]
            return pltpu.make_async_remote_copy(
                block,
                block,
                csem.at[u],
                crsem.at[u],
                device_id=device(z, y, x, 1 - c),
                device_id_type=MESH,
            )

        for u in range(len(mine)):
            local_copy(u).start()
        for at, (u, s) in enumerate(order):
            if at == FORWARD_AT:
                side.forward()
            steps, pending, _ = plans[u]
            if s == 1:
                local_copy(u).wait()
            for cond, make in steps[s][0] if s < 5 else pending:
                when(cond, lambda make=make: make().wait_recv())
            for cond, make in steps[s][1] if s < 5 else ():
                when(cond, lambda make=make: make().start())
            if s == 5:
                to_core(u, mine).start()
        for u in range(len(mine)):
            for cond, make in plans[u][2]:
                when(cond, lambda make=make: make().wait_send())
            to_core(u, mine).wait_send()
        for u in range(len(other)):
            to_core(u, other).wait_recv()

    pl.when(c == 0)(lambda: run(units[0], units[1], turns[0]))
    pl.when(c == 1)(lambda: run(units[1], units[0], turns[1]))
    side.wait()


ANY = pl.BlockSpec(memory_space=pl.ANY)
DMA = pltpu.SemaphoreType.DMA


SIDE = [DMA((16,)), DMA((16,)), DMA((1,))]


def gather(shards, rows, units, turns, collective_id, name):
    count = len(shards)
    most = max(len(units[0]), len(units[1]))
    shapes = [jax.ShapeDtypeStruct(GRID + s.shape, s.dtype) for s in shards]
    return pl.pallas_call(
        functools.partial(gather_kernel, units, turns, count),
        name=name,
        out_shape=shapes + [jax.ShapeDtypeStruct(GRID[:1] + rows.shape[3:], rows.dtype)],
        in_specs=[ANY] * (count + 1),
        out_specs=[ANY] * (count + 1),
        scratch_shapes=[
            DMA((most, 8)),
            DMA((most, 8)),
            DMA((most,)),
            DMA((most,)),
            DMA((most,)),
            pltpu.VMEM((4,) + GRID[:1] + rows.shape[3:], rows.dtype),
            pltpu.VMEM(GRID[:1] + rows.shape[3:], rows.dtype),
            DMA((7,)),
            DMA((7,)),
            DMA((2,)),
        ],
        compiler_params=pltpu.CompilerParams(collective_id=collective_id, has_side_effects=True),
    )(*shards, rows)


ORDERS = (
    ("zyx", "zxy", "xyz", "zxy", "zyx", "zyx", "yxz", "zxy", "zyx"),
    ("zxy", "zyx", "yxz", "zyx", "zxy", "zxy", "xyz", "zyx", "zxy"),
)
AFTER_Z = (0.6165, 0.5838, 0.5725, 1.6339, 4.1589)
AFTER_XY = (1.5672, 1.5028, 1.8589, 1.1737, 2.0677)
PER_TURN = 2.2146
FORWARD_AT = 40
SHIFT = 0.5711
SIZE = 4
TAIL = (0.1, 2)


def gather_units(shards):
    units = ([], [])
    load = [0, 0]
    whole = sum(s.size for s in shards) / (ROWS * 128)
    done = 0
    for m, shard in enumerate(shards):
        rows, columns = shard.shape
        tiles = columns // 128
        weight = rows / ROWS
        at = 0
        while at < tiles:
            size = SIZE if done < (1 - TAIL[0]) * whole else TAIL[1]
            step = max(1, round(size / weight))
            n = min(step, tiles - at)
            if 0 < tiles - at - n < max(1, round(size / weight / 2)):
                n = tiles - at
            core = 0 if load[0] <= load[1] else 1
            order = ORDERS[core][len(units[core]) % len(ORDERS[core])]
            units[core].append((m, at * 128, n * 128, order))
            load[core] += n * weight
            done += n * weight
            at += n
    turns = []
    for core in range(2):
        keys = []
        place = 0.0
        for u, (m, first, columns, order) in enumerate(units[core]):
            at = place / PER_TURN + core * SHIFT
            place += shards[m].shape[0] * columns / (ROWS * 128 * SIZE)
            keys.append((at, u, 0))
            for s, after in enumerate(AFTER_Z if order[0] == "z" else AFTER_XY):
                at += after
                keys.append((at, u, s + 1))
        turns.append(tuple((u, s) for _, u, s in sorted(keys)))
    return (tuple(units[0]), tuple(units[1])), tuple(turns)


def exchange_kernel(in_ref, out_ref, *sems):
    greet()
    side = Exchange(True, in_ref, out_ref, *sems)
    side.start()
    side.wait()


def exchange(values, collective_id, name):
    return pl.pallas_call(
        exchange_kernel,
        name=name,
        out_shape=jax.ShapeDtypeStruct((16,) + values.shape, values.dtype),
        in_specs=[ANY],
        out_specs=ANY,
        scratch_shapes=SIDE,
        compiler_params=pltpu.CompilerParams(collective_id=collective_id, has_side_effects=True),
    )(values)


RECV_SLOTS = 10
SEND_SLOTS = 8
FIRST_SLOTS = 4
UNIT = 384
ROWS = 72
PADDED = 80


def scatter_kernel(first, cols, source, dy_count, *refs):
    nv = len(first) - 1
    xt = refs[:nv]
    dy = refs[nv : nv + dy_count]
    out = refs[nv + dy_count + 1]
    (
        xts, dys, a_s1, a_s2, a_t, a_su, a_sd, e_s1, e_t, e_su, e_sd, e_sq,
        a_b1, a_b2, a_bu, a_bd, e_b1, e_bu, e_bd, e_bq, outs,
        ssem, rsem, xl, xs, xr, yl, ys, yr, ol, os, orr, es, er, el,
    ) = refs[nv + dy_count + 3 :]
    z, y, x, c = coords()
    total = first[-1] // 2
    sibling = device(z, y, x, 1 - c)
    up = device(z + 1, y, x, c)
    down = device(z - 1, y, x, c)
    greet()
    side = Broadcast(refs[nv + dy_count], refs[nv + dy_count + 2], es, er, el)
    lanes = pl.ds(pl.multiple_of(c * 128, 128), 128)
    offsets = []
    at = 0
    for k in range(dy_count):
        offsets.append(at)
        at += dy[k].shape[1]

    def remote(src, dst, send, recv, target):
        return pltpu.make_async_remote_copy(
            src, dst, send, recv, device_id=target, device_id_type=MESH
        )

    def x_views(v):
        return xt[v], xts.at[v, :, :, lanes]

    def x_local(v):
        return pltpu.make_async_copy(*x_views(v), xl.at[v])

    def x_remote(v):
        return remote(*x_views(v), xs.at[v], xr.at[v], sibling)

    def y_views(k):
        return dy[k], dys.at[lanes, pl.ds(offsets[k], dy[k].shape[1])]

    def y_local(k):
        return pltpu.make_async_copy(*y_views(k), yl.at[k])

    def y_remote(k):
        return remote(*y_views(k), ys.at[k], yr.at[k], sibling)

    fresh = [source[v] not in source[:v] for v in range(nv)]

    def bring(v):
        x_local(v).start()
        x_remote(v).start()
        if fresh[v]:
            y_local(source[v]).start()
            y_remote(source[v]).start()

    bring(0)
    bring(1)
    side.start()

    def arrive(tick):
        for v in range(nv):

            def wait(v=v):
                x_local(v).wait()
                x_remote(v).wait_recv()
                if fresh[v]:
                    y_local(source[v]).wait()
                    y_remote(source[v]).wait_recv()
                if v + 2 < nv:
                    bring(v + 2)

            pl.when(tick == (first[v] - c + 1) // 2)(wait)

    def unit(i):
        j = 2 * i + c
        v = jnp.int32(0)
        col = j * UNIT
        for k in range(1, nv):
            past = (j >= first[k]).astype(jnp.int32)
            v = v + past
            col = col + past * ((cols[k] - first[k] * UNIT) - (cols[k - 1] - first[k - 1] * UNIT))
        return v, pl.multiple_of(col, 128)

    def axes(i):
        o = lax.rem(i, 2)
        pb = x * (1 - o) + y * o
        qb = y * (1 - o) + x * o
        dp = z * 4 + y * 2 + x
        return o, pb, qb, (dp + (1 - 2 * pb) * (1 + o), c), (dp + (1 - 2 * qb) * (2 - o), c)

    def slots(i):
        return lax.rem(i, FIRST_SLOTS), lax.rem(i, SEND_SLOTS), lax.rem(i, RECV_SLOTS)

    def send(src, dst, i, k, target):
        return remote(
            src, dst, ssem.at[lax.rem(i, SEND_SLOTS), k], rsem.at[lax.rem(i, RECV_SLOTS), k], target
        )

    def first_copies(i):
        o, pb, qb, pn, qn = axes(i)
        f, s, w = slots(i)
        return [send(a_s1.at[f], a_b1.at[w], i, 0, pn), send(e_s1.at[f], e_b1.at[w], i, 8, pn)]

    def second_copy(i):
        o, pb, qb, pn, qn = axes(i)
        f, s, w = slots(i)
        return send(a_s2.at[s], a_b2.at[w], i, 1, qn)

    def last_copy(i):
        o, pb, qb, pn, qn = axes(i)
        f, s, w = slots(i)
        return send(e_sq.at[s], e_bq.at[w], i, 9, qn)

    def up_copy(i, k, e):
        f, s, w = slots(i)
        src, dst, n = (e_su, e_bu, 10) if e else (a_su, a_bu, 2)
        return send(src.at[s, k], dst.at[w, k], i, n + k, up)

    def down_copy(i, k, e):
        f, s, w = slots(i)
        src, dst, n = (e_sd, e_bd, 13) if e else (a_sd, a_bd, 5)
        return send(src.at[s, k], dst.at[w, k], i, n + k, down)

    def up_sends(k):
        return (z <= k) & (z < 3)

    def down_sends(k):
        return (3 - z <= k) & (z > 0)

    def up_comes(k):
        return (z >= 1) & (z <= k + 1)

    def down_comes(k):
        return (z <= 2) & (3 - z <= k + 1)

    def kept(i, e, d):
        f, s, w = slots(i)
        if e:
            return e_t.at[s, d]
        return a_t.at[s, d, axes(i)[2]]

    def z_send(i, k, e):
        f, s, w = slots(i)

        def pass_on(dest, stage, box, inner, copy):
            value = kept(i, e, dest)[...]
            if k == 0:
                stage[s, k] = value.astype(BF16)
            else:

                def add():
                    stage[s, k] = (value + box[w, k - 1].astype(F32)).astype(BF16)

                def begin():
                    stage[s, k] = value.astype(BF16)

                pl.when(inner)(add)
                pl.when(jnp.logical_not(inner))(begin)
            copy.start()

        pl.when(up_sends(k))(
            lambda: pass_on(
                z + 3 - k, e_su if e else a_su, e_bu if e else a_bu, z > 0, up_copy(i, k, e)
            )
        )
        pl.when(down_sends(k))(
            lambda: pass_on(
                z + k - 3, e_sd if e else a_sd, e_bd if e else a_bd, z < 3, down_copy(i, k, e)
            )
        )

    def z_wait(i, k, e):
        pl.when(up_comes(k))(lambda: up_copy(i, k, e).wait_recv())
        pl.when(down_comes(k))(lambda: down_copy(i, k, e).wait_recv())

    def z_close(i, e):
        f, s, w = slots(i)
        mine = kept(i, e, z)

        def below():
            mine[...] = mine[...] + (e_bu if e else a_bu)[w, 2].astype(F32)

        def above():
            mine[...] = mine[...] + (e_bd if e else a_bd)[w, 2].astype(F32)

        pl.when(z > 0)(below)
        pl.when(z < 3)(above)
        return mine

    def product(i, bit):
        v, col = unit(i)
        o = axes(i)[0]
        chips = [4 * k + bit * (1 + o) + q * (2 - o) for k in range(4) for q in range(2)]
        lhs = jnp.concatenate([xts[v, chip] for chip in chips], axis=0)
        whole = jnp.dot(lhs, dys[:, pl.ds(col, UNIT)], preferred_element_type=F32)
        return whole.reshape(8, PADDED, UNIT)[:, :ROWS]

    def stage0(i):
        f, s, w = slots(i)
        part = product(i, 1 - axes(i)[1])
        a_s1[f] = part[:, :, :128].astype(BF16).reshape(4, 2, ROWS, 128)
        e_s1[f] = part[:, :, 128:].astype(BF16).reshape(4, 2, ROWS, 256)
        for copy in first_copies(i):
            copy.start()

    def stage1(i):
        f, s, w = slots(i)
        o, pb, qb, pn, qn = axes(i)
        part = product(i, pb)
        for copy in first_copies(i):
            copy.wait_recv()
        a_t[s] = part[:, :, :128].reshape(4, 2, ROWS, 128) + a_b1[w].astype(F32)
        a_s2[s] = a_t[s, :, 1 - qb].astype(BF16)
        second_copy(i).start()
        e_t[s] = part[:, :, 128:].reshape(4, 2, ROWS, 256) + e_b1[w].astype(F32)
        z_send(i, 0, True)

    def a_second(i):
        f, s, w = slots(i)
        qb = axes(i)[2]
        second_copy(i).wait_recv()
        a_t[s, :, qb] = a_t[s, :, qb] + a_b2[w].astype(F32)
        z_send(i, 0, False)

    def z_step(i, k, e):
        z_wait(i, k - 1, e)
        z_send(i, k, e)

    def e_fourth(i):
        f, s, w = slots(i)
        z_wait(i, 2, True)
        z_close(i, True)
        e_sq[s] = e_t[s, z, 1 - axes(i)[2]].astype(BF16)
        last_copy(i).start()

    def out_view(i):
        return out.at[:, pl.ds(pl.multiple_of((2 * i + c) * UNIT, 128), UNIT)]

    def a_fifth(i):
        z_wait(i, 2, False)
        outs[i, :, :128] = z_close(i, False)[...]

    def e_fifth(i):
        f, s, w = slots(i)
        last_copy(i).wait_recv()
        outs[i, :, 128:] = e_t[s, z, axes(i)[2]] + e_bq[w].astype(F32)
        pltpu.make_async_copy(outs.at[i], out_view(i), ol.at[0]).start()
        remote(outs.at[i], out_view(i), os.at[0], orr.at[0], sibling).start()

    def first_sent(i):
        for copy in first_copies(i):
            copy.wait_send()

    def sent(i):
        second_copy(i).wait_send()
        last_copy(i).wait_send()
        for e in (False, True):
            for k in range(3):
                pl.when(up_sends(k))(lambda k=k, e=e: up_copy(i, k, e).wait_send())
                pl.when(down_sends(k))(lambda k=k, e=e: down_copy(i, k, e).wait_send())

    stages = (
        (a_second, 4),
        (functools.partial(z_step, k=2, e=False), 5),
        (e_fourth, 5),
        (functools.partial(z_step, k=1, e=False), 4),
        (a_fifth, 6),
        (functools.partial(z_step, k=1, e=True), 3),
        (stage0, 0),
        (e_fifth, 7),
        (functools.partial(z_step, k=2, e=True), 3),
        (stage1, 2),
    )

    def tick(t, carry):
        arrive(t)
        pl.when(t == 4)(side.forward)
        pl.when((t >= SEND_SLOTS) & (t - SEND_SLOTS < total))(lambda: sent(t - SEND_SLOTS))
        pl.when((t >= FIRST_SLOTS) & (t - FIRST_SLOTS < total))(lambda: first_sent(t - FIRST_SLOTS))
        for stage, lag in stages:
            i = t - lag
            pl.when((i >= 0) & (i < total))(functools.partial(stage, i))
        return carry

    lax.fori_loop(0, total + SEND_SLOTS, tick, 0)
    for v in range(nv):
        x_remote(v).wait_send()
    for k in range(dy_count):
        y_remote(k).wait_send()
    half = out.at[:, pl.ds(0, total * UNIT)]
    pltpu.make_async_copy(half, half, ol.at[0]).wait()
    everything = remote(half, half, os.at[0], orr.at[0], sibling)
    everything.wait_send()
    everything.wait_recv()
    side.wait()


def scatter(xts, dys, source, rows, collective_id, name):
    nv = len(xts)
    starts = []
    width = 0
    for d in dys:
        starts.append(width)
        width += d.shape[1]
    first = [0]
    cols = []
    for v in range(nv):
        cols.append(starts[source[v]])
        first.append(first[-1] + dys[source[v]].shape[1] // UNIT)
    total = first[-1] // 2
    s, f, r = SEND_SLOTS, FIRST_SLOTS, RECV_SLOTS
    vmem = pltpu.VMEM
    return pl.pallas_call(
        functools.partial(scatter_kernel, tuple(first), tuple(cols), tuple(source), len(dys)),
        name=name,
        out_shape=[
            jax.ShapeDtypeStruct((ROWS, first[-1] * UNIT), F32),
            jax.ShapeDtypeStruct(GRID + rows.shape, rows.dtype),
        ],
        in_specs=[ANY] * (nv + len(dys) + 1),
        out_specs=[ANY] * 2,
        scratch_shapes=[
            vmem((nv, 16, PADDED, 256), BF16),
            vmem((256, width), BF16),
            vmem((f, 4, 2, ROWS, 128), BF16),
            vmem((s, 4, ROWS, 128), BF16),
            vmem((s, 4, 2, ROWS, 128), F32),
            vmem((s, 3, ROWS, 128), BF16),
            vmem((s, 3, ROWS, 128), BF16),
            vmem((f, 4, 2, ROWS, 256), BF16),
            vmem((s, 4, 2, ROWS, 256), F32),
            vmem((s, 3, 2, ROWS, 256), BF16),
            vmem((s, 3, 2, ROWS, 256), BF16),
            vmem((s, ROWS, 256), BF16),
            vmem((r, 4, 2, ROWS, 128), BF16),
            vmem((r, 4, ROWS, 128), BF16),
            vmem((r, 3, ROWS, 128), BF16),
            vmem((r, 3, ROWS, 128), BF16),
            vmem((r, 4, 2, ROWS, 256), BF16),
            vmem((r, 3, 2, ROWS, 256), BF16),
            vmem((r, 3, 2, ROWS, 256), BF16),
            vmem((r, ROWS, 256), BF16),
            vmem((total, ROWS, UNIT), F32),
            DMA((s, 16)),
            DMA((r, 16)),
            DMA((nv,)),
            DMA((nv,)),
            DMA((nv,)),
            DMA((len(dys),)),
            DMA((len(dys),)),
            DMA((len(dys),)),
            DMA((1,)),
            DMA((1,)),
            DMA((1,)),
        ]
        + SIDE,
        compiler_params=pltpu.CompilerParams(
            collective_id=collective_id, has_side_effects=True, vmem_limit_bytes=62 * 1024 * 1024
        ),
    )(*xts, *dys, rows)


def layer_norm(values):
    center = values - jnp.mean(values, axis=-1, keepdims=True)
    spread = jnp.mean(center * center, axis=-1, keepdims=True)
    return center * lax.rsqrt(spread + 1e-06)


def head_norm(values, gain):
    shaped = values.reshape(values.shape[:-1] + (HEADS, HD))
    scaled = shaped * lax.rsqrt(jnp.mean(shaped * shaped, axis=-1, keepdims=True) + 1e-06)
    return scaled * gain.reshape(HEADS, HD)


def rope_tables(rows, columns):
    quarter = HD // 4
    freqs = jnp.exp(jnp.arange(quarter, dtype=F32) * (-math.log(10000.0) / quarter))
    places = jnp.stack([rows, columns], axis=-1).astype(F32)
    angles = places[..., None] * freqs
    return (jnp.cos(angles), jnp.sin(angles))


def rotate(values, cosine, sine):
    shaped = values.reshape(values.shape[:-1] + (2, 2, HD // 4))
    first = shaped[..., 0, :]
    second = shaped[..., 1, :]
    cosine = cosine[..., None, :, :]
    sine = sine[..., None, :, :]
    turned = jnp.stack([first * cosine - second * sine, first * sine + second * cosine], axis=-2)
    return turned.reshape(values.shape)


def embed_times(times, width):
    half_width = width // 2
    freqs = jnp.exp(jnp.arange(half_width, dtype=F32) * (-math.log(10000.0) / half_width))
    angles = times[..., None] * freqs
    return jnp.concatenate([jnp.cos(angles), jnp.sin(angles)], axis=-1)


def qk_prepare(query_raw, key_raw, gains, cosine, sine):
    return (
        rotate(head_norm(query_raw, gains[0]), cosine, sine),
        rotate(head_norm(key_raw, gains[1]), cosine, sine),
    )


def swish_product(gate, up):
    return jax.nn.silu(gate) * up


def attention_scores(queries, keys, allowed):
    scores = jnp.einsum("sqhd,skhd->shqk", queries, keys, preferred_element_type=F32) * (
        1.0 / math.sqrt(HD)
    )
    return jnp.where(allowed[:, None], scores, -1e30)


def dense(values, weight):
    return jnp.dot(values, weight, preferred_element_type=F32)


def dense_back(grads, weight):
    return lax.dot_general(grads, weight, (((1,), (1,)), ((), ())), preferred_element_type=F32)


def outer_sum(values, grads):
    return lax.dot_general(values, grads, (((0,), (0,)), ((), ())), preferred_element_type=F32)


def block_forward(flat, modulation, weights, context):
    batch, half, allowed, cosine, sine = context
    triple, mixing, expand, reduce_w, gains = weights
    width = flat.shape[1]
    shift1, scale1, gate1, shift2, scale2, gate2 = jnp.split(modulation, 6, axis=1)
    lifted1 = (layer_norm(flat) * (1.0 + scale1) + shift1).astype(BF16)
    projected = dense(lifted1, triple)
    query_raw, key_raw, value_raw = jnp.split(projected, 3, axis=1)
    queries, keys = qk_prepare(query_raw, key_raw, gains, cosine, sine)
    queries = queries.astype(BF16).reshape(batch, half, HEADS, HD)
    keys_local = keys.astype(BF16).reshape(batch, half, width)
    values_local = value_raw.astype(BF16).reshape(batch, half, width)
    key_heads = lax.all_gather(keys_local, "ctx", axis=1, tiled=True).reshape(batch, -1, HEADS, HD)
    value_heads = lax.all_gather(values_local, "ctx", axis=1, tiled=True)
    value_heads = value_heads.reshape(batch, -1, HEADS, HD)
    scores = attention_scores(queries, key_heads, allowed)
    top = jnp.max(scores, axis=-1, keepdims=True)
    raised = jnp.exp(scores - top)
    total = jnp.sum(raised, axis=-1, keepdims=True)
    softmax_low = (raised / total).astype(BF16)
    logsum = top + jnp.log(total)
    mixed = jnp.einsum("shqk,skhd->sqhd", softmax_low, value_heads, preferred_element_type=F32)
    mixed_low = mixed.reshape(-1, width).astype(BF16)
    attended = dense(mixed_low, mixing)
    resid = flat + gate1 * attended
    lifted2 = (layer_norm(resid) * (1.0 + scale2) + shift2).astype(BF16)
    expanded = dense(lifted2, expand)
    gate, up = jnp.split(expanded, 2, axis=1)
    hidden = swish_product(gate, up).astype(BF16)
    feed = dense(hidden, reduce_w)
    output = resid + gate2 * feed
    kept = (
        modulation,
        flat,
        lifted1,
        query_raw,
        key_raw,
        queries,
        key_heads,
        value_heads,
        logsum,
        mixed_low,
        attended,
        resid,
        lifted2,
        expanded,
        hidden,
        feed,
    )
    return (output, kept)


def block_backward(grad_out, kept, weights, context):
    batch, half, allowed, cosine, sine = context
    triple, mixing, expand, reduce_w, gains = weights
    (
        modulation,
        flat,
        lifted1,
        query_raw,
        key_raw,
        queries,
        key_heads,
        value_heads,
        logsum,
        mixed_low,
        attended,
        resid,
        lifted2,
        expanded,
        hidden,
        feed,
    ) = kept
    width = flat.shape[1]
    shift1, scale1, gate1, shift2, scale2, gate2 = jnp.split(modulation, 6, axis=1)
    grad_feed = (grad_out * gate2).astype(BF16)
    grad_hidden = dense_back(grad_feed, reduce_w)
    gate, up = jnp.split(expanded, 2, axis=1)
    unused_out, swish_pull = jax.vjp(swish_product, gate, up)
    grad_gate, grad_up = swish_pull(grad_hidden)
    grad_expanded = jnp.concatenate([grad_gate, grad_up], axis=1).astype(BF16)
    grad_lifted2 = dense_back(grad_expanded, expand)
    normed_second, second_pull = jax.vjp(layer_norm, resid)
    grad_resid = grad_out + second_pull(grad_lifted2 * (1.0 + scale2))[0]
    grad_attended = (grad_resid * gate1).astype(BF16)
    grad_mixed = dense_back(grad_attended, mixing).astype(BF16).reshape(batch, half, HEADS, HD)
    scores = attention_scores(queries, key_heads, allowed)
    chances = jnp.exp(scores - logsum)
    grad_chances = jnp.einsum(
        "sqhd,skhd->shqk", grad_mixed, value_heads, preferred_element_type=F32
    )
    grad_values = jnp.einsum(
        "shqk,sqhd->skhd", chances.astype(BF16), grad_mixed, preferred_element_type=F32
    )
    grad_scores = (
        chances * (grad_chances - jnp.sum(chances * grad_chances, axis=-1, keepdims=True))
    ).astype(BF16)
    scale = 1.0 / math.sqrt(HD)
    grad_queries = (
        jnp.einsum("shqk,skhd->sqhd", grad_scores, key_heads, preferred_element_type=F32) * scale
    )
    grad_keys = (
        jnp.einsum("shqk,sqhd->skhd", grad_scores, queries, preferred_element_type=F32) * scale
    )
    pair = jnp.stack(
        [grad_keys.reshape(batch, -1, width), grad_values.reshape(batch, -1, width)]
    ).astype(BF16)
    place = lax.axis_index("ctx")
    theirs = lax.dynamic_slice_in_dim(pair, (1 - place) * half, half, 2)
    theirs = lax.ppermute(theirs, "ctx", [(0, 1), (1, 0)])
    mine = lax.dynamic_slice_in_dim(pair, place * half, half, 2)
    pair = mine.astype(F32) + theirs.astype(F32)
    grad_keys, grad_values = pair[0], pair[1]

    def prepare(query_in, key_in, gain_in):
        return qk_prepare(query_in, key_in, gain_in, cosine, sine)

    unused_pair, prepare_pull = jax.vjp(prepare, query_raw, key_raw, gains)
    grad_query_raw, grad_key_raw, gains_grad = prepare_pull(
        (grad_queries.reshape(-1, HEADS, HD), grad_keys.reshape(-1, HEADS, HD))
    )
    grad_projected = jnp.concatenate(
        [grad_query_raw, grad_key_raw, grad_values.reshape(-1, width)], axis=1
    ).astype(BF16)
    grad_lifted1 = dense_back(grad_projected, triple)
    normed_first, first_pull = jax.vjp(layer_norm, flat)
    grad_flat = grad_resid + first_pull(grad_lifted1 * (1.0 + scale1))[0]
    grad_modulation = jnp.concatenate(
        [
            grad_lifted1,
            grad_lifted1 * normed_first,
            grad_resid * attended,
            grad_lifted2,
            grad_lifted2 * normed_second,
            grad_out * feed,
        ],
        axis=1,
    ).astype(BF16)
    factors = (
        (lifted1, grad_projected),
        (mixed_low, grad_attended),
        (lifted2, grad_expanded),
        (hidden, grad_feed),
    )
    return (grad_flat, grad_modulation, factors, gains_grad)


def meet_sibling():
    barrier = pltpu.get_barrier_semaphore()
    sibling = (lax.axis_index("dp"), 1 - lax.axis_index("ctx"))
    pl.semaphore_signal(barrier, inc=1, device_id=sibling, device_id_type=MESH)
    pl.semaphore_wait(barrier, 1)
    return sibling


def head_sum_matrix(width):
    channel = lax.broadcasted_iota(jnp.int32, (width, 128), 0)
    head = lax.broadcasted_iota(jnp.int32, (width, 128), 1)
    inside = (channel >= head * HD) & (channel < (head + 1) * HD)
    return jnp.where(inside, 1.0, 0.0).astype(F32)


def exact_dot(left, right):
    return jnp.dot(left, right, preferred_element_type=F32, precision=lax.Precision.HIGHEST)


def spread_heads(values, heads):
    return lax.dot_general(
        values,
        heads,
        (((1,), (1,)), ((), ())),
        preferred_element_type=F32,
        precision=lax.Precision.HIGHEST,
    )


def swap_pairs(values):
    width = values.shape[1]
    lane = lax.broadcasted_iota(jnp.int32, values.shape, 1)
    quarter = HD // 4
    early = lax.rem(lane, 2 * quarter) < quarter
    return jnp.where(
        early, pltpu.roll(values, width - quarter, 1), pltpu.roll(values, quarter, 1)
    )


def normalize(values):
    mean = jnp.mean(values, axis=1, keepdims=True)
    center = values - mean
    spread = jnp.mean(center * center, axis=1, keepdims=True)
    inverse = lax.rsqrt(spread + 1e-06)
    return center * inverse, inverse


def norm_back(normed, inverse, grad):
    mean = jnp.mean(grad, axis=1, keepdims=True)
    along = jnp.mean(grad * normed, axis=1, keepdims=True)
    return (grad - mean - normed * along) * inverse


def window(h, width):
    first = min((h * HD) // 128 * 128, width - 256)
    return first, h * HD - first


def head_mask(h, width, rows):
    first, at = window(h, width)
    lane = lax.broadcasted_iota(jnp.int32, (rows, 256), 1)
    return (lane >= at) & (lane < at + HD)


def turned(values):
    tokens, width = values.shape
    rows = values.T.reshape(-1, ROWS, tokens)
    return jnp.concatenate(
        [rows, jnp.zeros((width // ROWS, PADDED - ROWS, tokens), F32)], axis=1
    ).astype(BF16)


FF_TILE = 768
KV_TILE = 1152


def allowed_mask(seg_q, seg_k, pad_k, half):
    place_q = lax.axis_index("ctx") * half + lax.broadcasted_iota(jnp.int32, (half, 2 * half), 0)
    place_k = lax.broadcasted_iota(jnp.int32, (half, 2 * half), 1)
    return (seg_q[...] == seg_k[...]) & ((pad_k[...] == 0) | (place_q == place_k))


MOD_TILE = 768


def weight_tiles(weight, held, sem):
    tiles = []
    for t in range(weight.shape[1] // MOD_TILE):
        span = slice(t * MOD_TILE, (t + 1) * MOD_TILE)
        copy = pltpu.make_async_copy(
            weight.at[:, pl.ds(t * MOD_TILE, MOD_TILE)],
            held.at[:, pl.ds(t * MOD_TILE, MOD_TILE)],
            sem.at[t],
        )
        copy.start()
        tiles.append((span, copy))
    return tiles


def modulation_kernel(block, valid, cond, offset, weight, mod, before, latent, xt, held, sem):
    tiles = weight_tiles(weight, held, sem)
    kept = block[...] * valid[...]
    latent[...] = kept.astype(BF16)
    total = kept + cond[...]
    before[...] = total
    act = (total * jax.nn.sigmoid(total)).astype(BF16)
    xt[...] = turned(act.astype(F32))
    for span, copy in tiles:
        copy.wait()
        part = jnp.dot(act, held[:, span], preferred_element_type=F32)
        mod[:, span] = part + offset[:, span]


def modulation_back_kernel(grad, valid, before, weight, out, held, sem):
    tiles = weight_tiles(weight, held, sem)
    out[...] = jnp.zeros_like(out)
    for span, copy in tiles:
        copy.wait()
        out[...] = out[...] + dense_back(grad[:, span], held[:, span])
    sig = jax.nn.sigmoid(before[...])
    out[...] = valid[...] * (out[...] * (sig * (1.0 + before[...] * (1.0 - sig))))


def modulation_call(kernel, name, inputs, weight, outs):
    in_vmem = pl.BlockSpec(memory_space=pltpu.VMEM)
    return pl.pallas_call(
        kernel,
        name=name,
        out_shape=outs,
        in_specs=[in_vmem] * len(inputs) + [ANY],
        out_specs=[in_vmem] * len(outs),
        scratch_shapes=[pltpu.VMEM(weight.shape, BF16), DMA((weight.shape[1] // MOD_TILE,))],
        compiler_params=pltpu.CompilerParams(vmem_limit_bytes=62 * 1024 * 1024),
    )(*inputs, weight)


def decoder_modulation_of(block, valid, cond, offset, weight):
    rows, width = block.shape
    outs = [
        jax.ShapeDtypeStruct((rows, weight.shape[1]), F32),
        jax.ShapeDtypeStruct((rows, width), F32),
        jax.ShapeDtypeStruct((rows, width), BF16),
        jax.ShapeDtypeStruct((16, PADDED, rows), BF16),
    ]
    inputs = (block, valid, cond, offset.reshape(1, -1))
    return modulation_call(modulation_kernel, "modulation", inputs, weight, outs)


def modulation_back(grad, valid, before, weight):
    outs = [jax.ShapeDtypeStruct(before.shape, F32)]
    return modulation_call(
        modulation_back_kernel, "modulation_back", (grad, valid, before), weight, outs
    )[0]


class A(enum.IntEnum):
    flat = 1
    mod = 2
    gains = 3
    cosine = 4
    sine = 5
    seg_q = 6
    seg_k = 7
    pad_k = 8
    triple = 9
    mixing = 10
    expand = 11
    reduce = 12
    output = 13
    raw = 14
    queries = 15
    kv = 16
    lse = 17
    attended = 18
    resid = 19
    expanded = 20
    feed = 21
    xt1 = 22
    xtm = 23
    xt2 = 24
    xth0 = 25
    xth1 = 26
    xth2 = 27
    lift = 28
    grad_out = 29
    grad_flat = 30
    grad_mod = 31
    grad_feed = 32
    grad_expanded = 33
    grad_attended = 34
    grad_projected = 35
    gains_grad = 36
    grad_v = 38
    outgoing = 39
    incoming = 40
    marks = 41
    mark_sums = 42


class Traffic:
    def __init__(self, held, sources, targets, lsem, ssem):
        self.held = held
        names = [n for n in sources]
        self.loads = {
            n: pltpu.make_async_copy(sources[n], held[n], lsem.at[k]) for k, n in enumerate(names)
        }
        self.sources = sources
        self.tiles = {}
        self.more = None
        self.stores = {
            n: pltpu.make_async_copy(held[n], targets[n], ssem.at[k])
            for k, n in enumerate(targets)
        }
        self.waiting = set(names)

    def __getattr__(self, name):
        return self.held[A[name]]

    def fetch(self, *names):
        for n in names:
            if n in self.loads:
                self.loads[n].start()

    def fetch_tile(self, size, rows, columns, sem, t):
        spans = [(n, (pl.ds(t * size, size), slice(None))) for n in rows]
        for n in columns:
            for first in (0, self.held[n].shape[1] // 2):
                spans.append((n, (slice(None), pl.ds(first + t * size, size))))
        self.tiles[t] = [
            pltpu.make_async_copy(self.sources[n].at[at], self.held[n].at[at], sem.at[t, k])
            for k, (n, at) in enumerate(spans)
        ]
        for copy in self.tiles[t]:
            copy.start()
        self.waiting.difference_update(rows + columns)

    def need_tile(self, t):
        for copy in self.tiles.pop(t, ()):
            copy.wait()

    def need(self, *names):
        for n in names:
            if n in self.waiting:
                self.loads[n].wait()
                self.waiting.discard(n)

    def emit(self, *names):
        for n in names:
            if n in self.stores:
                self.stores[n].start()

    def close(self):
        for store in self.stores.values():
            store.wait()


def forward_body(r, sibling, ssem, rsem):
    half, width = r.flat.shape
    c = lax.axis_index("ctx")
    mine = pl.ds(pl.multiple_of(c * half, 128), half)
    theirs = pl.ds(pl.multiple_of((1 - c) * half, 128), half)
    hidden_size = r.reduce.shape[0]

    def part(k):
        return r.mod[:, k * width : (k + 1) * width]

    r.need(A.flat, A.mod)
    normed, unused = normalize(r.flat[...])
    lifted_low = (normed * (1.0 + part(1)) + part(0)).astype(BF16)
    r.need(A.triple)
    r.fetch(A.mixing, A.expand, A.reduce)
    heads = head_sum_matrix(width)

    def prepared(k):
        values = r.raw[:, k * width : (k + 1) * width]
        mean = exact_dot(values * values, heads) * (1.0 / HD)
        scaled = values * spread_heads(lax.rsqrt(mean + 1e-06), heads) * r.gains[k : k + 1, :]
        return scaled * r.cosine[...] + swap_pairs(scaled) * r.sine[...]

    def project(k):
        return jnp.dot(
            lifted_low, r.triple[:, k * width : (k + 1) * width], preferred_element_type=F32
        )

    r.raw[:, width:] = project(1)
    r.need(A.gains, A.cosine, A.sine)
    r.kv[0, mine] = prepared(1).astype(BF16)
    r.kv[1, mine] = project(2).astype(BF16)
    share = pltpu.make_async_remote_copy(
        r.kv.at[:, mine], r.kv.at[:, mine], ssem.at[0], rsem.at[0], device_id=sibling,
        device_id_type=MESH,
    )
    share.start()
    r.raw[:, :width] = project(0)
    r.emit(A.raw)
    r.queries[...] = prepared(0).astype(BF16)
    r.emit(A.queries)
    r.xt1[...] = turned(lifted_low.astype(F32))
    r.emit(A.xt1)
    r.need(A.seg_q, A.seg_k, A.pad_k)
    allowed = allowed_mask(r.seg_q, r.seg_k, r.pad_k, half)
    r.lift[...] = jnp.zeros_like(r.lift)
    lane = lax.broadcasted_iota(jnp.int32, (half, 128), 1)
    sums = jnp.zeros((half, 128), F32)
    pltpu.make_async_remote_copy(
        r.kv.at[:, theirs], r.kv.at[:, theirs], ssem.at[0], rsem.at[0], device_id=sibling,
        device_id_type=MESH,
    ).wait_recv()
    r.emit(A.kv)
    for h in range(width // HD):
        first, unused = window(h, width)
        span = slice(first, first + 256)
        mask = head_mask(h, width, half)
        query = jnp.where(mask, r.queries[:, span].astype(F32), 0.0).astype(BF16)
        scores = dense_back(query, r.kv[0, :, span]) * (1.0 / math.sqrt(HD))
        scores = jnp.where(allowed, scores, -1e30)
        top = jnp.max(scores, axis=1, keepdims=True)
        raised = jnp.exp(scores - top)
        total = jnp.sum(raised, axis=1, keepdims=True)
        low = (raised / total).astype(BF16)
        out = jnp.dot(low, r.kv[1, :, span], preferred_element_type=F32)
        r.lift[:, span] = r.lift[:, span] + jnp.where(mask, out, 0.0)
        sums = jnp.where(lane == h, top + jnp.log(total), sums)
    r.lse[...] = sums
    r.emit(A.lse)
    mixed_low = r.lift[...].astype(BF16)
    r.xtm[...] = turned(mixed_low.astype(F32))
    r.emit(A.xtm)
    r.need(A.mixing)
    r.attended[...] = jnp.dot(mixed_low, r.mixing[...], preferred_element_type=F32)
    r.emit(A.attended)
    r.resid[...] = r.flat[...] + part(2) * r.attended[...]
    r.emit(A.resid)
    normed, unused = normalize(r.resid[...])
    lifted_low = (normed * (1.0 + part(4)) + part(3)).astype(BF16)
    r.xt2[...] = turned(lifted_low.astype(F32))
    r.emit(A.xt2)
    r.feed[...] = jnp.zeros_like(r.feed)
    r.need(A.expand, A.reduce)
    xth = (r.xth0, r.xth1, r.xth2)
    for g in range(3):
        xth[g][...] = jnp.zeros_like(xth[g])
    for t in range(hidden_size // FF_TILE):
        one = slice(t * FF_TILE, (t + 1) * FF_TILE)
        two = slice(hidden_size + t * FF_TILE, hidden_size + (t + 1) * FF_TILE)
        gate = jnp.dot(lifted_low, r.expand[:, one], preferred_element_type=F32)
        up = jnp.dot(lifted_low, r.expand[:, two], preferred_element_type=F32)
        r.expanded[:, one] = gate
        r.expanded[:, two] = up
        hidden = (gate * jax.nn.sigmoid(gate) * up).astype(BF16)
        pieces = hidden.astype(F32).T.astype(BF16).reshape(FF_TILE // 192, 3, 64, half)
        for g in range(3):
            xth[g][t * (FF_TILE // 192) : (t + 1) * (FF_TILE // 192), :64] = pieces[:, g]
        r.feed[...] = r.feed[...] + jnp.dot(hidden, r.reduce[one], preferred_element_type=F32)
    r.emit(A.expanded, A.feed, A.xth0, A.xth1, A.xth2)
    r.output[...] = r.resid[...] + part(5) * r.feed[...]
    r.emit(A.output)
    share.wait_send()


def backward_body(r, sibling, ssem, rsem):
    half, width = r.flat.shape
    c = lax.axis_index("ctx")
    mine = pl.ds(pl.multiple_of(c * half, 128), half)
    theirs = pl.ds(pl.multiple_of((1 - c) * half, 128), half)
    hidden_size = r.reduce.shape[0]

    def part(k):
        return r.mod[:, k * width : (k + 1) * width]

    def keep(k, values):
        r.grad_mod[:, k * width : (k + 1) * width] = values.astype(BF16)

    r.need(A.grad_out, A.feed, A.mod)
    keep(5, r.grad_out[...] * r.feed[...])
    feed_low = (r.grad_out[...] * part(5)).astype(BF16)
    r.grad_feed[...] = feed_low
    r.emit(A.grad_feed)
    r.lift[...] = jnp.zeros_like(r.lift)
    for t in range(hidden_size // FF_TILE):
        r.need_tile(t)
        if r.more and t + 2 < hidden_size // FF_TILE:
            r.more(t + 2)
        if t == 2:
            r.fetch(A.attended, A.resid, A.mixing, A.queries, A.kv, A.lse, A.raw, A.flat, A.triple)
        one = slice(t * FF_TILE, (t + 1) * FF_TILE)
        two = slice(hidden_size + t * FF_TILE, hidden_size + (t + 1) * FF_TILE)
        grad_hidden = dense_back(feed_low, r.reduce[one])
        gate = r.expanded[:, one]
        up = r.expanded[:, two]
        sig = jax.nn.sigmoid(gate)
        grad_gate = (grad_hidden * up * (sig * (1.0 + gate * (1.0 - sig)))).astype(BF16)
        grad_up = (grad_hidden * (gate * sig)).astype(BF16)
        r.grad_expanded[:, one] = grad_gate
        r.grad_expanded[:, two] = grad_up
        r.lift[...] = r.lift[...] + dense_back(grad_gate, r.expand[:, one])
        r.lift[...] = r.lift[...] + dense_back(grad_up, r.expand[:, two])
    r.emit(A.grad_expanded)
    r.need(A.resid, A.attended)
    normed, inverse = normalize(r.resid[...])
    keep(3, r.lift[...])
    keep(4, r.lift[...] * normed)
    grad_resid = r.grad_out[...] + norm_back(normed, inverse, r.lift[...] * (1.0 + part(4)))
    keep(2, grad_resid * r.attended[...])
    if A.output in r.stores:
        r.stores.pop(A.output).wait()
    r.grad_flat[...] = grad_resid
    attended_low = (grad_resid * part(2)).astype(BF16)
    r.grad_attended[...] = attended_low
    r.emit(A.grad_attended)
    r.need(A.mixing)
    r.lift[...] = dense_back(attended_low, r.mixing[...])
    r.need(A.seg_q, A.seg_k, A.pad_k, A.queries, A.kv, A.lse)
    allowed = allowed_mask(r.seg_q, r.seg_k, r.pad_k, half)
    r.feed[...] = jnp.zeros_like(r.feed)
    r.resid[...] = jnp.zeros_like(r.resid)
    r.attended[...] = jnp.zeros_like(r.attended)
    r.grad_v[...] = jnp.zeros_like(r.grad_v)
    scale = 1.0 / math.sqrt(HD)
    lane = lax.broadcasted_iota(jnp.int32, (half, 128), 1)
    for h in range(width // HD):
        first, unused = window(h, width)
        span = slice(first, first + 256)
        mask = head_mask(h, width, half)
        query = jnp.where(mask, r.queries[:, span].astype(F32), 0.0).astype(BF16)
        grad_mixed = jnp.where(mask, r.lift[:, span], 0.0).astype(BF16)
        scores = dense_back(query, r.kv[0, :, span]) * scale
        logsum = jnp.sum(jnp.where(lane == h, r.lse[...], 0.0), axis=1, keepdims=True)
        chances = jnp.exp(jnp.where(allowed, scores, -1e30) - logsum)
        grad_chances = dense_back(grad_mixed, r.kv[1, :, span])
        along = jnp.sum(chances * grad_chances, axis=1, keepdims=True)
        scores_low = (chances * (grad_chances - along)).astype(BF16)
        out = jnp.dot(scores_low, r.kv[0, :, span], preferred_element_type=F32)
        r.feed[:, span] = r.feed[:, span] + jnp.where(mask, out, 0.0)
        part_k = outer_sum(scores_low, query)
        r.resid[:, span] = r.resid[:, span] + part_k[:half]
        r.attended[:, span] = r.attended[:, span] + part_k[half:]
        r.grad_v[:, span] = r.grad_v[:, span] + outer_sum(chances.astype(BF16), grad_mixed)
    their_k = jnp.where(c == 0, r.attended[...], r.resid[...])
    r.outgoing[0] = (their_k * scale).astype(BF16)
    r.outgoing[1] = r.grad_v[theirs, :].astype(BF16)
    share = pltpu.make_async_remote_copy(
        r.outgoing, r.incoming, ssem.at[1], rsem.at[1], device_id=sibling, device_id_type=MESH
    )
    share.start()
    heads = head_sum_matrix(width)
    r.need(A.raw, A.gains, A.cosine, A.sine)

    def prepare_back(k, grad):
        values = r.raw[:, k * width : (k + 1) * width]
        gain = r.gains[k : k + 1, :]
        mean = exact_dot(values * values, heads) * (1.0 / HD)
        inverse = spread_heads(lax.rsqrt(mean + 1e-06), heads)
        scaled = values * inverse
        turned_back = grad * r.cosine[...] + swap_pairs(grad * r.sine[...])
        r.gains_grad[k : k + 1, :] = jnp.sum(turned_back * scaled, axis=0, keepdims=True)
        turned_back = turned_back * gain
        along = spread_heads(exact_dot(turned_back * scaled, heads) * (1.0 / HD), heads)
        return (turned_back - scaled * along) * inverse

    r.grad_projected[:, :width] = prepare_back(0, r.feed[...] * scale).astype(BF16)
    r.need(A.triple)
    total = dense_back(r.grad_projected[:, :width], r.triple[:, :width])
    share.wait()
    own_k = jnp.where(c == 0, r.resid[...], r.attended[...]) * scale
    own_k = own_k.astype(BF16).astype(F32) + r.incoming[0].astype(F32)
    own_v = r.grad_v[mine, :].astype(BF16).astype(F32) + r.incoming[1].astype(F32)
    r.grad_projected[:, width : 2 * width] = prepare_back(1, own_k).astype(BF16)
    r.grad_projected[:, 2 * width :] = own_v.astype(BF16)
    r.emit(A.grad_projected, A.gains_grad)
    for k in (1, 2):
        span = slice(k * width, (k + 1) * width)
        total = total + dense_back(r.grad_projected[:, span], r.triple[:, span])
    r.need(A.flat)
    normed, inverse = normalize(r.flat[...])
    keep(0, total)
    keep(1, total * normed)
    r.emit(A.grad_mod)
    r.need(A.marks)
    for k in range(6):
        span = slice(k * width, (k + 1) * width)
        r.mark_sums[:, span] = jnp.dot(
            r.marks[...], r.grad_mod[:, span], preferred_element_type=F32
        )
    r.emit(A.mark_sums)
    r.grad_flat[...] = r.grad_flat[...] + norm_back(normed, inverse, total * (1.0 + part(1)))
    r.emit(A.grad_flat)


def block_shapes(half, width, hidden_size):
    rows = ((16, PADDED, half), BF16)
    token = ((half, width), F32)
    low = ((half, width), BF16)
    return {
        A.flat: token,
        A.mod: ((half, 6 * width), F32),
        A.gains: ((2, width), F32),
        A.cosine: token,
        A.sine: token,
        A.seg_q: ((half, 1), jnp.int32),
        A.seg_k: ((1, 2 * half), jnp.int32),
        A.pad_k: ((1, 2 * half), jnp.int32),
        A.triple: ((width, 3 * width), BF16),
        A.mixing: ((width, width), BF16),
        A.expand: ((width, 2 * hidden_size), BF16),
        A.reduce: ((hidden_size, width), BF16),
        A.output: token,
        A.raw: ((half, 2 * width), F32),
        A.queries: low,
        A.kv: ((2, 2 * half, width), BF16),
        A.lse: ((half, 128), F32),
        A.attended: token,
        A.resid: token,
        A.expanded: ((half, 2 * hidden_size), F32),
        A.feed: token,
        A.xt1: rows,
        A.xtm: rows,
        A.xt2: rows,
        A.xth0: rows,
        A.xth1: rows,
        A.xth2: rows,
        A.lift: token,
        A.grad_out: token,
        A.grad_flat: token,
        A.grad_mod: ((half, 6 * width), BF16),
        A.grad_feed: low,
        A.grad_expanded: ((half, 2 * hidden_size), BF16),
        A.grad_attended: low,
        A.grad_projected: ((half, 3 * width), BF16),
        A.gains_grad: ((2, width), F32),
        A.grad_v: ((2 * half, width), F32),
        A.outgoing: ((2, half, width), BF16),
        A.incoming: ((2, half, width), BF16),
        A.marks: ((8, half), BF16),
        A.mark_sums: ((8, 6 * width), F32),
    }


WEIGHTS = (A.triple, A.mixing, A.expand, A.reduce)
GIVEN = (A.gains, A.cosine, A.sine, A.seg_q, A.seg_k, A.pad_k) + WEIGHTS
SAVED = (A.raw, A.queries, A.kv, A.lse, A.attended, A.resid, A.expanded, A.feed)
LEFTS = (A.xt1, A.xtm, A.xt2, A.xth0, A.xth1, A.xth2)
GRADS = (
    A.grad_flat, A.grad_mod, A.grad_feed, A.grad_expanded, A.grad_attended, A.grad_projected,
    A.gains_grad, A.mark_sums,
)
WORK = (A.grad_v, A.outgoing, A.incoming)
EARLY = (A.gains, A.cosine, A.sine, A.seg_q, A.seg_k, A.pad_k)
PLANS = {
    "forward": ((A.flat, A.mod) + GIVEN, (A.output,) + SAVED + LEFTS, (A.lift,)),
    "backward": ((A.grad_out, A.marks, A.flat, A.mod) + GIVEN + SAVED, GRADS, (A.lift,) + WORK),
    "both": ((A.grad_out, A.marks, A.flat, A.mod) + GIVEN, (A.output,) + LEFTS + GRADS, SAVED + (A.lift,) + WORK),
}


def held_names(kind):
    inputs, outputs, others = PLANS[kind]
    names = inputs + outputs + others
    return tuple(n for n in names if kind != "both" or n != A.output)


def block_kernel(kind, *refs):
    inputs, outputs, others = PLANS[kind]
    sources = dict(zip(inputs, refs))
    targets = dict(zip(outputs, refs[len(inputs) :]))
    names = held_names(kind)
    held = dict(zip(names, refs[len(inputs) + len(outputs) :]))
    if kind == "both":
        held[A.output] = held[A.grad_flat]
    lsem, wsem, tsem, ssem, rsem = refs[len(inputs) + len(outputs) + len(names) :]
    r = Traffic(held, sources, targets, lsem, wsem)
    if kind == "backward":
        r.fetch(A.grad_out, A.feed, A.mod, A.marks, *EARLY)
        r.more = functools.partial(r.fetch_tile, FF_TILE, (A.reduce,), (A.expanded, A.expand), tsem)
        r.more(0)
        r.more(1)
    else:
        r.fetch(A.flat, A.mod, A.triple, *EARLY)
    sibling = meet_sibling()
    if kind != "backward":
        forward_body(r, sibling, ssem, rsem)
    if kind == "both":
        r.fetch(A.grad_out, A.marks)
        r.loads = {n: r.loads[n] for n in (A.grad_out, A.marks)}
    if kind != "forward":
        backward_body(r, sibling, ssem, rsem)
    r.close()


def run_block(kind, values, name):
    inputs, outputs, others = PLANS[kind]
    half, width = values[A.flat].shape
    table = block_shapes(half, width, values[A.reduce].shape[0])
    names = held_names(kind)
    results = pl.pallas_call(
        functools.partial(block_kernel, kind),
        name=name,
        out_shape=[jax.ShapeDtypeStruct(*table[n]) for n in outputs],
        in_specs=[ANY] * len(inputs),
        out_specs=[ANY] * len(outputs),
        scratch_shapes=[pltpu.VMEM(*table[n]) for n in names]
        + [DMA((len(inputs),)), DMA((len(outputs),)), DMA((4, 5)), DMA((2,)), DMA((2,))],
        compiler_params=pltpu.CompilerParams(
            collective_id={"forward": 5, "backward": 6, "both": 7}[kind],
            has_side_effects=True,
            vmem_limit_bytes=63 * 1024 * 1024,
        ),
    )(*[values[n] for n in inputs])
    return dict(zip(outputs, results))


def split_kernel(pieces, in_ref, *refs):
    *outs, held, arrived, left = refs
    for k, (n, row, rows, columns, at) in enumerate(pieces):
        span = (pl.ds(0, rows), pl.ds(at, columns))
        pltpu.make_async_copy(in_ref.at[span], held.at[span], arrived.at[k]).start()

    def leave(k):
        n, row, rows, columns, at = pieces[k]
        span = (pl.ds(0, rows), pl.ds(at, columns))
        return pltpu.make_async_copy(held.at[span], outs[n].at[pl.ds(row, rows), :], left.at[k])

    for k, (n, row, rows, columns, at) in enumerate(pieces):
        span = (pl.ds(0, rows), pl.ds(at, columns))
        pltpu.make_async_copy(in_ref.at[span], held.at[span], arrived.at[k]).wait()
        leave(k).start()
    for k in range(len(pieces)):
        leave(k).wait()


def split(values, shapes, pieces):
    return pl.pallas_call(
        functools.partial(split_kernel, tuple(pieces)),
        name="split",
        out_shape=[jax.ShapeDtypeStruct(shape, values.dtype) for shape in shapes],
        in_specs=[ANY],
        out_specs=[ANY] * len(shapes),
        scratch_shapes=[
            pltpu.VMEM(values.shape, values.dtype),
            DMA((len(pieces),)),
            DMA((len(pieces),)),
        ],
        compiler_params=pltpu.CompilerParams(vmem_limit_bytes=62 * 1024 * 1024),
    )(values)


def rope_lanes(cosine, sine):
    tokens = cosine.shape[0]

    def lanes(table, signs):
        table = jnp.stack([signs[0] * table, signs[1] * table], axis=2).reshape(tokens, 1, HD)
        return jnp.broadcast_to(table, (tokens, HEADS, HD)).reshape(tokens, HEADS * HD)

    return lanes(cosine, (1.0, 1.0)), lanes(sine, (-1.0, 1.0))


def fast_reduce(blocks, rows, collective_id, name):
    xts = []
    dys = []
    source = []
    for factors, extra in blocks:
        for lefts, right in factors:
            source += [len(dys)] * len(lefts)
            xts += lefts
            dys.append(right)
        tokens = right.shape[0]
        lines = -(-extra.shape[1] // tokens)
        packed = jnp.pad(extra, ((0, 0), (0, lines * tokens - extra.shape[1])))
        packed = packed.reshape(16, lines, tokens).astype(BF16)
        xts.append(jnp.pad(packed, ((0, 0), (0, PADDED - lines), (0, 0))))
        source.append(len(dys))
        dys.append(jnp.eye(tokens, UNIT, dtype=BF16))
    out, rows = scatter(xts, dys, source, rows, collective_id, name)
    shapes = []
    pieces = []
    smalls = []
    at = 0
    for factors, extra in blocks:
        for lefts, right in factors[:-1]:
            pieces.append((len(shapes), 0, ROWS, right.shape[1], at))
            shapes.append((ROWS, right.shape[1]))
            at += right.shape[1]
        width = factors[-1][1].shape[1]
        for g in range(3):
            pieces.append((len(shapes), 64 * g, 64, width, at))
            at += width
        shapes.append((192, width))
        lines = -(-extra.shape[1] // tokens)
        smalls.append(out[:lines, at : at + tokens].reshape(-1)[: extra.shape[1]])
        at += UNIT
    grads = split(out, shapes, pieces)
    results = []
    for (factors, extra), small in zip(blocks, smalls):
        results.append((grads[: len(factors)], small))
        grads = grads[len(factors) :]
    return results, rows


def whole_rows(gathered):
    return gathered.reshape((-1,) + gathered.shape[4:])


def fast_step(flat, cotangent, context, segment_local, valid, timesteps, encoder, decoder):
    width = flat.shape[1]
    offset_size = encoder[1].shape[0]
    gain_size = 2 * encoder[3].shape[1]
    small = jnp.concatenate(
        [
            encoder[1].astype(F32),
            decoder[1].astype(F32),
            encoder[3].astype(F32).reshape(-1),
            decoder[3].astype(F32).reshape(-1),
            timesteps.astype(F32).reshape(-1),
        ]
    )
    size = small.shape[0]
    small = jnp.pad(small, (0, 2048 - size)).reshape(16, 128)
    small = exchange(small, 0, "small").reshape(16, -1)
    encoder_offset = small[:, :offset_size].reshape(-1)
    decoder_offset = small[:, offset_size : 2 * offset_size].reshape(-1)
    at = 2 * offset_size
    encoder_gains = small[:, at : at + gain_size].reshape(16, 2, -1).swapaxes(0, 1).reshape(2, -1)
    at += gain_size
    decoder_gains = small[:, at : at + gain_size].reshape(16, 2, -1).swapaxes(0, 1).reshape(2, -1)
    at += gain_size
    all_times = small[:, at : at + timesteps.size]
    segments = timesteps.shape[1]
    picks = (segment_local[..., None] == jnp.arange(segments, dtype=jnp.int32)).astype(F32)
    picks = picks.reshape(-1, segments)

    all_cond = embed_times(all_times, width).reshape(-1, width)
    act_rows = jax.nn.silu(all_cond).astype(BF16)
    me = lax.axis_index("dp")
    rows = encoder[0].shape[0]
    act_mine = lax.dynamic_slice_in_dim(act_rows, me * rows, rows, 1)
    core = lax.axis_index("ctx")
    share = encoder[0].shape[1] // 2
    partial = dense(act_mine, lax.dynamic_slice_in_dim(encoder[0], core * share, share, 1))
    partial = partial.reshape(GRID + (8, -1))
    shards = (encoder[2], encoder[4], encoder[5], encoder[6])
    shards += (decoder[0], decoder[2], decoder[4], decoder[5], decoder[6])
    *wholes, partial = gather(shards, partial, *gather_units(shards), 1, "gather")
    wholes = [whole_rows(w) for w in wholes]
    encoder_weights = (*wholes[:4], encoder_gains)
    modulate = wholes[4]
    decoder_weights = (*wholes[5:], decoder_gains)
    partial = jnp.sum(partial, axis=0).reshape(segments, -1)
    others = lax.ppermute(partial, "ctx", [(0, 1), (1, 0)])
    modulation_rows = jnp.where(
        core == 0,
        jnp.concatenate([partial, others], axis=1),
        jnp.concatenate([others, partial], axis=1),
    )
    modulation_rows = modulation_rows + encoder_offset

    def pick(rows):
        return sum(jnp.where(picks[:, j : j + 1] > 0, rows[j], 0.0) for j in range(segments))

    encoder_modulation = pick(modulation_rows)
    cond_rows = lax.dynamic_slice_in_dim(all_cond, me * segments, segments, 0)
    cond = pick(cond_rows)

    shared = {**dict(zip(EARLY[1:], context)), A.flat: flat}
    encoder_in = {**dict(zip(WEIGHTS + EARLY[:1], encoder_weights)), **shared}
    encoder_in[A.mod] = encoder_modulation
    forward = run_block("forward", encoder_in, "encoder")
    decoder_modulation, decoder_pre, latent, act_xt = decoder_modulation_of(
        forward[A.output], valid, cond, decoder_offset, modulate
    )
    decoder_in = {**dict(zip(WEIGHTS + EARLY[:1], decoder_weights)), **shared}
    decoder_in[A.mod] = decoder_modulation
    decoder_in[A.grad_out] = valid * cotangent
    decoder_in[A.marks] = jnp.ones((8, flat.shape[0]), BF16)
    both = run_block("both", decoder_in, "decoder")
    velocity = valid * both[A.output]

    def pair_up(lefts, grads):
        return (
            ([lefts[A.xt1]], grads[A.grad_projected]),
            ([lefts[A.xtm]], grads[A.grad_attended]),
            ([lefts[A.xt2]], grads[A.grad_expanded]),
            ([lefts[A.xth0], lefts[A.xth1], lefts[A.xth2]], grads[A.grad_feed]),
        )

    factors = pair_up(both, both)
    grad_modulation = both[A.grad_mod]
    gains_grad = both[A.gains_grad]
    grad_latent = modulation_back(grad_modulation, valid, decoder_pre, modulate)
    offset_grad = both[A.mark_sums][0]
    extra = jnp.concatenate(
        [
            offset_grad.reshape(16, -1),
            gains_grad.reshape(2, 16, -1).swapaxes(0, 1).reshape(16, -1),
        ],
        axis=1,
    )
    first = ([act_xt], grad_modulation)
    decoder_block = ((factors[1], factors[0], factors[2], first, factors[3]), extra)

    encoder_in[A.grad_out] = grad_latent
    encoder_in[A.marks] = jnp.pad(picks.T, ((0, 8 - segments), (0, 0))).astype(BF16)
    backward = run_block("backward", {**encoder_in, **forward}, "encoder_back")
    factors = pair_up(forward, backward)
    grad_modulation = backward[A.grad_mod]
    gains_grad = backward[A.gains_grad]
    grad_rows = backward[A.mark_sums][:segments]
    grad_rows = grad_rows + lax.ppermute(grad_rows, "ctx", [(0, 1), (1, 0)])
    extra = gains_grad.reshape(2, 16, -1).swapaxes(0, 1).reshape(16, -1)
    results, all_rows = fast_reduce(
        (decoder_block, (factors, extra)), grad_rows.astype(BF16).reshape(16, -1), 2, "scatter"
    )
    (grads, small), (encoder_parts, encoder_small) = results
    decoder_grads = (
        grads[3],
        small[:offset_size],
        grads[1],
        small[offset_size:].reshape(2, -1),
        grads[0],
        grads[2],
        grads[4],
    )
    all_rows = all_rows.reshape(16 * segments, -1)
    modulate_grad = outer_sum(act_mine, all_rows)
    offset_grad = lax.dynamic_slice_in_dim(
        jnp.sum(all_rows.astype(F32), axis=0), me * offset_size, offset_size, 0
    )
    encoder_grads = (
        modulate_grad,
        offset_grad,
        encoder_parts[0],
        encoder_small.reshape(2, -1),
        encoder_parts[1],
        encoder_parts[2],
        encoder_parts[3],
    )
    token_grad = both[A.grad_flat] + backward[A.grad_flat]
    return velocity, latent, token_grad, encoder_grads, decoder_grads


def plain_gather(block):
    parts = [lax.all_gather(block[k], "dp", axis=0, tiled=True) for k in (0, 1, 2, 4, 5, 6)]
    gains = lax.all_gather(block[3], "dp", axis=1, tiled=True).astype(F32)
    modulate, offset, triple, mixing, expand, reduce_w = parts
    return modulate, offset.astype(F32), (triple, mixing, expand, reduce_w, gains)


def plain_reduce(factors, grad_modulation, gains_grad):
    def rows(values, dim=0):
        part = lax.psum_scatter(values, "dp", scatter_dimension=dim, tiled=True)
        return lax.psum(part.astype(BF16), "ctx").astype(F32)

    offset = rows(jnp.sum(grad_modulation, axis=0, dtype=F32))
    modulate, triple, mixing, expand, reduce_w = [rows(outer_sum(a, b)) for a, b in factors]
    return modulate, offset, triple, rows(gains_grad, 1), mixing, expand, reduce_w


def plain_step(flat, cotangent, context, segment_local, valid, timesteps, encoder, decoder):
    picks = (
        segment_local[..., None] == jnp.arange(timesteps.shape[-1], dtype=jnp.int32)
    ).astype(F32)
    times = jnp.sum(picks * timesteps[:, None, :].astype(F32), axis=-1)
    cond = embed_times(times, flat.shape[1]).reshape(flat.shape)
    modulate, offset, encoder_weights = plain_gather(encoder)
    encoder_act = jax.nn.silu(cond).astype(BF16)
    encoder_out, encoder_kept = block_forward(
        flat, dense(encoder_act, modulate) + offset, encoder_weights, context
    )
    latent_full = valid * encoder_out
    decoder_pre = latent_full + cond
    decoder_act = jax.nn.silu(decoder_pre).astype(BF16)
    modulate, offset, decoder_weights = plain_gather(decoder)
    decoder_out, decoder_kept = block_forward(
        flat, dense(decoder_act, modulate) + offset, decoder_weights, context
    )
    decoder_flat, grad_modulation, factors, gains_grad = block_backward(
        valid * cotangent, decoder_kept, decoder_weights, context
    )
    grad_act = dense_back(grad_modulation, modulate)
    decoder_grads = plain_reduce(
        ((decoder_act, grad_modulation),) + factors, grad_modulation, gains_grad
    )
    unused_silu, silu_pull = jax.vjp(jax.nn.silu, decoder_pre)
    encoder_flat, grad_modulation, factors, gains_grad = block_backward(
        valid * silu_pull(grad_act)[0], encoder_kept, encoder_weights, context
    )
    encoder_grads = plain_reduce(
        ((encoder_act, grad_modulation),) + factors, grad_modulation, gains_grad
    )
    return valid * decoder_out, latent_full, decoder_flat + encoder_flat, encoder_grads, decoder_grads


def local(fast, tokens, cotangent, segment, rows, columns, padding, timesteps, *weights):
    batch, half, width = tokens.shape
    start = lax.axis_index("ctx") * half
    segment_local = lax.dynamic_slice_in_dim(segment, start, half, 1)
    rows_local = lax.dynamic_slice_in_dim(rows, start, half, 1)
    columns_local = lax.dynamic_slice_in_dim(columns, start, half, 1)
    padding_local = lax.dynamic_slice_in_dim(padding, start, half, 1)
    place_query = start + jnp.arange(half, dtype=jnp.int32)
    place_key = jnp.arange(segment.shape[1], dtype=jnp.int32)
    allowed = (segment_local[:, :, None] == segment[:, None, :]) & (
        (padding[:, None, :] == 0) | (place_query[None, :, None] == place_key[None, None, :])
    )
    cosine, sine = rope_tables(rows_local.reshape(-1), columns_local.reshape(-1))
    context = (batch, half, allowed, cosine, sine)
    if fast:
        context = rope_lanes(cosine, sine)
        context += (segment_local.reshape(-1, 1), segment, padding)
    valid = (1 - padding_local).astype(F32).reshape(-1, 1)
    flat = tokens.reshape(-1, width).astype(F32)
    step = fast_step if fast else plain_step
    velocity, latent, token_grad, encoder_grads, decoder_grads = step(
        flat,
        cotangent.reshape(-1, width).astype(F32),
        context,
        segment_local,
        valid,
        timesteps,
        weights[:7],
        weights[7:],
    )
    return (
        velocity.astype(BF16).reshape(batch, half, width),
        latent.astype(BF16).reshape(batch, half, width),
        token_grad.reshape(batch, half, width),
        *encoder_grads,
        *decoder_grads,
    )


def solution(mesh):
    fast = dict(mesh.shape) == {"dp": math.prod(GRID), "ctx": 2}
    block = (
        P("dp", None),
        P("dp"),
        P("dp", None),
        P(None, "dp"),
        P("dp", None),
        P("dp", None),
        P("dp", None),
    )
    slots = P("dp", "ctx", None)
    return jax.shard_map(
        functools.partial(local, fast),
        mesh=mesh,
        in_specs=(slots, slots) + (P("dp", None),) * 5 + block + block,
        out_specs=(slots, slots, slots) + block + block,
        check_vma=False,
    )
```

```python
import enum
import functools
import math

import jax
import jax.numpy as jnp
from jax import lax
from jax.experimental import pallas as pl
from jax.experimental.pallas import tpu as pltpu
from jax.sharding import PartitionSpec as P

HEADS = 16
HD = 72
MESH = pl.DeviceIdType.MESH
GRID = (4, 2, 2)
BF16 = jnp.bfloat16
F32 = jnp.float32


def coords():
    dp = lax.axis_index("dp")
    return (lax.div(dp, 4), lax.rem(lax.div(dp, 2), 2), lax.rem(dp, 2), lax.axis_index("ctx"))


def device(z, y, x, c):
    return (z * 4 + y * 2 + x, c)


def when(cond, body):
    if cond is True:
        body()
    else:
        pl.when(cond)(body)


def greet():
    barrier = pltpu.get_barrier_semaphore()
    me = lax.axis_index("dp")
    c = lax.axis_index("ctx")
    for k in range(1, 16):
        pl.semaphore_signal(
            barrier, inc=1, device_id=(lax.rem(me + k, 16), c), device_id_type=MESH
        )
    pl.semaphore_signal(barrier, inc=1, device_id=(me, 1 - c), device_id_type=MESH)
    pl.semaphore_wait(barrier, 16)


class Exchange:
    def __init__(self, same, in_ref, out_ref, ssem, rsem, lsem):
        self.refs = (in_ref, out_ref, ssem, rsem, lsem)
        self.same = same
        self.me = lax.axis_index("dp")

    def source(self, target):
        return self.refs[0] if self.same else self.refs[0].at[target]

    def copy(self, k, target, slot):
        return pltpu.make_async_remote_copy(
            self.source(target),
            self.refs[1].at[slot],
            self.refs[2].at[k],
            self.refs[3].at[k],
            device_id=(target, lax.axis_index("ctx")),
            device_id_type=MESH,
        )

    def own(self):
        return pltpu.make_async_copy(
            self.source(self.me), self.refs[1].at[self.me], self.refs[4].at[0]
        )

    def start(self):
        for k in range(1, 16):
            self.copy(k, lax.rem(self.me + k, 16), self.me).start()
        self.own().start()

    def wait(self):
        self.own().wait()
        for k in range(1, 16):
            self.copy(k, lax.rem(self.me + k, 16), self.me).wait_send()
            origin = lax.rem(self.me + 16 - k, 16)
            self.copy(k, origin, origin).wait_recv()


class Sums:
    def __init__(self, in_ref, out_ref, box, total, ssem, rsem, lsem):
        self.refs = (in_ref, out_ref, box, total)
        self.sems = (ssem, rsem, lsem)
        self.z, self.y, self.x, self.c = coords()

    def remote(self, src, dst, k, target):
        return pltpu.make_async_remote_copy(
            src,
            dst,
            self.sems[0].at[k],
            self.sems[1].at[k],
            device_id=target,
            device_id_type=MESH,
        )

    def across(self, k):
        y = lax.rem(self.y + k // 2, 2)
        x = lax.rem(self.x + k % 2, 2)
        target = device(self.z, y, x, self.c)
        return self.remote(self.refs[0].at[:, y, x], self.refs[2].at[k], k, target)

    def own(self):
        return pltpu.make_async_copy(
            self.refs[0].at[:, self.y, self.x], self.refs[2].at[0], self.sems[2].at[0]
        )

    def along(self, k, arrival):
        there = lax.rem(self.z + (4 - k if arrival else k), 4)
        slot = there if arrival else self.z
        target = device(there, self.y, self.x, self.c)
        return self.remote(self.refs[3].at[there], self.refs[1].at[slot], 3 + k, target)

    def kept(self):
        return pltpu.make_async_copy(
            self.refs[3].at[self.z], self.refs[1].at[self.z], self.sems[2].at[1]
        )

    def start(self):
        for k in range(1, 4):
            self.across(k).start()
        self.own().start()

    def forward(self):
        self.own().wait()
        for k in range(1, 4):
            self.across(k).wait_recv()
        box = self.refs[2]
        self.refs[3][...] = (box[0] + box[1]) + (box[2] + box[3])
        for k in range(1, 4):
            self.along(k, False).start()
        self.kept().start()

    def wait(self):
        self.kept().wait()
        for k in range(1, 4):
            self.across(k).wait_send()
            self.along(k, False).wait_send()
            self.along(k, True).wait_recv()


class Broadcast:
    def __init__(self, in_ref, out_ref, ssem, rsem, lsem):
        self.refs = (in_ref, out_ref, ssem, rsem, lsem)
        self.z, self.y, self.x, self.c = coords()

    def own(self):
        return pltpu.make_async_copy(
            self.refs[0], self.refs[1].at[self.z, self.y, self.x], self.refs[4].at[0]
        )

    def along(self, k, arrival):
        there = lax.rem(self.z + (4 - k if arrival else k), 4)
        slot = there if arrival else self.z
        return pltpu.make_async_remote_copy(
            self.refs[0],
            self.refs[1].at[slot, self.y, self.x],
            self.refs[2].at[k],
            self.refs[3].at[k],
            device_id=device(there, self.y, self.x, self.c),
            device_id_type=MESH,
        )

    def across(self, k, arrival):
        y = lax.rem(self.y + k // 2, 2)
        x = lax.rem(self.x + k % 2, 2)
        block = self.refs[1].at[:, y, x] if arrival else self.refs[1].at[:, self.y, self.x]
        return pltpu.make_async_remote_copy(
            block,
            block,
            self.refs[2].at[3 + k],
            self.refs[3].at[3 + k],
            device_id=device(self.z, y, x, self.c),
            device_id_type=MESH,
        )

    def start(self):
        for k in range(1, 4):
            self.along(k, False).start()
        self.own().start()

    def forward(self):
        self.own().wait()
        for k in range(1, 4):
            self.along(k, True).wait_recv()
        for k in range(1, 4):
            self.across(k, False).start()

    def wait(self):
        for k in range(1, 4):
            self.along(k, False).wait_send()
            self.across(k, False).wait_send()
            self.across(k, True).wait_recv()


def gather_kernel(units, turns, count, *refs):
    w = refs[:count]
    o = refs[count + 1 : 2 * count + 1]
    ssem, rsem, lsem, csem, crsem, box, sums, es, er, el = refs[2 * count + 2 :]
    z, y, x, c = coords()
    greet()
    side = Sums(refs[count], refs[2 * count + 1], box, sums, es, er, el)
    side.start()
    up = device(z + 1, y, x, c)
    down = device(z - 1, y, x, c)
    partner = {"y": device(z, 1 - y, x, c), "x": device(z, y, 1 - x, c)}
    every = slice(None)

    def run(mine, other, order):
        def view(u, index):
            m, first, cols, _ = mine[u]
            return o[m].at[index[0], index[1], index[2], :, pl.ds(first, cols)]

        def copy(u, index, k, target, own=False):
            m, first, cols, _ = mine[u]
            dst = view(u, index)
            src = w[m].at[:, pl.ds(first, cols)] if own else dst
            return pltpu.make_async_remote_copy(
                src, dst, ssem.at[u, k], rsem.at[u, k], device_id=target, device_id_type=MESH
            )

        def local_copy(u):
            m, first, cols, _ = mine[u]
            return pltpu.make_async_copy(
                w[m].at[:, pl.ds(first, cols)], view(u, (z, y, x)), lsem.at[u]
            )

        def plan(u):
            held = {"z": False, "y": False, "x": False}

            def index(zz=z, flip=None):
                return (
                    every if held["z"] else zz,
                    every if held["y"] else (1 - y if flip == "y" else y),
                    every if held["x"] else (1 - x if flip == "x" else x),
                )

            steps = []
            pending = []
            sends = []
            own = True
            pair = 0
            for axis in mine[u][3]:
                if axis != "z":
                    send = [(True, functools.partial(copy, u, index(), pair, partner[axis], own))]
                    steps.append((pending, send))
                    sends += send
                    pending = [
                        (True, functools.partial(copy, u, index(flip=axis), pair, partner[axis]))
                    ]
                    pair += 1
                else:

                    def chain(shift, k, target, first=False):
                        return functools.partial(copy, u, index(zz=z + shift), k, target, first)

                    one = [(z < 3, chain(0, 2, up, own)), (z > 0, chain(0, 5, down, own))]
                    steps.append((pending, one))
                    middle = (z > 0) & (z < 3)
                    two = [(middle, chain(-1, 3, up)), (middle, chain(1, 6, down))]
                    steps.append(([(z > 0, chain(-1, 2, down)), (z < 3, chain(1, 5, up))], two))
                    three = [(z == 2, chain(-2, 4, up)), (z == 1, chain(2, 7, down))]
                    steps.append(([(z > 1, chain(-2, 3, down)), (z < 2, chain(2, 6, up))], three))
                    pending = [(z == 3, chain(-3, 4, down)), (z == 0, chain(3, 7, up))]
                    sends += one + two + three
                held[axis] = True
                own = False
            return steps, pending, sends

        plans = [plan(u) for u in range(len(mine))]

        def to_core(u, which):
            m, first, cols, _ = which[u]
            block = o[m].at[:, :, :, :, pl.ds(first, cols)]
            return pltpu.make_async_remote_copy(
                block,
                block,
                csem.at[u],
                crsem.at[u],
                device_id=device(z, y, x, 1 - c),
                device_id_type=MESH,
            )

        for u in range(len(mine)):
            local_copy(u).start()
        for at, (u, s) in enumerate(order):
            if at == FORWARD_AT:
                side.forward()
            steps, pending, _ = plans[u]
            if s == 1:
                local_copy(u).wait()
            for cond, make in steps[s][0] if s < 5 else pending:
                when(cond, lambda make=make: make().wait_recv())
            for cond, make in steps[s][1] if s < 5 else ():
                when(cond, lambda make=make: make().start())
            if s == 5:
                to_core(u, mine).start()
        for u in range(len(mine)):
            for cond, make in plans[u][2]:
                when(cond, lambda make=make: make().wait_send())
            to_core(u, mine).wait_send()
        for u in range(len(other)):
            to_core(u, other).wait_recv()

    pl.when(c == 0)(lambda: run(units[0], units[1], turns[0]))
    pl.when(c == 1)(lambda: run(units[1], units[0], turns[1]))
    side.wait()


ANY = pl.BlockSpec(memory_space=pl.ANY)
DMA = pltpu.SemaphoreType.DMA


SIDE = [DMA((16,)), DMA((16,)), DMA((1,))]


def gather(shards, rows, units, turns, collective_id, name):
    count = len(shards)
    most = max(len(units[0]), len(units[1]))
    shapes = [jax.ShapeDtypeStruct(GRID + s.shape, s.dtype) for s in shards]
    return pl.pallas_call(
        functools.partial(gather_kernel, units, turns, count),
        name=name,
        out_shape=shapes + [jax.ShapeDtypeStruct(GRID[:1] + rows.shape[3:], rows.dtype)],
        in_specs=[ANY] * (count + 1),
        out_specs=[ANY] * (count + 1),
        scratch_shapes=[
            DMA((most, 8)),
            DMA((most, 8)),
            DMA((most,)),
            DMA((most,)),
            DMA((most,)),
            pltpu.VMEM((4,) + GRID[:1] + rows.shape[3:], rows.dtype),
            pltpu.VMEM(GRID[:1] + rows.shape[3:], rows.dtype),
            DMA((7,)),
            DMA((7,)),
            DMA((2,)),
        ],
        compiler_params=pltpu.CompilerParams(collective_id=collective_id, has_side_effects=True),
    )(*shards, rows)


ORDERS = (
    ("zyx", "zxy", "xyz", "zxy", "zyx", "zyx", "yxz", "zxy", "zyx"),
    ("zxy", "zyx", "yxz", "zyx", "zxy", "zxy", "xyz", "zyx", "zxy"),
)
AFTER_Z = (0.6165, 0.5838, 0.5725, 1.6339, 4.1589)
AFTER_XY = (1.5672, 1.5028, 1.8589, 1.1737, 2.0677)
PER_TURN = 2.2146
FORWARD_AT = 40
SHIFT = 0.5711
SIZE = 4
TAIL = (0.1, 2)


def gather_units(shards):
    units = ([], [])
    load = [0, 0]
    whole = sum(s.size for s in shards) / (ROWS * 128)
    done = 0
    for m, shard in enumerate(shards):
        rows, columns = shard.shape
        tiles = columns // 128
        weight = rows / ROWS
        at = 0
        while at < tiles:
            size = SIZE if done < (1 - TAIL[0]) * whole else TAIL[1]
            step = max(1, round(size / weight))
            n = min(step, tiles - at)
            if 0 < tiles - at - n < max(1, round(size / weight / 2)):
                n = tiles - at
            core = 0 if load[0] <= load[1] else 1
            order = ORDERS[core][len(units[core]) % len(ORDERS[core])]
            units[core].append((m, at * 128, n * 128, order))
            load[core] += n * weight
            done += n * weight
            at += n
    turns = []
    for core in range(2):
        keys = []
        place = 0.0
        for u, (m, first, columns, order) in enumerate(units[core]):
            at = place / PER_TURN + core * SHIFT
            place += shards[m].shape[0] * columns / (ROWS * 128 * SIZE)
            keys.append((at, u, 0))
            for s, after in enumerate(AFTER_Z if order[0] == "z" else AFTER_XY):
                at += after
                keys.append((at, u, s + 1))
        turns.append(tuple((u, s) for _, u, s in sorted(keys)))
    return (tuple(units[0]), tuple(units[1])), tuple(turns)


def exchange_kernel(in_ref, out_ref, *sems):
    greet()
    side = Exchange(True, in_ref, out_ref, *sems)
    side.start()
    side.wait()


def exchange(values, collective_id, name):
    return pl.pallas_call(
        exchange_kernel,
        name=name,
        out_shape=jax.ShapeDtypeStruct((16,) + values.shape, values.dtype),
        in_specs=[ANY],
        out_specs=ANY,
        scratch_shapes=SIDE,
        compiler_params=pltpu.CompilerParams(collective_id=collective_id, has_side_effects=True),
    )(values)


RECV_SLOTS = 10
SEND_SLOTS = 8
FIRST_SLOTS = 4
UNIT = 384
ROWS = 72
PADDED = 80


def scatter_kernel(first, cols, source, dy_count, *refs):
    nv = len(first) - 1
    xt = refs[:nv]
    dy = refs[nv : nv + dy_count]
    out = refs[nv + dy_count + 1]
    (
        xts, dys, a_s1, a_s2, a_t, a_su, a_sd, e_s1, e_t, e_su, e_sd, e_sq,
        a_b1, a_b2, a_bu, a_bd, e_b1, e_bu, e_bd, e_bq, outs,
        ssem, rsem, xl, xs, xr, yl, ys, yr, ol, os, orr, es, er, el,
    ) = refs[nv + dy_count + 3 :]
    z, y, x, c = coords()
    total = first[-1] // 2
    sibling = device(z, y, x, 1 - c)
    up = device(z + 1, y, x, c)
    down = device(z - 1, y, x, c)
    greet()
    side = Broadcast(refs[nv + dy_count], refs[nv + dy_count + 2], es, er, el)
    lanes = pl.ds(pl.multiple_of(c * 128, 128), 128)
    offsets = []
    at = 0
    for k in range(dy_count):
        offsets.append(at)
        at += dy[k].shape[1]

    def remote(src, dst, send, recv, target):
        return pltpu.make_async_remote_copy(
            src, dst, send, recv, device_id=target, device_id_type=MESH
        )

    def x_views(v):
        return xt[v], xts.at[v, :, :, lanes]

    def x_local(v):
        return pltpu.make_async_copy(*x_views(v), xl.at[v])

    def x_remote(v):
        return remote(*x_views(v), xs.at[v], xr.at[v], sibling)

    def y_views(k):
        return dy[k], dys.at[lanes, pl.ds(offsets[k], dy[k].shape[1])]

    def y_local(k):
        return pltpu.make_async_copy(*y_views(k), yl.at[k])

    def y_remote(k):
        return remote(*y_views(k), ys.at[k], yr.at[k], sibling)

    fresh = [source[v] not in source[:v] for v in range(nv)]

    def bring(v):
        x_local(v).start()
        x_remote(v).start()
        if fresh[v]:
            y_local(source[v]).start()
            y_remote(source[v]).start()

    bring(0)
    bring(1)
    side.start()

    def arrive(tick):
        for v in range(nv):

            def wait(v=v):
                x_local(v).wait()
                x_remote(v).wait_recv()
                if fresh[v]:
                    y_local(source[v]).wait()
                    y_remote(source[v]).wait_recv()
                if v + 2 < nv:
                    bring(v + 2)

            pl.when(tick == (first[v] - c + 1) // 2)(wait)

    def unit(i):
        j = 2 * i + c
        v = jnp.int32(0)
        col = j * UNIT
        for k in range(1, nv):
            past = (j >= first[k]).astype(jnp.int32)
            v = v + past
            col = col + past * ((cols[k] - first[k] * UNIT) - (cols[k - 1] - first[k - 1] * UNIT))
        return v, pl.multiple_of(col, 128)

    def axes(i):
        o = lax.rem(i, 2)
        pb = x * (1 - o) + y * o
        qb = y * (1 - o) + x * o
        dp = z * 4 + y * 2 + x
        return o, pb, qb, (dp + (1 - 2 * pb) * (1 + o), c), (dp + (1 - 2 * qb) * (2 - o), c)

    def slots(i):
        return lax.rem(i, FIRST_SLOTS), lax.rem(i, SEND_SLOTS), lax.rem(i, RECV_SLOTS)

    def send(src, dst, i, k, target):
        return remote(
            src, dst, ssem.at[lax.rem(i, SEND_SLOTS), k], rsem.at[lax.rem(i, RECV_SLOTS), k], target
        )

    def first_copies(i):
        o, pb, qb, pn, qn = axes(i)
        f, s, w = slots(i)
        return [send(a_s1.at[f], a_b1.at[w], i, 0, pn), send(e_s1.at[f], e_b1.at[w], i, 8, pn)]

    def second_copy(i):
        o, pb, qb, pn, qn = axes(i)
        f, s, w = slots(i)
        return send(a_s2.at[s], a_b2.at[w], i, 1, qn)

    def last_copy(i):
        o, pb, qb, pn, qn = axes(i)
        f, s, w = slots(i)
        return send(e_sq.at[s], e_bq.at[w], i, 9, qn)

    def up_copy(i, k, e):
        f, s, w = slots(i)
        src, dst, n = (e_su, e_bu, 10) if e else (a_su, a_bu, 2)
        return send(src.at[s, k], dst.at[w, k], i, n + k, up)

    def down_copy(i, k, e):
        f, s, w = slots(i)
        src, dst, n = (e_sd, e_bd, 13) if e else (a_sd, a_bd, 5)
        return send(src.at[s, k], dst.at[w, k], i, n + k, down)

    def up_sends(k):
        return (z <= k) & (z < 3)

    def down_sends(k):
        return (3 - z <= k) & (z > 0)

    def up_comes(k):
        return (z >= 1) & (z <= k + 1)

    def down_comes(k):
        return (z <= 2) & (3 - z <= k + 1)

    def kept(i, e, d):
        f, s, w = slots(i)
        if e:
            return e_t.at[s, d]
        return a_t.at[s, d, axes(i)[2]]

    def z_send(i, k, e):
        f, s, w = slots(i)

        def pass_on(dest, stage, box, inner, copy):
            value = kept(i, e, dest)[...]
            if k == 0:
                stage[s, k] = value.astype(BF16)
            else:

                def add():
                    stage[s, k] = (value + box[w, k - 1].astype(F32)).astype(BF16)

                def begin():
                    stage[s, k] = value.astype(BF16)

                pl.when(inner)(add)
                pl.when(jnp.logical_not(inner))(begin)
            copy.start()

        pl.when(up_sends(k))(
            lambda: pass_on(
                z + 3 - k, e_su if e else a_su, e_bu if e else a_bu, z > 0, up_copy(i, k, e)
            )
        )
        pl.when(down_sends(k))(
            lambda: pass_on(
                z + k - 3, e_sd if e else a_sd, e_bd if e else a_bd, z < 3, down_copy(i, k, e)
            )
        )

    def z_wait(i, k, e):
        pl.when(up_comes(k))(lambda: up_copy(i, k, e).wait_recv())
        pl.when(down_comes(k))(lambda: down_copy(i, k, e).wait_recv())

    def z_close(i, e):
        f, s, w = slots(i)
        mine = kept(i, e, z)

        def below():
            mine[...] = mine[...] + (e_bu if e else a_bu)[w, 2].astype(F32)

        def above():
            mine[...] = mine[...] + (e_bd if e else a_bd)[w, 2].astype(F32)

        pl.when(z > 0)(below)
        pl.when(z < 3)(above)
        return mine

    def product(i, bit):
        v, col = unit(i)
        o = axes(i)[0]
        chips = [4 * k + bit * (1 + o) + q * (2 - o) for k in range(4) for q in range(2)]
        lhs = jnp.concatenate([xts[v, chip] for chip in chips], axis=0)
        whole = jnp.dot(lhs, dys[:, pl.ds(col, UNIT)], preferred_element_type=F32)
        return whole.reshape(8, PADDED, UNIT)[:, :ROWS]

    def stage0(i):
        f, s, w = slots(i)
        part = product(i, 1 - axes(i)[1])
        a_s1[f] = part[:, :, :128].astype(BF16).reshape(4, 2, ROWS, 128)
        e_s1[f] = part[:, :, 128:].astype(BF16).reshape(4, 2, ROWS, 256)
        for copy in first_copies(i):
            copy.start()

    def stage1(i):
        f, s, w = slots(i)
        o, pb, qb, pn, qn = axes(i)
        part = product(i, pb)
        for copy in first_copies(i):
            copy.wait_recv()
        a_t[s] = part[:, :, :128].reshape(4, 2, ROWS, 128) + a_b1[w].astype(F32)
        a_s2[s] = a_t[s, :, 1 - qb].astype(BF16)
        second_copy(i).start()
        e_t[s] = part[:, :, 128:].reshape(4, 2, ROWS, 256) + e_b1[w].astype(F32)
        z_send(i, 0, True)

    def a_second(i):
        f, s, w = slots(i)
        qb = axes(i)[2]
        second_copy(i).wait_recv()
        a_t[s, :, qb] = a_t[s, :, qb] + a_b2[w].astype(F32)
        z_send(i, 0, False)

    def z_step(i, k, e):
        z_wait(i, k - 1, e)
        z_send(i, k, e)

    def e_fourth(i):
        f, s, w = slots(i)
        z_wait(i, 2, True)
        z_close(i, True)
        e_sq[s] = e_t[s, z, 1 - axes(i)[2]].astype(BF16)
        last_copy(i).start()

    def out_view(i):
        return out.at[:, pl.ds(pl.multiple_of((2 * i + c) * UNIT, 128), UNIT)]

    def a_fifth(i):
        z_wait(i, 2, False)
        outs[i, :, :128] = z_close(i, False)[...]

    def e_fifth(i):
        f, s, w = slots(i)
        last_copy(i).wait_recv()
        outs[i, :, 128:] = e_t[s, z, axes(i)[2]] + e_bq[w].astype(F32)
        pltpu.make_async_copy(outs.at[i], out_view(i), ol.at[0]).start()
        remote(outs.at[i], out_view(i), os.at[0], orr.at[0], sibling).start()

    def first_sent(i):
        for copy in first_copies(i):
            copy.wait_send()

    def sent(i):
        second_copy(i).wait_send()
        last_copy(i).wait_send()
        for e in (False, True):
            for k in range(3):
                pl.when(up_sends(k))(lambda k=k, e=e: up_copy(i, k, e).wait_send())
                pl.when(down_sends(k))(lambda k=k, e=e: down_copy(i, k, e).wait_send())

    stages = (
        (a_second, 4),
        (functools.partial(z_step, k=2, e=False), 5),
        (e_fourth, 5),
        (functools.partial(z_step, k=1, e=False), 4),
        (a_fifth, 6),
        (functools.partial(z_step, k=1, e=True), 3),
        (stage0, 0),
        (e_fifth, 7),
        (functools.partial(z_step, k=2, e=True), 3),
        (stage1, 2),
    )

    def tick(t, carry):
        arrive(t)
        pl.when(t == 14)(side.forward)
        pl.when((t >= SEND_SLOTS) & (t - SEND_SLOTS < total))(lambda: sent(t - SEND_SLOTS))
        pl.when((t >= FIRST_SLOTS) & (t - FIRST_SLOTS < total))(lambda: first_sent(t - FIRST_SLOTS))
        for stage, lag in stages:
            i = t - lag
            pl.when((i >= 0) & (i < total))(functools.partial(stage, i))
        return carry

    lax.fori_loop(0, total + SEND_SLOTS, tick, 0)
    for v in range(nv):
        x_remote(v).wait_send()
    for k in range(dy_count):
        y_remote(k).wait_send()
    half = out.at[:, pl.ds(0, total * UNIT)]
    pltpu.make_async_copy(half, half, ol.at[0]).wait()
    everything = remote(half, half, os.at[0], orr.at[0], sibling)
    everything.wait_send()
    everything.wait_recv()
    side.wait()


def scatter(xts, dys, source, rows, collective_id, name):
    nv = len(xts)
    starts = []
    width = 0
    for d in dys:
        starts.append(width)
        width += d.shape[1]
    first = [0]
    cols = []
    for v in range(nv):
        cols.append(starts[source[v]])
        first.append(first[-1] + dys[source[v]].shape[1] // UNIT)
    total = first[-1] // 2
    s, f, r = SEND_SLOTS, FIRST_SLOTS, RECV_SLOTS
    vmem = pltpu.VMEM
    return pl.pallas_call(
        functools.partial(scatter_kernel, tuple(first), tuple(cols), tuple(source), len(dys)),
        name=name,
        out_shape=[
            jax.ShapeDtypeStruct((ROWS, first[-1] * UNIT), F32),
            jax.ShapeDtypeStruct(GRID + rows.shape, rows.dtype),
        ],
        in_specs=[ANY] * (nv + len(dys) + 1),
        out_specs=[ANY] * 2,
        scratch_shapes=[
            vmem((nv, 16, PADDED, 256), BF16),
            vmem((256, width), BF16),
            vmem((f, 4, 2, ROWS, 128), BF16),
            vmem((s, 4, ROWS, 128), BF16),
            vmem((s, 4, 2, ROWS, 128), F32),
            vmem((s, 3, ROWS, 128), BF16),
            vmem((s, 3, ROWS, 128), BF16),
            vmem((f, 4, 2, ROWS, 256), BF16),
            vmem((s, 4, 2, ROWS, 256), F32),
            vmem((s, 3, 2, ROWS, 256), BF16),
            vmem((s, 3, 2, ROWS, 256), BF16),
            vmem((s, ROWS, 256), BF16),
            vmem((r, 4, 2, ROWS, 128), BF16),
            vmem((r, 4, ROWS, 128), BF16),
            vmem((r, 3, ROWS, 128), BF16),
            vmem((r, 3, ROWS, 128), BF16),
            vmem((r, 4, 2, ROWS, 256), BF16),
            vmem((r, 3, 2, ROWS, 256), BF16),
            vmem((r, 3, 2, ROWS, 256), BF16),
            vmem((r, ROWS, 256), BF16),
            vmem((total, ROWS, UNIT), F32),
            DMA((s, 16)),
            DMA((r, 16)),
            DMA((nv,)),
            DMA((nv,)),
            DMA((nv,)),
            DMA((len(dys),)),
            DMA((len(dys),)),
            DMA((len(dys),)),
            DMA((1,)),
            DMA((1,)),
            DMA((1,)),
        ]
        + SIDE,
        compiler_params=pltpu.CompilerParams(
            collective_id=collective_id, has_side_effects=True, vmem_limit_bytes=62 * 1024 * 1024
        ),
    )(*xts, *dys, rows)


def layer_norm(values):
    center = values - jnp.mean(values, axis=-1, keepdims=True)
    spread = jnp.mean(center * center, axis=-1, keepdims=True)
    return center * lax.rsqrt(spread + 1e-06)


def head_norm(values, gain):
    shaped = values.reshape(values.shape[:-1] + (HEADS, HD))
    scaled = shaped * lax.rsqrt(jnp.mean(shaped * shaped, axis=-1, keepdims=True) + 1e-06)
    return scaled * gain.reshape(HEADS, HD)


def rope_tables(rows, columns):
    quarter = HD // 4
    freqs = jnp.exp(jnp.arange(quarter, dtype=F32) * (-math.log(10000.0) / quarter))
    places = jnp.stack([rows, columns], axis=-1).astype(F32)
    angles = places[..., None] * freqs
    return (jnp.cos(angles), jnp.sin(angles))


def rotate(values, cosine, sine):
    shaped = values.reshape(values.shape[:-1] + (2, 2, HD // 4))
    first = shaped[..., 0, :]
    second = shaped[..., 1, :]
    cosine = cosine[..., None, :, :]
    sine = sine[..., None, :, :]
    turned = jnp.stack([first * cosine - second * sine, first * sine + second * cosine], axis=-2)
    return turned.reshape(values.shape)


def embed_times(times, width):
    half_width = width // 2
    freqs = jnp.exp(jnp.arange(half_width, dtype=F32) * (-math.log(10000.0) / half_width))
    angles = times[..., None] * freqs
    return jnp.concatenate([jnp.cos(angles), jnp.sin(angles)], axis=-1)


def qk_prepare(query_raw, key_raw, gains, cosine, sine):
    return (
        rotate(head_norm(query_raw, gains[0]), cosine, sine),
        rotate(head_norm(key_raw, gains[1]), cosine, sine),
    )


def swish_product(gate, up):
    return jax.nn.silu(gate) * up


def attention_scores(queries, keys, allowed):
    scores = jnp.einsum("sqhd,skhd->shqk", queries, keys, preferred_element_type=F32) * (
        1.0 / math.sqrt(HD)
    )
    return jnp.where(allowed[:, None], scores, -1e30)


def dense(values, weight):
    return jnp.dot(values, weight, preferred_element_type=F32)


def dense_back(grads, weight):
    return lax.dot_general(grads, weight, (((1,), (1,)), ((), ())), preferred_element_type=F32)


def outer_sum(values, grads):
    return lax.dot_general(values, grads, (((0,), (0,)), ((), ())), preferred_element_type=F32)


def block_forward(flat, modulation, weights, context):
    batch, half, allowed, cosine, sine = context
    triple, mixing, expand, reduce_w, gains = weights
    width = flat.shape[1]
    shift1, scale1, gate1, shift2, scale2, gate2 = jnp.split(modulation, 6, axis=1)
    lifted1 = (layer_norm(flat) * (1.0 + scale1) + shift1).astype(BF16)
    projected = dense(lifted1, triple)
    query_raw, key_raw, value_raw = jnp.split(projected, 3, axis=1)
    queries, keys = qk_prepare(query_raw, key_raw, gains, cosine, sine)
    queries = queries.astype(BF16).reshape(batch, half, HEADS, HD)
    keys_local = keys.astype(BF16).reshape(batch, half, width)
    values_local = value_raw.astype(BF16).reshape(batch, half, width)
    key_heads = lax.all_gather(keys_local, "ctx", axis=1, tiled=True).reshape(batch, -1, HEADS, HD)
    value_heads = lax.all_gather(values_local, "ctx", axis=1, tiled=True)
    value_heads = value_heads.reshape(batch, -1, HEADS, HD)
    scores = attention_scores(queries, key_heads, allowed)
    top = jnp.max(scores, axis=-1, keepdims=True)
    raised = jnp.exp(scores - top)
    total = jnp.sum(raised, axis=-1, keepdims=True)
    softmax_low = (raised / total).astype(BF16)
    logsum = top + jnp.log(total)
    mixed = jnp.einsum("shqk,skhd->sqhd", softmax_low, value_heads, preferred_element_type=F32)
    mixed_low = mixed.reshape(-1, width).astype(BF16)
    attended = dense(mixed_low, mixing)
    resid = flat + gate1 * attended
    lifted2 = (layer_norm(resid) * (1.0 + scale2) + shift2).astype(BF16)
    expanded = dense(lifted2, expand)
    gate, up = jnp.split(expanded, 2, axis=1)
    hidden = swish_product(gate, up).astype(BF16)
    feed = dense(hidden, reduce_w)
    output = resid + gate2 * feed
    kept = (
        modulation,
        flat,
        lifted1,
        query_raw,
        key_raw,
        queries,
        key_heads,
        value_heads,
        logsum,
        mixed_low,
        attended,
        resid,
        lifted2,
        expanded,
        hidden,
        feed,
    )
    return (output, kept)


def block_backward(grad_out, kept, weights, context):
    batch, half, allowed, cosine, sine = context
    triple, mixing, expand, reduce_w, gains = weights
    (
        modulation,
        flat,
        lifted1,
        query_raw,
        key_raw,
        queries,
        key_heads,
        value_heads,
        logsum,
        mixed_low,
        attended,
        resid,
        lifted2,
        expanded,
        hidden,
        feed,
    ) = kept
    width = flat.shape[1]
    shift1, scale1, gate1, shift2, scale2, gate2 = jnp.split(modulation, 6, axis=1)
    grad_feed = (grad_out * gate2).astype(BF16)
    grad_hidden = dense_back(grad_feed, reduce_w)
    gate, up = jnp.split(expanded, 2, axis=1)
    unused_out, swish_pull = jax.vjp(swish_product, gate, up)
    grad_gate, grad_up = swish_pull(grad_hidden)
    grad_expanded = jnp.concatenate([grad_gate, grad_up], axis=1).astype(BF16)
    grad_lifted2 = dense_back(grad_expanded, expand)
    normed_second, second_pull = jax.vjp(layer_norm, resid)
    grad_resid = grad_out + second_pull(grad_lifted2 * (1.0 + scale2))[0]
    grad_attended = (grad_resid * gate1).astype(BF16)
    grad_mixed = dense_back(grad_attended, mixing).astype(BF16).reshape(batch, half, HEADS, HD)
    scores = attention_scores(queries, key_heads, allowed)
    chances = jnp.exp(scores - logsum)
    grad_chances = jnp.einsum(
        "sqhd,skhd->shqk", grad_mixed, value_heads, preferred_element_type=F32
    )
    grad_values = jnp.einsum(
        "shqk,sqhd->skhd", chances.astype(BF16), grad_mixed, preferred_element_type=F32
    )
    grad_scores = (
        chances * (grad_chances - jnp.sum(chances * grad_chances, axis=-1, keepdims=True))
    ).astype(BF16)
    scale = 1.0 / math.sqrt(HD)
    grad_queries = (
        jnp.einsum("shqk,skhd->sqhd", grad_scores, key_heads, preferred_element_type=F32) * scale
    )
    grad_keys = (
        jnp.einsum("shqk,sqhd->skhd", grad_scores, queries, preferred_element_type=F32) * scale
    )
    pair = jnp.stack(
        [grad_keys.reshape(batch, -1, width), grad_values.reshape(batch, -1, width)]
    ).astype(BF16)
    place = lax.axis_index("ctx")
    theirs = lax.dynamic_slice_in_dim(pair, (1 - place) * half, half, 2)
    theirs = lax.ppermute(theirs, "ctx", [(0, 1), (1, 0)])
    mine = lax.dynamic_slice_in_dim(pair, place * half, half, 2)
    pair = mine.astype(F32) + theirs.astype(F32)
    grad_keys, grad_values = pair[0], pair[1]

    def prepare(query_in, key_in, gain_in):
        return qk_prepare(query_in, key_in, gain_in, cosine, sine)

    unused_pair, prepare_pull = jax.vjp(prepare, query_raw, key_raw, gains)
    grad_query_raw, grad_key_raw, gains_grad = prepare_pull(
        (grad_queries.reshape(-1, HEADS, HD), grad_keys.reshape(-1, HEADS, HD))
    )
    grad_projected = jnp.concatenate(
        [grad_query_raw, grad_key_raw, grad_values.reshape(-1, width)], axis=1
    ).astype(BF16)
    grad_lifted1 = dense_back(grad_projected, triple)
    normed_first, first_pull = jax.vjp(layer_norm, flat)
    grad_flat = grad_resid + first_pull(grad_lifted1 * (1.0 + scale1))[0]
    grad_modulation = jnp.concatenate(
        [
            grad_lifted1,
            grad_lifted1 * normed_first,
            grad_resid * attended,
            grad_lifted2,
            grad_lifted2 * normed_second,
            grad_out * feed,
        ],
        axis=1,
    ).astype(BF16)
    factors = (
        (lifted1, grad_projected),
        (mixed_low, grad_attended),
        (lifted2, grad_expanded),
        (hidden, grad_feed),
    )
    return (grad_flat, grad_modulation, factors, gains_grad)


def meet_sibling():
    barrier = pltpu.get_barrier_semaphore()
    sibling = (lax.axis_index("dp"), 1 - lax.axis_index("ctx"))
    pl.semaphore_signal(barrier, inc=1, device_id=sibling, device_id_type=MESH)
    pl.semaphore_wait(barrier, 1)
    return sibling


def head_sum_matrix(width):
    channel = lax.broadcasted_iota(jnp.int32, (width, 128), 0)
    head = lax.broadcasted_iota(jnp.int32, (width, 128), 1)
    inside = (channel >= head * HD) & (channel < (head + 1) * HD)
    return jnp.where(inside, 1.0, 0.0).astype(F32)


def exact_dot(left, right):
    return jnp.dot(left, right, preferred_element_type=F32, precision=lax.Precision.HIGHEST)


def spread_heads(values, heads):
    return lax.dot_general(
        values,
        heads,
        (((1,), (1,)), ((), ())),
        preferred_element_type=F32,
        precision=lax.Precision.HIGHEST,
    )


def swap_pairs(values):
    width = values.shape[1]
    lane = lax.broadcasted_iota(jnp.int32, values.shape, 1)
    quarter = HD // 4
    early = lax.rem(lane, 2 * quarter) < quarter
    return jnp.where(
        early, pltpu.roll(values, width - quarter, 1), pltpu.roll(values, quarter, 1)
    )


def normalize(values):
    mean = jnp.mean(values, axis=1, keepdims=True)
    center = values - mean
    spread = jnp.mean(center * center, axis=1, keepdims=True)
    inverse = lax.rsqrt(spread + 1e-06)
    return center * inverse, inverse


def norm_back(normed, inverse, grad):
    mean = jnp.mean(grad, axis=1, keepdims=True)
    along = jnp.mean(grad * normed, axis=1, keepdims=True)
    return (grad - mean - normed * along) * inverse


def window(h, width):
    first = min((h * HD) // 128 * 128, width - 256)
    return first, h * HD - first


def head_mask(h, width, rows):
    first, at = window(h, width)
    lane = lax.broadcasted_iota(jnp.int32, (rows, 256), 1)
    return (lane >= at) & (lane < at + HD)


def turned(values):
    tokens, width = values.shape
    rows = values.T.reshape(-1, ROWS, tokens)
    return jnp.concatenate(
        [rows, jnp.zeros((width // ROWS, PADDED - ROWS, tokens), F32)], axis=1
    ).astype(BF16)


FF_TILE = 768
KV_TILE = 1152


def allowed_mask(seg_q, seg_k, pad_k, half):
    place_q = lax.axis_index("ctx") * half + lax.broadcasted_iota(jnp.int32, (half, 2 * half), 0)
    place_k = lax.broadcasted_iota(jnp.int32, (half, 2 * half), 1)
    return (seg_q[...] == seg_k[...]) & ((pad_k[...] == 0) | (place_q == place_k))


MOD_TILE = 768


def weight_tiles(weight, held, sem):
    tiles = []
    for t in range(weight.shape[1] // MOD_TILE):
        span = slice(t * MOD_TILE, (t + 1) * MOD_TILE)
        copy = pltpu.make_async_copy(
            weight.at[:, pl.ds(t * MOD_TILE, MOD_TILE)],
            held.at[:, pl.ds(t * MOD_TILE, MOD_TILE)],
            sem.at[t],
        )
        copy.start()
        tiles.append((span, copy))
    return tiles


def modulation_kernel(block, valid, cond, offset, weight, mod, before, latent, xt, held, sem):
    tiles = weight_tiles(weight, held, sem)
    kept = block[...] * valid[...]
    latent[...] = kept.astype(BF16)
    total = kept + cond[...]
    before[...] = total
    act = (total * jax.nn.sigmoid(total)).astype(BF16)
    xt[...] = turned(act.astype(F32))
    for span, copy in tiles:
        copy.wait()
        part = jnp.dot(act, held[:, span], preferred_element_type=F32)
        mod[:, span] = part + offset[:, span]


def modulation_back_kernel(grad, valid, before, weight, out, held, sem):
    tiles = weight_tiles(weight, held, sem)
    out[...] = jnp.zeros_like(out)
    for span, copy in tiles:
        copy.wait()
        out[...] = out[...] + dense_back(grad[:, span], held[:, span])
    sig = jax.nn.sigmoid(before[...])
    out[...] = valid[...] * (out[...] * (sig * (1.0 + before[...] * (1.0 - sig))))


def modulation_call(kernel, name, inputs, weight, outs):
    in_vmem = pl.BlockSpec(memory_space=pltpu.VMEM)
    return pl.pallas_call(
        kernel,
        name=name,
        out_shape=outs,
        in_specs=[in_vmem] * len(inputs) + [ANY],
        out_specs=[in_vmem] * len(outs),
        scratch_shapes=[pltpu.VMEM(weight.shape, BF16), DMA((weight.shape[1] // MOD_TILE,))],
        compiler_params=pltpu.CompilerParams(vmem_limit_bytes=62 * 1024 * 1024),
    )(*inputs, weight)


def decoder_modulation_of(block, valid, cond, offset, weight):
    rows, width = block.shape
    outs = [
        jax.ShapeDtypeStruct((rows, weight.shape[1]), F32),
        jax.ShapeDtypeStruct((rows, width), F32),
        jax.ShapeDtypeStruct((rows, width), BF16),
        jax.ShapeDtypeStruct((16, PADDED, rows), BF16),
    ]
    inputs = (block, valid, cond, offset.reshape(1, -1))
    return modulation_call(modulation_kernel, "modulation", inputs, weight, outs)


def modulation_back(grad, valid, before, weight):
    outs = [jax.ShapeDtypeStruct(before.shape, F32)]
    return modulation_call(
        modulation_back_kernel, "modulation_back", (grad, valid, before), weight, outs
    )[0]


class A(enum.IntEnum):
    flat = 1
    mod = 2
    gains = 3
    cosine = 4
    sine = 5
    seg_q = 6
    seg_k = 7
    pad_k = 8
    triple = 9
    mixing = 10
    expand = 11
    reduce = 12
    output = 13
    raw = 14
    queries = 15
    kv = 16
    lse = 17
    attended = 18
    resid = 19
    expanded = 20
    feed = 21
    xt1 = 22
    xtm = 23
    xt2 = 24
    xth0 = 25
    xth1 = 26
    xth2 = 27
    lift = 28
    grad_out = 29
    grad_flat = 30
    grad_mod = 31
    grad_feed = 32
    grad_expanded = 33
    grad_attended = 34
    grad_projected = 35
    gains_grad = 36
    grad_v = 38
    outgoing = 39
    incoming = 40
    marks = 41
    mark_sums = 42


class Traffic:
    def __init__(self, held, sources, targets, lsem, ssem):
        self.held = held
        names = [n for n in sources]
        self.loads = {
            n: pltpu.make_async_copy(sources[n], held[n], lsem.at[k]) for k, n in enumerate(names)
        }
        self.sources = sources
        self.tiles = {}
        self.more = None
        self.stores = {
            n: pltpu.make_async_copy(held[n], targets[n], ssem.at[k])
            for k, n in enumerate(targets)
        }
        self.waiting = set(names)

    def __getattr__(self, name):
        return self.held[A[name]]

    def fetch(self, *names):
        for n in names:
            if n in self.loads:
                self.loads[n].start()

    def fetch_tile(self, size, rows, columns, sem, t):
        spans = [(n, (pl.ds(t * size, size), slice(None))) for n in rows]
        for n in columns:
            for first in (0, self.held[n].shape[1] // 2):
                spans.append((n, (slice(None), pl.ds(first + t * size, size))))
        self.tiles[t] = [
            pltpu.make_async_copy(self.sources[n].at[at], self.held[n].at[at], sem.at[t, k])
            for k, (n, at) in enumerate(spans)
        ]
        for copy in self.tiles[t]:
            copy.start()
        self.waiting.difference_update(rows + columns)

    def fetch_parts(self, n, width, order, sem):
        for k in order:
            at = (slice(None), pl.ds(k * width, width))
            copy = pltpu.make_async_copy(
                self.sources[n].at[at], self.held[n].at[at], sem.at[0, k]
            )
            copy.start()
            self.tiles[n, k] = [copy]
        self.waiting.discard(n)

    def need_tile(self, t):
        for copy in self.tiles.pop(t, ()):
            copy.wait()

    def need(self, *names):
        for n in names:
            if n in self.waiting:
                self.loads[n].wait()
                self.waiting.discard(n)

    def emit(self, *names):
        for n in names:
            if n in self.stores:
                self.stores[n].start()

    def close(self):
        for store in self.stores.values():
            store.wait()


def forward_body(r, sibling, ssem, rsem):
    half, width = r.flat.shape
    c = lax.axis_index("ctx")
    mine = pl.ds(pl.multiple_of(c * half, 128), half)
    theirs = pl.ds(pl.multiple_of((1 - c) * half, 128), half)
    hidden_size = r.reduce.shape[0]

    def part(k):
        return r.mod[:, k * width : (k + 1) * width]

    r.need(A.flat, A.mod)
    normed, unused = normalize(r.flat[...])
    lifted_low = (normed * (1.0 + part(1)) + part(0)).astype(BF16)
    heads = head_sum_matrix(width)

    def prepared(k):
        values = r.raw[:, k * width : (k + 1) * width]
        mean = exact_dot(values * values, heads) * (1.0 / HD)
        scaled = values * spread_heads(lax.rsqrt(mean + 1e-06), heads) * r.gains[k : k + 1, :]
        return scaled * r.cosine[...] + swap_pairs(scaled) * r.sine[...]

    def project(k):
        r.need_tile((A.triple, k))
        return jnp.dot(
            lifted_low, r.triple[:, k * width : (k + 1) * width], preferred_element_type=F32
        )

    r.raw[:, width:] = project(1)
    r.fetch(A.mixing, A.expand, A.reduce)
    r.need(A.gains, A.cosine, A.sine)
    r.kv[0, mine] = prepared(1).astype(BF16)
    r.kv[1, mine] = project(2).astype(BF16)
    share = pltpu.make_async_remote_copy(
        r.kv.at[:, mine], r.kv.at[:, mine], ssem.at[0], rsem.at[0], device_id=sibling,
        device_id_type=MESH,
    )
    share.start()
    r.raw[:, :width] = project(0)
    r.emit(A.raw)
    r.queries[...] = prepared(0).astype(BF16)
    r.emit(A.queries)
    r.xt1[...] = turned(lifted_low.astype(F32))
    r.emit(A.xt1)
    r.need(A.seg_q, A.seg_k, A.pad_k)
    allowed = allowed_mask(r.seg_q, r.seg_k, r.pad_k, half)
    r.lift[...] = jnp.zeros_like(r.lift)
    lane = lax.broadcasted_iota(jnp.int32, (half, 128), 1)
    sums = jnp.zeros((half, 128), F32)
    pltpu.make_async_remote_copy(
        r.kv.at[:, theirs], r.kv.at[:, theirs], ssem.at[0], rsem.at[0], device_id=sibling,
        device_id_type=MESH,
    ).wait_recv()
    r.emit(A.kv)
    for h in range(width // HD):
        first, unused = window(h, width)
        span = slice(first, first + 256)
        mask = head_mask(h, width, half)
        query = jnp.where(mask, r.queries[:, span].astype(F32), 0.0).astype(BF16)
        scores = dense_back(query, r.kv[0, :, span]) * (1.0 / math.sqrt(HD))
        scores = jnp.where(allowed, scores, -1e30)
        top = jnp.max(scores, axis=1, keepdims=True)
        raised = jnp.exp(scores - top)
        total = jnp.sum(raised, axis=1, keepdims=True)
        low = (raised / total).astype(BF16)
        out = jnp.dot(low, r.kv[1, :, span], preferred_element_type=F32)
        r.lift[:, span] = r.lift[:, span] + jnp.where(mask, out, 0.0)
        sums = jnp.where(lane == h, top + jnp.log(total), sums)
    r.lse[...] = sums
    r.emit(A.lse)
    mixed_low = r.lift[...].astype(BF16)
    r.xtm[...] = turned(mixed_low.astype(F32))
    r.emit(A.xtm)
    r.need(A.mixing)
    r.attended[...] = jnp.dot(mixed_low, r.mixing[...], preferred_element_type=F32)
    r.emit(A.attended)
    r.resid[...] = r.flat[...] + part(2) * r.attended[...]
    r.emit(A.resid)
    normed, unused = normalize(r.resid[...])
    lifted_low = (normed * (1.0 + part(4)) + part(3)).astype(BF16)
    r.xt2[...] = turned(lifted_low.astype(F32))
    r.emit(A.xt2)
    r.feed[...] = jnp.zeros_like(r.feed)
    r.need(A.expand, A.reduce)
    xth = (r.xth0, r.xth1, r.xth2)
    for g in range(3):
        xth[g][...] = jnp.zeros_like(xth[g])
    for t in range(hidden_size // FF_TILE):
        one = slice(t * FF_TILE, (t + 1) * FF_TILE)
        two = slice(hidden_size + t * FF_TILE, hidden_size + (t + 1) * FF_TILE)
        gate = jnp.dot(lifted_low, r.expand[:, one], preferred_element_type=F32)
        up = jnp.dot(lifted_low, r.expand[:, two], preferred_element_type=F32)
        r.expanded[:, one] = gate
        r.expanded[:, two] = up
        hidden = (gate * jax.nn.sigmoid(gate) * up).astype(BF16)
        pieces = hidden.astype(F32).T.astype(BF16).reshape(FF_TILE // 192, 3, 64, half)
        for g in range(3):
            xth[g][t * (FF_TILE // 192) : (t + 1) * (FF_TILE // 192), :64] = pieces[:, g]
        r.feed[...] = r.feed[...] + jnp.dot(hidden, r.reduce[one], preferred_element_type=F32)
    r.emit(A.expanded, A.feed, A.xth0, A.xth1, A.xth2)
    r.output[...] = r.resid[...] + part(5) * r.feed[...]
    r.emit(A.output)
    share.wait_send()


def backward_body(r, sibling, ssem, rsem):
    half, width = r.flat.shape
    c = lax.axis_index("ctx")
    mine = pl.ds(pl.multiple_of(c * half, 128), half)
    theirs = pl.ds(pl.multiple_of((1 - c) * half, 128), half)
    hidden_size = r.reduce.shape[0]

    def part(k):
        return r.mod[:, k * width : (k + 1) * width]

    def keep(k, values):
        r.grad_mod[:, k * width : (k + 1) * width] = values.astype(BF16)

    r.need(A.grad_out, A.feed, A.mod)
    keep(5, r.grad_out[...] * r.feed[...])
    feed_low = (r.grad_out[...] * part(5)).astype(BF16)
    r.grad_feed[...] = feed_low
    r.emit(A.grad_feed)
    r.lift[...] = jnp.zeros_like(r.lift)
    for t in range(hidden_size // FF_TILE):
        r.need_tile(t)
        if r.more and t + 2 < hidden_size // FF_TILE:
            r.more(t + 2)
        if t == 2:
            r.fetch(A.attended, A.resid, A.mixing, A.queries, A.kv, A.lse, A.raw, A.flat, A.triple)
        one = slice(t * FF_TILE, (t + 1) * FF_TILE)
        two = slice(hidden_size + t * FF_TILE, hidden_size + (t + 1) * FF_TILE)
        grad_hidden = dense_back(feed_low, r.reduce[one])
        gate = r.expanded[:, one]
        up = r.expanded[:, two]
        sig = jax.nn.sigmoid(gate)
        grad_gate = (grad_hidden * up * (sig * (1.0 + gate * (1.0 - sig)))).astype(BF16)
        grad_up = (grad_hidden * (gate * sig)).astype(BF16)
        r.grad_expanded[:, one] = grad_gate
        r.grad_expanded[:, two] = grad_up
        r.lift[...] = r.lift[...] + dense_back(grad_gate, r.expand[:, one])
        r.lift[...] = r.lift[...] + dense_back(grad_up, r.expand[:, two])
    r.emit(A.grad_expanded)
    r.need(A.resid, A.attended)
    normed, inverse = normalize(r.resid[...])
    keep(3, r.lift[...])
    keep(4, r.lift[...] * normed)
    grad_resid = r.grad_out[...] + norm_back(normed, inverse, r.lift[...] * (1.0 + part(4)))
    keep(2, grad_resid * r.attended[...])
    if A.output in r.stores:
        r.stores.pop(A.output).wait()
    r.grad_flat[...] = grad_resid
    attended_low = (grad_resid * part(2)).astype(BF16)
    r.grad_attended[...] = attended_low
    r.emit(A.grad_attended)
    r.need(A.mixing)
    r.lift[...] = dense_back(attended_low, r.mixing[...])
    r.need(A.seg_q, A.seg_k, A.pad_k, A.queries, A.kv, A.lse)
    allowed = allowed_mask(r.seg_q, r.seg_k, r.pad_k, half)
    r.feed[...] = jnp.zeros_like(r.feed)
    r.resid[...] = jnp.zeros_like(r.resid)
    r.attended[...] = jnp.zeros_like(r.attended)
    r.grad_v[...] = jnp.zeros_like(r.grad_v)
    scale = 1.0 / math.sqrt(HD)
    lane = lax.broadcasted_iota(jnp.int32, (half, 128), 1)
    for h in range(width // HD):
        first, unused = window(h, width)
        span = slice(first, first + 256)
        mask = head_mask(h, width, half)
        query = jnp.where(mask, r.queries[:, span].astype(F32), 0.0).astype(BF16)
        grad_mixed = jnp.where(mask, r.lift[:, span], 0.0).astype(BF16)
        scores = dense_back(query, r.kv[0, :, span]) * scale
        logsum = jnp.sum(jnp.where(lane == h, r.lse[...], 0.0), axis=1, keepdims=True)
        chances = jnp.exp(jnp.where(allowed, scores, -1e30) - logsum)
        grad_chances = dense_back(grad_mixed, r.kv[1, :, span])
        along = jnp.sum(chances * grad_chances, axis=1, keepdims=True)
        scores_low = (chances * (grad_chances - along)).astype(BF16)
        out = jnp.dot(scores_low, r.kv[0, :, span], preferred_element_type=F32)
        r.feed[:, span] = r.feed[:, span] + jnp.where(mask, out, 0.0)
        part_k = outer_sum(scores_low, query)
        r.resid[:, span] = r.resid[:, span] + part_k[:half]
        r.attended[:, span] = r.attended[:, span] + part_k[half:]
        r.grad_v[:, span] = r.grad_v[:, span] + outer_sum(chances.astype(BF16), grad_mixed)
    their_k = jnp.where(c == 0, r.attended[...], r.resid[...])
    r.outgoing[0] = (their_k * scale).astype(BF16)
    r.outgoing[1] = r.grad_v[theirs, :].astype(BF16)
    share = pltpu.make_async_remote_copy(
        r.outgoing, r.incoming, ssem.at[1], rsem.at[1], device_id=sibling, device_id_type=MESH
    )
    share.start()
    heads = head_sum_matrix(width)
    r.need(A.raw, A.gains, A.cosine, A.sine)

    def prepare_back(k, grad):
        values = r.raw[:, k * width : (k + 1) * width]
        gain = r.gains[k : k + 1, :]
        mean = exact_dot(values * values, heads) * (1.0 / HD)
        inverse = spread_heads(lax.rsqrt(mean + 1e-06), heads)
        scaled = values * inverse
        turned_back = grad * r.cosine[...] + swap_pairs(grad * r.sine[...])
        r.gains_grad[k : k + 1, :] = jnp.sum(turned_back * scaled, axis=0, keepdims=True)
        turned_back = turned_back * gain
        along = spread_heads(exact_dot(turned_back * scaled, heads) * (1.0 / HD), heads)
        return (turned_back - scaled * along) * inverse

    r.grad_projected[:, :width] = prepare_back(0, r.feed[...] * scale).astype(BF16)
    r.need(A.triple)
    total = dense_back(r.grad_projected[:, :width], r.triple[:, :width])
    share.wait()
    own_k = jnp.where(c == 0, r.resid[...], r.attended[...]) * scale
    own_k = own_k.astype(BF16).astype(F32) + r.incoming[0].astype(F32)
    own_v = r.grad_v[mine, :].astype(BF16).astype(F32) + r.incoming[1].astype(F32)
    r.grad_projected[:, width : 2 * width] = prepare_back(1, own_k).astype(BF16)
    r.grad_projected[:, 2 * width :] = own_v.astype(BF16)
    r.emit(A.grad_projected, A.gains_grad)
    for k in (1, 2):
        span = slice(k * width, (k + 1) * width)
        total = total + dense_back(r.grad_projected[:, span], r.triple[:, span])
    r.need(A.flat)
    normed, inverse = normalize(r.flat[...])
    keep(0, total)
    keep(1, total * normed)
    r.emit(A.grad_mod)
    r.need(A.marks)
    for k in range(6):
        span = slice(k * width, (k + 1) * width)
        r.mark_sums[:, span] = jnp.dot(
            r.marks[...], r.grad_mod[:, span], preferred_element_type=F32
        )
    r.emit(A.mark_sums)
    r.grad_flat[...] = r.grad_flat[...] + norm_back(normed, inverse, total * (1.0 + part(1)))
    r.emit(A.grad_flat)


def block_shapes(half, width, hidden_size):
    rows = ((16, PADDED, half), BF16)
    token = ((half, width), F32)
    low = ((half, width), BF16)
    return {
        A.flat: token,
        A.mod: ((half, 6 * width), F32),
        A.gains: ((2, width), F32),
        A.cosine: token,
        A.sine: token,
        A.seg_q: ((half, 1), jnp.int32),
        A.seg_k: ((1, 2 * half), jnp.int32),
        A.pad_k: ((1, 2 * half), jnp.int32),
        A.triple: ((width, 3 * width), BF16),
        A.mixing: ((width, width), BF16),
        A.expand: ((width, 2 * hidden_size), BF16),
        A.reduce: ((hidden_size, width), BF16),
        A.output: token,
        A.raw: ((half, 2 * width), F32),
        A.queries: low,
        A.kv: ((2, 2 * half, width), BF16),
        A.lse: ((half, 128), F32),
        A.attended: token,
        A.resid: token,
        A.expanded: ((half, 2 * hidden_size), F32),
        A.feed: token,
        A.xt1: rows,
        A.xtm: rows,
        A.xt2: rows,
        A.xth0: rows,
        A.xth1: rows,
        A.xth2: rows,
        A.lift: token,
        A.grad_out: token,
        A.grad_flat: token,
        A.grad_mod: ((half, 6 * width), BF16),
        A.grad_feed: low,
        A.grad_expanded: ((half, 2 * hidden_size), BF16),
        A.grad_attended: low,
        A.grad_projected: ((half, 3 * width), BF16),
        A.gains_grad: ((2, width), F32),
        A.grad_v: ((2 * half, width), F32),
        A.outgoing: ((2, half, width), BF16),
        A.incoming: ((2, half, width), BF16),
        A.marks: ((8, half), BF16),
        A.mark_sums: ((8, 6 * width), F32),
    }


WEIGHTS = (A.triple, A.mixing, A.expand, A.reduce)
GIVEN = (A.gains, A.cosine, A.sine, A.seg_q, A.seg_k, A.pad_k) + WEIGHTS
SAVED = (A.raw, A.queries, A.kv, A.lse, A.attended, A.resid, A.expanded, A.feed)
LEFTS = (A.xt1, A.xtm, A.xt2, A.xth0, A.xth1, A.xth2)
GRADS = (
    A.grad_flat, A.grad_mod, A.grad_feed, A.grad_expanded, A.grad_attended, A.grad_projected,
    A.gains_grad, A.mark_sums,
)
WORK = (A.grad_v, A.outgoing, A.incoming)
EARLY = (A.gains, A.cosine, A.sine, A.seg_q, A.seg_k, A.pad_k)
PLANS = {
    "forward": ((A.flat, A.mod) + GIVEN, (A.output,) + SAVED + LEFTS, (A.lift,)),
    "backward": ((A.grad_out, A.marks, A.flat, A.mod) + GIVEN + SAVED, GRADS, (A.lift,) + WORK),
    "both": ((A.grad_out, A.marks, A.flat, A.mod) + GIVEN, (A.output,) + LEFTS + GRADS, SAVED + (A.lift,) + WORK),
}


def held_names(kind):
    inputs, outputs, others = PLANS[kind]
    names = inputs + outputs + others
    return tuple(n for n in names if kind != "both" or n != A.output)


def block_kernel(kind, *refs):
    inputs, outputs, others = PLANS[kind]
    sources = dict(zip(inputs, refs))
    targets = dict(zip(outputs, refs[len(inputs) :]))
    names = held_names(kind)
    held = dict(zip(names, refs[len(inputs) + len(outputs) :]))
    if kind == "both":
        held[A.output] = held[A.grad_flat]
    lsem, wsem, tsem, ssem, rsem = refs[len(inputs) + len(outputs) + len(names) :]
    r = Traffic(held, sources, targets, lsem, wsem)
    if kind == "backward":
        r.fetch(A.grad_out, A.feed, A.mod, A.marks, *EARLY)
        r.more = functools.partial(r.fetch_tile, FF_TILE, (A.reduce,), (A.expanded, A.expand), tsem)
        r.more(0)
        r.more(1)
    else:
        r.fetch(A.flat, A.mod, *EARLY)
        r.fetch_parts(A.triple, r.flat.shape[1], (1, 2, 0), tsem)
    sibling = meet_sibling()
    if kind != "backward":
        forward_body(r, sibling, ssem, rsem)
    if kind == "both":
        r.fetch(A.grad_out, A.marks)
        r.loads = {n: r.loads[n] for n in (A.grad_out, A.marks)}
    if kind != "forward":
        backward_body(r, sibling, ssem, rsem)
    r.close()


def run_block(kind, values, name):
    inputs, outputs, others = PLANS[kind]
    half, width = values[A.flat].shape
    table = block_shapes(half, width, values[A.reduce].shape[0])
    names = held_names(kind)
    results = pl.pallas_call(
        functools.partial(block_kernel, kind),
        name=name,
        out_shape=[jax.ShapeDtypeStruct(*table[n]) for n in outputs],
        in_specs=[ANY] * len(inputs),
        out_specs=[ANY] * len(outputs),
        scratch_shapes=[pltpu.VMEM(*table[n]) for n in names]
        + [DMA((len(inputs),)), DMA((len(outputs),)), DMA((4, 5)), DMA((2,)), DMA((2,))],
        compiler_params=pltpu.CompilerParams(
            collective_id={"forward": 5, "backward": 6, "both": 7}[kind],
            has_side_effects=True,
            vmem_limit_bytes=63 * 1024 * 1024,
        ),
    )(*[values[n] for n in inputs])
    return dict(zip(outputs, results))


def split_kernel(pieces, in_ref, *refs):
    *outs, held, arrived, left = refs
    for k, (n, row, rows, columns, at) in enumerate(pieces):
        span = (pl.ds(0, rows), pl.ds(at, columns))
        pltpu.make_async_copy(in_ref.at[span], held.at[span], arrived.at[k]).start()

    def leave(k):
        n, row, rows, columns, at = pieces[k]
        span = (pl.ds(0, rows), pl.ds(at, columns))
        return pltpu.make_async_copy(held.at[span], outs[n].at[pl.ds(row, rows), :], left.at[k])

    for k, (n, row, rows, columns, at) in enumerate(pieces):
        span = (pl.ds(0, rows), pl.ds(at, columns))
        pltpu.make_async_copy(in_ref.at[span], held.at[span], arrived.at[k]).wait()
        leave(k).start()
    for k in range(len(pieces)):
        leave(k).wait()


def split(values, shapes, pieces):
    return pl.pallas_call(
        functools.partial(split_kernel, tuple(pieces)),
        name="split",
        out_shape=[jax.ShapeDtypeStruct(shape, values.dtype) for shape in shapes],
        in_specs=[ANY],
        out_specs=[ANY] * len(shapes),
        scratch_shapes=[
            pltpu.VMEM(values.shape, values.dtype),
            DMA((len(pieces),)),
            DMA((len(pieces),)),
        ],
        compiler_params=pltpu.CompilerParams(vmem_limit_bytes=62 * 1024 * 1024),
    )(values)


def rope_lanes(cosine, sine):
    tokens = cosine.shape[0]

    def lanes(table, signs):
        table = jnp.stack([signs[0] * table, signs[1] * table], axis=2).reshape(tokens, 1, HD)
        return jnp.broadcast_to(table, (tokens, HEADS, HD)).reshape(tokens, HEADS * HD)

    return lanes(cosine, (1.0, 1.0)), lanes(sine, (-1.0, 1.0))


def fast_reduce(blocks, rows, collective_id, name):
    xts = []
    dys = []
    source = []
    for factors, extra in blocks:
        for lefts, right in factors:
            source += [len(dys)] * len(lefts)
            xts += lefts
            dys.append(right)
        tokens = right.shape[0]
        lines = -(-extra.shape[1] // tokens)
        packed = jnp.pad(extra, ((0, 0), (0, lines * tokens - extra.shape[1])))
        packed = packed.reshape(16, lines, tokens).astype(BF16)
        xts.append(jnp.pad(packed, ((0, 0), (0, PADDED - lines), (0, 0))))
        source.append(len(dys))
        dys.append(jnp.eye(tokens, UNIT, dtype=BF16))
    out, rows = scatter(xts, dys, source, rows, collective_id, name)
    shapes = []
    pieces = []
    smalls = []
    at = 0
    for factors, extra in blocks:
        for lefts, right in factors[:-1]:
            pieces.append((len(shapes), 0, ROWS, right.shape[1], at))
            shapes.append((ROWS, right.shape[1]))
            at += right.shape[1]
        width = factors[-1][1].shape[1]
        for g in range(3):
            pieces.append((len(shapes), 64 * g, 64, width, at))
            at += width
        shapes.append((192, width))
        lines = -(-extra.shape[1] // tokens)
        smalls.append(out[:lines, at : at + tokens].reshape(-1)[: extra.shape[1]])
        at += UNIT
    grads = split(out, shapes, pieces)
    results = []
    for (factors, extra), small in zip(blocks, smalls):
        results.append((grads[: len(factors)], small))
        grads = grads[len(factors) :]
    return results, rows


def whole_rows(gathered):
    return gathered.reshape((-1,) + gathered.shape[4:])


def fast_step(flat, cotangent, context, segment_local, valid, timesteps, encoder, decoder):
    width = flat.shape[1]
    offset_size = encoder[1].shape[0]
    gain_size = 2 * encoder[3].shape[1]
    small = jnp.concatenate(
        [
            encoder[1].astype(F32),
            decoder[1].astype(F32),
            encoder[3].astype(F32).reshape(-1),
            decoder[3].astype(F32).reshape(-1),
            timesteps.astype(F32).reshape(-1),
        ]
    )
    size = small.shape[0]
    small = jnp.pad(small, (0, 2048 - size)).reshape(16, 128)
    small = exchange(small, 0, "small").reshape(16, -1)
    encoder_offset = small[:, :offset_size].reshape(-1)
    decoder_offset = small[:, offset_size : 2 * offset_size].reshape(-1)
    at = 2 * offset_size
    encoder_gains = small[:, at : at + gain_size].reshape(16, 2, -1).swapaxes(0, 1).reshape(2, -1)
    at += gain_size
    decoder_gains = small[:, at : at + gain_size].reshape(16, 2, -1).swapaxes(0, 1).reshape(2, -1)
    at += gain_size
    all_times = small[:, at : at + timesteps.size]
    segments = timesteps.shape[1]
    picks = (segment_local[..., None] == jnp.arange(segments, dtype=jnp.int32)).astype(F32)
    picks = picks.reshape(-1, segments)

    all_cond = embed_times(all_times, width).reshape(-1, width)
    act_rows = jax.nn.silu(all_cond).astype(BF16)
    me = lax.axis_index("dp")
    rows = encoder[0].shape[0]
    act_mine = lax.dynamic_slice_in_dim(act_rows, me * rows, rows, 1)
    core = lax.axis_index("ctx")
    share = encoder[0].shape[1] // 2
    partial = dense(act_mine, lax.dynamic_slice_in_dim(encoder[0], core * share, share, 1))
    partial = partial.reshape(GRID + (8, -1))
    shards = (encoder[2], encoder[4], encoder[5], encoder[6])
    shards += (decoder[0], decoder[2], decoder[4], decoder[5], decoder[6])
    *wholes, partial = gather(shards, partial, *gather_units(shards), 1, "gather")
    wholes = [whole_rows(w) for w in wholes]
    encoder_weights = (*wholes[:4], encoder_gains)
    modulate = wholes[4]
    decoder_weights = (*wholes[5:], decoder_gains)
    partial = jnp.sum(partial, axis=0).reshape(segments, -1)
    others = lax.ppermute(partial, "ctx", [(0, 1), (1, 0)])
    modulation_rows = jnp.where(
        core == 0,
        jnp.concatenate([partial, others], axis=1),
        jnp.concatenate([others, partial], axis=1),
    )
    modulation_rows = modulation_rows + encoder_offset

    def pick(rows):
        return sum(jnp.where(picks[:, j : j + 1] > 0, rows[j], 0.0) for j in range(segments))

    encoder_modulation = pick(modulation_rows)
    cond_rows = lax.dynamic_slice_in_dim(all_cond, me * segments, segments, 0)
    cond = pick(cond_rows)

    shared = {**dict(zip(EARLY[1:], context)), A.flat: flat}
    encoder_in = {**dict(zip(WEIGHTS + EARLY[:1], encoder_weights)), **shared}
    encoder_in[A.mod] = encoder_modulation
    forward = run_block("forward", encoder_in, "encoder")
    decoder_modulation, decoder_pre, latent, act_xt = decoder_modulation_of(
        forward[A.output], valid, cond, decoder_offset, modulate
    )
    decoder_in = {**dict(zip(WEIGHTS + EARLY[:1], decoder_weights)), **shared}
    decoder_in[A.mod] = decoder_modulation
    decoder_in[A.grad_out] = valid * cotangent
    decoder_in[A.marks] = jnp.ones((8, flat.shape[0]), BF16)
    both = run_block("both", decoder_in, "decoder")
    velocity = valid * both[A.output]

    def pair_up(lefts, grads):
        return (
            ([lefts[A.xt1]], grads[A.grad_projected]),
            ([lefts[A.xtm]], grads[A.grad_attended]),
            ([lefts[A.xt2]], grads[A.grad_expanded]),
            ([lefts[A.xth0], lefts[A.xth1], lefts[A.xth2]], grads[A.grad_feed]),
        )

    factors = pair_up(both, both)
    grad_modulation = both[A.grad_mod]
    gains_grad = both[A.gains_grad]
    grad_latent = modulation_back(grad_modulation, valid, decoder_pre, modulate)
    offset_grad = both[A.mark_sums][0]
    extra = jnp.concatenate(
        [
            offset_grad.reshape(16, -1),
            gains_grad.reshape(2, 16, -1).swapaxes(0, 1).reshape(16, -1),
        ],
        axis=1,
    )
    first = ([act_xt], grad_modulation)
    decoder_block = ((factors[1], factors[0], factors[2], first, factors[3]), extra)

    encoder_in[A.grad_out] = grad_latent
    encoder_in[A.marks] = jnp.pad(picks.T, ((0, 8 - segments), (0, 0))).astype(BF16)
    backward = run_block("backward", {**encoder_in, **forward}, "encoder_back")
    factors = pair_up(forward, backward)
    grad_modulation = backward[A.grad_mod]
    gains_grad = backward[A.gains_grad]
    grad_rows = backward[A.mark_sums][:segments]
    grad_rows = grad_rows + lax.ppermute(grad_rows, "ctx", [(0, 1), (1, 0)])
    extra = gains_grad.reshape(2, 16, -1).swapaxes(0, 1).reshape(16, -1)
    results, all_rows = fast_reduce(
        (decoder_block, (factors, extra)), grad_rows.astype(BF16).reshape(16, -1), 2, "scatter"
    )
    (grads, small), (encoder_parts, encoder_small) = results
    decoder_grads = (
        grads[3],
        small[:offset_size],
        grads[1],
        small[offset_size:].reshape(2, -1),
        grads[0],
        grads[2],
        grads[4],
    )
    all_rows = all_rows.reshape(16 * segments, -1)
    modulate_grad = outer_sum(act_mine, all_rows)
    offset_grad = lax.dynamic_slice_in_dim(
        jnp.sum(all_rows.astype(F32), axis=0), me * offset_size, offset_size, 0
    )
    encoder_grads = (
        modulate_grad,
        offset_grad,
        encoder_parts[0],
        encoder_small.reshape(2, -1),
        encoder_parts[1],
        encoder_parts[2],
        encoder_parts[3],
    )
    token_grad = both[A.grad_flat] + backward[A.grad_flat]
    return velocity, latent, token_grad, encoder_grads, decoder_grads


def plain_gather(block):
    parts = [lax.all_gather(block[k], "dp", axis=0, tiled=True) for k in (0, 1, 2, 4, 5, 6)]
    gains = lax.all_gather(block[3], "dp", axis=1, tiled=True).astype(F32)
    modulate, offset, triple, mixing, expand, reduce_w = parts
    return modulate, offset.astype(F32), (triple, mixing, expand, reduce_w, gains)


def plain_reduce(factors, grad_modulation, gains_grad):
    def rows(values, dim=0):
        part = lax.psum_scatter(values, "dp", scatter_dimension=dim, tiled=True)
        return lax.psum(part.astype(BF16), "ctx").astype(F32)

    offset = rows(jnp.sum(grad_modulation, axis=0, dtype=F32))
    modulate, triple, mixing, expand, reduce_w = [rows(outer_sum(a, b)) for a, b in factors]
    return modulate, offset, triple, rows(gains_grad, 1), mixing, expand, reduce_w


def plain_step(flat, cotangent, context, segment_local, valid, timesteps, encoder, decoder):
    picks = (
        segment_local[..., None] == jnp.arange(timesteps.shape[-1], dtype=jnp.int32)
    ).astype(F32)
    times = jnp.sum(picks * timesteps[:, None, :].astype(F32), axis=-1)
    cond = embed_times(times, flat.shape[1]).reshape(flat.shape)
    modulate, offset, encoder_weights = plain_gather(encoder)
    encoder_act = jax.nn.silu(cond).astype(BF16)
    encoder_out, encoder_kept = block_forward(
        flat, dense(encoder_act, modulate) + offset, encoder_weights, context
    )
    latent_full = valid * encoder_out
    decoder_pre = latent_full + cond
    decoder_act = jax.nn.silu(decoder_pre).astype(BF16)
    modulate, offset, decoder_weights = plain_gather(decoder)
    decoder_out, decoder_kept = block_forward(
        flat, dense(decoder_act, modulate) + offset, decoder_weights, context
    )
    decoder_flat, grad_modulation, factors, gains_grad = block_backward(
        valid * cotangent, decoder_kept, decoder_weights, context
    )
    grad_act = dense_back(grad_modulation, modulate)
    decoder_grads = plain_reduce(
        ((decoder_act, grad_modulation),) + factors, grad_modulation, gains_grad
    )
    unused_silu, silu_pull = jax.vjp(jax.nn.silu, decoder_pre)
    encoder_flat, grad_modulation, factors, gains_grad = block_backward(
        valid * silu_pull(grad_act)[0], encoder_kept, encoder_weights, context
    )
    encoder_grads = plain_reduce(
        ((encoder_act, grad_modulation),) + factors, grad_modulation, gains_grad
    )
    return valid * decoder_out, latent_full, decoder_flat + encoder_flat, encoder_grads, decoder_grads


def local(fast, tokens, cotangent, segment, rows, columns, padding, timesteps, *weights):
    batch, half, width = tokens.shape
    start = lax.axis_index("ctx") * half
    segment_local = lax.dynamic_slice_in_dim(segment, start, half, 1)
    rows_local = lax.dynamic_slice_in_dim(rows, start, half, 1)
    columns_local = lax.dynamic_slice_in_dim(columns, start, half, 1)
    padding_local = lax.dynamic_slice_in_dim(padding, start, half, 1)
    place_query = start + jnp.arange(half, dtype=jnp.int32)
    place_key = jnp.arange(segment.shape[1], dtype=jnp.int32)
    allowed = (segment_local[:, :, None] == segment[:, None, :]) & (
        (padding[:, None, :] == 0) | (place_query[None, :, None] == place_key[None, None, :])
    )
    cosine, sine = rope_tables(rows_local.reshape(-1), columns_local.reshape(-1))
    context = (batch, half, allowed, cosine, sine)
    if fast:
        context = rope_lanes(cosine, sine)
        context += (segment_local.reshape(-1, 1), segment, padding)
    valid = (1 - padding_local).astype(F32).reshape(-1, 1)
    flat = tokens.reshape(-1, width).astype(F32)
    step = fast_step if fast else plain_step
    velocity, latent, token_grad, encoder_grads, decoder_grads = step(
        flat,
        cotangent.reshape(-1, width).astype(F32),
        context,
        segment_local,
        valid,
        timesteps,
        weights[:7],
        weights[7:],
    )
    return (
        velocity.astype(BF16).reshape(batch, half, width),
        latent.astype(BF16).reshape(batch, half, width),
        token_grad.reshape(batch, half, width),
        *encoder_grads,
        *decoder_grads,
    )


def solution(mesh):
    fast = dict(mesh.shape) == {"dp": math.prod(GRID), "ctx": 2}
    block = (
        P("dp", None),
        P("dp"),
        P("dp", None),
        P(None, "dp"),
        P("dp", None),
        P("dp", None),
        P("dp", None),
    )
    slots = P("dp", "ctx", None)
    return jax.shard_map(
        functools.partial(local, fast),
        mesh=mesh,
        in_specs=(slots, slots) + (P("dp", None),) * 5 + block + block,
        out_specs=(slots, slots, slots) + block + block,
        check_vma=False,
    )
```
